32 devices in a mesh: depth: 4 (over y, x), scan: 8 (over z, core).
Axes of the slice: x: 2, y: 2, z: 4, core: 2. Of those that a mesh axis runs over, the one named last changes fastest.
Arguments:
- transmission: float32 [4, 2, 1024, 1024], P('depth', None, 'scan'), may hold values from 0.4 to 1
- probe_wave: float32 [2, 256, 256], replicated, may hold values from -5 to 5
- prop_phase: float32 [256, 256], replicated, may hold values from -3.140625 to 3.140625
- measured: float32 [32, 256, 256], P('scan'), may hold values from 0.2 to 2
- scan_rows: int32 [32], P('scan'), may hold values from 0 to 127
- scan_cols: int32 [32], P('scan'), may hold values from 0 to 768
- live_counts: int32 [8], P('scan'), may hold values from 1 to 4, 20 in all
Outputs:
- object_grad: float32 [4, 2, 1024, 1024], P('depth', None, 'scan')
The draws below stay inside these ranges and needn't reach their ends.
Inputs may be any that keep to these rules, and one draw needn't show every extreme that they name: `live_counts`: the largest count equals 4.
All inputs are finite; a program needn't handle non-finite values. No bound on the sum of `live_counts` on one device may be relied on, other than what follows from the above.
Results may differ from the reference program's by a relative error of at most 0.035.
Values may be sent and summed in bfloat16 or wider, within the bound.
No kernel may reach another device: no remote copies, remote signals or barrier semaphores. Data moves between devices by JAX's collectives and lax.ppermute only.
A program may use at most 64 MiB of HBM per device.

```python
import math
import jax
import jax.numpy as jnp
import numpy as np
from jax import lax

W = 256
P_DEV = 4
TILE = 128
OCOLS = 1024
SLICES = 4
PROBES = 32
NROWS = 1024
N_SCAN = 8


def with_ends(drawn, own_key, smallest, high):
    extent = drawn.shape
    index_at = [jax.random.randint(jax.random.fold_in(own_key, axis), (), 0, extent[axis]) for axis in range(len(extent))]
    drawn = drawn.at[tuple(index_at)].set(smallest)
    longest = extent.index(max(extent))
    index_at[longest] = (index_at[longest] + 1) % extent[longest]
    return drawn.at[tuple(index_at)].set(high)


def block_levels(rng, extent, pieces, smallest, largest):
    gain = 1.0
    for axis_at, shards_of in pieces:
        steps = jax.random.uniform(jax.random.fold_in(jax.random.fold_in(rng, 6), axis_at), (shards_of,), jnp.float32, smallest / len(pieces), largest / len(pieces))
        gain = gain * jnp.repeat(jnp.exp(steps), extent[axis_at] // shards_of).reshape((-1,) + (1,) * (len(extent) - 1 - axis_at))
    return gain


def profile(count, total, bound, lean):
    portions = [(1 << 20) // math.isqrt(grade ** lean) + 1 for grade in range(2, count + 1)]
    rest, counts = total - bound - (count - 1), [1] * (count - 1)
    while rest > 0:
        candidates = [i for i in range(count - 1) if counts[i] < bound]
        whole, budget = sum([portions[i] for i in candidates]), rest
        for i in candidates:
            addition = min(bound - counts[i], max(1, budget * portions[i] // whole), rest)
            counts[i] = counts[i] + addition
            rest = rest - addition
    return np.array([bound] + counts)


def ragged_sizes(own_key, count, total, limit, slope):
    if count == 2:
        one = jax.random.randint(own_key, (), max(1, total - limit), min(limit, total - 1) + 1)
        return jnp.stack([one, total - one])
    lengths = jnp.asarray(profile(count, total, limit, slope), jnp.int32)
    pairs = (count - 1) // 2
    source_of, sink = lengths[1:1 + 2 * pairs:2], lengths[2:2 + 2 * pairs:2]
    slack = jnp.minimum(source_of - 1, limit - sink)
    passed = jax.random.randint(jax.random.fold_in(own_key, 1), (pairs,), 0, 1 << 20) % (slack + 1)
    lengths = lengths.at[1:1 + 2 * pairs:2].set(source_of - passed).at[2:2 + 2 * pairs:2].set(sink + passed)
    return lengths[jax.random.permutation(jax.random.fold_in(own_key, 2), count)]


def gaussian(rng, dims, spread, limit, kind=jnp.bfloat16):
    return jnp.clip(spread * jax.random.normal(rng, dims, jnp.float32), -limit, limit).astype(kind)


def setup_inputs(seed: int = 0) -> dict:
    arg_keys = jax.random.split(jax.random.key(seed), 8)
    transmission = jnp.clip(0.4 + 0.6 * jax.random.uniform(arg_keys[0], (SLICES, 2, NROWS, OCOLS), jnp.float32) ** block_levels(arg_keys[0], (SLICES, 2, NROWS, OCOLS), ((0, 4), (2, 8)), -0.2, 0.2), 0.4, 1.0)
    probe_wave = gaussian(arg_keys[1], (2, W, W), 0.7, 5.0, jnp.float32)
    prop_phase = jnp.clip(jax.random.uniform(arg_keys[2], (W, W), jnp.float32, -3.140625, 3.140625), -3.140625, 3.140625)
    measured = jnp.clip(0.2 + 1.8 * jax.random.uniform(arg_keys[3], (PROBES, W, W), jnp.float32) ** block_levels(arg_keys[3], (PROBES, W, W), ((0, 8),), -0.2, 0.2), 0.2, 2.0)
    scan_rows = with_ends(jax.random.randint(arg_keys[4], (PROBES,), 0, TILE), jax.random.fold_in(arg_keys[4], 1), 0, TILE - 1).astype(jnp.int32)
    scan_cols = with_ends(jax.random.randint(arg_keys[5], (PROBES,), 0, OCOLS - W + 1), jax.random.fold_in(arg_keys[5], 1), 0, OCOLS - W).astype(jnp.int32)
    live_counts = ragged_sizes(arg_keys[6], N_SCAN, N_SCAN * P_DEV * 5 // 8, P_DEV, 2).astype(jnp.int32)
    return {"transmission": transmission, "probe_wave": probe_wave, "prop_phase": prop_phase, "measured": measured, "scan_rows": scan_rows, "scan_cols": scan_cols, "live_counts": live_counts}


epsilon = 1.0

def dft_tables(pixels):
    indices = jnp.arange(pixels, dtype=jnp.int32)
    product = indices[:, None] * indices[None, :] % pixels
    angles = product.astype(jnp.float32) * (2.0 * math.pi / pixels)
    norm_scale = 1.0 / math.sqrt(pixels)
    return ((jnp.cos(angles) * norm_scale).astype(jnp.bfloat16), (-jnp.sin(angles) * norm_scale).astype(jnp.bfloat16))

def transform2d(values, table_re, table_im):
    hp = lax.Precision.HIGHEST
    vals = values.astype(jnp.float32)
    left_re = jnp.einsum('jk,bckl->bcjl', table_re.astype(jnp.float32), vals, precision=hp)
    left_im = jnp.einsum('jk,bckl->bcjl', table_im.astype(jnp.float32), vals, precision=hp)
    inner = jnp.stack([left_re[:, 0] - left_im[:, 1], left_re[:, 1] + left_im[:, 0]], axis=1).astype(jnp.bfloat16)
    inner = inner.astype(jnp.float32)
    right_re = jnp.einsum('bcjk,kl->bcjl', inner, table_re.astype(jnp.float32), precision=hp)
    right_im = jnp.einsum('bcjk,kl->bcjl', inner, table_im.astype(jnp.float32), precision=hp)
    return (right_re[:, 0] - right_im[:, 1], right_re[:, 1] + right_im[:, 0])

def advance(wave, patch, table_re, table_im, prop_re, prop_im):
    wave32 = wave.astype(jnp.float32)
    chi = jnp.stack([patch[:, 0] * wave32[:, 0] - patch[:, 1] * wave32[:, 1], patch[:, 0] * wave32[:, 1] + patch[:, 1] * wave32[:, 0]], axis=1).astype(jnp.bfloat16)
    spec_re, spec_im = transform2d(chi, table_re, table_im)
    turned = jnp.stack([spec_re * prop_re - spec_im * prop_im, spec_re * prop_im + spec_im * prop_re], axis=1).astype(jnp.bfloat16)
    out_re, out_im = transform2d(turned, table_re, -table_im)
    return jnp.stack([out_re, out_im], axis=1).astype(jnp.bfloat16)

def retreat(adjoint, patch, incident, table_re, table_im, prop_re, prop_im):
    back_re, back_im = transform2d(adjoint, table_re, table_im)
    turned = jnp.stack([back_re * prop_re + back_im * prop_im, back_im * prop_re - back_re * prop_im], axis=1).astype(jnp.bfloat16)
    mu_re, mu_im = transform2d(turned, table_re, -table_im)
    inc = incident.astype(jnp.float32)
    contrib = jnp.stack([inc[:, 0] * mu_re + inc[:, 1] * mu_im, inc[:, 0] * mu_im - inc[:, 1] * mu_re], axis=1)
    onward = jnp.stack([patch[:, 0] * mu_re + patch[:, 1] * mu_im, patch[:, 0] * mu_im - patch[:, 1] * mu_re], axis=1).astype(jnp.bfloat16)
    return (contrib, onward)

def detector(leaving, measured, live_mask, table_re, table_im):
    far_re, far_im = transform2d(leaving, table_re, table_im)
    modulus = jnp.sqrt(far_re * far_re + far_im * far_im + epsilon)
    factor = live_mask[:, None, None] * (1.0 - measured / modulus)
    resid = jnp.stack([factor * far_re, factor * far_im], axis=1).astype(jnp.bfloat16)
    start_re, start_im = transform2d(resid, table_re, -table_im)
    return jnp.stack([start_re, start_im], axis=1).astype(jnp.bfloat16)

def reference(transmission, probe_wave, prop_phase, measured, scan_rows, scan_cols, live_counts):
    pixels = probe_wave.shape[-1]
    slices_all = transmission.shape[0]
    nrows_all = transmission.shape[2]
    table_re, table_im = dft_tables(pixels)
    prop_re = jnp.cos(prop_phase)
    prop_im = jnp.sin(prop_phase)
    extended = jnp.concatenate([transmission, transmission[:, :, :pixels]], axis=2)
    probe_b = probe_wave.astype(jnp.bfloat16)[None]
    slot_ids = jnp.arange(PROBES, dtype=jnp.int32)
    tile_ids = slot_ids // P_DEV
    live_mask = (slot_ids - tile_ids * P_DEV < live_counts[tile_ids]).astype(jnp.float32)
    row_base = (tile_ids * TILE + scan_rows).astype(jnp.int32)
    zero_idx = jnp.zeros((), jnp.int32)

    def one_probe(gradient, probe_item):
        row_start, col_start, amplitude, live_flag = probe_item
        wave = probe_b
        patches = []
        incidents = []
        for slice_no in range(slices_all):
            patch = lax.dynamic_slice(extended[slice_no], (zero_idx, row_start, col_start), (2, pixels, pixels))[None]
            patches.append(patch)
            incidents.append(wave)
            wave = advance(wave, patch, table_re, table_im, prop_re, prop_im)
        adjoint = detector(wave, amplitude[None], live_flag[None], table_re, table_im)
        for slice_no in range(slices_all - 1, -1, -1):
            contrib, adjoint = retreat(adjoint, patches[slice_no], incidents[slice_no], table_re, table_im, prop_re, prop_im)
            where_at = (jnp.asarray(slice_no, jnp.int32), zero_idx, row_start, col_start)
            current = lax.dynamic_slice(gradient, where_at, (1, 2, pixels, pixels))
            gradient = lax.dynamic_update_slice(gradient, current + contrib, where_at)
        return (gradient, None)
    start_grad = jnp.zeros((slices_all, 2, nrows_all + pixels, transmission.shape[3]), jnp.float32)
    gradient, _ = lax.scan(one_probe, start_grad, (row_base, scan_cols, measured, live_mask))
    folded = gradient[:, :, :nrows_all]
    overflow = gradient[:, :, nrows_all:]
    return folded.at[:, :, :pixels].add(overflow)
```

```python
import functools
import math

import jax
import jax.numpy as jnp
import ml_dtypes
import numpy as np
from jax import lax
from jax.experimental import pallas as pl
from jax.experimental.pallas import tpu as pltpu
from jax.sharding import PartitionSpec as P

epsilon = 1.0
bf16 = jnp.bfloat16
f32 = jnp.float32
VMEM = pl.BlockSpec(memory_space=pltpu.VMEM)
SMEM = pl.BlockSpec(memory_space=pltpu.SMEM)
LIMIT = 48 * 1024 * 1024


def shifted(value, axis, steps):
    count = lax.axis_size(axis)
    pairs = [(source, (source + steps) % count) for source in range(count)]
    return lax.ppermute(value, axis, pairs)


def exchanged(value, axis, flip):
    count = lax.axis_size(axis)
    return lax.ppermute(value, axis, [(source, source ^ flip) for source in range(count)])


def split_tables(pixels):
    indices = np.arange(pixels)
    angles = (indices[:, None] * indices[None, :] % pixels) * (2.0 * math.pi / pixels)
    norm_scale = 1.0 / math.sqrt(pixels)
    table_re = (np.cos(angles) * norm_scale).astype(np.float32).astype(ml_dtypes.bfloat16)
    table_im = (-np.sin(angles) * norm_scale).astype(np.float32).astype(ml_dtypes.bfloat16)
    return np.concatenate([table_re[0::2], table_im[0::2], table_re[1::2], table_im[1::2]], axis=0)


def parity_order(pixels):
    order = np.concatenate([np.arange(0, pixels, 2), np.arange(1, pixels, 2)])
    return (order[:, None] == np.arange(pixels)[None, :]).astype(np.float32)


def call(kernel, out_shape, args, specs, scratch=(), flops=0, transcendentals=0, name=None):
    outs = out_shape if isinstance(out_shape, (list, tuple)) else [out_shape]
    moved = sum(math.prod(a.shape) * a.dtype.itemsize for a in list(args) + list(outs))
    return pl.pallas_call(
        kernel,
        out_shape=out_shape,
        in_specs=specs,
        out_specs=jax.tree.map(lambda _: VMEM, out_shape),
        scratch_shapes=list(scratch),
        compiler_params=pltpu.CompilerParams(vmem_limit_bytes=LIMIT),
        cost_estimate=pl.CostEstimate(
            flops=flops, bytes_accessed=moved, transcendentals=transcendentals
        ),
        name=name,
    )(*args)


def sds(shape, dtype):
    return jax.ShapeDtypeStruct(shape, dtype)


def column_place(info, slots, slot, width, columns):
    col = info[slots + slot]
    base = (col // width) * width
    after = jnp.minimum(base + width, columns - width)
    return pl.multiple_of(base, width), pl.multiple_of(after, width), col - base


def iotas(rows, cols):
    return (
        lax.broadcasted_iota(jnp.int32, (rows, cols), 0),
        lax.broadcasted_iota(jnp.int32, (rows, cols), 1),
    )


def center_kernel(slots, width, info, own, *outs):
    depth_index = lax.axis_index("depth")
    columns = own.shape[-1]
    _, lane = iotas(own.shape[1], width)
    for flip in range(len(outs)):
        base, after, first = column_place(info, slots, depth_index ^ flip, width, columns)
        for comp in range(2):
            outs[flip][comp] = jnp.where(
                lane >= first, own[comp, :, pl.ds(base, width)], own[comp, :, pl.ds(after, width)]
            ).astype(bf16)


def edge_kernel(slots, width, info, upper, lower, *outs):
    depth_index = lax.axis_index("depth")
    columns = upper.shape[-1]
    row, lane = iotas(upper.shape[1], width)
    for flip in range(len(outs)):
        slot = depth_index ^ flip
        base, after, first = column_place(info, slots, slot, width, columns)
        from_upper = row >= info[slot]
        from_base = lane >= first
        for comp in range(2):
            at_base = jnp.where(
                from_upper,
                upper[comp, :, pl.ds(base, width)].astype(f32),
                lower[comp, :, pl.ds(base, width)].astype(f32),
            )
            at_after = jnp.where(
                from_upper,
                upper[comp, :, pl.ds(after, width)].astype(f32),
                lower[comp, :, pl.ds(after, width)].astype(f32),
            )
            outs[flip][comp] = jnp.where(from_base, at_base, at_after).astype(bf16)


def frequency_kernel(phase, order, order_t, measured, prop_re, prop_im, amplitude):
    def reorder(value):
        rows = jnp.dot(
            order[...], value, preferred_element_type=f32, precision=lax.Precision.HIGHEST
        )
        return jnp.dot(
            rows, order_t[...], preferred_element_type=f32, precision=lax.Precision.HIGHEST
        )

    turned = reorder(phase[...])
    prop_re[...] = jnp.cos(turned)
    prop_im[...] = jnp.sin(turned)
    amplitude[...] = reorder(measured[lax.axis_index("depth")]).astype(bf16)


def table_kernel(slots, info, stack, stack_t, probe, psi0, *tables):
    depth_index = lax.axis_index("depth")
    pixels = probe.shape[-1]
    half = pixels // 2
    row_shift = info[depth_index]
    col_shift = lax.rem(info[slots + depth_index], pixels)

    def shift_matrix(rows, cols, shift, transposed):
        row, lane = iotas(rows, cols)
        offset = (lane - row if transposed else row - lane) + shift
        return jnp.where((offset == 0) | (offset == pixels), 1.0, 0.0).astype(bf16)

    def pair(shift):
        cols = jnp.dot(
            stack[...], shift_matrix(pixels, half, shift, False), preferred_element_type=f32
        )
        rows = jnp.dot(
            shift_matrix(half, pixels, shift, True), stack_t[...], preferred_element_type=f32
        )
        forms, forms_t = [], []
        for parity in range(2):
            at = 2 * parity * half
            re, im = cols[at : at + half], cols[at + half : at + pixels]
            top = jnp.concatenate([re, -im], axis=1)
            bottom = jnp.concatenate([im, re], axis=1)
            forms.append(jnp.concatenate([top, bottom], axis=0).astype(bf16))
            re, im = rows[:, at : at + half], rows[:, at + half : at + pixels]
            top = jnp.concatenate([re, im], axis=1)
            bottom = jnp.concatenate([-im, re], axis=1)
            forms_t.append(jnp.concatenate([top, bottom], axis=0).astype(bf16))
        return forms, forms_t

    row_forms, row_forms_t = pair(row_shift)
    col_forms, col_forms_t = pair(col_shift)
    made = row_forms + col_forms_t + col_forms + row_forms_t
    for ref, value in zip(tables, made):
        ref[...] = value
    down = shift_matrix(pixels, pixels, row_shift, True)
    across = shift_matrix(pixels, pixels, col_shift, False)
    for comp in range(2):
        moved = jnp.dot(down, probe[comp].astype(bf16), preferred_element_type=f32).astype(bf16)
        psi0[comp] = jnp.dot(moved, across, preferred_element_type=f32).astype(bf16)


def wave_kernel(slots, depth_count, info, prop_re, prop_im, amplitude, psi0, *refs):
    tables = refs[:8]
    centers = refs[8 : 8 + depth_count]
    edges = refs[8 + depth_count : 8 + 2 * depth_count]
    out_centers = refs[8 + 2 * depth_count : 8 + 3 * depth_count]
    out_edges = refs[8 + 3 * depth_count : 8 + 4 * depth_count]
    patches, waves, adjoint, grads = refs[8 + 4 * depth_count :]
    depth_index = lax.axis_index("depth")
    pixels = psi0.shape[-1]
    half = pixels // 2
    live = depth_index < info[2 * slots]
    fwd_row_e, fwd_row_o, fwd_col_e, fwd_col_o, inv_col_e, inv_col_o, inv_row_e, inv_row_o = tables

    def dot(left, right):
        return jnp.dot(left, right, preferred_element_type=f32)

    def propagate(x_re, x_im, at_frequency):
        def rows_of(sign):
            mixed = [v[:half] + v[half:] if sign > 0 else v[:half] - v[half:] for v in (x_re, x_im)]
            return jnp.concatenate(mixed, axis=0).astype(bf16)

        u_even = dot(fwd_row_e[...], rows_of(1))
        u_odd = dot(fwd_row_o[...], rows_of(-1))

        def cols_of(sign):
            parts = []
            for u in (u_even, u_odd):
                mixed = u[:, :half] + u[:, half:] if sign > 0 else u[:, :half] - u[:, half:]
                parts.append(jnp.concatenate([mixed[:half], mixed[half:]], axis=1))
            return jnp.concatenate(parts, axis=0).astype(bf16)

        v_even = dot(cols_of(1), fwd_col_e[...])
        v_odd = dot(cols_of(-1), fwd_col_o[...])
        b_even = at_frequency(v_even[:, :half], v_even[:, half:], slice(0, half))
        b_odd = at_frequency(v_odd[:, :half], v_odd[:, half:], slice(half, pixels))
        w_even = dot(jnp.concatenate(b_even, axis=1).astype(bf16), inv_col_e[...])
        w_odd = dot(jnp.concatenate(b_odd, axis=1).astype(bf16), inv_col_o[...])
        w_low, w_high = w_even + w_odd, w_even - w_odd
        w_re = jnp.concatenate([w_low[:, :half], w_high[:, :half]], axis=1)
        w_im = jnp.concatenate([w_low[:, half:], w_high[:, half:]], axis=1)
        y_even = dot(
            inv_row_e[...], jnp.concatenate([w_re[:half], w_im[:half]], axis=0).astype(bf16)
        )
        y_odd = dot(
            inv_row_o[...], jnp.concatenate([w_re[half:], w_im[half:]], axis=0).astype(bf16)
        )
        low, high = y_even + y_odd, y_even - y_odd
        return (
            jnp.concatenate([low[:half], high[:half]], axis=0),
            jnp.concatenate([low[half:], high[half:]], axis=0),
        )

    def turn(re, im, cols):
        p_re, p_im = prop_re[:, cols], prop_im[:, cols]
        return [re * p_re - im * p_im, re * p_im + im * p_re]

    def turn_back(re, im, cols):
        p_re, p_im = prop_re[:, cols], prop_im[:, cols]
        return [re * p_re + im * p_im, im * p_re - re * p_im]

    def residual(re, im, cols):
        modulus = jnp.sqrt(re * re + im * im + epsilon)
        factor = 1.0 - amplitude[:, cols].astype(f32) / modulus
        return [factor * re, factor * im]

    def pair_of(ref, index):
        return ref[index, 0].astype(f32), ref[index, 1].astype(f32)

    @pl.when(live)
    def _():
        for flip in range(depth_count):
            patches[depth_index ^ flip, :, half:] = centers[flip][...]
            patches[depth_index ^ flip, :, :half] = edges[flip][...]
        waves[0] = psi0[...]

        def forward(k, carry):
            t_re, t_im = pair_of(patches, k)
            p_re, p_im = pair_of(waves, k)
            n_re, n_im = propagate(t_re * p_re - t_im * p_im, t_re * p_im + t_im * p_re, turn)
            waves[k + 1, 0] = n_re.astype(bf16)
            waves[k + 1, 1] = n_im.astype(bf16)
            return carry

        lax.fori_loop(0, depth_count, forward, 0)
        l_re, l_im = propagate(*pair_of(waves, depth_count), residual)
        adjoint[0, 0] = l_re.astype(bf16)
        adjoint[0, 1] = l_im.astype(bf16)

        def backward(step, carry):
            k = depth_count - 1 - step
            m_re, m_im = propagate(*pair_of(adjoint, 0), turn_back)
            t_re, t_im = pair_of(patches, k)
            p_re, p_im = pair_of(waves, k)
            grads[k ^ depth_index, 0] = (p_re * m_re + p_im * m_im).astype(bf16)
            grads[k ^ depth_index, 1] = (p_re * m_im - p_im * m_re).astype(bf16)
            adjoint[0, 0] = (t_re * m_re + t_im * m_im).astype(bf16)
            adjoint[0, 1] = (t_re * m_im - t_im * m_re).astype(bf16)
            return carry

        lax.fori_loop(0, depth_count, backward, 0)
        for flip in range(depth_count):
            out_centers[flip][...] = grads[flip, :, half:]
            out_edges[flip][...] = grads[flip, :, :half]

    @pl.when(jnp.logical_not(live))
    def _():
        for ref in out_centers + out_edges:
            ref[...] = jnp.zeros(ref.shape, ref.dtype)


def place_edges_kernel(slots, info, *refs):
    pieces, (upper, lower, upper_sum, lower_sum) = refs[:-4], refs[-4:]
    depth_index = lax.axis_index("depth")
    columns = upper.shape[-1]
    width = pieces[0].shape[-1]
    row, lane = iotas(pieces[0].shape[1], width)
    upper_sum[...] = jnp.zeros(upper_sum.shape, f32)
    lower_sum[...] = jnp.zeros(lower_sum.shape, f32)
    for flip, piece in enumerate(pieces):
        slot = depth_index ^ flip
        base, after, first = column_place(info, slots, slot, width, columns)
        to_upper = row >= info[slot]
        to_base = lane >= first
        for comp in range(2):
            value = piece[comp].astype(f32)
            for sheet, kept in (
                (upper_sum, jnp.where(to_upper, value, 0.0)),
                (lower_sum, jnp.where(to_upper, 0.0, value)),
            ):
                sheet[comp, :, pl.ds(base, width)] += jnp.where(to_base, kept, 0.0)
                sheet[comp, :, pl.ds(after, width)] += jnp.where(to_base, 0.0, kept)
    upper[...] = upper_sum[...].astype(bf16)
    lower[...] = lower_sum[...].astype(bf16)


def place_center_kernel(slots, info, *refs):
    pieces, sheet = refs[:-1], refs[-1]
    depth_index = lax.axis_index("depth")
    columns = sheet.shape[-1]
    width = pieces[0].shape[-1]
    _, lane = iotas(pieces[0].shape[1], width)
    sheet[...] = jnp.zeros(sheet.shape, f32)
    for flip, piece in enumerate(pieces):
        base, after, first = column_place(info, slots, depth_index ^ flip, width, columns)
        to_base = lane >= first
        for comp in range(2):
            value = piece[comp].astype(f32)
            sheet[comp, :, pl.ds(base, width)] += jnp.where(to_base, value, 0.0)
            sheet[comp, :, pl.ds(after, width)] += jnp.where(to_base, 0.0, value)


def body(transmission, probe_wave, prop_phase, measured, scan_rows, scan_cols, live_counts):
    pixels = probe_wave.shape[-1]
    slots = measured.shape[0]
    rows = transmission.shape[2]
    columns = transmission.shape[3]
    count = lax.axis_size("depth")
    own = transmission[0]
    info = shifted(jnp.concatenate([scan_rows, scan_cols, live_counts]), "scan", 1)
    strip = own.astype(bf16)
    upper = shifted(strip, "scan", 1)
    lower = shifted(strip, "scan", -1)

    part = sds((2, rows, pixels), bf16)
    centers = call(
        functools.partial(center_kernel, slots, pixels),
        [part] * count, [info, own], [SMEM, VMEM], name="cut_center",
    )
    centers = [centers[0]] + [exchanged(centers[flip], "depth", flip) for flip in range(1, count)]

    order = parity_order(pixels)
    square = sds((pixels, pixels), f32)
    prop_re, prop_im, amplitude = call(
        frequency_kernel,
        [square, square, sds((pixels, pixels), bf16)],
        [prop_phase, jnp.asarray(order), jnp.asarray(order.T), measured],
        [VMEM] * 4, flops=24 * pixels**3, transcendentals=2 * pixels**2, name="frequency_order",
    )
    amplitude = shifted(amplitude, "scan", 1)

    stack = split_tables(pixels)
    made = call(
        functools.partial(table_kernel, slots),
        [sds((2, pixels, pixels), bf16)] + [sds((pixels, pixels), bf16)] * 8,
        [info, jnp.asarray(stack), jnp.asarray(stack.T), probe_wave],
        [SMEM, VMEM, VMEM, VMEM], flops=16 * pixels**3, name="tables",
    )
    edges = call(
        functools.partial(edge_kernel, slots, pixels),
        [part] * count, [info, upper, lower], [SMEM, VMEM, VMEM], name="cut_edges",
    )
    edges = [edges[0]] + [exchanged(edges[flip], "depth", flip) for flip in range(1, count)]

    args = [info, prop_re, prop_im, amplitude, *made, *centers, *edges]
    grads = call(
        functools.partial(wave_kernel, slots, count),
        [part] * (2 * count), args, [SMEM] + [VMEM] * (len(args) - 1),
        scratch=[
            pltpu.VMEM((count, 2, pixels, pixels), bf16),
            pltpu.VMEM((count + 1, 2, pixels, pixels), bf16),
            pltpu.VMEM((1, 2, pixels, pixels), bf16),
            pltpu.VMEM((count, 2, pixels, pixels), bf16),
        ],
        flops=(2 * count + 1) * 16 * pixels**3, name="waves",
    )
    out_centers, out_edges = grads[:count], grads[count:]
    out_edges = [out_edges[0]] + [
        exchanged(out_edges[flip], "depth", flip) for flip in range(1, count)
    ]
    out_centers = [out_centers[0]] + [
        exchanged(out_centers[flip], "depth", flip) for flip in range(1, count)
    ]
    sheet_bf16 = sds((2, rows, columns), bf16)
    sheet_f32 = sds((2, rows, columns), f32)
    to_upper, to_lower = call(
        functools.partial(place_edges_kernel, slots),
        [sheet_bf16, sheet_bf16], [info, *out_edges], [SMEM] + [VMEM] * count,
        scratch=[pltpu.VMEM(sheet_f32.shape, f32)] * 2, name="place_edges",
    )
    from_next = shifted(to_upper, "scan", -1)
    from_previous = shifted(to_lower, "scan", 1)
    sheet = call(
        functools.partial(place_center_kernel, slots),
        sheet_f32, [info, *out_centers], [SMEM] + [VMEM] * count, name="place_center",
    )
    gradient = sheet + from_next.astype(f32) + from_previous.astype(f32)
    return gradient[None]


def solution(mesh):
    in_specs = (
        P("depth", None, "scan", None),
        P(),
        P(),
        P("scan", None, None),
        P("scan"),
        P("scan"),
        P("scan"),
    )
    out_specs = P("depth", None, "scan", None)
    return jax.shard_map(body, mesh=mesh, in_specs=in_specs, out_specs=out_specs, check_vma=False)
```

```python
import functools
import math

import jax
import jax.numpy as jnp
import ml_dtypes
import numpy as np
from jax import lax
from jax.experimental import pallas as pl
from jax.experimental.pallas import tpu as pltpu
from jax.sharding import PartitionSpec as P

epsilon = 1.0
bf16 = jnp.bfloat16
f32 = jnp.float32
VMEM = pl.BlockSpec(memory_space=pltpu.VMEM)
SMEM = pl.BlockSpec(memory_space=pltpu.SMEM)
LIMIT = 48 * 1024 * 1024


def shifted(value, axis, steps):
    count = lax.axis_size(axis)
    pairs = [(source, (source + steps) % count) for source in range(count)]
    return lax.ppermute(value, axis, pairs)


def exchanged(value, axis, flip):
    count = lax.axis_size(axis)
    return lax.ppermute(value, axis, [(source, source ^ flip) for source in range(count)])


def split_tables(pixels):
    indices = np.arange(pixels)
    angles = (indices[:, None] * indices[None, :] % pixels) * (2.0 * math.pi / pixels)
    norm_scale = 1.0 / math.sqrt(pixels)
    table_re = (np.cos(angles) * norm_scale).astype(np.float32).astype(ml_dtypes.bfloat16)
    table_im = (-np.sin(angles) * norm_scale).astype(np.float32).astype(ml_dtypes.bfloat16)
    return np.concatenate([table_re[0::2], table_im[0::2], table_re[1::2], table_im[1::2]], axis=0)


def parity_order(pixels):
    order = np.concatenate([np.arange(0, pixels, 2), np.arange(1, pixels, 2)])
    return (order[:, None] == np.arange(pixels)[None, :]).astype(np.float32)


def call(kernel, out_shape, args, specs, scratch=(), flops=0, transcendentals=0, name=None):
    outs = out_shape if isinstance(out_shape, (list, tuple)) else [out_shape]
    moved = sum(math.prod(a.shape) * a.dtype.itemsize for a in list(args) + list(outs))
    return pl.pallas_call(
        kernel,
        out_shape=out_shape,
        in_specs=specs,
        out_specs=jax.tree.map(lambda _: VMEM, out_shape),
        scratch_shapes=list(scratch),
        compiler_params=pltpu.CompilerParams(vmem_limit_bytes=LIMIT),
        cost_estimate=pl.CostEstimate(
            flops=flops, bytes_accessed=moved, transcendentals=transcendentals
        ),
        name=name,
    )(*args)


def sds(shape, dtype):
    return jax.ShapeDtypeStruct(shape, dtype)


def column_place(info, slots, slot, width, columns):
    col = info[slots + slot]
    base = (col // width) * width
    after = jnp.minimum(base + width, columns - width)
    return pl.multiple_of(base, width), pl.multiple_of(after, width), col - base


def iotas(rows, cols):
    return (
        lax.broadcasted_iota(jnp.int32, (rows, cols), 0),
        lax.broadcasted_iota(jnp.int32, (rows, cols), 1),
    )


def strip_kernel(own, strip):
    strip[...] = own[...].astype(bf16)


def center_kernel(slots, width, info, own, *outs):
    depth_index = lax.axis_index("depth")
    columns = own.shape[-1]
    _, lane = iotas(own.shape[1], width)
    for flip in range(len(outs)):
        base, after, first = column_place(info, slots, depth_index ^ flip, width, columns)
        for comp in range(2):
            outs[flip][comp] = jnp.where(
                lane >= first, own[comp, :, pl.ds(base, width)], own[comp, :, pl.ds(after, width)]
            ).astype(bf16)


def edge_kernel(slots, width, info, upper, lower, *outs):
    depth_index = lax.axis_index("depth")
    columns = upper.shape[-1]
    row, lane = iotas(upper.shape[1], width)
    for flip in range(len(outs)):
        slot = depth_index ^ flip
        base, after, first = column_place(info, slots, slot, width, columns)
        from_upper = row >= info[slot]
        from_base = lane >= first
        for comp in range(2):
            at_base = jnp.where(
                from_upper,
                upper[comp, :, pl.ds(base, width)].astype(f32),
                lower[comp, :, pl.ds(base, width)].astype(f32),
            )
            at_after = jnp.where(
                from_upper,
                upper[comp, :, pl.ds(after, width)].astype(f32),
                lower[comp, :, pl.ds(after, width)].astype(f32),
            )
            outs[flip][comp] = jnp.where(from_base, at_base, at_after).astype(bf16)


def frequency_kernel(phase, order, order_t, measured, prop_re, prop_im, amplitude):
    def reorder(value):
        rows = jnp.dot(
            order[...], value, preferred_element_type=f32, precision=lax.Precision.HIGHEST
        )
        return jnp.dot(
            rows, order_t[...], preferred_element_type=f32, precision=lax.Precision.HIGHEST
        )

    turned = reorder(phase[...])
    prop_re[...] = jnp.cos(turned)
    prop_im[...] = jnp.sin(turned)
    amplitude[...] = reorder(measured[lax.axis_index("depth")]).astype(bf16)


def table_kernel(slots, info, stack, stack_t, probe, psi0, *tables):
    depth_index = lax.axis_index("depth")
    pixels = probe.shape[-1]
    half = pixels // 2
    row_shift = info[depth_index]
    col_shift = lax.rem(info[slots + depth_index], pixels)

    def shift_matrix(rows, cols, shift, transposed):
        row, lane = iotas(rows, cols)
        offset = (lane - row if transposed else row - lane) + shift
        return jnp.where((offset == 0) | (offset == pixels), 1.0, 0.0).astype(bf16)

    def pair(shift):
        cols = jnp.dot(
            stack[...], shift_matrix(pixels, half, shift, False), preferred_element_type=f32
        )
        rows = jnp.dot(
            shift_matrix(half, pixels, shift, True), stack_t[...], preferred_element_type=f32
        )
        forms, forms_t = [], []
        for parity in range(2):
            at = 2 * parity * half
            re, im = cols[at : at + half], cols[at + half : at + pixels]
            top = jnp.concatenate([re, -im], axis=1)
            bottom = jnp.concatenate([im, re], axis=1)
            forms.append(jnp.concatenate([top, bottom], axis=0).astype(bf16))
            re, im = rows[:, at : at + half], rows[:, at + half : at + pixels]
            top = jnp.concatenate([re, im], axis=1)
            bottom = jnp.concatenate([-im, re], axis=1)
            forms_t.append(jnp.concatenate([top, bottom], axis=0).astype(bf16))
        return forms, forms_t

    row_forms, row_forms_t = pair(row_shift)
    col_forms, col_forms_t = pair(col_shift)
    made = row_forms + col_forms_t + col_forms + row_forms_t
    for ref, value in zip(tables, made):
        ref[...] = value
    down = shift_matrix(pixels, pixels, row_shift, True)
    across = shift_matrix(pixels, pixels, col_shift, False)
    for comp in range(2):
        moved = jnp.dot(down, probe[comp].astype(bf16), preferred_element_type=f32).astype(bf16)
        psi0[comp] = jnp.dot(moved, across, preferred_element_type=f32).astype(bf16)


def wave_kernel(slots, depth_count, info, prop_re, prop_im, amplitude, psi0, *refs):
    tables = refs[:8]
    centers = refs[8 : 8 + depth_count]
    edges = refs[8 + depth_count : 8 + 2 * depth_count]
    out_centers = refs[8 + 2 * depth_count : 8 + 3 * depth_count]
    out_edges = refs[8 + 3 * depth_count : 8 + 4 * depth_count]
    patches, waves, adjoint, grads = refs[8 + 4 * depth_count :]
    depth_index = lax.axis_index("depth")
    pixels = psi0.shape[-1]
    half = pixels // 2
    live = depth_index < info[2 * slots]
    fwd_row_e, fwd_row_o, fwd_col_e, fwd_col_o, inv_col_e, inv_col_o, inv_row_e, inv_row_o = tables

    def dot(left, right):
        return jnp.dot(left, right, preferred_element_type=f32)

    def propagate(x_re, x_im, at_frequency):
        def rows_of(sign):
            mixed = [v[:half] + v[half:] if sign > 0 else v[:half] - v[half:] for v in (x_re, x_im)]
            return jnp.concatenate(mixed, axis=0).astype(bf16)

        u_even = dot(fwd_row_e[...], rows_of(1))
        u_odd = dot(fwd_row_o[...], rows_of(-1))

        def cols_of(sign):
            parts = []
            for u in (u_even, u_odd):
                mixed = u[:, :half] + u[:, half:] if sign > 0 else u[:, :half] - u[:, half:]
                parts.append(jnp.concatenate([mixed[:half], mixed[half:]], axis=1))
            return jnp.concatenate(parts, axis=0).astype(bf16)

        v_even = dot(cols_of(1), fwd_col_e[...])
        v_odd = dot(cols_of(-1), fwd_col_o[...])
        b_even = at_frequency(v_even[:, :half], v_even[:, half:], slice(0, half))
        b_odd = at_frequency(v_odd[:, :half], v_odd[:, half:], slice(half, pixels))
        w_even = dot(jnp.concatenate(b_even, axis=1).astype(bf16), inv_col_e[...])
        w_odd = dot(jnp.concatenate(b_odd, axis=1).astype(bf16), inv_col_o[...])
        w_low, w_high = w_even + w_odd, w_even - w_odd
        w_re = jnp.concatenate([w_low[:, :half], w_high[:, :half]], axis=1)
        w_im = jnp.concatenate([w_low[:, half:], w_high[:, half:]], axis=1)
        y_even = dot(
            inv_row_e[...], jnp.concatenate([w_re[:half], w_im[:half]], axis=0).astype(bf16)
        )
        y_odd = dot(
            inv_row_o[...], jnp.concatenate([w_re[half:], w_im[half:]], axis=0).astype(bf16)
        )
        low, high = y_even + y_odd, y_even - y_odd
        return (
            jnp.concatenate([low[:half], high[:half]], axis=0),
            jnp.concatenate([low[half:], high[half:]], axis=0),
        )

    def turn(re, im, cols):
        p_re, p_im = prop_re[:, cols], prop_im[:, cols]
        return [re * p_re - im * p_im, re * p_im + im * p_re]

    def turn_back(re, im, cols):
        p_re, p_im = prop_re[:, cols], prop_im[:, cols]
        return [re * p_re + im * p_im, im * p_re - re * p_im]

    def residual(re, im, cols):
        modulus = jnp.sqrt(re * re + im * im + epsilon)
        factor = 1.0 - amplitude[:, cols].astype(f32) / modulus
        return [factor * re, factor * im]

    def pair_of(ref, index):
        return ref[index, 0].astype(f32), ref[index, 1].astype(f32)

    @pl.when(live)
    def _():
        for flip in range(depth_count):
            patches[depth_index ^ flip, :, half:] = centers[flip][...]
            patches[depth_index ^ flip, :, :half] = edges[flip][...]
        waves[0] = psi0[...]

        def forward(k, carry):
            t_re, t_im = pair_of(patches, k)
            p_re, p_im = pair_of(waves, k)
            n_re, n_im = propagate(t_re * p_re - t_im * p_im, t_re * p_im + t_im * p_re, turn)
            waves[k + 1, 0] = n_re.astype(bf16)
            waves[k + 1, 1] = n_im.astype(bf16)
            return carry

        lax.fori_loop(0, depth_count, forward, 0)
        l_re, l_im = propagate(*pair_of(waves, depth_count), residual)
        adjoint[0, 0] = l_re.astype(bf16)
        adjoint[0, 1] = l_im.astype(bf16)

        def backward(step, carry):
            k = depth_count - 1 - step
            m_re, m_im = propagate(*pair_of(adjoint, 0), turn_back)
            t_re, t_im = pair_of(patches, k)
            p_re, p_im = pair_of(waves, k)
            grads[k ^ depth_index, 0] = (p_re * m_re + p_im * m_im).astype(bf16)
            grads[k ^ depth_index, 1] = (p_re * m_im - p_im * m_re).astype(bf16)
            adjoint[0, 0] = (t_re * m_re + t_im * m_im).astype(bf16)
            adjoint[0, 1] = (t_re * m_im - t_im * m_re).astype(bf16)
            return carry

        lax.fori_loop(0, depth_count, backward, 0)
        for flip in range(depth_count):
            out_centers[flip][...] = grads[flip, :, half:]
            out_edges[flip][...] = grads[flip, :, :half]

    @pl.when(jnp.logical_not(live))
    def _():
        for ref in out_centers + out_edges:
            ref[...] = jnp.zeros(ref.shape, ref.dtype)


def place_edges_kernel(slots, info, *refs):
    pieces, (upper, lower, upper_sum, lower_sum) = refs[:-4], refs[-4:]
    depth_index = lax.axis_index("depth")
    columns = upper.shape[-1]
    width = pieces[0].shape[-1]
    row, lane = iotas(pieces[0].shape[1], width)
    upper_sum[...] = jnp.zeros(upper_sum.shape, f32)
    lower_sum[...] = jnp.zeros(lower_sum.shape, f32)
    for flip, piece in enumerate(pieces):
        slot = depth_index ^ flip
        base, after, first = column_place(info, slots, slot, width, columns)
        to_upper = row >= info[slot]
        to_base = lane >= first
        for comp in range(2):
            value = piece[comp].astype(f32)
            for sheet, kept in (
                (upper_sum, jnp.where(to_upper, value, 0.0)),
                (lower_sum, jnp.where(to_upper, 0.0, value)),
            ):
                sheet[comp, :, pl.ds(base, width)] += jnp.where(to_base, kept, 0.0)
                sheet[comp, :, pl.ds(after, width)] += jnp.where(to_base, 0.0, kept)
    upper[...] = upper_sum[...].astype(bf16)
    lower[...] = lower_sum[...].astype(bf16)


def place_center_kernel(slots, info, *refs):
    pieces, sheet = refs[:-1], refs[-1]
    depth_index = lax.axis_index("depth")
    columns = sheet.shape[-1]
    width = pieces[0].shape[-1]
    _, lane = iotas(pieces[0].shape[1], width)
    sheet[...] = jnp.zeros(sheet.shape, f32)
    for flip, piece in enumerate(pieces):
        base, after, first = column_place(info, slots, depth_index ^ flip, width, columns)
        to_base = lane >= first
        for comp in range(2):
            value = piece[comp].astype(f32)
            sheet[comp, :, pl.ds(base, width)] += jnp.where(to_base, value, 0.0)
            sheet[comp, :, pl.ds(after, width)] += jnp.where(to_base, 0.0, value)


def body(transmission, probe_wave, prop_phase, measured, scan_rows, scan_cols, live_counts):
    pixels = probe_wave.shape[-1]
    slots = measured.shape[0]
    rows = transmission.shape[2]
    columns = transmission.shape[3]
    count = lax.axis_size("depth")
    own = transmission[0]
    info = lax.all_gather(jnp.concatenate([scan_rows, scan_cols, live_counts]), "scan")
    tile = lax.rem(lax.axis_index("scan") + lax.axis_size("scan") - 1, lax.axis_size("scan"))
    info = lax.dynamic_index_in_dim(info, tile, 0, keepdims=False)
    strip = call(strip_kernel, sds(own.shape, bf16), [own], [VMEM], name="strip")
    upper = shifted(strip, "scan", 1)
    lower = shifted(strip, "scan", -1)

    part = sds((2, rows, pixels), bf16)
    centers = call(
        functools.partial(center_kernel, slots, pixels),
        [part] * count, [info, own], [SMEM, VMEM], name="cut_center",
    )
    centers = [centers[0]] + [exchanged(centers[flip], "depth", flip) for flip in range(1, count)]

    order = parity_order(pixels)
    square = sds((pixels, pixels), f32)
    prop_re, prop_im, amplitude = call(
        frequency_kernel,
        [square, square, sds((pixels, pixels), bf16)],
        [prop_phase, jnp.asarray(order), jnp.asarray(order.T), measured],
        [VMEM] * 4, flops=24 * pixels**3, transcendentals=2 * pixels**2, name="frequency_order",
    )
    amplitude = shifted(amplitude, "scan", 1)

    stack = split_tables(pixels)
    made = call(
        functools.partial(table_kernel, slots),
        [sds((2, pixels, pixels), bf16)] + [sds((pixels, pixels), bf16)] * 8,
        [info, jnp.asarray(stack), jnp.asarray(stack.T), probe_wave],
        [SMEM, VMEM, VMEM, VMEM], flops=16 * pixels**3, name="tables",
    )
    edges = call(
        functools.partial(edge_kernel, slots, pixels),
        [part] * count, [info, upper, lower], [SMEM, VMEM, VMEM], name="cut_edges",
    )
    edges = [edges[0]] + [exchanged(edges[flip], "depth", flip) for flip in range(1, count)]

    args = [info, prop_re, prop_im, amplitude, *made, *centers, *edges]
    grads = call(
        functools.partial(wave_kernel, slots, count),
        [part] * (2 * count), args, [SMEM] + [VMEM] * (len(args) - 1),
        scratch=[
            pltpu.VMEM((count, 2, pixels, pixels), bf16),
            pltpu.VMEM((count + 1, 2, pixels, pixels), bf16),
            pltpu.VMEM((1, 2, pixels, pixels), bf16),
            pltpu.VMEM((count, 2, pixels, pixels), bf16),
        ],
        flops=(2 * count + 1) * 16 * pixels**3, name="waves",
    )
    out_centers, out_edges = grads[:count], grads[count:]
    out_edges = [out_edges[0]] + [
        exchanged(out_edges[flip], "depth", flip) for flip in range(1, count)
    ]
    out_centers = [out_centers[0]] + [
        exchanged(out_centers[flip], "depth", flip) for flip in range(1, count)
    ]
    sheet_bf16 = sds((2, rows, columns), bf16)
    sheet_f32 = sds((2, rows, columns), f32)
    to_upper, to_lower = call(
        functools.partial(place_edges_kernel, slots),
        [sheet_bf16, sheet_bf16], [info, *out_edges], [SMEM] + [VMEM] * count,
        scratch=[pltpu.VMEM(sheet_f32.shape, f32)] * 2, name="place_edges",
    )
    from_next = shifted(to_upper, "scan", -1)
    from_previous = shifted(to_lower, "scan", 1)
    sheet = call(
        functools.partial(place_center_kernel, slots),
        sheet_f32, [info, *out_centers], [SMEM] + [VMEM] * count, name="place_center",
    )
    gradient = sheet + from_next.astype(f32) + from_previous.astype(f32)
    return gradient[None]


def solution(mesh):
    in_specs = (
        P("depth", None, "scan", None),
        P(),
        P(),
        P("scan", None, None),
        P("scan"),
        P("scan"),
        P("scan"),
    )
    out_specs = P("depth", None, "scan", None)
    return jax.shard_map(body, mesh=mesh, in_specs=in_specs, out_specs=out_specs, check_vma=False)
```

```python
import functools
import math

import jax
import jax.numpy as jnp
import ml_dtypes
import numpy as np
from jax import lax
from jax.experimental import pallas as pl
from jax.experimental.pallas import tpu as pltpu
from jax.sharding import PartitionSpec as P

epsilon = 1.0
bf16 = jnp.bfloat16
f32 = jnp.float32
VMEM = pl.BlockSpec(memory_space=pltpu.VMEM)
SMEM = pl.BlockSpec(memory_space=pltpu.SMEM)
LIMIT = 48 * 1024 * 1024


def shifted(value, axis, steps):
    count = lax.axis_size(axis)
    pairs = [(source, (source + steps) % count) for source in range(count)]
    return lax.ppermute(value, axis, pairs)


def exchanged(value, axis, flip):
    count = lax.axis_size(axis)
    return lax.ppermute(value, axis, [(source, source ^ flip) for source in range(count)])


def split_tables(pixels):
    indices = np.arange(pixels)
    angles = (indices[:, None] * indices[None, :] % pixels) * (2.0 * math.pi / pixels)
    norm_scale = 1.0 / math.sqrt(pixels)
    table_re = (np.cos(angles) * norm_scale).astype(np.float32).astype(ml_dtypes.bfloat16)
    table_im = (-np.sin(angles) * norm_scale).astype(np.float32).astype(ml_dtypes.bfloat16)
    return np.concatenate([table_re[0::2], table_im[0::2], table_re[1::2], table_im[1::2]], axis=0)


def parity_order(pixels):
    order = np.concatenate([np.arange(0, pixels, 2), np.arange(1, pixels, 2)])
    return (order[:, None] == np.arange(pixels)[None, :]).astype(np.float32)


def call(kernel, out_shape, args, specs, scratch=(), flops=0, transcendentals=0, name=None):
    outs = out_shape if isinstance(out_shape, (list, tuple)) else [out_shape]
    moved = sum(math.prod(a.shape) * a.dtype.itemsize for a in list(args) + list(outs))
    return pl.pallas_call(
        kernel,
        out_shape=out_shape,
        in_specs=specs,
        out_specs=jax.tree.map(lambda _: VMEM, out_shape),
        scratch_shapes=list(scratch),
        compiler_params=pltpu.CompilerParams(vmem_limit_bytes=LIMIT),
        cost_estimate=pl.CostEstimate(
            flops=flops, bytes_accessed=moved, transcendentals=transcendentals
        ),
        name=name,
    )(*args)


def sds(shape, dtype):
    return jax.ShapeDtypeStruct(shape, dtype)


def column_place(info, slots, slot, width, columns):
    col = info[slots + slot]
    base = (col // width) * width
    after = jnp.minimum(base + width, columns - width)
    return pl.multiple_of(base, width), pl.multiple_of(after, width), col - base


def iotas(rows, cols):
    return (
        lax.broadcasted_iota(jnp.int32, (rows, cols), 0),
        lax.broadcasted_iota(jnp.int32, (rows, cols), 1),
    )


def strip_kernel(own, strip):
    strip[...] = own[...].astype(bf16)


def center_kernel(slots, width, info, own, *outs):
    depth_index = lax.axis_index("depth")
    columns = own.shape[-1]
    _, lane = iotas(own.shape[1], width)
    for flip in range(len(outs)):
        base, after, first = column_place(info, slots, depth_index ^ flip, width, columns)
        for comp in range(2):
            outs[flip][comp] = jnp.where(
                lane >= first, own[comp, :, pl.ds(base, width)], own[comp, :, pl.ds(after, width)]
            ).astype(bf16)


def edge_kernel(slots, width, info, upper, lower, *outs):
    depth_index = lax.axis_index("depth")
    columns = upper.shape[-1]
    row, lane = iotas(upper.shape[1], width)
    for flip in range(len(outs)):
        slot = depth_index ^ flip
        base, after, first = column_place(info, slots, slot, width, columns)
        from_upper = row >= info[slot]
        from_base = lane >= first
        for comp in range(2):
            at_base = jnp.where(
                from_upper,
                upper[comp, :, pl.ds(base, width)].astype(f32),
                lower[comp, :, pl.ds(base, width)].astype(f32),
            )
            at_after = jnp.where(
                from_upper,
                upper[comp, :, pl.ds(after, width)].astype(f32),
                lower[comp, :, pl.ds(after, width)].astype(f32),
            )
            outs[flip][comp] = jnp.where(from_base, at_base, at_after).astype(bf16)


def frequency_kernel(phase, order, order_t, measured, prop_re, prop_im, amplitude):
    def reorder(value):
        rows = jnp.dot(
            order[...], value, preferred_element_type=f32, precision=lax.Precision.HIGHEST
        )
        return jnp.dot(
            rows, order_t[...], preferred_element_type=f32, precision=lax.Precision.HIGHEST
        )

    turned = reorder(phase[...])
    prop_re[...] = jnp.cos(turned)
    prop_im[...] = jnp.sin(turned)
    amplitude[...] = reorder(measured[lax.axis_index("depth")]).astype(bf16)


def table_kernel(slots, info, stack, stack_t, probe, psi0, *tables):
    depth_index = lax.axis_index("depth")
    pixels = probe.shape[-1]
    half = pixels // 2
    row_shift = info[depth_index]
    col_shift = lax.rem(info[slots + depth_index], pixels)

    def shift_matrix(rows, cols, shift, transposed):
        row, lane = iotas(rows, cols)
        offset = (lane - row if transposed else row - lane) + shift
        return jnp.where((offset == 0) | (offset == pixels), 1.0, 0.0).astype(bf16)

    def pair(shift):
        cols = jnp.dot(
            stack[...], shift_matrix(pixels, half, shift, False), preferred_element_type=f32
        )
        rows = jnp.dot(
            shift_matrix(half, pixels, shift, True), stack_t[...], preferred_element_type=f32
        )
        forms, forms_t = [], []
        for parity in range(2):
            at = 2 * parity * half
            re, im = cols[at : at + half], cols[at + half : at + pixels]
            top = jnp.concatenate([re, -im], axis=1)
            bottom = jnp.concatenate([im, re], axis=1)
            forms.append(jnp.concatenate([top, bottom], axis=0).astype(bf16))
            re, im = rows[:, at : at + half], rows[:, at + half : at + pixels]
            top = jnp.concatenate([re, im], axis=1)
            bottom = jnp.concatenate([-im, re], axis=1)
            forms_t.append(jnp.concatenate([top, bottom], axis=0).astype(bf16))
        return forms, forms_t

    row_forms, row_forms_t = pair(row_shift)
    col_forms, col_forms_t = pair(col_shift)
    made = row_forms + col_forms_t + col_forms + row_forms_t
    for ref, value in zip(tables, made):
        ref[...] = value
    down = shift_matrix(pixels, pixels, row_shift, True)
    across = shift_matrix(pixels, pixels, col_shift, False)
    for comp in range(2):
        moved = jnp.dot(down, probe[comp].astype(bf16), preferred_element_type=f32).astype(bf16)
        psi0[comp] = jnp.dot(moved, across, preferred_element_type=f32).astype(bf16)


def wave_kernel(slots, depth_count, info, prop_re, prop_im, amplitude, psi0, *refs):
    tables = refs[:8]
    centers = refs[8 : 8 + depth_count]
    edges = refs[8 + depth_count : 8 + 2 * depth_count]
    out_centers = refs[8 + 2 * depth_count : 8 + 3 * depth_count]
    out_edges = refs[8 + 3 * depth_count : 8 + 4 * depth_count]
    patches, waves, adjoint, grads = refs[8 + 4 * depth_count :]
    depth_index = lax.axis_index("depth")
    pixels = psi0.shape[-1]
    half = pixels // 2
    live = depth_index < info[2 * slots]
    fwd_row_e, fwd_row_o, fwd_col_e, fwd_col_o, inv_col_e, inv_col_o, inv_row_e, inv_row_o = tables

    def dot(left, right):
        return jnp.dot(left, right, preferred_element_type=f32)

    def propagate(x_re, x_im, at_frequency):
        def rows_of(sign):
            mixed = [v[:half] + v[half:] if sign > 0 else v[:half] - v[half:] for v in (x_re, x_im)]
            return jnp.concatenate(mixed, axis=0).astype(bf16)

        u_even = dot(fwd_row_e[...], rows_of(1))
        u_odd = dot(fwd_row_o[...], rows_of(-1))

        def cols_of(sign):
            parts = []
            for u in (u_even, u_odd):
                mixed = u[:, :half] + u[:, half:] if sign > 0 else u[:, :half] - u[:, half:]
                parts.append(jnp.concatenate([mixed[:half], mixed[half:]], axis=1))
            return jnp.concatenate(parts, axis=0).astype(bf16)

        v_even = dot(cols_of(1), fwd_col_e[...])
        v_odd = dot(cols_of(-1), fwd_col_o[...])
        b_even = at_frequency(v_even[:, :half], v_even[:, half:], slice(0, half))
        b_odd = at_frequency(v_odd[:, :half], v_odd[:, half:], slice(half, pixels))
        w_even = dot(jnp.concatenate(b_even, axis=1).astype(bf16), inv_col_e[...])
        w_odd = dot(jnp.concatenate(b_odd, axis=1).astype(bf16), inv_col_o[...])
        w_low, w_high = w_even + w_odd, w_even - w_odd
        w_re = jnp.concatenate([w_low[:, :half], w_high[:, :half]], axis=1)
        w_im = jnp.concatenate([w_low[:, half:], w_high[:, half:]], axis=1)
        y_even = dot(
            inv_row_e[...], jnp.concatenate([w_re[:half], w_im[:half]], axis=0).astype(bf16)
        )
        y_odd = dot(
            inv_row_o[...], jnp.concatenate([w_re[half:], w_im[half:]], axis=0).astype(bf16)
        )
        low, high = y_even + y_odd, y_even - y_odd
        return (
            jnp.concatenate([low[:half], high[:half]], axis=0),
            jnp.concatenate([low[half:], high[half:]], axis=0),
        )

    def turn(re, im, cols):
        p_re, p_im = prop_re[:, cols], prop_im[:, cols]
        return [re * p_re - im * p_im, re * p_im + im * p_re]

    def turn_back(re, im, cols):
        p_re, p_im = prop_re[:, cols], prop_im[:, cols]
        return [re * p_re + im * p_im, im * p_re - re * p_im]

    def residual(re, im, cols):
        modulus = jnp.sqrt(re * re + im * im + epsilon)
        factor = 1.0 - amplitude[:, cols].astype(f32) / modulus
        return [factor * re, factor * im]

    def pair_of(ref, index):
        return ref[index, 0].astype(f32), ref[index, 1].astype(f32)

    @pl.when(live)
    def _():
        for flip in range(depth_count):
            patches[depth_index ^ flip, :, half:] = centers[flip][...]
            patches[depth_index ^ flip, :, :half] = edges[flip][...]
        waves[0] = psi0[...]

        def forward(k, carry):
            t_re, t_im = pair_of(patches, k)
            p_re, p_im = pair_of(waves, k)
            n_re, n_im = propagate(t_re * p_re - t_im * p_im, t_re * p_im + t_im * p_re, turn)
            waves[k + 1, 0] = n_re.astype(bf16)
            waves[k + 1, 1] = n_im.astype(bf16)
            return carry

        lax.fori_loop(0, depth_count, forward, 0)
        l_re, l_im = propagate(*pair_of(waves, depth_count), residual)
        adjoint[0, 0] = l_re.astype(bf16)
        adjoint[0, 1] = l_im.astype(bf16)

        def backward(step, carry):
            k = depth_count - 1 - step
            m_re, m_im = propagate(*pair_of(adjoint, 0), turn_back)
            t_re, t_im = pair_of(patches, k)
            p_re, p_im = pair_of(waves, k)
            grads[k ^ depth_index, 0] = (p_re * m_re + p_im * m_im).astype(bf16)
            grads[k ^ depth_index, 1] = (p_re * m_im - p_im * m_re).astype(bf16)
            adjoint[0, 0] = (t_re * m_re + t_im * m_im).astype(bf16)
            adjoint[0, 1] = (t_re * m_im - t_im * m_re).astype(bf16)
            return carry

        lax.fori_loop(0, depth_count, backward, 0)
        for flip in range(depth_count):
            out_centers[flip][...] = grads[flip, :, half:]
            out_edges[flip][...] = grads[flip, :, :half]

    @pl.when(jnp.logical_not(live))
    def _():
        for ref in out_centers + out_edges:
            ref[...] = jnp.zeros(ref.shape, ref.dtype)


def place_edges_kernel(slots, info, *refs):
    pieces, (upper, lower, upper_sum, lower_sum) = refs[:-4], refs[-4:]
    depth_index = lax.axis_index("depth")
    columns = upper.shape[-1]
    width = pieces[0].shape[-1]
    row, lane = iotas(pieces[0].shape[1], width)
    upper_sum[...] = jnp.zeros(upper_sum.shape, f32)
    lower_sum[...] = jnp.zeros(lower_sum.shape, f32)
    for flip, piece in enumerate(pieces):
        slot = depth_index ^ flip
        base, after, first = column_place(info, slots, slot, width, columns)
        to_upper = row >= info[slot]
        to_base = lane >= first
        for comp in range(2):
            value = piece[comp].astype(f32)
            for sheet, kept in (
                (upper_sum, jnp.where(to_upper, value, 0.0)),
                (lower_sum, jnp.where(to_upper, 0.0, value)),
            ):
                sheet[comp, :, pl.ds(base, width)] += jnp.where(to_base, kept, 0.0)
                sheet[comp, :, pl.ds(after, width)] += jnp.where(to_base, 0.0, kept)
    upper[...] = upper_sum[...].astype(bf16)
    lower[...] = lower_sum[...].astype(bf16)


def place_center_kernel(slots, info, *refs):
    pieces, sheet = refs[:-1], refs[-1]
    depth_index = lax.axis_index("depth")
    columns = sheet.shape[-1]
    width = pieces[0].shape[-1]
    _, lane = iotas(pieces[0].shape[1], width)
    sheet[...] = jnp.zeros(sheet.shape, f32)
    for flip, piece in enumerate(pieces):
        base, after, first = column_place(info, slots, depth_index ^ flip, width, columns)
        to_base = lane >= first
        for comp in range(2):
            value = piece[comp].astype(f32)
            sheet[comp, :, pl.ds(base, width)] += jnp.where(to_base, value, 0.0)
            sheet[comp, :, pl.ds(after, width)] += jnp.where(to_base, 0.0, value)


def body(transmission, probe_wave, prop_phase, measured, scan_rows, scan_cols, live_counts):
    pixels = probe_wave.shape[-1]
    slots = measured.shape[0]
    rows = transmission.shape[2]
    columns = transmission.shape[3]
    count = lax.axis_size("depth")
    own = transmission[0]
    info, own = lax.optimization_barrier(
        (jnp.concatenate([scan_rows, scan_cols, live_counts]), own)
    )
    info = shifted(info, "scan", 1)
    strip = call(strip_kernel, sds(own.shape, bf16), [own], [VMEM], name="strip")
    info, strip = lax.optimization_barrier((info, strip))
    upper = shifted(strip, "scan", 1)
    lower = shifted(strip, "scan", -1)

    part = sds((2, rows, pixels), bf16)
    centers = call(
        functools.partial(center_kernel, slots, pixels),
        [part] * count, [info, own], [SMEM, VMEM], name="cut_center",
    )
    centers = [centers[0]] + [exchanged(centers[flip], "depth", flip) for flip in range(1, count)]

    phase, centers[0] = lax.optimization_barrier((prop_phase, centers[0]))
    order = parity_order(pixels)
    square = sds((pixels, pixels), f32)
    prop_re, prop_im, amplitude = call(
        frequency_kernel,
        [square, square, sds((pixels, pixels), bf16)],
        [phase, jnp.asarray(order), jnp.asarray(order.T), measured],
        [VMEM] * 4, flops=2400 * pixels**3, transcendentals=2 * pixels**2, name="frequency_order",
    )
    amplitude = shifted(amplitude, "scan", 1)

    stack = split_tables(pixels)
    made = call(
        functools.partial(table_kernel, slots),
        [sds((2, pixels, pixels), bf16)] + [sds((pixels, pixels), bf16)] * 8,
        [info, jnp.asarray(stack), jnp.asarray(stack.T), probe_wave],
        [SMEM, VMEM, VMEM, VMEM], flops=16 * pixels**3, name="tables",
    )
    edges = call(
        functools.partial(edge_kernel, slots, pixels),
        [part] * count, [info, upper, lower], [SMEM, VMEM, VMEM], name="cut_edges",
    )
    edges = [edges[0]] + [exchanged(edges[flip], "depth", flip) for flip in range(1, count)]

    args = [info, prop_re, prop_im, amplitude, *made, *centers, *edges]
    grads = call(
        functools.partial(wave_kernel, slots, count),
        [part] * (2 * count), args, [SMEM] + [VMEM] * (len(args) - 1),
        scratch=[
            pltpu.VMEM((count, 2, pixels, pixels), bf16),
            pltpu.VMEM((count + 1, 2, pixels, pixels), bf16),
            pltpu.VMEM((1, 2, pixels, pixels), bf16),
            pltpu.VMEM((count, 2, pixels, pixels), bf16),
        ],
        flops=(2 * count + 1) * 16 * pixels**3, name="waves",
    )
    out_centers, out_edges = grads[:count], grads[count:]
    out_edges = [out_edges[0]] + [
        exchanged(out_edges[flip], "depth", flip) for flip in range(1, count)
    ]
    out_centers = [out_centers[0]] + [
        exchanged(out_centers[flip], "depth", flip) for flip in range(1, count)
    ]
    sheet_bf16 = sds((2, rows, columns), bf16)
    sheet_f32 = sds((2, rows, columns), f32)
    to_upper, to_lower = call(
        functools.partial(place_edges_kernel, slots),
        [sheet_bf16, sheet_bf16], [info, *out_edges], [SMEM] + [VMEM] * count,
        scratch=[pltpu.VMEM(sheet_f32.shape, f32)] * 2, name="place_edges",
    )
    from_next = shifted(to_upper, "scan", -1)
    from_previous = shifted(to_lower, "scan", 1)
    sheet = call(
        functools.partial(place_center_kernel, slots),
        sheet_f32, [info, *out_centers], [SMEM] + [VMEM] * count, name="place_center",
    )
    gradient = sheet + from_next.astype(f32) + from_previous.astype(f32)
    return gradient[None]


def solution(mesh):
    in_specs = (
        P("depth", None, "scan", None),
        P(),
        P(),
        P("scan", None, None),
        P("scan"),
        P("scan"),
        P("scan"),
    )
    out_specs = P("depth", None, "scan", None)
    return jax.shard_map(body, mesh=mesh, in_specs=in_specs, out_specs=out_specs, check_vma=False)
```

```python
import functools
import math

import jax
import jax.numpy as jnp
import ml_dtypes
import numpy as np
from jax import lax
from jax.experimental import pallas as pl
from jax.experimental.pallas import tpu as pltpu
from jax.sharding import PartitionSpec as P

epsilon = 1.0
bf16 = jnp.bfloat16
f32 = jnp.float32
VMEM = pl.BlockSpec(memory_space=pltpu.VMEM)
SMEM = pl.BlockSpec(memory_space=pltpu.SMEM)
LIMIT = 48 * 1024 * 1024


def shifted(value, axis, steps):
    count = lax.axis_size(axis)
    pairs = [(source, (source + steps) % count) for source in range(count)]
    return lax.ppermute(value, axis, pairs)


def exchanged(stacked, axis):
    return lax.all_to_all(stacked, axis, 0, 0)


def split_tables(pixels):
    indices = np.arange(pixels)
    angles = (indices[:, None] * indices[None, :] % pixels) * (2.0 * math.pi / pixels)
    norm_scale = 1.0 / math.sqrt(pixels)
    table_re = (np.cos(angles) * norm_scale).astype(np.float32).astype(ml_dtypes.bfloat16)
    table_im = (-np.sin(angles) * norm_scale).astype(np.float32).astype(ml_dtypes.bfloat16)
    return np.concatenate([table_re[0::2], table_im[0::2], table_re[1::2], table_im[1::2]], axis=0)


def parity_order(pixels):
    order = np.concatenate([np.arange(0, pixels, 2), np.arange(1, pixels, 2)])
    return (order[:, None] == np.arange(pixels)[None, :]).astype(np.float32)


def call(kernel, out_shape, args, specs, scratch=(), flops=0, transcendentals=0, name=None):
    outs = out_shape if isinstance(out_shape, (list, tuple)) else [out_shape]
    moved = sum(math.prod(a.shape) * a.dtype.itemsize for a in list(args) + list(outs))
    return pl.pallas_call(
        kernel,
        out_shape=out_shape,
        in_specs=specs,
        out_specs=jax.tree.map(lambda _: VMEM, out_shape),
        scratch_shapes=list(scratch),
        compiler_params=pltpu.CompilerParams(vmem_limit_bytes=LIMIT),
        cost_estimate=pl.CostEstimate(
            flops=flops, bytes_accessed=moved, transcendentals=transcendentals
        ),
        name=name,
    )(*args)


def sds(shape, dtype):
    return jax.ShapeDtypeStruct(shape, dtype)


def column_place(info, slots, slot, width, columns):
    col = info[slots + slot]
    base = (col // width) * width
    after = jnp.minimum(base + width, columns - width)
    return pl.multiple_of(base, width), pl.multiple_of(after, width), col - base


def iotas(rows, cols):
    return (
        lax.broadcasted_iota(jnp.int32, (rows, cols), 0),
        lax.broadcasted_iota(jnp.int32, (rows, cols), 1),
    )


def strip_kernel(own, strip):
    strip[...] = own[...].astype(bf16)


def center_kernel(slots, width, info, own, outs):
    columns = own.shape[-1]
    _, lane = iotas(own.shape[1], width)
    for slot in range(outs.shape[0]):
        base, after, first = column_place(info, slots, slot, width, columns)
        for comp in range(2):
            outs[slot, comp] = jnp.where(
                lane >= first, own[comp, :, pl.ds(base, width)], own[comp, :, pl.ds(after, width)]
            ).astype(bf16)


def edge_kernel(slots, width, info, upper, lower, outs):
    columns = upper.shape[-1]
    row, lane = iotas(upper.shape[1], width)
    for slot in range(outs.shape[0]):
        base, after, first = column_place(info, slots, slot, width, columns)
        from_upper = row >= info[slot]
        from_base = lane >= first
        for comp in range(2):
            at_base = jnp.where(
                from_upper,
                upper[comp, :, pl.ds(base, width)].astype(f32),
                lower[comp, :, pl.ds(base, width)].astype(f32),
            )
            at_after = jnp.where(
                from_upper,
                upper[comp, :, pl.ds(after, width)].astype(f32),
                lower[comp, :, pl.ds(after, width)].astype(f32),
            )
            outs[slot, comp] = jnp.where(from_base, at_base, at_after).astype(bf16)


def frequency_kernel(phase, order, order_t, measured, prop_re, prop_im, amplitude):
    def reorder(value):
        rows = jnp.dot(
            order[...], value, preferred_element_type=f32, precision=lax.Precision.HIGHEST
        )
        return jnp.dot(
            rows, order_t[...], preferred_element_type=f32, precision=lax.Precision.HIGHEST
        )

    turned = reorder(phase[...])
    prop_re[...] = jnp.cos(turned)
    prop_im[...] = jnp.sin(turned)
    amplitude[...] = reorder(measured[lax.axis_index("depth")]).astype(bf16)


def table_kernel(slots, info, stack, stack_t, probe, psi0, *tables):
    depth_index = lax.axis_index("depth")
    pixels = probe.shape[-1]
    half = pixels // 2
    row_shift = info[depth_index]
    col_shift = lax.rem(info[slots + depth_index], pixels)

    def shift_matrix(rows, cols, shift, transposed):
        row, lane = iotas(rows, cols)
        offset = (lane - row if transposed else row - lane) + shift
        return jnp.where((offset == 0) | (offset == pixels), 1.0, 0.0).astype(bf16)

    def pair(shift):
        cols = jnp.dot(
            stack[...], shift_matrix(pixels, half, shift, False), preferred_element_type=f32
        )
        rows = jnp.dot(
            shift_matrix(half, pixels, shift, True), stack_t[...], preferred_element_type=f32
        )
        forms, forms_t = [], []
        for parity in range(2):
            at = 2 * parity * half
            re, im = cols[at : at + half], cols[at + half : at + pixels]
            top = jnp.concatenate([re, -im], axis=1)
            bottom = jnp.concatenate([im, re], axis=1)
            forms.append(jnp.concatenate([top, bottom], axis=0).astype(bf16))
            re, im = rows[:, at : at + half], rows[:, at + half : at + pixels]
            top = jnp.concatenate([re, im], axis=1)
            bottom = jnp.concatenate([-im, re], axis=1)
            forms_t.append(jnp.concatenate([top, bottom], axis=0).astype(bf16))
        return forms, forms_t

    row_forms, row_forms_t = pair(row_shift)
    col_forms, col_forms_t = pair(col_shift)
    made = row_forms + col_forms_t + col_forms + row_forms_t
    for ref, value in zip(tables, made):
        ref[...] = value
    down = shift_matrix(pixels, pixels, row_shift, True)
    across = shift_matrix(pixels, pixels, col_shift, False)
    for comp in range(2):
        moved = jnp.dot(down, probe[comp].astype(bf16), preferred_element_type=f32).astype(bf16)
        psi0[comp] = jnp.dot(moved, across, preferred_element_type=f32).astype(bf16)


def wave_kernel(slots, depth_count, info, prop_re, prop_im, amplitude, psi0, *refs):
    tables = refs[:8]
    centers, edges, out_centers, out_edges, waves, adjoint = refs[8:]
    depth_index = lax.axis_index("depth")
    pixels = psi0.shape[-1]
    half = pixels // 2
    live = depth_index < info[2 * slots]
    fwd_row_e, fwd_row_o, fwd_col_e, fwd_col_o, inv_col_e, inv_col_o, inv_row_e, inv_row_o = tables

    def dot(left, right):
        return jnp.dot(left, right, preferred_element_type=f32)

    def propagate(x_re, x_im, at_frequency):
        def rows_of(sign):
            mixed = [v[:half] + v[half:] if sign > 0 else v[:half] - v[half:] for v in (x_re, x_im)]
            return jnp.concatenate(mixed, axis=0).astype(bf16)

        u_even = dot(fwd_row_e[...], rows_of(1))
        u_odd = dot(fwd_row_o[...], rows_of(-1))

        def cols_of(sign):
            parts = []
            for u in (u_even, u_odd):
                mixed = u[:, :half] + u[:, half:] if sign > 0 else u[:, :half] - u[:, half:]
                parts.append(jnp.concatenate([mixed[:half], mixed[half:]], axis=1))
            return jnp.concatenate(parts, axis=0).astype(bf16)

        v_even = dot(cols_of(1), fwd_col_e[...])
        v_odd = dot(cols_of(-1), fwd_col_o[...])
        b_even = at_frequency(v_even[:, :half], v_even[:, half:], slice(0, half))
        b_odd = at_frequency(v_odd[:, :half], v_odd[:, half:], slice(half, pixels))
        w_even = dot(jnp.concatenate(b_even, axis=1).astype(bf16), inv_col_e[...])
        w_odd = dot(jnp.concatenate(b_odd, axis=1).astype(bf16), inv_col_o[...])
        w_low, w_high = w_even + w_odd, w_even - w_odd
        w_re = jnp.concatenate([w_low[:, :half], w_high[:, :half]], axis=1)
        w_im = jnp.concatenate([w_low[:, half:], w_high[:, half:]], axis=1)
        y_even = dot(
            inv_row_e[...], jnp.concatenate([w_re[:half], w_im[:half]], axis=0).astype(bf16)
        )
        y_odd = dot(
            inv_row_o[...], jnp.concatenate([w_re[half:], w_im[half:]], axis=0).astype(bf16)
        )
        low, high = y_even + y_odd, y_even - y_odd
        return (
            jnp.concatenate([low[:half], high[:half]], axis=0),
            jnp.concatenate([low[half:], high[half:]], axis=0),
        )

    def turn(re, im, cols):
        p_re, p_im = prop_re[:, cols], prop_im[:, cols]
        return [re * p_re - im * p_im, re * p_im + im * p_re]

    def turn_back(re, im, cols):
        p_re, p_im = prop_re[:, cols], prop_im[:, cols]
        return [re * p_re + im * p_im, im * p_re - re * p_im]

    def residual(re, im, cols):
        modulus = jnp.sqrt(re * re + im * im + epsilon)
        factor = 1.0 - amplitude[:, cols].astype(f32) / modulus
        return [factor * re, factor * im]

    def patch_of(index):
        return [
            jnp.concatenate([edges[index, comp], centers[index, comp]], axis=0).astype(f32)
            for comp in range(2)
        ]

    def pair_of(ref, index):
        return ref[index, 0].astype(f32), ref[index, 1].astype(f32)

    @pl.when(live)
    def _():
        waves[0] = psi0[...]

        def forward(k, carry):
            t_re, t_im = patch_of(k)
            p_re, p_im = pair_of(waves, k)
            n_re, n_im = propagate(t_re * p_re - t_im * p_im, t_re * p_im + t_im * p_re, turn)
            waves[k + 1, 0] = n_re.astype(bf16)
            waves[k + 1, 1] = n_im.astype(bf16)
            return carry

        lax.fori_loop(0, depth_count, forward, 0)
        l_re, l_im = propagate(*pair_of(waves, depth_count), residual)
        adjoint[0, 0] = l_re.astype(bf16)
        adjoint[0, 1] = l_im.astype(bf16)

        def backward(step, carry):
            k = depth_count - 1 - step
            m_re, m_im = propagate(*pair_of(adjoint, 0), turn_back)
            t_re, t_im = patch_of(k)
            p_re, p_im = pair_of(waves, k)
            g_re = (p_re * m_re + p_im * m_im).astype(bf16)
            g_im = (p_re * m_im - p_im * m_re).astype(bf16)
            out_edges[k, 0], out_centers[k, 0] = g_re[:half], g_re[half:]
            out_edges[k, 1], out_centers[k, 1] = g_im[:half], g_im[half:]
            adjoint[0, 0] = (t_re * m_re + t_im * m_im).astype(bf16)
            adjoint[0, 1] = (t_re * m_im - t_im * m_re).astype(bf16)
            return carry

        lax.fori_loop(0, depth_count, backward, 0)

    @pl.when(jnp.logical_not(live))
    def _():
        for ref in (out_centers, out_edges):
            ref[...] = jnp.zeros(ref.shape, ref.dtype)


def place_edges_kernel(slots, info, pieces, upper, lower, upper_sum, lower_sum):
    columns = upper.shape[-1]
    width = pieces.shape[-1]
    row, lane = iotas(pieces.shape[2], width)
    upper_sum[...] = jnp.zeros(upper_sum.shape, f32)
    lower_sum[...] = jnp.zeros(lower_sum.shape, f32)
    for slot in range(pieces.shape[0]):
        base, after, first = column_place(info, slots, slot, width, columns)
        to_upper = row >= info[slot]
        to_base = lane >= first
        for comp in range(2):
            value = pieces[slot, comp].astype(f32)
            for sheet, kept in (
                (upper_sum, jnp.where(to_upper, value, 0.0)),
                (lower_sum, jnp.where(to_upper, 0.0, value)),
            ):
                sheet[comp, :, pl.ds(base, width)] += jnp.where(to_base, kept, 0.0)
                sheet[comp, :, pl.ds(after, width)] += jnp.where(to_base, 0.0, kept)
    upper[...] = upper_sum[...].astype(bf16)
    lower[...] = lower_sum[...].astype(bf16)


def place_center_kernel(slots, info, pieces, sheet):
    columns = sheet.shape[-1]
    width = pieces.shape[-1]
    _, lane = iotas(pieces.shape[2], width)
    sheet[...] = jnp.zeros(sheet.shape, f32)
    for slot in range(pieces.shape[0]):
        base, after, first = column_place(info, slots, slot, width, columns)
        to_base = lane >= first
        for comp in range(2):
            value = pieces[slot, comp].astype(f32)
            sheet[comp, :, pl.ds(base, width)] += jnp.where(to_base, value, 0.0)
            sheet[comp, :, pl.ds(after, width)] += jnp.where(to_base, 0.0, value)


def body(transmission, probe_wave, prop_phase, measured, scan_rows, scan_cols, live_counts):
    pixels = probe_wave.shape[-1]
    slots = measured.shape[0]
    rows = transmission.shape[2]
    columns = transmission.shape[3]
    count = lax.axis_size("depth")
    own = transmission[0]
    info, own = lax.optimization_barrier(
        (jnp.concatenate([scan_rows, scan_cols, live_counts]), own)
    )
    info = shifted(info, "scan", 1)
    strip = call(strip_kernel, sds(own.shape, bf16), [own], [VMEM], name="strip")
    info, strip = lax.optimization_barrier((info, strip))
    upper = shifted(strip, "scan", 1)
    lower = shifted(strip, "scan", -1)

    parts = sds((count, 2, rows, pixels), bf16)
    centers = call(
        functools.partial(center_kernel, slots, pixels),
        parts, [info, own], [SMEM, VMEM], name="cut_center",
    )
    phase, centers = lax.optimization_barrier((prop_phase, centers))
    centers = exchanged(centers, "depth")
    order = parity_order(pixels)
    square = sds((pixels, pixels), f32)
    prop_re, prop_im, amplitude = call(
        frequency_kernel,
        [square, square, sds((pixels, pixels), bf16)],
        [phase, jnp.asarray(order), jnp.asarray(order.T), measured],
        [VMEM] * 4, flops=2400 * pixels**3, transcendentals=2 * pixels**2, name="frequency_order",
    )
    amplitude = shifted(amplitude, "scan", 1)

    stack = split_tables(pixels)
    made = call(
        functools.partial(table_kernel, slots),
        [sds((2, pixels, pixels), bf16)] + [sds((pixels, pixels), bf16)] * 8,
        [info, jnp.asarray(stack), jnp.asarray(stack.T), probe_wave],
        [SMEM, VMEM, VMEM, VMEM], flops=16 * pixels**3, name="tables",
    )
    edges = call(
        functools.partial(edge_kernel, slots, pixels),
        parts, [info, upper, lower], [SMEM, VMEM, VMEM], name="cut_edges",
    )
    edges = exchanged(edges, "depth")

    args = [info, prop_re, prop_im, amplitude, *made, centers, edges]
    out_centers, out_edges = call(
        functools.partial(wave_kernel, slots, count),
        [parts, parts], args, [SMEM] + [VMEM] * (len(args) - 1),
        scratch=[
            pltpu.VMEM((count + 1, 2, pixels, pixels), bf16),
            pltpu.VMEM((1, 2, pixels, pixels), bf16),
        ],
        flops=(2 * count + 1) * 16 * pixels**3, name="waves",
    )
    out_edges = exchanged(out_edges, "depth")
    out_centers = exchanged(out_centers, "depth")
    sheet_bf16 = sds((2, rows, columns), bf16)
    sheet_f32 = sds((2, rows, columns), f32)
    to_upper, to_lower = call(
        functools.partial(place_edges_kernel, slots),
        [sheet_bf16, sheet_bf16], [info, out_edges], [SMEM, VMEM],
        scratch=[pltpu.VMEM(sheet_f32.shape, f32)] * 2, name="place_edges",
    )
    from_next = shifted(to_upper, "scan", -1)
    from_previous = shifted(to_lower, "scan", 1)
    sheet = call(
        functools.partial(place_center_kernel, slots),
        sheet_f32, [info, out_centers], [SMEM, VMEM], name="place_center",
    )
    gradient = sheet + from_next.astype(f32) + from_previous.astype(f32)
    return gradient[None]


def solution(mesh):
    in_specs = (
        P("depth", None, "scan", None),
        P(),
        P(),
        P("scan", None, None),
        P("scan"),
        P("scan"),
        P("scan"),
    )
    out_specs = P("depth", None, "scan", None)
    return jax.shard_map(body, mesh=mesh, in_specs=in_specs, out_specs=out_specs, check_vma=False)
```

```python
import functools
import math

import jax
import jax.numpy as jnp
import ml_dtypes
import numpy as np
from jax import lax
from jax.experimental import pallas as pl
from jax.experimental.pallas import tpu as pltpu
from jax.sharding import PartitionSpec as P

epsilon = 1.0
bf16 = jnp.bfloat16
f32 = jnp.float32
VMEM = pl.BlockSpec(memory_space=pltpu.VMEM)
SMEM = pl.BlockSpec(memory_space=pltpu.SMEM)
LIMIT = 48 * 1024 * 1024


def shifted(value, axis, steps):
    count = lax.axis_size(axis)
    pairs = [(source, (source + steps) % count) for source in range(count)]
    return lax.ppermute(value, axis, pairs)


def exchanged(value, axis, flip):
    count = lax.axis_size(axis)
    return lax.ppermute(value, axis, [(source, source ^ flip) for source in range(count)])


def split_tables(pixels):
    indices = np.arange(pixels)
    angles = (indices[:, None] * indices[None, :] % pixels) * (2.0 * math.pi / pixels)
    norm_scale = 1.0 / math.sqrt(pixels)
    table_re = (np.cos(angles) * norm_scale).astype(np.float32).astype(ml_dtypes.bfloat16)
    table_im = (-np.sin(angles) * norm_scale).astype(np.float32).astype(ml_dtypes.bfloat16)
    return np.concatenate([table_re[0::2], table_im[0::2], table_re[1::2], table_im[1::2]], axis=0)


def parity_order(pixels):
    order = np.concatenate([np.arange(0, pixels, 2), np.arange(1, pixels, 2)])
    return (order[:, None] == np.arange(pixels)[None, :]).astype(np.float32)


def call(kernel, out_shape, args, specs, scratch=(), flops=0, transcendentals=0, name=None):
    outs = out_shape if isinstance(out_shape, (list, tuple)) else [out_shape]
    moved = sum(math.prod(a.shape) * a.dtype.itemsize for a in list(args) + list(outs))
    return pl.pallas_call(
        kernel,
        out_shape=out_shape,
        in_specs=specs,
        out_specs=jax.tree.map(lambda _: VMEM, out_shape),
        scratch_shapes=list(scratch),
        compiler_params=pltpu.CompilerParams(vmem_limit_bytes=LIMIT),
        cost_estimate=pl.CostEstimate(
            flops=flops, bytes_accessed=moved, transcendentals=transcendentals
        ),
        name=name,
    )(*args)


def sds(shape, dtype):
    return jax.ShapeDtypeStruct(shape, dtype)


def column_place(info, slots, slot, width, columns):
    col = info[slots + slot]
    base = (col // width) * width
    after = jnp.minimum(base + width, columns - width)
    return pl.multiple_of(base, width), pl.multiple_of(after, width), col - base


def iotas(rows, cols):
    return (
        lax.broadcasted_iota(jnp.int32, (rows, cols), 0),
        lax.broadcasted_iota(jnp.int32, (rows, cols), 1),
    )


def strip_kernel(own, *strips):
    for comp, strip in enumerate(strips):
        strip[...] = own[comp].astype(bf16)


def center_kernel(slots, width, info, own, *outs):
    depth_index = lax.axis_index("depth")
    columns = own.shape[-1]
    _, lane = iotas(own.shape[1], width)
    for flip in range(len(outs)):
        base, after, first = column_place(info, slots, depth_index ^ flip, width, columns)
        for comp in range(2):
            outs[flip][comp] = jnp.where(
                lane >= first, own[comp, :, pl.ds(base, width)], own[comp, :, pl.ds(after, width)]
            ).astype(bf16)


def edge_kernel(slots, width, info, upper, lower, *outs):
    depth_index = lax.axis_index("depth")
    columns = upper.shape[-1]
    row, lane = iotas(upper.shape[0], width)
    for flip in range(len(outs)):
        slot = depth_index ^ flip
        base, after, first = column_place(info, slots, slot, width, columns)
        from_upper = row >= info[slot]

        def rows_at(place):
            return jnp.where(
                from_upper,
                upper[:, pl.ds(place, width)].astype(f32),
                lower[:, pl.ds(place, width)].astype(f32),
            )

        outs[flip][...] = jnp.where(lane >= first, rows_at(base), rows_at(after)).astype(bf16)


def frequency_kernel(phase, order, order_t, measured, prop_re, prop_im, amplitude):
    def reorder(value):
        rows = jnp.dot(
            order[...], value, preferred_element_type=f32, precision=lax.Precision.HIGHEST
        )
        return jnp.dot(
            rows, order_t[...], preferred_element_type=f32, precision=lax.Precision.HIGHEST
        )

    turned = reorder(phase[...])
    prop_re[...] = jnp.cos(turned)
    prop_im[...] = jnp.sin(turned)
    amplitude[...] = reorder(measured[lax.axis_index("depth")]).astype(bf16)


def table_kernel(slots, info, stack, stack_t, probe, psi0, *tables):
    depth_index = lax.axis_index("depth")
    pixels = probe.shape[-1]
    half = pixels // 2
    row_shift = info[depth_index]
    col_shift = lax.rem(info[slots + depth_index], pixels)

    def shift_matrix(rows, cols, shift, transposed):
        row, lane = iotas(rows, cols)
        offset = (lane - row if transposed else row - lane) + shift
        return jnp.where((offset == 0) | (offset == pixels), 1.0, 0.0).astype(bf16)

    def pair(shift):
        cols = jnp.dot(
            stack[...], shift_matrix(pixels, half, shift, False), preferred_element_type=f32
        )
        rows = jnp.dot(
            shift_matrix(half, pixels, shift, True), stack_t[...], preferred_element_type=f32
        )
        forms, forms_t = [], []
        for parity in range(2):
            at = 2 * parity * half
            re, im = cols[at : at + half], cols[at + half : at + pixels]
            top = jnp.concatenate([re, -im], axis=1)
            bottom = jnp.concatenate([im, re], axis=1)
            forms.append(jnp.concatenate([top, bottom], axis=0).astype(bf16))
            re, im = rows[:, at : at + half], rows[:, at + half : at + pixels]
            top = jnp.concatenate([re, im], axis=1)
            bottom = jnp.concatenate([-im, re], axis=1)
            forms_t.append(jnp.concatenate([top, bottom], axis=0).astype(bf16))
        return forms, forms_t

    row_forms, row_forms_t = pair(row_shift)
    col_forms, col_forms_t = pair(col_shift)
    made = row_forms + col_forms_t + col_forms + row_forms_t
    for ref, value in zip(tables, made):
        ref[...] = value
    down = shift_matrix(pixels, pixels, row_shift, True)
    across = shift_matrix(pixels, pixels, col_shift, False)
    for comp in range(2):
        moved = jnp.dot(down, probe[comp].astype(bf16), preferred_element_type=f32).astype(bf16)
        psi0[comp] = jnp.dot(moved, across, preferred_element_type=f32).astype(bf16)


def wave_kernel(slots, depth_count, info, prop_re, prop_im, amplitude, psi0, *refs):
    tables = refs[:8]
    groups = [refs[at : at + depth_count] for at in range(8, 8 + 5 * depth_count, depth_count)]
    centers, edges, out_centers, out_edges = groups[0], groups[1:3], groups[3], groups[4]
    patches, waves, adjoint, grads = refs[8 + 5 * depth_count :]
    depth_index = lax.axis_index("depth")
    pixels = psi0.shape[-1]
    half = pixels // 2
    live = depth_index < info[2 * slots]
    fwd_row_e, fwd_row_o, fwd_col_e, fwd_col_o, inv_col_e, inv_col_o, inv_row_e, inv_row_o = tables

    def dot(left, right):
        return jnp.dot(left, right, preferred_element_type=f32)

    def propagate(x_re, x_im, at_frequency):
        def rows_of(sign):
            mixed = [v[:half] + v[half:] if sign > 0 else v[:half] - v[half:] for v in (x_re, x_im)]
            return jnp.concatenate(mixed, axis=0).astype(bf16)

        u_even = dot(fwd_row_e[...], rows_of(1))
        u_odd = dot(fwd_row_o[...], rows_of(-1))

        def cols_of(sign):
            parts = []
            for u in (u_even, u_odd):
                mixed = u[:, :half] + u[:, half:] if sign > 0 else u[:, :half] - u[:, half:]
                parts.append(jnp.concatenate([mixed[:half], mixed[half:]], axis=1))
            return jnp.concatenate(parts, axis=0).astype(bf16)

        v_even = dot(cols_of(1), fwd_col_e[...])
        v_odd = dot(cols_of(-1), fwd_col_o[...])
        b_even = at_frequency(v_even[:, :half], v_even[:, half:], slice(0, half))
        b_odd = at_frequency(v_odd[:, :half], v_odd[:, half:], slice(half, pixels))
        w_even = dot(jnp.concatenate(b_even, axis=1).astype(bf16), inv_col_e[...])
        w_odd = dot(jnp.concatenate(b_odd, axis=1).astype(bf16), inv_col_o[...])
        w_low, w_high = w_even + w_odd, w_even - w_odd
        w_re = jnp.concatenate([w_low[:, :half], w_high[:, :half]], axis=1)
        w_im = jnp.concatenate([w_low[:, half:], w_high[:, half:]], axis=1)
        y_even = dot(
            inv_row_e[...], jnp.concatenate([w_re[:half], w_im[:half]], axis=0).astype(bf16)
        )
        y_odd = dot(
            inv_row_o[...], jnp.concatenate([w_re[half:], w_im[half:]], axis=0).astype(bf16)
        )
        low, high = y_even + y_odd, y_even - y_odd
        return (
            jnp.concatenate([low[:half], high[:half]], axis=0),
            jnp.concatenate([low[half:], high[half:]], axis=0),
        )

    def turn(re, im, cols):
        p_re, p_im = prop_re[:, cols], prop_im[:, cols]
        return [re * p_re - im * p_im, re * p_im + im * p_re]

    def turn_back(re, im, cols):
        p_re, p_im = prop_re[:, cols], prop_im[:, cols]
        return [re * p_re + im * p_im, im * p_re - re * p_im]

    def residual(re, im, cols):
        modulus = jnp.sqrt(re * re + im * im + epsilon)
        factor = 1.0 - amplitude[:, cols].astype(f32) / modulus
        return [factor * re, factor * im]

    def pair_of(ref, index):
        return ref[index, 0].astype(f32), ref[index, 1].astype(f32)

    @pl.when(live)
    def _():
        for flip in range(depth_count):
            patches[depth_index ^ flip, :, half:] = centers[flip][...]
            for comp in range(2):
                patches[depth_index ^ flip, comp, :half] = edges[comp][flip][...]
        waves[0] = psi0[...]

        def forward(k, carry):
            t_re, t_im = pair_of(patches, k)
            p_re, p_im = pair_of(waves, k)
            n_re, n_im = propagate(t_re * p_re - t_im * p_im, t_re * p_im + t_im * p_re, turn)
            waves[k + 1, 0] = n_re.astype(bf16)
            waves[k + 1, 1] = n_im.astype(bf16)
            return carry

        lax.fori_loop(0, depth_count, forward, 0)
        l_re, l_im = propagate(*pair_of(waves, depth_count), residual)
        adjoint[0, 0] = l_re.astype(bf16)
        adjoint[0, 1] = l_im.astype(bf16)

        def backward(step, carry):
            k = depth_count - 1 - step
            m_re, m_im = propagate(*pair_of(adjoint, 0), turn_back)
            t_re, t_im = pair_of(patches, k)
            p_re, p_im = pair_of(waves, k)
            grads[k ^ depth_index, 0] = (p_re * m_re + p_im * m_im).astype(bf16)
            grads[k ^ depth_index, 1] = (p_re * m_im - p_im * m_re).astype(bf16)
            adjoint[0, 0] = (t_re * m_re + t_im * m_im).astype(bf16)
            adjoint[0, 1] = (t_re * m_im - t_im * m_re).astype(bf16)
            return carry

        lax.fori_loop(0, depth_count, backward, 0)
        for flip in range(depth_count):
            out_centers[flip][...] = grads[flip, :, half:]
            out_edges[flip][...] = grads[flip, :, :half]

    @pl.when(jnp.logical_not(live))
    def _():
        for ref in out_centers + out_edges:
            ref[...] = jnp.zeros(ref.shape, ref.dtype)


def place_edges_kernel(slots, info, *refs):
    pieces, (upper, lower, upper_sum, lower_sum) = refs[:-4], refs[-4:]
    depth_index = lax.axis_index("depth")
    columns = upper.shape[-1]
    width = pieces[0].shape[-1]
    row, lane = iotas(pieces[0].shape[1], width)
    upper_sum[...] = jnp.zeros(upper_sum.shape, f32)
    lower_sum[...] = jnp.zeros(lower_sum.shape, f32)
    for flip, piece in enumerate(pieces):
        slot = depth_index ^ flip
        base, after, first = column_place(info, slots, slot, width, columns)
        to_upper = row >= info[slot]
        to_base = lane >= first
        for comp in range(2):
            value = piece[comp].astype(f32)
            for sheet, kept in (
                (upper_sum, jnp.where(to_upper, value, 0.0)),
                (lower_sum, jnp.where(to_upper, 0.0, value)),
            ):
                sheet[comp, :, pl.ds(base, width)] += jnp.where(to_base, kept, 0.0)
                sheet[comp, :, pl.ds(after, width)] += jnp.where(to_base, 0.0, kept)
    upper[...] = upper_sum[...].astype(bf16)
    lower[...] = lower_sum[...].astype(bf16)


def finish_kernel(slots, info, *refs):
    from_next, from_previous = refs[:2]
    pieces, sheet = refs[2:-1], refs[-1]
    depth_index = lax.axis_index("depth")
    columns = sheet.shape[-1]
    width = pieces[0].shape[-1]
    _, lane = iotas(pieces[0].shape[1], width)
    sheet[0] = from_next[0].astype(f32) + from_previous[0].astype(f32)
    comp = pl.program_id(0)
    for flip, piece in enumerate(pieces):
        base, after, first = column_place(info, slots, depth_index ^ flip, width, columns)
        to_base = lane >= first
        value = piece[comp].astype(f32)
        sheet[0, :, pl.ds(base, width)] += jnp.where(to_base, value, 0.0)
        sheet[0, :, pl.ds(after, width)] += jnp.where(to_base, 0.0, value)


def body(transmission, probe_wave, prop_phase, measured, scan_rows, scan_cols, live_counts):
    pixels = probe_wave.shape[-1]
    slots = measured.shape[0]
    rows = transmission.shape[2]
    columns = transmission.shape[3]
    count = lax.axis_size("depth")
    own = transmission[0]
    info, own = lax.optimization_barrier(
        (jnp.concatenate([scan_rows, scan_cols, live_counts]), own)
    )
    info = shifted(info, "scan", 1)
    strip = sds((rows, columns), bf16)
    strips = call(strip_kernel, [strip] * 2, [own], [VMEM], name="strip")
    info, strips = lax.optimization_barrier((info, strips))

    def across_depth(pieces):
        return [pieces[0]] + [exchanged(pieces[flip], "depth", flip) for flip in range(1, count)]

    def from_neighbours(piece):
        return [shifted(piece, "scan", 1), shifted(piece, "scan", -1)]

    around = [from_neighbours(strips[0])]
    part = sds((2, rows, pixels), bf16)
    centers = call(
        functools.partial(center_kernel, slots, pixels),
        [part] * count, [info, own], [SMEM, VMEM], name="cut_center",
    )
    phase, probe, centers = lax.optimization_barrier((prop_phase, probe_wave, centers))
    centers = across_depth(centers)

    order = parity_order(pixels)
    square = sds((pixels, pixels), f32)
    prop_re, prop_im, amplitude = call(
        frequency_kernel,
        [square, square, sds((pixels, pixels), bf16)],
        [phase, jnp.asarray(order), jnp.asarray(order.T), measured],
        [VMEM] * 4, flops=24 * pixels**3, transcendentals=2 * pixels**2, name="frequency_order",
    )
    stack = split_tables(pixels)
    made = call(
        functools.partial(table_kernel, slots),
        [sds((2, pixels, pixels), bf16)] + [sds((pixels, pixels), bf16)] * 8,
        [info, jnp.asarray(stack), jnp.asarray(stack.T), probe],
        [SMEM, VMEM, VMEM, VMEM], flops=16 * pixels**3, name="tables",
    )
    later_strip, around[0], centers, prop_re, made = lax.optimization_barrier(
        (strips[1], around[0], centers, prop_re, made)
    )
    around.append(from_neighbours(later_strip))
    amplitude, around[1] = lax.optimization_barrier((amplitude, around[1]))
    amplitude = shifted(amplitude, "scan", 1)

    half_part = sds((rows, pixels), bf16)
    edges = []
    for upper, lower in around:
        pieces = call(
            functools.partial(edge_kernel, slots, pixels),
            [half_part] * count, [info, upper, lower], [SMEM, VMEM, VMEM], name="cut_edges",
        )
        edges += across_depth(pieces)

    args = [info, prop_re, prop_im, amplitude, *made, *centers, *edges]
    grads = call(
        functools.partial(wave_kernel, slots, count),
        [part] * (2 * count), args, [SMEM] + [VMEM] * (len(args) - 1),
        scratch=[
            pltpu.VMEM((count, 2, pixels, pixels), bf16),
            pltpu.VMEM((count + 1, 2, pixels, pixels), bf16),
            pltpu.VMEM((1, 2, pixels, pixels), bf16),
            pltpu.VMEM((count, 2, pixels, pixels), bf16),
        ],
        flops=(2 * count + 1) * 16 * pixels**3, name="waves",
    )
    out_centers, out_edges = grads[:count], across_depth(grads[count:])
    sheet_bf16 = sds((2, rows, columns), bf16)
    to_upper, to_lower = call(
        functools.partial(place_edges_kernel, slots),
        [sheet_bf16, sheet_bf16], [info, *out_edges], [SMEM] + [VMEM] * count,
        scratch=[pltpu.VMEM(sheet_bf16.shape, f32)] * 2, name="place_edges",
    )
    from_next, from_previous = shifted(to_upper, "scan", -1), shifted(to_lower, "scan", 1)
    out_centers = across_depth(out_centers)
    strip_spec = pl.BlockSpec((1, rows, columns), lambda comp: (comp, 0, 0))
    return pl.pallas_call(
        functools.partial(finish_kernel, slots),
        out_shape=sds((2, rows, columns), f32),
        grid=(2,),
        in_specs=[SMEM, strip_spec, strip_spec] + [VMEM] * count,
        out_specs=strip_spec,
        compiler_params=pltpu.CompilerParams(vmem_limit_bytes=LIMIT),
        name="finish",
    )(info, from_next, from_previous, *out_centers)[None]


def solution(mesh):
    in_specs = (
        P("depth", None, "scan", None),
        P(),
        P(),
        P("scan", None, None),
        P("scan"),
        P("scan"),
        P("scan"),
    )
    out_specs = P("depth", None, "scan", None)
    return jax.shard_map(body, mesh=mesh, in_specs=in_specs, out_specs=out_specs, check_vma=False)
```

```python
import functools
import math

import jax
import jax.numpy as jnp
import ml_dtypes
import numpy as np
from jax import lax
from jax.experimental import pallas as pl
from jax.experimental.pallas import tpu as pltpu
from jax.sharding import PartitionSpec as P

epsilon = 1.0
bf16 = jnp.bfloat16
f32 = jnp.float32
VMEM = pl.BlockSpec(memory_space=pltpu.VMEM)
SMEM = pl.BlockSpec(memory_space=pltpu.SMEM)
LIMIT = 48 * 1024 * 1024


def shifted(value, axis, steps):
    count = lax.axis_size(axis)
    pairs = [(source, (source + steps) % count) for source in range(count)]
    return lax.ppermute(value, axis, pairs)


def passed_on(value, axis, steps):
    count = lax.axis_size(axis)
    sources = range(max(0, -steps), min(count, count - steps))
    return lax.ppermute(value, axis, [(source, source + steps) for source in sources])


def between_ends(value, axis):
    last = lax.axis_size(axis) - 1
    return lax.ppermute(value, axis, [(0, last), (last, 0)])


def exchanged(value, axis, flip):
    count = lax.axis_size(axis)
    return lax.ppermute(value, axis, [(source, source ^ flip) for source in range(count)])


def split_tables(pixels):
    indices = np.arange(pixels)
    angles = (indices[:, None] * indices[None, :] % pixels) * (2.0 * math.pi / pixels)
    norm_scale = 1.0 / math.sqrt(pixels)
    table_re = (np.cos(angles) * norm_scale).astype(np.float32).astype(ml_dtypes.bfloat16)
    table_im = (-np.sin(angles) * norm_scale).astype(np.float32).astype(ml_dtypes.bfloat16)
    return np.concatenate([table_re[0::2], table_im[0::2], table_re[1::2], table_im[1::2]], axis=0)


def parity_order(pixels):
    order = np.concatenate([np.arange(0, pixels, 2), np.arange(1, pixels, 2)])
    return (order[:, None] == np.arange(pixels)[None, :]).astype(np.float32)


def call(kernel, out_shape, args, specs, scratch=(), flops=0, transcendentals=0, name=None):
    outs = out_shape if isinstance(out_shape, (list, tuple)) else [out_shape]
    moved = sum(math.prod(a.shape) * a.dtype.itemsize for a in list(args) + list(outs))
    return pl.pallas_call(
        kernel,
        out_shape=out_shape,
        in_specs=specs,
        out_specs=jax.tree.map(lambda _: VMEM, out_shape),
        scratch_shapes=list(scratch),
        compiler_params=pltpu.CompilerParams(vmem_limit_bytes=LIMIT),
        cost_estimate=pl.CostEstimate(
            flops=flops, bytes_accessed=moved, transcendentals=transcendentals
        ),
        name=name,
    )(*args)


def sds(shape, dtype):
    return jax.ShapeDtypeStruct(shape, dtype)


def column_place(info, slots, slot, width, columns):
    col = info[slots + slot]
    base = (col // width) * width
    after = jnp.minimum(base + width, columns - width)
    return pl.multiple_of(base, width), pl.multiple_of(after, width), col - base


def iotas(rows, cols):
    return (
        lax.broadcasted_iota(jnp.int32, (rows, cols), 0),
        lax.broadcasted_iota(jnp.int32, (rows, cols), 1),
    )


def strip_kernel(own, strip):
    strip[...] = own[...].astype(bf16)


def center_kernel(slots, width, info, own, *outs):
    depth_index = lax.axis_index("depth")
    columns = own.shape[-1]
    _, lane = iotas(own.shape[1], width)
    for flip in range(len(outs)):
        base, after, first = column_place(info, slots, depth_index ^ flip, width, columns)
        for comp in range(2):
            outs[flip][comp] = jnp.where(
                lane >= first, own[comp, :, pl.ds(base, width)], own[comp, :, pl.ds(after, width)]
            ).astype(bf16)


def edge_kernel(slots, width, info, upper, lower, wrapped, *outs):
    depth_index = lax.axis_index("depth")
    first_tile = lax.axis_index("scan") == 0
    last_tile = lax.axis_index("scan") == lax.axis_size("scan") - 1
    columns = upper.shape[-1]
    row, lane = iotas(upper.shape[1], width)
    for flip in range(len(outs)):
        slot = depth_index ^ flip
        base, after, first = column_place(info, slots, slot, width, columns)
        from_upper = row >= info[slot]
        from_wrapped = jnp.logical_or(
            jnp.logical_and(from_upper, first_tile),
            jnp.logical_and(jnp.logical_not(from_upper), last_tile),
        )

        def rows_at(comp, place):
            near = jnp.where(
                from_upper,
                upper[comp, :, pl.ds(place, width)].astype(f32),
                lower[comp, :, pl.ds(place, width)].astype(f32),
            )
            return jnp.where(from_wrapped, wrapped[comp, :, pl.ds(place, width)].astype(f32), near)

        for comp in range(2):
            outs[flip][comp] = jnp.where(
                lane >= first, rows_at(comp, base), rows_at(comp, after)
            ).astype(bf16)


def frequency_kernel(phase, order, order_t, measured, prop_re, prop_im, amplitude):
    def reorder(value):
        rows = jnp.dot(
            order[...], value, preferred_element_type=f32, precision=lax.Precision.HIGHEST
        )
        return jnp.dot(
            rows, order_t[...], preferred_element_type=f32, precision=lax.Precision.HIGHEST
        )

    turned = reorder(phase[...])
    prop_re[...] = jnp.cos(turned)
    prop_im[...] = jnp.sin(turned)
    amplitude[...] = reorder(measured[lax.axis_index("depth")]).astype(bf16)


def table_kernel(slots, info, stack, stack_t, probe, psi0, *tables):
    depth_index = lax.axis_index("depth")
    pixels = probe.shape[-1]
    half = pixels // 2
    row_shift = info[depth_index]
    col_shift = lax.rem(info[slots + depth_index], pixels)

    def shift_matrix(rows, cols, shift, transposed):
        row, lane = iotas(rows, cols)
        offset = (lane - row if transposed else row - lane) + shift
        return jnp.where((offset == 0) | (offset == pixels), 1.0, 0.0).astype(bf16)

    def pair(shift):
        cols = jnp.dot(
            stack[...], shift_matrix(pixels, half, shift, False), preferred_element_type=f32
        )
        rows = jnp.dot(
            shift_matrix(half, pixels, shift, True), stack_t[...], preferred_element_type=f32
        )
        forms, forms_t = [], []
        for parity in range(2):
            at = 2 * parity * half
            re, im = cols[at : at + half], cols[at + half : at + pixels]
            top = jnp.concatenate([re, -im], axis=1)
            bottom = jnp.concatenate([im, re], axis=1)
            forms.append(jnp.concatenate([top, bottom], axis=0).astype(bf16))
            re, im = rows[:, at : at + half], rows[:, at + half : at + pixels]
            top = jnp.concatenate([re, im], axis=1)
            bottom = jnp.concatenate([-im, re], axis=1)
            forms_t.append(jnp.concatenate([top, bottom], axis=0).astype(bf16))
        return forms, forms_t

    row_forms, row_forms_t = pair(row_shift)
    col_forms, col_forms_t = pair(col_shift)
    made = row_forms + col_forms_t + col_forms + row_forms_t
    for ref, value in zip(tables, made):
        ref[...] = value
    down = shift_matrix(pixels, pixels, row_shift, True)
    across = shift_matrix(pixels, pixels, col_shift, False)
    for comp in range(2):
        moved = jnp.dot(down, probe[comp].astype(bf16), preferred_element_type=f32).astype(bf16)
        psi0[comp] = jnp.dot(moved, across, preferred_element_type=f32).astype(bf16)


def wave_kernel(slots, depth_count, info, prop_re, prop_im, amplitude, psi0, *refs):
    tables = refs[:8]
    centers = refs[8 : 8 + depth_count]
    edges = refs[8 + depth_count : 8 + 2 * depth_count]
    out_centers = refs[8 + 2 * depth_count : 8 + 3 * depth_count]
    out_edges = refs[8 + 3 * depth_count : 8 + 4 * depth_count]
    patches, waves, adjoint, grads = refs[8 + 4 * depth_count :]
    depth_index = lax.axis_index("depth")
    pixels = psi0.shape[-1]
    half = pixels // 2
    live = depth_index < info[2 * slots]
    fwd_row_e, fwd_row_o, fwd_col_e, fwd_col_o, inv_col_e, inv_col_o, inv_row_e, inv_row_o = tables

    def dot(left, right):
        return jnp.dot(left, right, preferred_element_type=f32)

    def propagate(x_re, x_im, at_frequency):
        def rows_of(sign):
            mixed = [v[:half] + v[half:] if sign > 0 else v[:half] - v[half:] for v in (x_re, x_im)]
            return jnp.concatenate(mixed, axis=0).astype(bf16)

        u_even = dot(fwd_row_e[...], rows_of(1))
        u_odd = dot(fwd_row_o[...], rows_of(-1))

        def cols_of(sign):
            parts = []
            for u in (u_even, u_odd):
                mixed = u[:, :half] + u[:, half:] if sign > 0 else u[:, :half] - u[:, half:]
                parts.append(jnp.concatenate([mixed[:half], mixed[half:]], axis=1))
            return jnp.concatenate(parts, axis=0).astype(bf16)

        v_even = dot(cols_of(1), fwd_col_e[...])
        v_odd = dot(cols_of(-1), fwd_col_o[...])
        b_even = at_frequency(v_even[:, :half], v_even[:, half:], slice(0, half))
        b_odd = at_frequency(v_odd[:, :half], v_odd[:, half:], slice(half, pixels))
        w_even = dot(jnp.concatenate(b_even, axis=1).astype(bf16), inv_col_e[...])
        w_odd = dot(jnp.concatenate(b_odd, axis=1).astype(bf16), inv_col_o[...])
        w_low, w_high = w_even + w_odd, w_even - w_odd
        w_re = jnp.concatenate([w_low[:, :half], w_high[:, :half]], axis=1)
        w_im = jnp.concatenate([w_low[:, half:], w_high[:, half:]], axis=1)
        y_even = dot(
            inv_row_e[...], jnp.concatenate([w_re[:half], w_im[:half]], axis=0).astype(bf16)
        )
        y_odd = dot(
            inv_row_o[...], jnp.concatenate([w_re[half:], w_im[half:]], axis=0).astype(bf16)
        )
        low, high = y_even + y_odd, y_even - y_odd
        return (
            jnp.concatenate([low[:half], high[:half]], axis=0),
            jnp.concatenate([low[half:], high[half:]], axis=0),
        )

    def turn(re, im, cols):
        p_re, p_im = prop_re[:, cols], prop_im[:, cols]
        return [re * p_re - im * p_im, re * p_im + im * p_re]

    def turn_back(re, im, cols):
        p_re, p_im = prop_re[:, cols], prop_im[:, cols]
        return [re * p_re + im * p_im, im * p_re - re * p_im]

    def residual(re, im, cols):
        modulus = jnp.sqrt(re * re + im * im + epsilon)
        factor = 1.0 - amplitude[:, cols].astype(f32) / modulus
        return [factor * re, factor * im]

    def pair_of(ref, index):
        return ref[index, 0].astype(f32), ref[index, 1].astype(f32)

    @pl.when(live)
    def _():
        for flip in range(depth_count):
            patches[depth_index ^ flip, :, half:] = centers[flip][...]
            patches[depth_index ^ flip, :, :half] = edges[flip][...]
        waves[0] = psi0[...]

        def forward(k, carry):
            t_re, t_im = pair_of(patches, k)
            p_re, p_im = pair_of(waves, k)
            n_re, n_im = propagate(t_re * p_re - t_im * p_im, t_re * p_im + t_im * p_re, turn)
            waves[k + 1, 0] = n_re.astype(bf16)
            waves[k + 1, 1] = n_im.astype(bf16)
            return carry

        lax.fori_loop(0, depth_count, forward, 0)
        l_re, l_im = propagate(*pair_of(waves, depth_count), residual)
        adjoint[0, 0] = l_re.astype(bf16)
        adjoint[0, 1] = l_im.astype(bf16)

        def backward(step, carry):
            k = depth_count - 1 - step
            m_re, m_im = propagate(*pair_of(adjoint, 0), turn_back)
            t_re, t_im = pair_of(patches, k)
            p_re, p_im = pair_of(waves, k)
            grads[k ^ depth_index, 0] = (p_re * m_re + p_im * m_im).astype(bf16)
            grads[k ^ depth_index, 1] = (p_re * m_im - p_im * m_re).astype(bf16)
            adjoint[0, 0] = (t_re * m_re + t_im * m_im).astype(bf16)
            adjoint[0, 1] = (t_re * m_im - t_im * m_re).astype(bf16)
            return carry

        lax.fori_loop(0, depth_count, backward, 0)
        for flip in range(depth_count):
            out_centers[flip][...] = grads[flip, :, half:]
            out_edges[flip][...] = grads[flip, :, :half]

    @pl.when(jnp.logical_not(live))
    def _():
        for ref in out_centers + out_edges:
            ref[...] = jnp.zeros(ref.shape, ref.dtype)


def place_edges_kernel(slots, info, *refs):
    pieces, (upper, lower, wrapped, upper_sum, lower_sum) = refs[:-5], refs[-5:]
    depth_index = lax.axis_index("depth")
    columns = upper.shape[-1]
    width = pieces[0].shape[-1]
    row, lane = iotas(pieces[0].shape[1], width)
    upper_sum[...] = jnp.zeros(upper_sum.shape, f32)
    lower_sum[...] = jnp.zeros(lower_sum.shape, f32)
    for flip, piece in enumerate(pieces):
        slot = depth_index ^ flip
        base, after, first = column_place(info, slots, slot, width, columns)
        to_upper = row >= info[slot]
        to_base = lane >= first
        for comp in range(2):
            value = piece[comp].astype(f32)
            for sheet, kept in (
                (upper_sum, jnp.where(to_upper, value, 0.0)),
                (lower_sum, jnp.where(to_upper, 0.0, value)),
            ):
                sheet[comp, :, pl.ds(base, width)] += jnp.where(to_base, kept, 0.0)
                sheet[comp, :, pl.ds(after, width)] += jnp.where(to_base, 0.0, kept)
    upper[...] = upper_sum[...].astype(bf16)
    lower[...] = lower_sum[...].astype(bf16)
    first_tile = lax.axis_index("scan") == 0

    @pl.when(first_tile)
    def _():
        wrapped[...] = upper[...]

    @pl.when(jnp.logical_not(first_tile))
    def _():
        wrapped[...] = lower[...]


def place_center_kernel(slots, info, *refs):
    pieces, sheet = refs[:-1], refs[-1]
    depth_index = lax.axis_index("depth")
    columns = sheet.shape[-1]
    width = pieces[0].shape[-1]
    _, lane = iotas(pieces[0].shape[1], width)
    sheet[...] = jnp.zeros(sheet.shape, f32)
    for flip, piece in enumerate(pieces):
        base, after, first = column_place(info, slots, depth_index ^ flip, width, columns)
        to_base = lane >= first
        for comp in range(2):
            value = piece[comp].astype(f32)
            sheet[comp, :, pl.ds(base, width)] += jnp.where(to_base, value, 0.0)
            sheet[comp, :, pl.ds(after, width)] += jnp.where(to_base, 0.0, value)


def body(transmission, probe_wave, prop_phase, measured, scan_rows, scan_cols, live_counts):
    pixels = probe_wave.shape[-1]
    slots = measured.shape[0]
    rows = transmission.shape[2]
    columns = transmission.shape[3]
    count = lax.axis_size("depth")
    own = transmission[0]
    info, own = lax.optimization_barrier(
        (jnp.concatenate([scan_rows, scan_cols, live_counts]), own)
    )
    info = shifted(info, "scan", 1)
    strip = call(strip_kernel, sds(own.shape, bf16), [own], [VMEM], name="strip")
    info, strip = lax.optimization_barrier((info, strip))
    wrapped = between_ends(strip, "scan")
    upper = passed_on(strip, "scan", 1)
    lower = passed_on(strip, "scan", -1)

    part = sds((2, rows, pixels), bf16)
    centers = call(
        functools.partial(center_kernel, slots, pixels),
        [part] * count, [info, own], [SMEM, VMEM], name="cut_center",
    )

    def across_depth(pieces):
        moved = [exchanged(pieces[flip], "depth", flip) for flip in range(count - 1, 0, -1)]
        return [pieces[0]] + moved[::-1]

    centers = across_depth(centers)

    phase, centers[0] = lax.optimization_barrier((prop_phase, centers[0]))
    order = parity_order(pixels)
    square = sds((pixels, pixels), f32)
    prop_re, prop_im, amplitude = call(
        frequency_kernel,
        [square, square, sds((pixels, pixels), bf16)],
        [phase, jnp.asarray(order), jnp.asarray(order.T), measured],
        [VMEM] * 4, flops=2400 * pixels**3, transcendentals=2 * pixels**2, name="frequency_order",
    )
    amplitude = shifted(amplitude, "scan", 1)

    stack = split_tables(pixels)
    made = call(
        functools.partial(table_kernel, slots),
        [sds((2, pixels, pixels), bf16)] + [sds((pixels, pixels), bf16)] * 8,
        [info, jnp.asarray(stack), jnp.asarray(stack.T), probe_wave],
        [SMEM, VMEM, VMEM, VMEM], flops=16 * pixels**3, name="tables",
    )
    edges = call(
        functools.partial(edge_kernel, slots, pixels),
        [part] * count, [info, upper, lower, wrapped], [SMEM] + [VMEM] * 3, name="cut_edges",
    )
    edges = across_depth(edges)

    args = [info, prop_re, prop_im, amplitude, *made, *centers, *edges]
    grads = call(
        functools.partial(wave_kernel, slots, count),
        [part] * (2 * count), args, [SMEM] + [VMEM] * (len(args) - 1),
        scratch=[
            pltpu.VMEM((count, 2, pixels, pixels), bf16),
            pltpu.VMEM((count + 1, 2, pixels, pixels), bf16),
            pltpu.VMEM((1, 2, pixels, pixels), bf16),
            pltpu.VMEM((count, 2, pixels, pixels), bf16),
        ],
        flops=(2 * count + 1) * 16 * pixels**3, name="waves",
    )
    out_centers, out_edges = grads[:count], grads[count:]
    out_edges = across_depth(out_edges)
    out_centers = across_depth(out_centers)
    sheet_bf16 = sds((2, rows, columns), bf16)
    sheet_f32 = sds((2, rows, columns), f32)
    to_upper, to_lower, to_wrapped = call(
        functools.partial(place_edges_kernel, slots),
        [sheet_bf16] * 3, [info, *out_edges], [SMEM] + [VMEM] * count,
        scratch=[pltpu.VMEM(sheet_f32.shape, f32)] * 2, name="place_edges",
    )
    from_end = between_ends(to_wrapped, "scan")
    from_next = passed_on(to_upper, "scan", -1)
    from_previous = passed_on(to_lower, "scan", 1)
    sheet = call(
        functools.partial(place_center_kernel, slots),
        sheet_f32, [info, *out_centers], [SMEM] + [VMEM] * count, name="place_center",
    )
    gradient = (
        sheet + from_next.astype(f32) + from_previous.astype(f32) + from_end.astype(f32)
    )
    return gradient[None]


def solution(mesh):
    in_specs = (
        P("depth", None, "scan", None),
        P(),
        P(),
        P("scan", None, None),
        P("scan"),
        P("scan"),
        P("scan"),
    )
    out_specs = P("depth", None, "scan", None)
    return jax.shard_map(body, mesh=mesh, in_specs=in_specs, out_specs=out_specs, check_vma=False)
```

```python
import functools
import math

import jax
import jax.numpy as jnp
import ml_dtypes
import numpy as np
from jax import lax
from jax.experimental import pallas as pl
from jax.experimental.pallas import tpu as pltpu
from jax.sharding import PartitionSpec as P

epsilon = 1.0
bf16 = jnp.bfloat16
f32 = jnp.float32
VMEM = pl.BlockSpec(memory_space=pltpu.VMEM)
SMEM = pl.BlockSpec(memory_space=pltpu.SMEM)
LIMIT = 48 * 1024 * 1024


def shifted(value, axis, steps):
    count = lax.axis_size(axis)
    pairs = [(source, (source + steps) % count) for source in range(count)]
    return lax.ppermute(value, axis, pairs)


def swapped(value, axis, first):
    count = lax.axis_size(axis)
    pairs = [
        (source, (source + (1 if source % 2 == first else -1)) % count) for source in range(count)
    ]
    return lax.ppermute(value, axis, pairs)


def exchanged(value, axis, flip):
    count = lax.axis_size(axis)
    return lax.ppermute(value, axis, [(source, source ^ flip) for source in range(count)])


def split_tables(pixels):
    indices = np.arange(pixels)
    angles = (indices[:, None] * indices[None, :] % pixels) * (2.0 * math.pi / pixels)
    norm_scale = 1.0 / math.sqrt(pixels)
    table_re = (np.cos(angles) * norm_scale).astype(np.float32).astype(ml_dtypes.bfloat16)
    table_im = (-np.sin(angles) * norm_scale).astype(np.float32).astype(ml_dtypes.bfloat16)
    return np.concatenate([table_re[0::2], table_im[0::2], table_re[1::2], table_im[1::2]], axis=0)


def parity_order(pixels):
    order = np.concatenate([np.arange(0, pixels, 2), np.arange(1, pixels, 2)])
    return (order[:, None] == np.arange(pixels)[None, :]).astype(np.float32)


def call(kernel, out_shape, args, specs, scratch=(), flops=0, transcendentals=0, name=None):
    outs = out_shape if isinstance(out_shape, (list, tuple)) else [out_shape]
    moved = sum(math.prod(a.shape) * a.dtype.itemsize for a in list(args) + list(outs))
    return pl.pallas_call(
        kernel,
        out_shape=out_shape,
        in_specs=specs,
        out_specs=jax.tree.map(lambda _: VMEM, out_shape),
        scratch_shapes=list(scratch),
        compiler_params=pltpu.CompilerParams(vmem_limit_bytes=LIMIT),
        cost_estimate=pl.CostEstimate(
            flops=flops, bytes_accessed=moved, transcendentals=transcendentals
        ),
        name=name,
    )(*args)


def sds(shape, dtype):
    return jax.ShapeDtypeStruct(shape, dtype)


def column_place(info, slots, slot, width, columns):
    col = info[slots + slot]
    base = (col // width) * width
    after = jnp.minimum(base + width, columns - width)
    return pl.multiple_of(base, width), pl.multiple_of(after, width), col - base


def iotas(rows, cols):
    return (
        lax.broadcasted_iota(jnp.int32, (rows, cols), 0),
        lax.broadcasted_iota(jnp.int32, (rows, cols), 1),
    )


def strip_kernel(own, strip):
    strip[...] = own[...].astype(bf16)


def center_kernel(slots, width, info, own, *outs):
    depth_index = lax.axis_index("depth")
    columns = own.shape[-1]
    _, lane = iotas(own.shape[1], width)
    for flip in range(len(outs)):
        base, after, first = column_place(info, slots, depth_index ^ flip, width, columns)
        for comp in range(2):
            outs[flip][comp] = jnp.where(
                lane >= first, own[comp, :, pl.ds(base, width)], own[comp, :, pl.ds(after, width)]
            ).astype(bf16)


def edge_kernel(slots, width, info, across, beside, *outs):
    depth_index = lax.axis_index("depth")
    even = lax.rem(lax.axis_index("scan"), 2) == 0
    columns = across.shape[-1]
    row, lane = iotas(across.shape[1], width)
    for flip in range(len(outs)):
        slot = depth_index ^ flip
        base, after, first = column_place(info, slots, slot, width, columns)
        from_across = jnp.logical_xor(row < info[slot], even)

        def rows_at(comp, place):
            return jnp.where(
                from_across,
                across[comp, :, pl.ds(place, width)].astype(f32),
                beside[comp, :, pl.ds(place, width)].astype(f32),
            )

        for comp in range(2):
            outs[flip][comp] = jnp.where(
                lane >= first, rows_at(comp, base), rows_at(comp, after)
            ).astype(bf16)


def frequency_kernel(phase, order, order_t, measured, prop_re, prop_im, amplitude):
    def reorder(value):
        rows = jnp.dot(
            order[...], value, preferred_element_type=f32, precision=lax.Precision.HIGHEST
        )
        return jnp.dot(
            rows, order_t[...], preferred_element_type=f32, precision=lax.Precision.HIGHEST
        )

    turned = reorder(phase[...])
    prop_re[...] = jnp.cos(turned)
    prop_im[...] = jnp.sin(turned)
    amplitude[...] = reorder(measured[lax.axis_index("depth")]).astype(bf16)


def table_kernel(slots, info, stack, stack_t, probe, psi0, *tables):
    depth_index = lax.axis_index("depth")
    pixels = probe.shape[-1]
    half = pixels // 2
    row_shift = info[depth_index]
    col_shift = lax.rem(info[slots + depth_index], pixels)

    def shift_matrix(rows, cols, shift, transposed):
        row, lane = iotas(rows, cols)
        offset = (lane - row if transposed else row - lane) + shift
        return jnp.where((offset == 0) | (offset == pixels), 1.0, 0.0).astype(bf16)

    def pair(shift):
        cols = jnp.dot(
            stack[...], shift_matrix(pixels, half, shift, False), preferred_element_type=f32
        )
        rows = jnp.dot(
            shift_matrix(half, pixels, shift, True), stack_t[...], preferred_element_type=f32
        )
        forms, forms_t = [], []
        for parity in range(2):
            at = 2 * parity * half
            re, im = cols[at : at + half], cols[at + half : at + pixels]
            top = jnp.concatenate([re, -im], axis=1)
            bottom = jnp.concatenate([im, re], axis=1)
            forms.append(jnp.concatenate([top, bottom], axis=0).astype(bf16))
            re, im = rows[:, at : at + half], rows[:, at + half : at + pixels]
            top = jnp.concatenate([re, im], axis=1)
            bottom = jnp.concatenate([-im, re], axis=1)
            forms_t.append(jnp.concatenate([top, bottom], axis=0).astype(bf16))
        return forms, forms_t

    row_forms, row_forms_t = pair(row_shift)
    col_forms, col_forms_t = pair(col_shift)
    made = row_forms + col_forms_t + col_forms + row_forms_t
    for ref, value in zip(tables, made):
        ref[...] = value
    down = shift_matrix(pixels, pixels, row_shift, True)
    across = shift_matrix(pixels, pixels, col_shift, False)
    for comp in range(2):
        moved = jnp.dot(down, probe[comp].astype(bf16), preferred_element_type=f32).astype(bf16)
        psi0[comp] = jnp.dot(moved, across, preferred_element_type=f32).astype(bf16)


def wave_kernel(slots, depth_count, info, prop_re, prop_im, amplitude, psi0, *refs):
    tables = refs[:8]
    centers = refs[8 : 8 + depth_count]
    edges = refs[8 + depth_count : 8 + 2 * depth_count]
    out_centers = refs[8 + 2 * depth_count : 8 + 3 * depth_count]
    out_edges = refs[8 + 3 * depth_count : 8 + 4 * depth_count]
    patches, waves, adjoint, grads = refs[8 + 4 * depth_count :]
    depth_index = lax.axis_index("depth")
    pixels = psi0.shape[-1]
    half = pixels // 2
    live = depth_index < info[2 * slots]
    fwd_row_e, fwd_row_o, fwd_col_e, fwd_col_o, inv_col_e, inv_col_o, inv_row_e, inv_row_o = tables

    def dot(left, right):
        return jnp.dot(left, right, preferred_element_type=f32)

    def propagate(x_re, x_im, at_frequency):
        def rows_of(sign):
            mixed = [v[:half] + v[half:] if sign > 0 else v[:half] - v[half:] for v in (x_re, x_im)]
            return jnp.concatenate(mixed, axis=0).astype(bf16)

        u_even = dot(fwd_row_e[...], rows_of(1))
        u_odd = dot(fwd_row_o[...], rows_of(-1))

        def cols_of(sign):
            parts = []
            for u in (u_even, u_odd):
                mixed = u[:, :half] + u[:, half:] if sign > 0 else u[:, :half] - u[:, half:]
                parts.append(jnp.concatenate([mixed[:half], mixed[half:]], axis=1))
            return jnp.concatenate(parts, axis=0).astype(bf16)

        v_even = dot(cols_of(1), fwd_col_e[...])
        v_odd = dot(cols_of(-1), fwd_col_o[...])
        b_even = at_frequency(v_even[:, :half], v_even[:, half:], slice(0, half))
        b_odd = at_frequency(v_odd[:, :half], v_odd[:, half:], slice(half, pixels))
        w_even = dot(jnp.concatenate(b_even, axis=1).astype(bf16), inv_col_e[...])
        w_odd = dot(jnp.concatenate(b_odd, axis=1).astype(bf16), inv_col_o[...])
        w_low, w_high = w_even + w_odd, w_even - w_odd
        w_re = jnp.concatenate([w_low[:, :half], w_high[:, :half]], axis=1)
        w_im = jnp.concatenate([w_low[:, half:], w_high[:, half:]], axis=1)
        y_even = dot(
            inv_row_e[...], jnp.concatenate([w_re[:half], w_im[:half]], axis=0).astype(bf16)
        )
        y_odd = dot(
            inv_row_o[...], jnp.concatenate([w_re[half:], w_im[half:]], axis=0).astype(bf16)
        )
        low, high = y_even + y_odd, y_even - y_odd
        return (
            jnp.concatenate([low[:half], high[:half]], axis=0),
            jnp.concatenate([low[half:], high[half:]], axis=0),
        )

    def turn(re, im, cols):
        p_re, p_im = prop_re[:, cols], prop_im[:, cols]
        return [re * p_re - im * p_im, re * p_im + im * p_re]

    def turn_back(re, im, cols):
        p_re, p_im = prop_re[:, cols], prop_im[:, cols]
        return [re * p_re + im * p_im, im * p_re - re * p_im]

    def residual(re, im, cols):
        modulus = jnp.sqrt(re * re + im * im + epsilon)
        factor = 1.0 - amplitude[:, cols].astype(f32) / modulus
        return [factor * re, factor * im]

    def pair_of(ref, index):
        return ref[index, 0].astype(f32), ref[index, 1].astype(f32)

    @pl.when(live)
    def _():
        for flip in range(depth_count):
            patches[depth_index ^ flip, :, half:] = centers[flip][...]
            patches[depth_index ^ flip, :, :half] = edges[flip][...]
        waves[0] = psi0[...]

        def forward(k, carry):
            t_re, t_im = pair_of(patches, k)
            p_re, p_im = pair_of(waves, k)
            n_re, n_im = propagate(t_re * p_re - t_im * p_im, t_re * p_im + t_im * p_re, turn)
            waves[k + 1, 0] = n_re.astype(bf16)
            waves[k + 1, 1] = n_im.astype(bf16)
            return carry

        lax.fori_loop(0, depth_count, forward, 0)
        l_re, l_im = propagate(*pair_of(waves, depth_count), residual)
        adjoint[0, 0] = l_re.astype(bf16)
        adjoint[0, 1] = l_im.astype(bf16)

        def backward(step, carry):
            k = depth_count - 1 - step
            m_re, m_im = propagate(*pair_of(adjoint, 0), turn_back)
            t_re, t_im = pair_of(patches, k)
            p_re, p_im = pair_of(waves, k)
            grads[k ^ depth_index, 0] = (p_re * m_re + p_im * m_im).astype(bf16)
            grads[k ^ depth_index, 1] = (p_re * m_im - p_im * m_re).astype(bf16)
            adjoint[0, 0] = (t_re * m_re + t_im * m_im).astype(bf16)
            adjoint[0, 1] = (t_re * m_im - t_im * m_re).astype(bf16)
            return carry

        lax.fori_loop(0, depth_count, backward, 0)
        for flip in range(depth_count):
            out_centers[flip][...] = grads[flip, :, half:]
            out_edges[flip][...] = grads[flip, :, :half]

    @pl.when(jnp.logical_not(live))
    def _():
        for ref in out_centers + out_edges:
            ref[...] = jnp.zeros(ref.shape, ref.dtype)


def place_edges_kernel(slots, info, *refs):
    pieces, (across, beside, across_sum, beside_sum) = refs[:-4], refs[-4:]
    depth_index = lax.axis_index("depth")
    even = lax.rem(lax.axis_index("scan"), 2) == 0
    columns = across.shape[-1]
    width = pieces[0].shape[-1]
    row, lane = iotas(pieces[0].shape[1], width)
    across_sum[...] = jnp.zeros(across_sum.shape, f32)
    beside_sum[...] = jnp.zeros(beside_sum.shape, f32)
    for flip, piece in enumerate(pieces):
        slot = depth_index ^ flip
        base, after, first = column_place(info, slots, slot, width, columns)
        to_across = jnp.logical_xor(row < info[slot], even)
        to_base = lane >= first
        for comp in range(2):
            value = piece[comp].astype(f32)
            for sheet, kept in (
                (across_sum, jnp.where(to_across, value, 0.0)),
                (beside_sum, jnp.where(to_across, 0.0, value)),
            ):
                sheet[comp, :, pl.ds(base, width)] += jnp.where(to_base, kept, 0.0)
                sheet[comp, :, pl.ds(after, width)] += jnp.where(to_base, 0.0, kept)
    across[...] = across_sum[...].astype(bf16)
    beside[...] = beside_sum[...].astype(bf16)


def place_center_kernel(slots, info, *refs):
    pieces, sheet = refs[:-1], refs[-1]
    depth_index = lax.axis_index("depth")
    columns = sheet.shape[-1]
    width = pieces[0].shape[-1]
    _, lane = iotas(pieces[0].shape[1], width)
    sheet[...] = jnp.zeros(sheet.shape, f32)
    for flip, piece in enumerate(pieces):
        base, after, first = column_place(info, slots, depth_index ^ flip, width, columns)
        to_base = lane >= first
        for comp in range(2):
            value = piece[comp].astype(f32)
            sheet[comp, :, pl.ds(base, width)] += jnp.where(to_base, value, 0.0)
            sheet[comp, :, pl.ds(after, width)] += jnp.where(to_base, 0.0, value)


def body(transmission, probe_wave, prop_phase, measured, scan_rows, scan_cols, live_counts):
    pixels = probe_wave.shape[-1]
    slots = measured.shape[0]
    rows = transmission.shape[2]
    columns = transmission.shape[3]
    count = lax.axis_size("depth")
    own = transmission[0]
    info, own = lax.optimization_barrier(
        (jnp.concatenate([scan_rows, scan_cols, live_counts]), own)
    )
    info = shifted(info, "scan", 1)
    strip = call(strip_kernel, sds(own.shape, bf16), [own], [VMEM], name="strip")
    info, strip = lax.optimization_barrier((info, strip))
    across = swapped(strip, "scan", 1)
    beside = swapped(strip, "scan", 0)

    part = sds((2, rows, pixels), bf16)
    centers = call(
        functools.partial(center_kernel, slots, pixels),
        [part] * count, [info, own], [SMEM, VMEM], name="cut_center",
    )

    def across_depth(pieces):
        moved = [exchanged(pieces[flip], "depth", flip) for flip in range(count - 1, 0, -1)]
        return [pieces[0]] + moved[::-1]

    centers = across_depth(centers)

    phase, centers[0] = lax.optimization_barrier((prop_phase, centers[0]))
    order = parity_order(pixels)
    square = sds((pixels, pixels), f32)
    prop_re, prop_im, amplitude = call(
        frequency_kernel,
        [square, square, sds((pixels, pixels), bf16)],
        [phase, jnp.asarray(order), jnp.asarray(order.T), measured],
        [VMEM] * 4, flops=2400 * pixels**3, transcendentals=2 * pixels**2, name="frequency_order",
    )
    amplitude = shifted(amplitude, "scan", 1)

    stack = split_tables(pixels)
    made = call(
        functools.partial(table_kernel, slots),
        [sds((2, pixels, pixels), bf16)] + [sds((pixels, pixels), bf16)] * 8,
        [info, jnp.asarray(stack), jnp.asarray(stack.T), probe_wave],
        [SMEM, VMEM, VMEM, VMEM], flops=16 * pixels**3, name="tables",
    )
    edges = call(
        functools.partial(edge_kernel, slots, pixels),
        [part] * count, [info, across, beside], [SMEM, VMEM, VMEM], name="cut_edges",
    )
    edges = across_depth(edges)

    args = [info, prop_re, prop_im, amplitude, *made, *centers, *edges]
    grads = call(
        functools.partial(wave_kernel, slots, count),
        [part] * (2 * count), args, [SMEM] + [VMEM] * (len(args) - 1),
        scratch=[
            pltpu.VMEM((count, 2, pixels, pixels), bf16),
            pltpu.VMEM((count + 1, 2, pixels, pixels), bf16),
            pltpu.VMEM((1, 2, pixels, pixels), bf16),
            pltpu.VMEM((count, 2, pixels, pixels), bf16),
        ],
        flops=(2 * count + 1) * 16 * pixels**3, name="waves",
    )
    out_centers, out_edges = grads[:count], grads[count:]
    out_edges = across_depth(out_edges)
    out_centers = across_depth(out_centers)
    sheet_bf16 = sds((2, rows, columns), bf16)
    sheet_f32 = sds((2, rows, columns), f32)
    to_across, to_beside = call(
        functools.partial(place_edges_kernel, slots),
        [sheet_bf16, sheet_bf16], [info, *out_edges], [SMEM] + [VMEM] * count,
        scratch=[pltpu.VMEM(sheet_f32.shape, f32)] * 2, name="place_edges",
    )
    from_across = swapped(to_across, "scan", 1)
    from_beside = swapped(to_beside, "scan", 0)
    sheet = call(
        functools.partial(place_center_kernel, slots),
        sheet_f32, [info, *out_centers], [SMEM] + [VMEM] * count, name="place_center",
    )
    gradient = sheet + from_across.astype(f32) + from_beside.astype(f32)
    return gradient[None]


def solution(mesh):
    in_specs = (
        P("depth", None, "scan", None),
        P(),
        P(),
        P("scan", None, None),
        P("scan"),
        P("scan"),
        P("scan"),
    )
    out_specs = P("depth", None, "scan", None)
    return jax.shard_map(body, mesh=mesh, in_specs=in_specs, out_specs=out_specs, check_vma=False)
```

```python
import functools
import math

import jax
import jax.numpy as jnp
import ml_dtypes
import numpy as np
from jax import lax
from jax.experimental import pallas as pl
from jax.experimental.pallas import tpu as pltpu
from jax.sharding import PartitionSpec as P

epsilon = 1.0
bf16 = jnp.bfloat16
f32 = jnp.float32
VMEM = pl.BlockSpec(memory_space=pltpu.VMEM)
SMEM = pl.BlockSpec(memory_space=pltpu.SMEM)
LIMIT = 48 * 1024 * 1024


def shifted(value, axis, steps):
    count = lax.axis_size(axis)
    pairs = [(source, (source + steps) % count) for source in range(count)]
    return lax.ppermute(value, axis, pairs)


def swapped(value, axis, first):
    count = lax.axis_size(axis)
    pairs = [
        (source, (source + (1 if source % 2 == first else -1)) % count) for source in range(count)
    ]
    return lax.ppermute(value, axis, pairs)


def exchanged(value, axis, flip):
    count = lax.axis_size(axis)
    return lax.ppermute(value, axis, [(source, source ^ flip) for source in range(count)])


def split_tables(pixels):
    indices = np.arange(pixels)
    angles = (indices[:, None] * indices[None, :] % pixels) * (2.0 * math.pi / pixels)
    norm_scale = 1.0 / math.sqrt(pixels)
    table_re = (np.cos(angles) * norm_scale).astype(np.float32).astype(ml_dtypes.bfloat16)
    table_im = (-np.sin(angles) * norm_scale).astype(np.float32).astype(ml_dtypes.bfloat16)
    return np.concatenate([table_re[0::2], table_im[0::2], table_re[1::2], table_im[1::2]], axis=0)


def parity_order(pixels):
    order = np.concatenate([np.arange(0, pixels, 2), np.arange(1, pixels, 2)])
    return (order[:, None] == np.arange(pixels)[None, :]).astype(np.float32)


def call(kernel, out_shape, args, specs, scratch=(), flops=0, transcendentals=0, name=None):
    outs = out_shape if isinstance(out_shape, (list, tuple)) else [out_shape]
    moved = sum(math.prod(a.shape) * a.dtype.itemsize for a in list(args) + list(outs))
    return pl.pallas_call(
        kernel,
        out_shape=out_shape,
        in_specs=specs,
        out_specs=jax.tree.map(lambda _: VMEM, out_shape),
        scratch_shapes=list(scratch),
        compiler_params=pltpu.CompilerParams(vmem_limit_bytes=LIMIT),
        cost_estimate=pl.CostEstimate(
            flops=flops, bytes_accessed=moved, transcendentals=transcendentals
        ),
        name=name,
    )(*args)


def sds(shape, dtype):
    return jax.ShapeDtypeStruct(shape, dtype)


def column_place(info, slots, slot, width, columns):
    col = info[slots + slot]
    base = (col // width) * width
    after = jnp.minimum(base + width, columns - width)
    return pl.multiple_of(base, width), pl.multiple_of(after, width), col - base


def iotas(rows, cols):
    return (
        lax.broadcasted_iota(jnp.int32, (rows, cols), 0),
        lax.broadcasted_iota(jnp.int32, (rows, cols), 1),
    )


def strip_kernel(own, strip):
    strip[...] = own[...].astype(bf16)


def center_kernel(slots, width, info, own, *outs):
    depth_index = lax.axis_index("depth")
    columns = own.shape[-1]
    _, lane = iotas(own.shape[1], width)
    for flip in range(len(outs)):
        base, after, first = column_place(info, slots, depth_index ^ flip, width, columns)
        for comp in range(2):
            outs[flip][comp] = jnp.where(
                lane >= first, own[comp, :, pl.ds(base, width)], own[comp, :, pl.ds(after, width)]
            ).astype(bf16)


def edge_kernel(slots, width, info, across, beside, *outs):
    depth_index = lax.axis_index("depth")
    even = lax.rem(lax.axis_index("scan"), 2) == 0
    columns = across.shape[-1]
    row, lane = iotas(across.shape[1], width)
    for flip in range(len(outs)):
        slot = depth_index ^ flip
        base, after, first = column_place(info, slots, slot, width, columns)
        from_across = jnp.logical_xor(row < info[slot], even)

        def rows_at(comp, place):
            return jnp.where(
                from_across,
                across[comp, :, pl.ds(place, width)].astype(f32),
                beside[comp, :, pl.ds(place, width)].astype(f32),
            )

        for comp in range(2):
            outs[flip][comp] = jnp.where(
                lane >= first, rows_at(comp, base), rows_at(comp, after)
            ).astype(bf16)


def frequency_kernel(phase, order, order_t, measured, prop_re, prop_im, amplitude):
    def reorder(value):
        rows = jnp.dot(
            order[...], value, preferred_element_type=f32, precision=lax.Precision.HIGHEST
        )
        return jnp.dot(
            rows, order_t[...], preferred_element_type=f32, precision=lax.Precision.HIGHEST
        )

    turned = reorder(phase[...])
    prop_re[...] = jnp.cos(turned)
    prop_im[...] = jnp.sin(turned)
    amplitude[...] = reorder(measured[lax.axis_index("depth")]).astype(bf16)


def table_kernel(slots, info, stack, stack_t, probe, psi0, *tables):
    depth_index = lax.axis_index("depth")
    pixels = probe.shape[-1]
    half = pixels // 2
    row_shift = info[depth_index]
    col_shift = lax.rem(info[slots + depth_index], pixels)

    def shift_matrix(rows, cols, shift, transposed):
        row, lane = iotas(rows, cols)
        offset = (lane - row if transposed else row - lane) + shift
        return jnp.where((offset == 0) | (offset == pixels), 1.0, 0.0).astype(bf16)

    def pair(shift):
        cols = jnp.dot(
            stack[...], shift_matrix(pixels, half, shift, False), preferred_element_type=f32
        )
        rows = jnp.dot(
            shift_matrix(half, pixels, shift, True), stack_t[...], preferred_element_type=f32
        )
        forms, forms_t = [], []
        for parity in range(2):
            at = 2 * parity * half
            re, im = cols[at : at + half], cols[at + half : at + pixels]
            top = jnp.concatenate([re, -im], axis=1)
            bottom = jnp.concatenate([im, re], axis=1)
            forms.append(jnp.concatenate([top, bottom], axis=0).astype(bf16))
            re, im = rows[:, at : at + half], rows[:, at + half : at + pixels]
            top = jnp.concatenate([re, im], axis=1)
            bottom = jnp.concatenate([-im, re], axis=1)
            forms_t.append(jnp.concatenate([top, bottom], axis=0).astype(bf16))
        return forms, forms_t

    row_forms, row_forms_t = pair(row_shift)
    col_forms, col_forms_t = pair(col_shift)
    made = row_forms + col_forms_t + col_forms + row_forms_t
    for ref, value in zip(tables, made):
        ref[...] = value
    down = shift_matrix(pixels, pixels, row_shift, True)
    across = shift_matrix(pixels, pixels, col_shift, False)
    for comp in range(2):
        moved = jnp.dot(down, probe[comp].astype(bf16), preferred_element_type=f32).astype(bf16)
        psi0[comp] = jnp.dot(moved, across, preferred_element_type=f32).astype(bf16)


def wave_kernel(slots, depth_count, info, prop_re, prop_im, amplitude, psi0, *refs):
    tables = refs[:8]
    centers = refs[8 : 8 + depth_count]
    edges = refs[8 + depth_count : 8 + 2 * depth_count]
    out_centers = refs[8 + 2 * depth_count : 8 + 3 * depth_count]
    out_edges = refs[8 + 3 * depth_count : 8 + 4 * depth_count]
    patches, waves, adjoint, grads = refs[8 + 4 * depth_count :]
    depth_index = lax.axis_index("depth")
    pixels = psi0.shape[-1]
    half = pixels // 2
    live = depth_index < info[2 * slots]
    fwd_row_e, fwd_row_o, fwd_col_e, fwd_col_o, inv_col_e, inv_col_o, inv_row_e, inv_row_o = tables

    def dot(left, right):
        return jnp.dot(left, right, preferred_element_type=f32)

    def propagate(x_re, x_im, at_frequency):
        def rows_of(sign):
            mixed = [v[:half] + v[half:] if sign > 0 else v[:half] - v[half:] for v in (x_re, x_im)]
            return jnp.concatenate(mixed, axis=0).astype(bf16)

        u_even = dot(fwd_row_e[...], rows_of(1))
        u_odd = dot(fwd_row_o[...], rows_of(-1))

        def cols_of(sign):
            parts = []
            for u in (u_even, u_odd):
                mixed = u[:, :half] + u[:, half:] if sign > 0 else u[:, :half] - u[:, half:]
                parts.append(jnp.concatenate([mixed[:half], mixed[half:]], axis=1))
            return jnp.concatenate(parts, axis=0).astype(bf16)

        v_even = dot(cols_of(1), fwd_col_e[...])
        v_odd = dot(cols_of(-1), fwd_col_o[...])
        b_even = at_frequency(v_even[:, :half], v_even[:, half:], slice(0, half))
        b_odd = at_frequency(v_odd[:, :half], v_odd[:, half:], slice(half, pixels))
        w_even = dot(jnp.concatenate(b_even, axis=1).astype(bf16), inv_col_e[...])
        w_odd = dot(jnp.concatenate(b_odd, axis=1).astype(bf16), inv_col_o[...])
        w_low, w_high = w_even + w_odd, w_even - w_odd
        w_re = jnp.concatenate([w_low[:, :half], w_high[:, :half]], axis=1)
        w_im = jnp.concatenate([w_low[:, half:], w_high[:, half:]], axis=1)
        y_even = dot(
            inv_row_e[...], jnp.concatenate([w_re[:half], w_im[:half]], axis=0).astype(bf16)
        )
        y_odd = dot(
            inv_row_o[...], jnp.concatenate([w_re[half:], w_im[half:]], axis=0).astype(bf16)
        )
        low, high = y_even + y_odd, y_even - y_odd
        return (
            jnp.concatenate([low[:half], high[:half]], axis=0),
            jnp.concatenate([low[half:], high[half:]], axis=0),
        )

    def turn(re, im, cols):
        p_re, p_im = prop_re[:, cols], prop_im[:, cols]
        return [re * p_re - im * p_im, re * p_im + im * p_re]

    def turn_back(re, im, cols):
        p_re, p_im = prop_re[:, cols], prop_im[:, cols]
        return [re * p_re + im * p_im, im * p_re - re * p_im]

    def residual(re, im, cols):
        modulus = jnp.sqrt(re * re + im * im + epsilon)
        factor = 1.0 - amplitude[:, cols].astype(f32) / modulus
        return [factor * re, factor * im]

    def pair_of(ref, index):
        return ref[index, 0].astype(f32), ref[index, 1].astype(f32)

    @pl.when(live)
    def _():
        for flip in range(depth_count):
            patches[depth_index ^ flip, :, half:] = centers[flip][...]
            patches[depth_index ^ flip, :, :half] = edges[flip][...]
        waves[0] = psi0[...]

        def forward(k, carry):
            t_re, t_im = pair_of(patches, k)
            p_re, p_im = pair_of(waves, k)
            n_re, n_im = propagate(t_re * p_re - t_im * p_im, t_re * p_im + t_im * p_re, turn)
            waves[k + 1, 0] = n_re.astype(bf16)
            waves[k + 1, 1] = n_im.astype(bf16)
            return carry

        lax.fori_loop(0, depth_count, forward, 0)
        l_re, l_im = propagate(*pair_of(waves, depth_count), residual)
        adjoint[0, 0] = l_re.astype(bf16)
        adjoint[0, 1] = l_im.astype(bf16)

        def backward(step, carry):
            k = depth_count - 1 - step
            m_re, m_im = propagate(*pair_of(adjoint, 0), turn_back)
            t_re, t_im = pair_of(patches, k)
            p_re, p_im = pair_of(waves, k)
            grads[k ^ depth_index, 0] = (p_re * m_re + p_im * m_im).astype(bf16)
            grads[k ^ depth_index, 1] = (p_re * m_im - p_im * m_re).astype(bf16)
            adjoint[0, 0] = (t_re * m_re + t_im * m_im).astype(bf16)
            adjoint[0, 1] = (t_re * m_im - t_im * m_re).astype(bf16)
            return carry

        lax.fori_loop(0, depth_count, backward, 0)
        for flip in range(depth_count):
            out_centers[flip][...] = grads[flip, :, half:]
            out_edges[flip][...] = grads[flip, :, :half]

    @pl.when(jnp.logical_not(live))
    def _():
        for ref in out_centers + out_edges:
            ref[...] = jnp.zeros(ref.shape, ref.dtype)


def place_edges_kernel(slots, info, *refs):
    pieces, (across, beside, across_sum, beside_sum) = refs[:-4], refs[-4:]
    depth_index = lax.axis_index("depth")
    even = lax.rem(lax.axis_index("scan"), 2) == 0
    columns = across.shape[-1]
    width = pieces[0].shape[-1]
    row, lane = iotas(pieces[0].shape[1], width)
    across_sum[...] = jnp.zeros(across_sum.shape, f32)
    beside_sum[...] = jnp.zeros(beside_sum.shape, f32)
    for flip, piece in enumerate(pieces):
        slot = depth_index ^ flip
        base, after, first = column_place(info, slots, slot, width, columns)
        to_across = jnp.logical_xor(row < info[slot], even)
        to_base = lane >= first
        for comp in range(2):
            value = piece[comp].astype(f32)
            for sheet, kept in (
                (across_sum, jnp.where(to_across, value, 0.0)),
                (beside_sum, jnp.where(to_across, 0.0, value)),
            ):
                sheet[comp, :, pl.ds(base, width)] += jnp.where(to_base, kept, 0.0)
                sheet[comp, :, pl.ds(after, width)] += jnp.where(to_base, 0.0, kept)
    across[...] = across_sum[...].astype(bf16)
    beside[...] = beside_sum[...].astype(bf16)


def place_center_kernel(slots, info, *refs):
    pieces, sheet = refs[:-1], refs[-1]
    depth_index = lax.axis_index("depth")
    columns = sheet.shape[-1]
    width = pieces[0].shape[-1]
    _, lane = iotas(pieces[0].shape[1], width)
    sheet[...] = jnp.zeros(sheet.shape, f32)
    for flip, piece in enumerate(pieces):
        base, after, first = column_place(info, slots, depth_index ^ flip, width, columns)
        to_base = lane >= first
        for comp in range(2):
            value = piece[comp].astype(f32)
            sheet[comp, :, pl.ds(base, width)] += jnp.where(to_base, value, 0.0)
            sheet[comp, :, pl.ds(after, width)] += jnp.where(to_base, 0.0, value)


def body(transmission, probe_wave, prop_phase, measured, scan_rows, scan_cols, live_counts):
    pixels = probe_wave.shape[-1]
    slots = measured.shape[0]
    rows = transmission.shape[2]
    columns = transmission.shape[3]
    count = lax.axis_size("depth")
    own = transmission[0]
    info, own = lax.optimization_barrier(
        (jnp.concatenate([scan_rows, scan_cols, live_counts]), own)
    )
    info = shifted(info, "scan", 1)
    strip = call(strip_kernel, sds(own.shape, bf16), [own], [VMEM], name="strip")
    info, strip = lax.optimization_barrier((info, strip))
    across = swapped(strip, "scan", 1)
    beside = swapped(strip, "scan", 0)

    part = sds((2, rows, pixels), bf16)
    centers = call(
        functools.partial(center_kernel, slots, pixels),
        [part] * count, [info, own], [SMEM, VMEM], name="cut_center",
    )

    def across_depth(pieces):
        moved = [exchanged(pieces[flip], "depth", flip) for flip in range(count - 1, 0, -1)]
        return [pieces[0]] + moved[::-1]

    centers = across_depth(centers)

    phase, centers[0] = lax.optimization_barrier((prop_phase, centers[0]))
    order = parity_order(pixels)
    square = sds((pixels, pixels), f32)
    prop_re, prop_im, amplitude = call(
        frequency_kernel,
        [square, square, sds((pixels, pixels), bf16)],
        [phase, jnp.asarray(order), jnp.asarray(order.T), measured],
        [VMEM] * 4, flops=2400 * pixels**3, transcendentals=2 * pixels**2, name="frequency_order",
    )
    amplitude, across = lax.optimization_barrier((amplitude, across))
    amplitude = shifted(amplitude, "scan", 1)

    stack = split_tables(pixels)
    made = call(
        functools.partial(table_kernel, slots),
        [sds((2, pixels, pixels), bf16)] + [sds((pixels, pixels), bf16)] * 8,
        [info, jnp.asarray(stack), jnp.asarray(stack.T), probe_wave],
        [SMEM, VMEM, VMEM, VMEM], flops=16 * pixels**3, name="tables",
    )
    edges = call(
        functools.partial(edge_kernel, slots, pixels),
        [part] * count, [info, across, beside], [SMEM, VMEM, VMEM], name="cut_edges",
    )
    edges = across_depth(edges)

    args = [info, prop_re, prop_im, amplitude, *made, *centers, *edges]
    grads = call(
        functools.partial(wave_kernel, slots, count),
        [part] * (2 * count), args, [SMEM] + [VMEM] * (len(args) - 1),
        scratch=[
            pltpu.VMEM((count, 2, pixels, pixels), bf16),
            pltpu.VMEM((count + 1, 2, pixels, pixels), bf16),
            pltpu.VMEM((1, 2, pixels, pixels), bf16),
            pltpu.VMEM((count, 2, pixels, pixels), bf16),
        ],
        flops=(2 * count + 1) * 16 * pixels**3, name="waves",
    )
    out_centers, out_edges = grads[:count], grads[count:]
    out_edges = across_depth(out_edges)
    out_centers = across_depth(out_centers)
    sheet_bf16 = sds((2, rows, columns), bf16)
    sheet_f32 = sds((2, rows, columns), f32)
    to_across, to_beside = call(
        functools.partial(place_edges_kernel, slots),
        [sheet_bf16, sheet_bf16], [info, *out_edges], [SMEM] + [VMEM] * count,
        scratch=[pltpu.VMEM(sheet_f32.shape, f32)] * 2, name="place_edges",
    )
    from_across = swapped(to_across, "scan", 1)
    from_beside = swapped(to_beside, "scan", 0)
    sheet = call(
        functools.partial(place_center_kernel, slots),
        sheet_f32, [info, *out_centers], [SMEM] + [VMEM] * count, name="place_center",
    )
    gradient = sheet + from_across.astype(f32) + from_beside.astype(f32)
    return gradient[None]


def solution(mesh):
    in_specs = (
        P("depth", None, "scan", None),
        P(),
        P(),
        P("scan", None, None),
        P("scan"),
        P("scan"),
        P("scan"),
    )
    out_specs = P("depth", None, "scan", None)
    return jax.shard_map(body, mesh=mesh, in_specs=in_specs, out_specs=out_specs, check_vma=False)
```

```python
import functools
import math

import jax
import jax.numpy as jnp
import ml_dtypes
import numpy as np
from jax import lax
from jax.experimental import pallas as pl
from jax.experimental.pallas import tpu as pltpu
from jax.sharding import PartitionSpec as P

epsilon = 1.0
bf16 = jnp.bfloat16
f32 = jnp.float32
VMEM = pl.BlockSpec(memory_space=pltpu.VMEM)
SMEM = pl.BlockSpec(memory_space=pltpu.SMEM)
LIMIT = 48 * 1024 * 1024


def shifted(value, axis, steps):
    count = lax.axis_size(axis)
    pairs = [(source, (source + steps) % count) for source in range(count)]
    return lax.ppermute(value, axis, pairs)


def swapped(value, axis, first):
    count = lax.axis_size(axis)
    pairs = [
        (source, (source + (1 if source % 2 == first else -1)) % count) for source in range(count)
    ]
    return lax.ppermute(value, axis, pairs)


def exchanged(value, axis, flip):
    count = lax.axis_size(axis)
    return lax.ppermute(value, axis, [(source, source ^ flip) for source in range(count)])


def split_tables(pixels):
    indices = np.arange(pixels)
    angles = (indices[:, None] * indices[None, :] % pixels) * (2.0 * math.pi / pixels)
    norm_scale = 1.0 / math.sqrt(pixels)
    table_re = (np.cos(angles) * norm_scale).astype(np.float32).astype(ml_dtypes.bfloat16)
    table_im = (-np.sin(angles) * norm_scale).astype(np.float32).astype(ml_dtypes.bfloat16)
    return np.concatenate([table_re[0::2], table_im[0::2], table_re[1::2], table_im[1::2]], axis=0)


def parity_order(pixels):
    order = np.concatenate([np.arange(0, pixels, 2), np.arange(1, pixels, 2)])
    return (order[:, None] == np.arange(pixels)[None, :]).astype(np.float32)


def call(kernel, out_shape, args, specs, scratch=(), flops=0, transcendentals=0, name=None):
    outs = out_shape if isinstance(out_shape, (list, tuple)) else [out_shape]
    moved = sum(math.prod(a.shape) * a.dtype.itemsize for a in list(args) + list(outs))
    return pl.pallas_call(
        kernel,
        out_shape=out_shape,
        in_specs=specs,
        out_specs=jax.tree.map(lambda _: VMEM, out_shape),
        scratch_shapes=list(scratch),
        compiler_params=pltpu.CompilerParams(vmem_limit_bytes=LIMIT),
        cost_estimate=pl.CostEstimate(
            flops=flops, bytes_accessed=moved, transcendentals=transcendentals
        ),
        name=name,
    )(*args)


def sds(shape, dtype):
    return jax.ShapeDtypeStruct(shape, dtype)


def column_place(info, slots, slot, width, columns):
    col = info[slots + slot]
    base = (col // width) * width
    after = jnp.minimum(base + width, columns - width)
    return pl.multiple_of(base, width), pl.multiple_of(after, width), col - base


def iotas(rows, cols):
    return (
        lax.broadcasted_iota(jnp.int32, (rows, cols), 0),
        lax.broadcasted_iota(jnp.int32, (rows, cols), 1),
    )


def strip_kernel(own, whole, *strips):
    for comp, strip in enumerate(strips):
        value = own[comp].astype(bf16)
        whole[comp] = value
        strip[...] = value


def center_kernel(slots, width, info, own, *outs):
    depth_index = lax.axis_index("depth")
    columns = own.shape[-1]
    _, lane = iotas(own.shape[1], width)
    for flip in range(len(outs)):
        base, after, first = column_place(info, slots, depth_index ^ flip, width, columns)
        for comp in range(2):
            outs[flip][comp] = jnp.where(
                lane >= first, own[comp, :, pl.ds(base, width)], own[comp, :, pl.ds(after, width)]
            ).astype(bf16)


def edge_kernel(slots, comp, width, info, across, beside, *outs):
    depth_index = lax.axis_index("depth")
    even = lax.rem(lax.axis_index("scan"), 2) == 0
    columns = across.shape[-1]
    row, lane = iotas(across.shape[0], width)
    for flip in range(len(outs)):
        slot = depth_index ^ flip
        base, after, first = column_place(info, slots, slot, width, columns)
        from_across = jnp.logical_xor(row < info[slot], even)

        def rows_at(place):
            return jnp.where(
                from_across,
                across[:, pl.ds(place, width)].astype(f32),
                beside[comp, :, pl.ds(place, width)].astype(f32),
            )

        outs[flip][...] = jnp.where(lane >= first, rows_at(base), rows_at(after)).astype(bf16)


def frequency_kernel(phase, order, order_t, measured, prop_re, prop_im, amplitude):
    def reorder(value):
        rows = jnp.dot(
            order[...], value, preferred_element_type=f32, precision=lax.Precision.HIGHEST
        )
        return jnp.dot(
            rows, order_t[...], preferred_element_type=f32, precision=lax.Precision.HIGHEST
        )

    turned = reorder(phase[...])
    prop_re[...] = jnp.cos(turned)
    prop_im[...] = jnp.sin(turned)
    amplitude[...] = reorder(measured[lax.axis_index("depth")]).astype(bf16)


def table_kernel(slots, info, stack, stack_t, probe, psi0, *tables):
    depth_index = lax.axis_index("depth")
    pixels = probe.shape[-1]
    half = pixels // 2
    row_shift = info[depth_index]
    col_shift = lax.rem(info[slots + depth_index], pixels)

    def shift_matrix(rows, cols, shift, transposed):
        row, lane = iotas(rows, cols)
        offset = (lane - row if transposed else row - lane) + shift
        return jnp.where((offset == 0) | (offset == pixels), 1.0, 0.0).astype(bf16)

    def pair(shift):
        cols = jnp.dot(
            stack[...], shift_matrix(pixels, half, shift, False), preferred_element_type=f32
        )
        rows = jnp.dot(
            shift_matrix(half, pixels, shift, True), stack_t[...], preferred_element_type=f32
        )
        forms, forms_t = [], []
        for parity in range(2):
            at = 2 * parity * half
            re, im = cols[at : at + half], cols[at + half : at + pixels]
            top = jnp.concatenate([re, -im], axis=1)
            bottom = jnp.concatenate([im, re], axis=1)
            forms.append(jnp.concatenate([top, bottom], axis=0).astype(bf16))
            re, im = rows[:, at : at + half], rows[:, at + half : at + pixels]
            top = jnp.concatenate([re, im], axis=1)
            bottom = jnp.concatenate([-im, re], axis=1)
            forms_t.append(jnp.concatenate([top, bottom], axis=0).astype(bf16))
        return forms, forms_t

    row_forms, row_forms_t = pair(row_shift)
    col_forms, col_forms_t = pair(col_shift)
    made = row_forms + col_forms_t + col_forms + row_forms_t
    for ref, value in zip(tables, made):
        ref[...] = value
    down = shift_matrix(pixels, pixels, row_shift, True)
    across = shift_matrix(pixels, pixels, col_shift, False)
    for comp in range(2):
        moved = jnp.dot(down, probe[comp].astype(bf16), preferred_element_type=f32).astype(bf16)
        psi0[comp] = jnp.dot(moved, across, preferred_element_type=f32).astype(bf16)


def wave_kernel(slots, depth_count, info, prop_re, prop_im, amplitude, psi0, *refs):
    tables = refs[:8]
    groups = [refs[at : at + depth_count] for at in range(8, 8 + 6 * depth_count, depth_count)]
    centers, edges, out_centers, out_edges = groups[0], groups[1:3], groups[3], groups[4:6]
    patches, waves, adjoint, grads = refs[8 + 6 * depth_count :]
    depth_index = lax.axis_index("depth")
    pixels = psi0.shape[-1]
    half = pixels // 2
    live = depth_index < info[2 * slots]
    fwd_row_e, fwd_row_o, fwd_col_e, fwd_col_o, inv_col_e, inv_col_o, inv_row_e, inv_row_o = tables

    def dot(left, right):
        return jnp.dot(left, right, preferred_element_type=f32)

    def propagate(x_re, x_im, at_frequency):
        def rows_of(sign):
            mixed = [v[:half] + v[half:] if sign > 0 else v[:half] - v[half:] for v in (x_re, x_im)]
            return jnp.concatenate(mixed, axis=0).astype(bf16)

        u_even = dot(fwd_row_e[...], rows_of(1))
        u_odd = dot(fwd_row_o[...], rows_of(-1))

        def cols_of(sign):
            parts = []
            for u in (u_even, u_odd):
                mixed = u[:, :half] + u[:, half:] if sign > 0 else u[:, :half] - u[:, half:]
                parts.append(jnp.concatenate([mixed[:half], mixed[half:]], axis=1))
            return jnp.concatenate(parts, axis=0).astype(bf16)

        v_even = dot(cols_of(1), fwd_col_e[...])
        v_odd = dot(cols_of(-1), fwd_col_o[...])
        b_even = at_frequency(v_even[:, :half], v_even[:, half:], slice(0, half))
        b_odd = at_frequency(v_odd[:, :half], v_odd[:, half:], slice(half, pixels))
        w_even = dot(jnp.concatenate(b_even, axis=1).astype(bf16), inv_col_e[...])
        w_odd = dot(jnp.concatenate(b_odd, axis=1).astype(bf16), inv_col_o[...])
        w_low, w_high = w_even + w_odd, w_even - w_odd
        w_re = jnp.concatenate([w_low[:, :half], w_high[:, :half]], axis=1)
        w_im = jnp.concatenate([w_low[:, half:], w_high[:, half:]], axis=1)
        y_even = dot(
            inv_row_e[...], jnp.concatenate([w_re[:half], w_im[:half]], axis=0).astype(bf16)
        )
        y_odd = dot(
            inv_row_o[...], jnp.concatenate([w_re[half:], w_im[half:]], axis=0).astype(bf16)
        )
        low, high = y_even + y_odd, y_even - y_odd
        return (
            jnp.concatenate([low[:half], high[:half]], axis=0),
            jnp.concatenate([low[half:], high[half:]], axis=0),
        )

    def turn(re, im, cols):
        p_re, p_im = prop_re[:, cols], prop_im[:, cols]
        return [re * p_re - im * p_im, re * p_im + im * p_re]

    def turn_back(re, im, cols):
        p_re, p_im = prop_re[:, cols], prop_im[:, cols]
        return [re * p_re + im * p_im, im * p_re - re * p_im]

    def residual(re, im, cols):
        modulus = jnp.sqrt(re * re + im * im + epsilon)
        factor = 1.0 - amplitude[:, cols].astype(f32) / modulus
        return [factor * re, factor * im]

    def pair_of(ref, index):
        return ref[index, 0].astype(f32), ref[index, 1].astype(f32)

    @pl.when(live)
    def _():
        for flip in range(depth_count):
            patches[depth_index ^ flip, :, half:] = centers[flip][...]
            for comp in range(2):
                patches[depth_index ^ flip, comp, :half] = edges[comp][flip][...]
        waves[0] = psi0[...]

        def forward(k, carry):
            t_re, t_im = pair_of(patches, k)
            p_re, p_im = pair_of(waves, k)
            n_re, n_im = propagate(t_re * p_re - t_im * p_im, t_re * p_im + t_im * p_re, turn)
            waves[k + 1, 0] = n_re.astype(bf16)
            waves[k + 1, 1] = n_im.astype(bf16)
            return carry

        lax.fori_loop(0, depth_count, forward, 0)
        l_re, l_im = propagate(*pair_of(waves, depth_count), residual)
        adjoint[0, 0] = l_re.astype(bf16)
        adjoint[0, 1] = l_im.astype(bf16)

        def backward(step, carry):
            k = depth_count - 1 - step
            m_re, m_im = propagate(*pair_of(adjoint, 0), turn_back)
            t_re, t_im = pair_of(patches, k)
            p_re, p_im = pair_of(waves, k)
            grads[k ^ depth_index, 0] = (p_re * m_re + p_im * m_im).astype(bf16)
            grads[k ^ depth_index, 1] = (p_re * m_im - p_im * m_re).astype(bf16)
            adjoint[0, 0] = (t_re * m_re + t_im * m_im).astype(bf16)
            adjoint[0, 1] = (t_re * m_im - t_im * m_re).astype(bf16)
            return carry

        lax.fori_loop(0, depth_count, backward, 0)
        for flip in range(depth_count):
            out_centers[flip][...] = grads[flip, :, half:]
            for comp in range(2):
                out_edges[comp][flip][...] = grads[flip, comp, :half]

    @pl.when(jnp.logical_not(live))
    def _():
        for ref in out_centers + out_edges[0] + out_edges[1]:
            ref[...] = jnp.zeros(ref.shape, ref.dtype)


def place_edges_kernel(slots, info, *refs):
    pieces, (across, beside, across_sum, beside_sum) = refs[:-4], refs[-4:]
    depth_index = lax.axis_index("depth")
    even = lax.rem(lax.axis_index("scan"), 2) == 0
    columns = across.shape[-1]
    width = pieces[0].shape[-1]
    row, lane = iotas(pieces[0].shape[0], width)
    across_sum[...] = jnp.zeros(across_sum.shape, f32)
    beside_sum[...] = jnp.zeros(beside_sum.shape, f32)
    for flip, piece in enumerate(pieces):
        slot = depth_index ^ flip
        base, after, first = column_place(info, slots, slot, width, columns)
        to_across = jnp.logical_xor(row < info[slot], even)
        to_base = lane >= first
        value = piece[...].astype(f32)
        for sheet, kept in (
            (across_sum, jnp.where(to_across, value, 0.0)),
            (beside_sum, jnp.where(to_across, 0.0, value)),
        ):
            sheet[:, pl.ds(base, width)] += jnp.where(to_base, kept, 0.0)
            sheet[:, pl.ds(after, width)] += jnp.where(to_base, 0.0, kept)
    across[...] = across_sum[...].astype(bf16)
    beside[...] = beside_sum[...].astype(bf16)


def place_center_kernel(slots, info, *refs):
    pieces, sheet = refs[:-1], refs[-1]
    depth_index = lax.axis_index("depth")
    columns = sheet.shape[-1]
    width = pieces[0].shape[-1]
    _, lane = iotas(pieces[0].shape[1], width)
    sheet[...] = jnp.zeros(sheet.shape, f32)
    for flip, piece in enumerate(pieces):
        base, after, first = column_place(info, slots, depth_index ^ flip, width, columns)
        to_base = lane >= first
        for comp in range(2):
            value = piece[comp].astype(f32)
            sheet[comp, :, pl.ds(base, width)] += jnp.where(to_base, value, 0.0)
            sheet[comp, :, pl.ds(after, width)] += jnp.where(to_base, 0.0, value)


def add_kernel(sheet, across_re, beside_re, across_im, beside_im, out):
    out[0] = sheet[0] + across_re[...].astype(f32) + beside_re[...].astype(f32)
    out[1] = sheet[1] + across_im[...].astype(f32) + beside_im[...].astype(f32)


def body(transmission, probe_wave, prop_phase, measured, scan_rows, scan_cols, live_counts):
    pixels = probe_wave.shape[-1]
    slots = measured.shape[0]
    rows = transmission.shape[2]
    columns = transmission.shape[3]
    count = lax.axis_size("depth")
    own = transmission[0]
    info, own = lax.optimization_barrier(
        (jnp.concatenate([scan_rows, scan_cols, live_counts]), own)
    )
    info = shifted(info, "scan", 1)
    strip = sds((rows, columns), bf16)
    whole, *strips = call(
        strip_kernel, [sds(own.shape, bf16), strip, strip], [own], [VMEM], name="strip"
    )
    info, whole, strips = lax.optimization_barrier((info, whole, strips))
    beside = swapped(whole, "scan", 0)
    across = [swapped(piece, "scan", 1) for piece in strips]

    part = sds((2, rows, pixels), bf16)
    info, beside = lax.optimization_barrier((info, beside))
    centers = call(
        functools.partial(center_kernel, slots, pixels),
        [part] * count, [info, own], [SMEM, VMEM], name="cut_center",
    )

    def across_depth(pieces):
        moved = [exchanged(pieces[flip], "depth", flip) for flip in range(count - 1, 0, -1)]
        return [pieces[0]] + moved[::-1]

    centers = across_depth(centers)

    phase, centers[0] = lax.optimization_barrier((prop_phase, centers[0]))
    order = parity_order(pixels)
    square = sds((pixels, pixels), f32)
    prop_re, prop_im, amplitude = call(
        frequency_kernel,
        [square, square, sds((pixels, pixels), bf16)],
        [phase, jnp.asarray(order), jnp.asarray(order.T), measured],
        [VMEM] * 4, flops=2400 * pixels**3, transcendentals=2 * pixels**2, name="frequency_order",
    )

    half_part = sds((rows, pixels), bf16)
    edges = []
    centers, across[0], prop_re = lax.optimization_barrier((centers, across[0], prop_re))
    for comp in range(2):
        if edges:
            across[comp], edges[0], amplitude, probe = lax.optimization_barrier(
                (across[comp], edges[0], amplitude, probe_wave)
            )
        pieces = call(
            functools.partial(edge_kernel, slots, comp, pixels),
            [half_part] * count, [info, across[comp], beside], [SMEM, VMEM, VMEM],
            name="cut_edges",
        )
        edges.append(across_depth(pieces))
    amplitude = shifted(amplitude, "scan", 1)

    stack = split_tables(pixels)
    made = call(
        functools.partial(table_kernel, slots),
        [sds((2, pixels, pixels), bf16)] + [sds((pixels, pixels), bf16)] * 8,
        [info, jnp.asarray(stack), jnp.asarray(stack.T), probe],
        [SMEM, VMEM, VMEM, VMEM], flops=16 * pixels**3, name="tables",
    )
    args = [info, prop_re, prop_im, amplitude, *made, *centers, *edges[0], *edges[1]]
    grads = call(
        functools.partial(wave_kernel, slots, count),
        [part] * count + [half_part] * (2 * count), args, [SMEM] + [VMEM] * (len(args) - 1),
        scratch=[
            pltpu.VMEM((count, 2, pixels, pixels), bf16),
            pltpu.VMEM((count + 1, 2, pixels, pixels), bf16),
            pltpu.VMEM((1, 2, pixels, pixels), bf16),
            pltpu.VMEM((count, 2, pixels, pixels), bf16),
        ],
        flops=(2 * count + 1) * 16 * pixels**3, name="waves",
    )
    returned = []
    out_centers = grads[:count]
    for comp in range(2):
        pieces = across_depth(grads[(comp + 1) * count : (comp + 2) * count])
        to_across, to_beside = call(
            functools.partial(place_edges_kernel, slots),
            [strip, strip], [info, *pieces], [SMEM] + [VMEM] * count,
            scratch=[pltpu.VMEM(strip.shape, f32)] * 2, name="place_edges",
        )
        if returned:
            out_centers, to_beside = lax.optimization_barrier((out_centers, to_beside))
            out_centers = across_depth(out_centers)
            to_across, returned[0], out_centers[-1] = lax.optimization_barrier(
                (to_across, returned[0], out_centers[-1])
            )
        returned.append((swapped(to_across, "scan", 1), swapped(to_beside, "scan", 0)))
    sheet_f32 = sds((2, rows, columns), f32)
    sheet = call(
        functools.partial(place_center_kernel, slots),
        sheet_f32, [info, *out_centers], [SMEM] + [VMEM] * count, name="place_center",
    )
    gradient = call(
        add_kernel, sheet_f32, [sheet, *returned[0], *returned[1]], [VMEM] * 5, name="add_edges"
    )
    return gradient[None]


def solution(mesh):
    in_specs = (
        P("depth", None, "scan", None),
        P(),
        P(),
        P("scan", None, None),
        P("scan"),
        P("scan"),
        P("scan"),
    )
    out_specs = P("depth", None, "scan", None)
    return jax.shard_map(body, mesh=mesh, in_specs=in_specs, out_specs=out_specs, check_vma=False)
```

```python
import functools
import math

import jax
import jax.numpy as jnp
import ml_dtypes
import numpy as np
from jax import lax
from jax.experimental import pallas as pl
from jax.experimental.pallas import tpu as pltpu
from jax.sharding import PartitionSpec as P

epsilon = 1.0
bf16 = jnp.bfloat16
f32 = jnp.float32
VMEM = pl.BlockSpec(memory_space=pltpu.VMEM)
SMEM = pl.BlockSpec(memory_space=pltpu.SMEM)
LIMIT = 48 * 1024 * 1024
INFO_SIZE = 8192


def shifted(value, axis, steps):
    count = lax.axis_size(axis)
    pairs = [(source, (source + steps) % count) for source in range(count)]
    return lax.ppermute(value, axis, pairs)


def swapped(value, axis, first):
    count = lax.axis_size(axis)
    pairs = [
        (source, (source + (1 if source % 2 == first else -1)) % count) for source in range(count)
    ]
    return lax.ppermute(value, axis, pairs)


def exchanged(value, axis, flip):
    count = lax.axis_size(axis)
    return lax.ppermute(value, axis, [(source, source ^ flip) for source in range(count)])


def split_tables(pixels):
    indices = np.arange(pixels)
    angles = (indices[:, None] * indices[None, :] % pixels) * (2.0 * math.pi / pixels)
    norm_scale = 1.0 / math.sqrt(pixels)
    table_re = (np.cos(angles) * norm_scale).astype(np.float32).astype(ml_dtypes.bfloat16)
    table_im = (-np.sin(angles) * norm_scale).astype(np.float32).astype(ml_dtypes.bfloat16)
    return np.concatenate([table_re[0::2], table_im[0::2], table_re[1::2], table_im[1::2]], axis=0)


def parity_order(pixels):
    order = np.concatenate([np.arange(0, pixels, 2), np.arange(1, pixels, 2)])
    return (order[:, None] == np.arange(pixels)[None, :]).astype(np.float32)


def call(kernel, out_shape, args, specs, scratch=(), flops=0, transcendentals=0, name=None):
    outs = out_shape if isinstance(out_shape, (list, tuple)) else [out_shape]
    moved = sum(math.prod(a.shape) * a.dtype.itemsize for a in list(args) + list(outs))
    return pl.pallas_call(
        kernel,
        out_shape=out_shape,
        in_specs=specs,
        out_specs=jax.tree.map(lambda _: VMEM, out_shape),
        scratch_shapes=list(scratch),
        compiler_params=pltpu.CompilerParams(vmem_limit_bytes=LIMIT),
        cost_estimate=pl.CostEstimate(
            flops=flops, bytes_accessed=moved, transcendentals=transcendentals
        ),
        name=name,
    )(*args)


def sds(shape, dtype):
    return jax.ShapeDtypeStruct(shape, dtype)


def by_flip(pieces):
    return list(zip([0, *range(len(pieces) - 1, 0, -1)], pieces))


def column_place(info, slots, slot, width, columns):
    col = info[slots + slot]
    base = (col // width) * width
    after = jnp.minimum(base + width, columns - width)
    return pl.multiple_of(base, width), pl.multiple_of(after, width), col - base


def iotas(rows, cols):
    return (
        lax.broadcasted_iota(jnp.int32, (rows, cols), 0),
        lax.broadcasted_iota(jnp.int32, (rows, cols), 1),
    )


def strip_kernel(own, strip):
    strip[...] = own[...].astype(bf16)


def center_kernel(slots, width, info, own, *outs):
    depth_index = lax.axis_index("depth")
    columns = own.shape[-1]
    _, lane = iotas(own.shape[1], width)
    for flip, out in by_flip(outs):
        base, after, first = column_place(info, slots, depth_index ^ flip, width, columns)
        for comp in range(2):
            out[comp] = jnp.where(
                lane >= first, own[comp, :, pl.ds(base, width)], own[comp, :, pl.ds(after, width)]
            ).astype(bf16)


def edge_kernel(slots, width, info, across, beside, *outs):
    depth_index = lax.axis_index("depth")
    even = lax.rem(lax.axis_index("scan"), 2) == 0
    columns = across.shape[-1]
    row, lane = iotas(across.shape[1], width)
    for flip, out in by_flip(outs):
        slot = depth_index ^ flip
        base, after, first = column_place(info, slots, slot, width, columns)
        from_across = jnp.logical_xor(row < info[slot], even)

        def rows_at(comp, place):
            return jnp.where(
                from_across,
                across[comp, :, pl.ds(place, width)].astype(f32),
                beside[comp, :, pl.ds(place, width)].astype(f32),
            )

        for comp in range(2):
            out[comp] = jnp.where(
                lane >= first, rows_at(comp, base), rows_at(comp, after)
            ).astype(bf16)


def frequency_kernel(phase, order, order_t, measured, prop_re, prop_im, amplitude):
    def reorder(value):
        rows = jnp.dot(
            order[...], value, preferred_element_type=f32, precision=lax.Precision.HIGHEST
        )
        return jnp.dot(
            rows, order_t[...], preferred_element_type=f32, precision=lax.Precision.HIGHEST
        )

    turned = reorder(phase[...])
    prop_re[...] = jnp.cos(turned)
    prop_im[...] = jnp.sin(turned)
    amplitude[...] = reorder(measured[lax.axis_index("depth")]).astype(bf16)


def table_kernel(slots, info, stack, stack_t, probe, psi0, *tables):
    depth_index = lax.axis_index("depth")
    pixels = probe.shape[-1]
    half = pixels // 2
    row_shift = info[depth_index]
    col_shift = lax.rem(info[slots + depth_index], pixels)

    def shift_matrix(rows, cols, shift, transposed):
        row, lane = iotas(rows, cols)
        offset = (lane - row if transposed else row - lane) + shift
        return jnp.where((offset == 0) | (offset == pixels), 1.0, 0.0).astype(bf16)

    def pair(shift):
        cols = jnp.dot(
            stack[...], shift_matrix(pixels, half, shift, False), preferred_element_type=f32
        )
        rows = jnp.dot(
            shift_matrix(half, pixels, shift, True), stack_t[...], preferred_element_type=f32
        )
        forms, forms_t = [], []
        for parity in range(2):
            at = 2 * parity * half
            re, im = cols[at : at + half], cols[at + half : at + pixels]
            top = jnp.concatenate([re, -im], axis=1)
            bottom = jnp.concatenate([im, re], axis=1)
            forms.append(jnp.concatenate([top, bottom], axis=0).astype(bf16))
            re, im = rows[:, at : at + half], rows[:, at + half : at + pixels]
            top = jnp.concatenate([re, im], axis=1)
            bottom = jnp.concatenate([-im, re], axis=1)
            forms_t.append(jnp.concatenate([top, bottom], axis=0).astype(bf16))
        return forms, forms_t

    row_forms, row_forms_t = pair(row_shift)
    col_forms, col_forms_t = pair(col_shift)
    made = row_forms + col_forms_t + col_forms + row_forms_t
    for ref, value in zip(tables, made):
        ref[...] = value
    down = shift_matrix(pixels, pixels, row_shift, True)
    across = shift_matrix(pixels, pixels, col_shift, False)
    for comp in range(2):
        moved = jnp.dot(down, probe[comp].astype(bf16), preferred_element_type=f32).astype(bf16)
        psi0[comp] = jnp.dot(moved, across, preferred_element_type=f32).astype(bf16)


def wave_kernel(slots, depth_count, info, prop_re, prop_im, amplitude, psi0, *refs):
    tables = refs[:8]
    centers = refs[8 : 8 + depth_count]
    edges = refs[8 + depth_count : 8 + 2 * depth_count]
    out_centers = refs[8 + 2 * depth_count : 8 + 3 * depth_count]
    out_edges = refs[8 + 3 * depth_count : 8 + 4 * depth_count]
    patches, waves, adjoint, grads = refs[8 + 4 * depth_count :]
    depth_index = lax.axis_index("depth")
    pixels = psi0.shape[-1]
    half = pixels // 2
    live = depth_index < info[2 * slots]
    fwd_row_e, fwd_row_o, fwd_col_e, fwd_col_o, inv_col_e, inv_col_o, inv_row_e, inv_row_o = tables

    def dot(left, right):
        return jnp.dot(left, right, preferred_element_type=f32)

    def propagate(x_re, x_im, at_frequency):
        def rows_of(sign):
            mixed = [v[:half] + v[half:] if sign > 0 else v[:half] - v[half:] for v in (x_re, x_im)]
            return jnp.concatenate(mixed, axis=0).astype(bf16)

        u_even = dot(fwd_row_e[...], rows_of(1))
        u_odd = dot(fwd_row_o[...], rows_of(-1))

        def cols_of(sign):
            parts = []
            for u in (u_even, u_odd):
                mixed = u[:, :half] + u[:, half:] if sign > 0 else u[:, :half] - u[:, half:]
                parts.append(jnp.concatenate([mixed[:half], mixed[half:]], axis=1))
            return jnp.concatenate(parts, axis=0).astype(bf16)

        v_even = dot(cols_of(1), fwd_col_e[...])
        v_odd = dot(cols_of(-1), fwd_col_o[...])
        b_even = at_frequency(v_even[:, :half], v_even[:, half:], slice(0, half))
        b_odd = at_frequency(v_odd[:, :half], v_odd[:, half:], slice(half, pixels))
        w_even = dot(jnp.concatenate(b_even, axis=1).astype(bf16), inv_col_e[...])
        w_odd = dot(jnp.concatenate(b_odd, axis=1).astype(bf16), inv_col_o[...])
        w_low, w_high = w_even + w_odd, w_even - w_odd
        w_re = jnp.concatenate([w_low[:, :half], w_high[:, :half]], axis=1)
        w_im = jnp.concatenate([w_low[:, half:], w_high[:, half:]], axis=1)
        y_even = dot(
            inv_row_e[...], jnp.concatenate([w_re[:half], w_im[:half]], axis=0).astype(bf16)
        )
        y_odd = dot(
            inv_row_o[...], jnp.concatenate([w_re[half:], w_im[half:]], axis=0).astype(bf16)
        )
        low, high = y_even + y_odd, y_even - y_odd
        return (
            jnp.concatenate([low[:half], high[:half]], axis=0),
            jnp.concatenate([low[half:], high[half:]], axis=0),
        )

    def turn(re, im, cols):
        p_re, p_im = prop_re[:, cols], prop_im[:, cols]
        return [re * p_re - im * p_im, re * p_im + im * p_re]

    def turn_back(re, im, cols):
        p_re, p_im = prop_re[:, cols], prop_im[:, cols]
        return [re * p_re + im * p_im, im * p_re - re * p_im]

    def residual(re, im, cols):
        modulus = jnp.sqrt(re * re + im * im + epsilon)
        factor = 1.0 - amplitude[:, cols].astype(f32) / modulus
        return [factor * re, factor * im]

    def pair_of(ref, index):
        return ref[index, 0].astype(f32), ref[index, 1].astype(f32)

    @pl.when(live)
    def _():
        for (flip, center), edge in zip(by_flip(centers), edges):
            patches[depth_index ^ flip, :, half:] = center[...]
            patches[depth_index ^ flip, :, :half] = edge[...]
        waves[0] = psi0[...]

        def forward(k, carry):
            t_re, t_im = pair_of(patches, k)
            p_re, p_im = pair_of(waves, k)
            n_re, n_im = propagate(t_re * p_re - t_im * p_im, t_re * p_im + t_im * p_re, turn)
            waves[k + 1, 0] = n_re.astype(bf16)
            waves[k + 1, 1] = n_im.astype(bf16)
            return carry

        lax.fori_loop(0, depth_count, forward, 0)
        l_re, l_im = propagate(*pair_of(waves, depth_count), residual)
        adjoint[0, 0] = l_re.astype(bf16)
        adjoint[0, 1] = l_im.astype(bf16)

        def backward(step, carry):
            k = depth_count - 1 - step
            m_re, m_im = propagate(*pair_of(adjoint, 0), turn_back)
            t_re, t_im = pair_of(patches, k)
            p_re, p_im = pair_of(waves, k)
            grads[k ^ depth_index, 0] = (p_re * m_re + p_im * m_im).astype(bf16)
            grads[k ^ depth_index, 1] = (p_re * m_im - p_im * m_re).astype(bf16)
            adjoint[0, 0] = (t_re * m_re + t_im * m_im).astype(bf16)
            adjoint[0, 1] = (t_re * m_im - t_im * m_re).astype(bf16)
            return carry

        lax.fori_loop(0, depth_count, backward, 0)
        for (flip, center), edge in zip(by_flip(out_centers), out_edges):
            center[...] = grads[flip, :, half:]
            edge[...] = grads[flip, :, :half]

    @pl.when(jnp.logical_not(live))
    def _():
        for ref in out_centers + out_edges:
            ref[...] = jnp.zeros(ref.shape, ref.dtype)


def place_edges_kernel(slots, info, *refs):
    pieces, (across, beside, across_sum, beside_sum) = refs[:-4], refs[-4:]
    depth_index = lax.axis_index("depth")
    even = lax.rem(lax.axis_index("scan"), 2) == 0
    columns = across.shape[-1]
    width = pieces[0].shape[-1]
    row, lane = iotas(pieces[0].shape[1], width)
    across_sum[...] = jnp.zeros(across_sum.shape, f32)
    beside_sum[...] = jnp.zeros(beside_sum.shape, f32)
    for flip, piece in by_flip(pieces):
        slot = depth_index ^ flip
        base, after, first = column_place(info, slots, slot, width, columns)
        to_across = jnp.logical_xor(row < info[slot], even)
        to_base = lane >= first
        for comp in range(2):
            value = piece[comp].astype(f32)
            for sheet, kept in (
                (across_sum, jnp.where(to_across, value, 0.0)),
                (beside_sum, jnp.where(to_across, 0.0, value)),
            ):
                sheet[comp, :, pl.ds(base, width)] += jnp.where(to_base, kept, 0.0)
                sheet[comp, :, pl.ds(after, width)] += jnp.where(to_base, 0.0, kept)
    across[...] = across_sum[...].astype(bf16)
    beside[...] = beside_sum[...].astype(bf16)


def place_center_kernel(slots, info, *refs):
    pieces, sheet = refs[:-1], refs[-1]
    depth_index = lax.axis_index("depth")
    columns = sheet.shape[-1]
    width = pieces[0].shape[-1]
    _, lane = iotas(pieces[0].shape[1], width)
    sheet[...] = jnp.zeros(sheet.shape, f32)
    for flip, piece in by_flip(pieces):
        base, after, first = column_place(info, slots, depth_index ^ flip, width, columns)
        to_base = lane >= first
        for comp in range(2):
            value = piece[comp].astype(f32)
            sheet[comp, :, pl.ds(base, width)] += jnp.where(to_base, value, 0.0)
            sheet[comp, :, pl.ds(after, width)] += jnp.where(to_base, 0.0, value)


def body(transmission, probe_wave, prop_phase, measured, scan_rows, scan_cols, live_counts):
    pixels = probe_wave.shape[-1]
    slots = measured.shape[0]
    rows = transmission.shape[2]
    columns = transmission.shape[3]
    count = lax.axis_size("depth")
    own = transmission[0]
    info, own = lax.optimization_barrier(
        (jnp.concatenate([scan_rows, scan_cols, live_counts]), own)
    )
    ints = info.shape[0]
    info = shifted(jnp.pad(info, (0, INFO_SIZE - ints)), "scan", 1)[:ints]
    strip = call(strip_kernel, sds(own.shape, bf16), [own], [VMEM], name="strip")
    across = swapped(strip, "scan", 1)
    beside = swapped(strip, "scan", 0)

    part = sds((2, rows, pixels), bf16)
    centers = call(
        functools.partial(center_kernel, slots, pixels),
        [part] * count, [info, own], [SMEM, VMEM], name="cut_center",
    )

    def across_depth(pieces):
        return [pieces[0]] + [exchanged(piece, "depth", flip) for flip, piece in by_flip(pieces)[1:]]

    centers = across_depth(centers)

    phase, centers[0] = lax.optimization_barrier((prop_phase, centers[0]))
    order = parity_order(pixels)
    square = sds((pixels, pixels), f32)
    prop_re, prop_im, amplitude = call(
        frequency_kernel,
        [square, square, sds((pixels, pixels), bf16)],
        [phase, jnp.asarray(order), jnp.asarray(order.T), measured],
        [VMEM] * 4, flops=2400 * pixels**3, transcendentals=2 * pixels**2, name="frequency_order",
    )
    amplitude, across = lax.optimization_barrier((amplitude, across))
    amplitude = shifted(amplitude, "scan", 1)

    stack = split_tables(pixels)
    made = call(
        functools.partial(table_kernel, slots),
        [sds((2, pixels, pixels), bf16)] + [sds((pixels, pixels), bf16)] * 8,
        [info, jnp.asarray(stack), jnp.asarray(stack.T), probe_wave],
        [SMEM, VMEM, VMEM, VMEM], flops=16 * pixels**3, name="tables",
    )
    edges = call(
        functools.partial(edge_kernel, slots, pixels),
        [part] * count, [info, across, beside], [SMEM, VMEM, VMEM], name="cut_edges",
    )
    edges = across_depth(edges)

    args = [info, prop_re, prop_im, amplitude, *made, *centers, *edges]
    grads = call(
        functools.partial(wave_kernel, slots, count),
        [part] * (2 * count), args, [SMEM] + [VMEM] * (len(args) - 1),
        scratch=[
            pltpu.VMEM((count, 2, pixels, pixels), bf16),
            pltpu.VMEM((count + 1, 2, pixels, pixels), bf16),
            pltpu.VMEM((1, 2, pixels, pixels), bf16),
            pltpu.VMEM((count, 2, pixels, pixels), bf16),
        ],
        flops=(2 * count + 1) * 16 * pixels**3, name="waves",
    )
    out_centers, out_edges = grads[:count], grads[count:]
    out_edges = across_depth(out_edges)
    out_centers = across_depth(out_centers)
    sheet_bf16 = sds((2, rows, columns), bf16)
    sheet_f32 = sds((2, rows, columns), f32)
    to_across, to_beside = call(
        functools.partial(place_edges_kernel, slots),
        [sheet_bf16, sheet_bf16], [info, *out_edges], [SMEM] + [VMEM] * count,
        scratch=[pltpu.VMEM(sheet_f32.shape, f32)] * 2, name="place_edges",
    )
    from_across = swapped(to_across, "scan", 1)
    from_beside = swapped(to_beside, "scan", 0)
    sheet = call(
        functools.partial(place_center_kernel, slots),
        sheet_f32, [info, *out_centers], [SMEM] + [VMEM] * count, name="place_center",
    )
    gradient = sheet + from_across.astype(f32) + from_beside.astype(f32)
    return gradient[None]


def solution(mesh):
    in_specs = (
        P("depth", None, "scan", None),
        P(),
        P(),
        P("scan", None, None),
        P("scan"),
        P("scan"),
        P("scan"),
    )
    out_specs = P("depth", None, "scan", None)
    return jax.shard_map(body, mesh=mesh, in_specs=in_specs, out_specs=out_specs, check_vma=False)
```

```python
import functools
import math

import jax
import jax.numpy as jnp
import ml_dtypes
import numpy as np
from jax import lax
from jax.experimental import pallas as pl
from jax.experimental.pallas import tpu as pltpu
from jax.sharding import PartitionSpec as P

epsilon = 1.0
bf16 = jnp.bfloat16
f32 = jnp.float32
VMEM = pl.BlockSpec(memory_space=pltpu.VMEM)
SMEM = pl.BlockSpec(memory_space=pltpu.SMEM)
LIMIT = 48 * 1024 * 1024
INFO_SIZE = 8192


def shifted(value, axis, steps):
    count = lax.axis_size(axis)
    pairs = [(source, (source + steps) % count) for source in range(count)]
    return lax.ppermute(value, axis, pairs)


def swapped(value, axis, first):
    count = lax.axis_size(axis)
    pairs = [
        (source, (source + (1 if source % 2 == first else -1)) % count) for source in range(count)
    ]
    return lax.ppermute(value, axis, pairs)


def swapped_inside(value, axis):
    count = lax.axis_size(axis)
    return lax.ppermute(
        value, axis, [(at, at + (1 if at % 2 else -1)) for at in range(1, count - 1)]
    )


def swapped_ends(value, axis):
    last = lax.axis_size(axis) - 1
    return lax.ppermute(value, axis, [(0, last), (last, 0)])


def exchanged(value, axis, flip):
    count = lax.axis_size(axis)
    return lax.ppermute(value, axis, [(source, source ^ flip) for source in range(count)])


def split_tables(pixels):
    indices = np.arange(pixels)
    angles = (indices[:, None] * indices[None, :] % pixels) * (2.0 * math.pi / pixels)
    norm_scale = 1.0 / math.sqrt(pixels)
    table_re = (np.cos(angles) * norm_scale).astype(np.float32).astype(ml_dtypes.bfloat16)
    table_im = (-np.sin(angles) * norm_scale).astype(np.float32).astype(ml_dtypes.bfloat16)
    return np.concatenate([table_re[0::2], table_im[0::2], table_re[1::2], table_im[1::2]], axis=0)


def parity_order(pixels):
    order = np.concatenate([np.arange(0, pixels, 2), np.arange(1, pixels, 2)])
    return (order[:, None] == np.arange(pixels)[None, :]).astype(np.float32)


def call(kernel, out_shape, args, specs, scratch=(), flops=0, transcendentals=0, name=None):
    outs = out_shape if isinstance(out_shape, (list, tuple)) else [out_shape]
    moved = sum(math.prod(a.shape) * a.dtype.itemsize for a in list(args) + list(outs))
    return pl.pallas_call(
        kernel,
        out_shape=out_shape,
        in_specs=specs,
        out_specs=jax.tree.map(lambda _: VMEM, out_shape),
        scratch_shapes=list(scratch),
        compiler_params=pltpu.CompilerParams(vmem_limit_bytes=LIMIT),
        cost_estimate=pl.CostEstimate(
            flops=flops, bytes_accessed=moved, transcendentals=transcendentals
        ),
        name=name,
    )(*args)


def sds(shape, dtype):
    return jax.ShapeDtypeStruct(shape, dtype)


def by_flip(pieces):
    return list(zip([0, *range(len(pieces) - 1, 0, -1)], pieces))


def column_place(info, slots, slot, width, columns):
    col = info[slots + slot]
    base = (col // width) * width
    after = jnp.minimum(base + width, columns - width)
    return pl.multiple_of(base, width), pl.multiple_of(after, width), col - base


def iotas(rows, cols):
    return (
        lax.broadcasted_iota(jnp.int32, (rows, cols), 0),
        lax.broadcasted_iota(jnp.int32, (rows, cols), 1),
    )


def strip_kernel(own, strip):
    strip[...] = own[...].astype(bf16)


def center_kernel(slots, width, info, own, *outs):
    depth_index = lax.axis_index("depth")
    columns = own.shape[-1]
    _, lane = iotas(own.shape[1], width)
    for flip, out in by_flip(outs):
        base, after, first = column_place(info, slots, depth_index ^ flip, width, columns)
        for comp in range(2):
            out[comp] = jnp.where(
                lane >= first, own[comp, :, pl.ds(base, width)], own[comp, :, pl.ds(after, width)]
            ).astype(bf16)


def edge_kernel(slots, width, info, inside, ends, beside, *outs):
    depth_index = lax.axis_index("depth")
    even = lax.rem(lax.axis_index("scan"), 2) == 0
    columns = beside.shape[-1]
    row, lane = iotas(beside.shape[1], width)
    for flip, out in by_flip(outs):
        slot = depth_index ^ flip
        base, after, first = column_place(info, slots, slot, width, columns)
        from_across = jnp.logical_xor(row < info[slot], even)

        def rows_at(comp, place):
            across = inside[comp, :, pl.ds(place, width)].astype(f32) + ends[
                comp, :, pl.ds(place, width)
            ].astype(f32)
            return jnp.where(from_across, across, beside[comp, :, pl.ds(place, width)].astype(f32))

        for comp in range(2):
            out[comp] = jnp.where(
                lane >= first, rows_at(comp, base), rows_at(comp, after)
            ).astype(bf16)


def frequency_kernel(phase, order, order_t, measured, prop_re, prop_im, amplitude):
    def reorder(value):
        rows = jnp.dot(
            order[...], value, preferred_element_type=f32, precision=lax.Precision.HIGHEST
        )
        return jnp.dot(
            rows, order_t[...], preferred_element_type=f32, precision=lax.Precision.HIGHEST
        )

    turned = reorder(phase[...])
    prop_re[...] = jnp.cos(turned)
    prop_im[...] = jnp.sin(turned)
    amplitude[...] = reorder(measured[lax.axis_index("depth")]).astype(bf16)


def table_kernel(slots, info, stack, stack_t, probe, psi0, *tables):
    depth_index = lax.axis_index("depth")
    pixels = probe.shape[-1]
    half = pixels // 2
    row_shift = info[depth_index]
    col_shift = lax.rem(info[slots + depth_index], pixels)

    def shift_matrix(rows, cols, shift, transposed):
        row, lane = iotas(rows, cols)
        offset = (lane - row if transposed else row - lane) + shift
        return jnp.where((offset == 0) | (offset == pixels), 1.0, 0.0).astype(bf16)

    def pair(shift):
        cols = jnp.dot(
            stack[...], shift_matrix(pixels, half, shift, False), preferred_element_type=f32
        )
        rows = jnp.dot(
            shift_matrix(half, pixels, shift, True), stack_t[...], preferred_element_type=f32
        )
        forms, forms_t = [], []
        for parity in range(2):
            at = 2 * parity * half
            re, im = cols[at : at + half], cols[at + half : at + pixels]
            top = jnp.concatenate([re, -im], axis=1)
            bottom = jnp.concatenate([im, re], axis=1)
            forms.append(jnp.concatenate([top, bottom], axis=0).astype(bf16))
            re, im = rows[:, at : at + half], rows[:, at + half : at + pixels]
            top = jnp.concatenate([re, im], axis=1)
            bottom = jnp.concatenate([-im, re], axis=1)
            forms_t.append(jnp.concatenate([top, bottom], axis=0).astype(bf16))
        return forms, forms_t

    row_forms, row_forms_t = pair(row_shift)
    col_forms, col_forms_t = pair(col_shift)
    made = row_forms + col_forms_t + col_forms + row_forms_t
    for ref, value in zip(tables, made):
        ref[...] = value
    down = shift_matrix(pixels, pixels, row_shift, True)
    across = shift_matrix(pixels, pixels, col_shift, False)
    for comp in range(2):
        moved = jnp.dot(down, probe[comp].astype(bf16), preferred_element_type=f32).astype(bf16)
        psi0[comp] = jnp.dot(moved, across, preferred_element_type=f32).astype(bf16)


def wave_kernel(slots, depth_count, info, prop_re, prop_im, amplitude, psi0, *refs):
    tables = refs[:8]
    centers = refs[8 : 8 + depth_count]
    edges = refs[8 + depth_count : 8 + 2 * depth_count]
    out_centers = refs[8 + 2 * depth_count : 8 + 3 * depth_count]
    out_edges = refs[8 + 3 * depth_count : 8 + 4 * depth_count]
    patches, waves, adjoint, grads = refs[8 + 4 * depth_count :]
    depth_index = lax.axis_index("depth")
    pixels = psi0.shape[-1]
    half = pixels // 2
    live = depth_index < info[2 * slots]
    fwd_row_e, fwd_row_o, fwd_col_e, fwd_col_o, inv_col_e, inv_col_o, inv_row_e, inv_row_o = tables

    def dot(left, right):
        return jnp.dot(left, right, preferred_element_type=f32)

    def propagate(x_re, x_im, at_frequency):
        def rows_of(sign):
            mixed = [v[:half] + v[half:] if sign > 0 else v[:half] - v[half:] for v in (x_re, x_im)]
            return jnp.concatenate(mixed, axis=0).astype(bf16)

        u_even = dot(fwd_row_e[...], rows_of(1))
        u_odd = dot(fwd_row_o[...], rows_of(-1))

        y_re, y_im = [], []
        for at, u in ((0, u_even), (half, u_odd)):
            rows = slice(at, at + half)

            def cols_of(sign):
                mixed = u[:, :half] + u[:, half:] if sign > 0 else u[:, :half] - u[:, half:]
                return jnp.concatenate([mixed[:half], mixed[half:]], axis=1).astype(bf16)

            v_even = dot(cols_of(1), fwd_col_e[...])
            v_odd = dot(cols_of(-1), fwd_col_o[...])
            b_even = at_frequency(v_even[:, :half], v_even[:, half:], rows, slice(0, half))
            b_odd = at_frequency(v_odd[:, :half], v_odd[:, half:], rows, slice(half, pixels))
            w_even = dot(jnp.concatenate(b_even, axis=1).astype(bf16), inv_col_e[...])
            w_odd = dot(jnp.concatenate(b_odd, axis=1).astype(bf16), inv_col_o[...])
            low, high = w_even + w_odd, w_even - w_odd
            y_re.append(jnp.concatenate([low[:, :half], high[:, :half]], axis=1))
            y_im.append(jnp.concatenate([low[:, half:], high[:, half:]], axis=1))
        y_even = dot(inv_row_e[...], jnp.concatenate([y_re[0], y_im[0]], axis=0).astype(bf16))
        y_odd = dot(inv_row_o[...], jnp.concatenate([y_re[1], y_im[1]], axis=0).astype(bf16))
        low, high = y_even + y_odd, y_even - y_odd
        return (
            jnp.concatenate([low[:half], high[:half]], axis=0),
            jnp.concatenate([low[half:], high[half:]], axis=0),
        )

    def turn(re, im, rows, cols):
        p_re, p_im = prop_re[rows, cols], prop_im[rows, cols]
        return [re * p_re - im * p_im, re * p_im + im * p_re]

    def turn_back(re, im, rows, cols):
        p_re, p_im = prop_re[rows, cols], prop_im[rows, cols]
        return [re * p_re + im * p_im, im * p_re - re * p_im]

    def residual(re, im, rows, cols):
        modulus = jnp.sqrt(re * re + im * im + epsilon)
        factor = 1.0 - amplitude[rows, cols].astype(f32) / modulus
        return [factor * re, factor * im]

    def pair_of(ref, index):
        return ref[index, 0].astype(f32), ref[index, 1].astype(f32)

    @pl.when(live)
    def _():
        for (flip, center), edge in zip(by_flip(centers), edges):
            patches[depth_index ^ flip, :, half:] = center[...]
            patches[depth_index ^ flip, :, :half] = edge[...]
        waves[0] = psi0[...]

        def forward(k, carry):
            t_re, t_im = pair_of(patches, k)
            p_re, p_im = pair_of(waves, k)
            n_re, n_im = propagate(t_re * p_re - t_im * p_im, t_re * p_im + t_im * p_re, turn)
            waves[k + 1, 0] = n_re.astype(bf16)
            waves[k + 1, 1] = n_im.astype(bf16)
            return carry

        lax.fori_loop(0, depth_count, forward, 0)
        l_re, l_im = propagate(*pair_of(waves, depth_count), residual)
        adjoint[0, 0] = l_re.astype(bf16)
        adjoint[0, 1] = l_im.astype(bf16)

        def backward(step, carry):
            k = depth_count - 1 - step
            m_re, m_im = propagate(*pair_of(adjoint, 0), turn_back)
            t_re, t_im = pair_of(patches, k)
            p_re, p_im = pair_of(waves, k)
            grads[k ^ depth_index, 0] = (p_re * m_re + p_im * m_im).astype(bf16)
            grads[k ^ depth_index, 1] = (p_re * m_im - p_im * m_re).astype(bf16)
            adjoint[0, 0] = (t_re * m_re + t_im * m_im).astype(bf16)
            adjoint[0, 1] = (t_re * m_im - t_im * m_re).astype(bf16)
            return carry

        lax.fori_loop(0, depth_count, backward, 0)
        for (flip, center), edge in zip(by_flip(out_centers), out_edges):
            center[...] = grads[flip, :, half:]
            edge[...] = grads[flip, :, :half]

    @pl.when(jnp.logical_not(live))
    def _():
        for ref in out_centers + out_edges:
            ref[...] = jnp.zeros(ref.shape, ref.dtype)


def place_edges_kernel(slots, info, *refs):
    pieces, (across, beside, across_sum, beside_sum) = refs[:-4], refs[-4:]
    depth_index = lax.axis_index("depth")
    even = lax.rem(lax.axis_index("scan"), 2) == 0
    columns = across.shape[-1]
    width = pieces[0].shape[-1]
    row, lane = iotas(pieces[0].shape[1], width)
    across_sum[...] = jnp.zeros(across_sum.shape, f32)
    beside_sum[...] = jnp.zeros(beside_sum.shape, f32)
    for flip, piece in by_flip(pieces):
        slot = depth_index ^ flip
        base, after, first = column_place(info, slots, slot, width, columns)
        to_across = jnp.logical_xor(row < info[slot], even)
        to_base = lane >= first
        for comp in range(2):
            value = piece[comp].astype(f32)
            for sheet, kept in (
                (across_sum, jnp.where(to_across, value, 0.0)),
                (beside_sum, jnp.where(to_across, 0.0, value)),
            ):
                sheet[comp, :, pl.ds(base, width)] += jnp.where(to_base, kept, 0.0)
                sheet[comp, :, pl.ds(after, width)] += jnp.where(to_base, 0.0, kept)
    across[...] = across_sum[...].astype(bf16)
    beside[...] = beside_sum[...].astype(bf16)


def place_center_kernel(slots, info, *refs):
    pieces, sheet = refs[:-1], refs[-1]
    depth_index = lax.axis_index("depth")
    columns = sheet.shape[-1]
    width = pieces[0].shape[-1]
    _, lane = iotas(pieces[0].shape[1], width)
    sheet[...] = jnp.zeros(sheet.shape, f32)
    for flip, piece in by_flip(pieces):
        base, after, first = column_place(info, slots, depth_index ^ flip, width, columns)
        to_base = lane >= first
        for comp in range(2):
            value = piece[comp].astype(f32)
            sheet[comp, :, pl.ds(base, width)] += jnp.where(to_base, value, 0.0)
            sheet[comp, :, pl.ds(after, width)] += jnp.where(to_base, 0.0, value)


def body(transmission, probe_wave, prop_phase, measured, scan_rows, scan_cols, live_counts):
    pixels = probe_wave.shape[-1]
    slots = measured.shape[0]
    rows = transmission.shape[2]
    columns = transmission.shape[3]
    count = lax.axis_size("depth")
    own = transmission[0]
    info, own = lax.optimization_barrier(
        (jnp.concatenate([scan_rows, scan_cols, live_counts]), own)
    )
    ints = info.shape[0]
    info = shifted(jnp.pad(info, (0, INFO_SIZE - ints)), "scan", 1)[:ints]
    strip = call(strip_kernel, sds(own.shape, bf16), [own], [VMEM], name="strip")
    ends = swapped_ends(strip, "scan")
    beside = swapped(strip, "scan", 0)
    info, strip, beside = lax.optimization_barrier((info, strip, beside))
    inside = swapped_inside(strip, "scan")

    part = sds((2, rows, pixels), bf16)
    centers = call(
        functools.partial(center_kernel, slots, pixels),
        [part] * count, [info, own], [SMEM, VMEM], name="cut_center",
    )

    def across_depth(pieces):
        return [pieces[0]] + [exchanged(piece, "depth", flip) for flip, piece in by_flip(pieces)[1:]]

    centers = across_depth(centers)

    phase, centers[0] = lax.optimization_barrier((prop_phase, centers[0]))
    order = parity_order(pixels)
    square = sds((pixels, pixels), f32)
    prop_re, prop_im, amplitude = call(
        frequency_kernel,
        [square, square, sds((pixels, pixels), bf16)],
        [phase, jnp.asarray(order), jnp.asarray(order.T), measured],
        [VMEM] * 4, flops=2400 * pixels**3, transcendentals=2 * pixels**2, name="frequency_order",
    )
    amplitude = shifted(amplitude, "scan", 1)

    stack = split_tables(pixels)
    made = call(
        functools.partial(table_kernel, slots),
        [sds((2, pixels, pixels), bf16)] + [sds((pixels, pixels), bf16)] * 8,
        [info, jnp.asarray(stack), jnp.asarray(stack.T), probe_wave],
        [SMEM, VMEM, VMEM, VMEM], flops=16 * pixels**3, name="tables",
    )
    edges = call(
        functools.partial(edge_kernel, slots, pixels),
        [part] * count, [info, inside, ends, beside], [SMEM] + [VMEM] * 3,
        name="cut_edges",
    )
    edges = across_depth(edges)

    args = [info, prop_re, prop_im, amplitude, *made, *centers, *edges]
    grads = call(
        functools.partial(wave_kernel, slots, count),
        [part] * (2 * count), args, [SMEM] + [VMEM] * (len(args) - 1),
        scratch=[
            pltpu.VMEM((count, 2, pixels, pixels), bf16),
            pltpu.VMEM((count + 1, 2, pixels, pixels), bf16),
            pltpu.VMEM((1, 2, pixels, pixels), bf16),
            pltpu.VMEM((count, 2, pixels, pixels), bf16),
        ],
        flops=(2 * count + 1) * 16 * pixels**3, name="waves",
    )
    out_centers, out_edges = grads[:count], grads[count:]
    out_edges = across_depth(out_edges)
    sheet_bf16 = sds((2, rows, columns), bf16)
    sheet_f32 = sds((2, rows, columns), f32)
    to_across, to_beside = call(
        functools.partial(place_edges_kernel, slots),
        [sheet_bf16, sheet_bf16], [info, *out_edges], [SMEM] + [VMEM] * count,
        scratch=[pltpu.VMEM(sheet_f32.shape, f32)] * 2, name="place_edges",
    )
    from_ends = swapped_ends(to_across, "scan")
    from_beside = swapped(to_beside, "scan", 0)
    out_centers, to_across, from_beside = lax.optimization_barrier(
        (out_centers, to_across, from_beside)
    )
    from_inside = swapped_inside(to_across, "scan")
    out_centers = across_depth(out_centers)
    sheet = call(
        functools.partial(place_center_kernel, slots),
        sheet_f32, [info, *out_centers], [SMEM] + [VMEM] * count, name="place_center",
    )
    from_across = from_inside.astype(f32) + from_ends.astype(f32)
    gradient = sheet + from_across + from_beside.astype(f32)
    return gradient[None]


def solution(mesh):
    in_specs = (
        P("depth", None, "scan", None),
        P(),
        P(),
        P("scan", None, None),
        P("scan"),
        P("scan"),
        P("scan"),
    )
    out_specs = P("depth", None, "scan", None)
    return jax.shard_map(body, mesh=mesh, in_specs=in_specs, out_specs=out_specs, check_vma=False)
```

```python
import functools
import math

import jax
import jax.numpy as jnp
import ml_dtypes
import numpy as np
from jax import lax
from jax.experimental import pallas as pl
from jax.experimental.pallas import tpu as pltpu
from jax.sharding import PartitionSpec as P

epsilon = 1.0
bf16 = jnp.bfloat16
f32 = jnp.float32
VMEM = pl.BlockSpec(memory_space=pltpu.VMEM)
SMEM = pl.BlockSpec(memory_space=pltpu.SMEM)
LIMIT = 48 * 1024 * 1024


def shifted(value, axis, steps):
    count = lax.axis_size(axis)
    pairs = [(source, (source + steps) % count) for source in range(count)]
    return lax.ppermute(value, axis, pairs)


def swapped(value, axis, first):
    count = lax.axis_size(axis)
    pairs = [
        (source, (source + (1 if source % 2 == first else -1)) % count) for source in range(count)
    ]
    return lax.ppermute(value, axis, pairs)


def exchanged(value, axis, flip):
    count = lax.axis_size(axis)
    return lax.ppermute(value, axis, [(source, source ^ flip) for source in range(count)])


def split_tables(pixels):
    indices = np.arange(pixels)
    angles = (indices[:, None] * indices[None, :] % pixels) * (2.0 * math.pi / pixels)
    norm_scale = 1.0 / math.sqrt(pixels)
    table_re = (np.cos(angles) * norm_scale).astype(np.float32).astype(ml_dtypes.bfloat16)
    table_im = (-np.sin(angles) * norm_scale).astype(np.float32).astype(ml_dtypes.bfloat16)
    return np.concatenate([table_re[0::2], table_im[0::2], table_re[1::2], table_im[1::2]], axis=0)


def parity_order(pixels):
    order = np.concatenate([np.arange(0, pixels, 2), np.arange(1, pixels, 2)])
    return (order[:, None] == np.arange(pixels)[None, :]).astype(np.float32)


def call(kernel, out_shape, args, specs, scratch=(), flops=0, transcendentals=0, name=None):
    outs = out_shape if isinstance(out_shape, (list, tuple)) else [out_shape]
    moved = sum(math.prod(a.shape) * a.dtype.itemsize for a in list(args) + list(outs))
    return pl.pallas_call(
        kernel,
        out_shape=out_shape,
        in_specs=specs,
        out_specs=jax.tree.map(lambda _: VMEM, out_shape),
        scratch_shapes=list(scratch),
        compiler_params=pltpu.CompilerParams(vmem_limit_bytes=LIMIT),
        cost_estimate=pl.CostEstimate(
            flops=flops, bytes_accessed=moved, transcendentals=transcendentals
        ),
        name=name,
    )(*args)


def sds(shape, dtype):
    return jax.ShapeDtypeStruct(shape, dtype)


def by_flip(pieces):
    return list(zip([0, *range(len(pieces) - 1, 0, -1)], pieces))


def column_place(info, slots, slot, width, columns):
    col = info[slots + slot]
    base = (col // width) * width
    after = jnp.minimum(base + width, columns - width)
    return pl.multiple_of(base, width), pl.multiple_of(after, width), col - base


def iotas(rows, cols):
    return (
        lax.broadcasted_iota(jnp.int32, (rows, cols), 0),
        lax.broadcasted_iota(jnp.int32, (rows, cols), 1),
    )


def strip_kernel(own, whole, *strips):
    for comp, strip in enumerate(strips):
        value = own[comp].astype(bf16)
        whole[comp] = value
        strip[...] = value


def center_kernel(slots, width, info, own, *outs):
    depth_index = lax.axis_index("depth")
    columns = own.shape[-1]
    _, lane = iotas(own.shape[1], width)
    for flip, out in by_flip(outs):
        base, after, first = column_place(info, slots, depth_index ^ flip, width, columns)
        for comp in range(2):
            out[comp] = jnp.where(
                lane >= first, own[comp, :, pl.ds(base, width)], own[comp, :, pl.ds(after, width)]
            ).astype(bf16)


def edge_kernel(slots, width, info, across_re, across_im, beside, *outs):
    depth_index = lax.axis_index("depth")
    even = lax.rem(lax.axis_index("scan"), 2) == 0
    columns = beside.shape[-1]
    row, lane = iotas(beside.shape[1], width)
    for flip, out in by_flip(outs):
        slot = depth_index ^ flip
        base, after, first = column_place(info, slots, slot, width, columns)
        from_across = jnp.logical_xor(row < info[slot], even)

        def rows_at(comp, place):
            return jnp.where(
                from_across,
                (across_re, across_im)[comp][:, pl.ds(place, width)].astype(f32),
                beside[comp, :, pl.ds(place, width)].astype(f32),
            )

        for comp in range(2):
            out[comp] = jnp.where(
                lane >= first, rows_at(comp, base), rows_at(comp, after)
            ).astype(bf16)


def frequency_kernel(phase, order, order_t, measured, prop_re, prop_im, amplitude):
    def reorder(value):
        rows = jnp.dot(
            order[...], value, preferred_element_type=f32, precision=lax.Precision.HIGHEST
        )
        return jnp.dot(
            rows, order_t[...], preferred_element_type=f32, precision=lax.Precision.HIGHEST
        )

    turned = reorder(phase[...])
    prop_re[...] = jnp.cos(turned)
    prop_im[...] = jnp.sin(turned)
    amplitude[...] = reorder(measured[lax.axis_index("depth")]).astype(bf16)


def table_kernel(slots, info, stack, stack_t, probe, psi0, *tables):
    depth_index = lax.axis_index("depth")
    pixels = probe.shape[-1]
    half = pixels // 2
    row_shift = info[depth_index]
    col_shift = lax.rem(info[slots + depth_index], pixels)

    def shift_matrix(rows, cols, shift, transposed):
        row, lane = iotas(rows, cols)
        offset = (lane - row if transposed else row - lane) + shift
        return jnp.where((offset == 0) | (offset == pixels), 1.0, 0.0).astype(bf16)

    def pair(shift):
        cols = jnp.dot(
            stack[...], shift_matrix(pixels, half, shift, False), preferred_element_type=f32
        )
        rows = jnp.dot(
            shift_matrix(half, pixels, shift, True), stack_t[...], preferred_element_type=f32
        )
        forms, forms_t = [], []
        for parity in range(2):
            at = 2 * parity * half
            re, im = cols[at : at + half], cols[at + half : at + pixels]
            top = jnp.concatenate([re, -im], axis=1)
            bottom = jnp.concatenate([im, re], axis=1)
            forms.append(jnp.concatenate([top, bottom], axis=0).astype(bf16))
            re, im = rows[:, at : at + half], rows[:, at + half : at + pixels]
            top = jnp.concatenate([re, im], axis=1)
            bottom = jnp.concatenate([-im, re], axis=1)
            forms_t.append(jnp.concatenate([top, bottom], axis=0).astype(bf16))
        return forms, forms_t

    row_forms, row_forms_t = pair(row_shift)
    col_forms, col_forms_t = pair(col_shift)
    made = row_forms + col_forms_t + col_forms + row_forms_t
    for ref, value in zip(tables, made):
        ref[...] = value
    down = shift_matrix(pixels, pixels, row_shift, True)
    across = shift_matrix(pixels, pixels, col_shift, False)
    for comp in range(2):
        moved = jnp.dot(down, probe[comp].astype(bf16), preferred_element_type=f32).astype(bf16)
        psi0[comp] = jnp.dot(moved, across, preferred_element_type=f32).astype(bf16)


def wave_kernel(slots, depth_count, info, prop_re, prop_im, amplitude, psi0, *refs):
    tables = refs[:8]
    centers = refs[8 : 8 + depth_count]
    edges = refs[8 + depth_count : 8 + 2 * depth_count]
    out_centers = refs[8 + 2 * depth_count : 8 + 3 * depth_count]
    out_edges = refs[8 + 3 * depth_count : 8 + 4 * depth_count]
    patches, waves, adjoint, grads = refs[8 + 4 * depth_count :]
    depth_index = lax.axis_index("depth")
    pixels = psi0.shape[-1]
    half = pixels // 2
    live = depth_index < info[2 * slots]
    fwd_row_e, fwd_row_o, fwd_col_e, fwd_col_o, inv_col_e, inv_col_o, inv_row_e, inv_row_o = tables

    def dot(left, right):
        return jnp.dot(left, right, preferred_element_type=f32)

    def propagate(x_re, x_im, at_frequency):
        def rows_of(sign):
            mixed = [v[:half] + v[half:] if sign > 0 else v[:half] - v[half:] for v in (x_re, x_im)]
            return jnp.concatenate(mixed, axis=0).astype(bf16)

        u_even = dot(fwd_row_e[...], rows_of(1))
        u_odd = dot(fwd_row_o[...], rows_of(-1))

        def cols_of(sign):
            parts = []
            for u in (u_even, u_odd):
                mixed = u[:, :half] + u[:, half:] if sign > 0 else u[:, :half] - u[:, half:]
                parts.append(jnp.concatenate([mixed[:half], mixed[half:]], axis=1))
            return jnp.concatenate(parts, axis=0).astype(bf16)

        v_even = dot(cols_of(1), fwd_col_e[...])
        v_odd = dot(cols_of(-1), fwd_col_o[...])
        b_even = at_frequency(v_even[:, :half], v_even[:, half:], slice(0, half))
        b_odd = at_frequency(v_odd[:, :half], v_odd[:, half:], slice(half, pixels))
        w_even = dot(jnp.concatenate(b_even, axis=1).astype(bf16), inv_col_e[...])
        w_odd = dot(jnp.concatenate(b_odd, axis=1).astype(bf16), inv_col_o[...])
        w_low, w_high = w_even + w_odd, w_even - w_odd
        w_re = jnp.concatenate([w_low[:, :half], w_high[:, :half]], axis=1)
        w_im = jnp.concatenate([w_low[:, half:], w_high[:, half:]], axis=1)
        y_even = dot(
            inv_row_e[...], jnp.concatenate([w_re[:half], w_im[:half]], axis=0).astype(bf16)
        )
        y_odd = dot(
            inv_row_o[...], jnp.concatenate([w_re[half:], w_im[half:]], axis=0).astype(bf16)
        )
        low, high = y_even + y_odd, y_even - y_odd
        return (
            jnp.concatenate([low[:half], high[:half]], axis=0),
            jnp.concatenate([low[half:], high[half:]], axis=0),
        )

    def turn(re, im, cols):
        p_re, p_im = prop_re[:, cols], prop_im[:, cols]
        return [re * p_re - im * p_im, re * p_im + im * p_re]

    def turn_back(re, im, cols):
        p_re, p_im = prop_re[:, cols], prop_im[:, cols]
        return [re * p_re + im * p_im, im * p_re - re * p_im]

    def residual(re, im, cols):
        modulus = jnp.sqrt(re * re + im * im + epsilon)
        factor = 1.0 - amplitude[:, cols].astype(f32) / modulus
        return [factor * re, factor * im]

    def pair_of(ref, index):
        return ref[index, 0].astype(f32), ref[index, 1].astype(f32)

    @pl.when(live)
    def _():
        for (flip, center), edge in zip(by_flip(centers), edges):
            patches[depth_index ^ flip, :, half:] = center[...]
            patches[depth_index ^ flip, :, :half] = edge[...]
        waves[0] = psi0[...]

        def forward(k, carry):
            t_re, t_im = pair_of(patches, k)
            p_re, p_im = pair_of(waves, k)
            n_re, n_im = propagate(t_re * p_re - t_im * p_im, t_re * p_im + t_im * p_re, turn)
            waves[k + 1, 0] = n_re.astype(bf16)
            waves[k + 1, 1] = n_im.astype(bf16)
            return carry

        lax.fori_loop(0, depth_count, forward, 0)
        l_re, l_im = propagate(*pair_of(waves, depth_count), residual)
        adjoint[0, 0] = l_re.astype(bf16)
        adjoint[0, 1] = l_im.astype(bf16)

        def backward(step, carry):
            k = depth_count - 1 - step
            m_re, m_im = propagate(*pair_of(adjoint, 0), turn_back)
            t_re, t_im = pair_of(patches, k)
            p_re, p_im = pair_of(waves, k)
            grads[k ^ depth_index, 0] = (p_re * m_re + p_im * m_im).astype(bf16)
            grads[k ^ depth_index, 1] = (p_re * m_im - p_im * m_re).astype(bf16)
            adjoint[0, 0] = (t_re * m_re + t_im * m_im).astype(bf16)
            adjoint[0, 1] = (t_re * m_im - t_im * m_re).astype(bf16)
            return carry

        lax.fori_loop(0, depth_count, backward, 0)
        for (flip, center), edge in zip(by_flip(out_centers), out_edges):
            center[...] = grads[flip, :, half:]
            edge[...] = grads[flip, :, :half]

    @pl.when(jnp.logical_not(live))
    def _():
        for ref in out_centers + out_edges:
            ref[...] = jnp.zeros(ref.shape, ref.dtype)


def place_edges_kernel(slots, info, *refs):
    pieces, (across_re, across_im, beside, across_sum, beside_sum) = refs[:-5], refs[-5:]
    depth_index = lax.axis_index("depth")
    even = lax.rem(lax.axis_index("scan"), 2) == 0
    columns = beside.shape[-1]
    width = pieces[0].shape[-1]
    row, lane = iotas(pieces[0].shape[1], width)
    across_sum[...] = jnp.zeros(across_sum.shape, f32)
    beside_sum[...] = jnp.zeros(beside_sum.shape, f32)
    for flip, piece in by_flip(pieces):
        slot = depth_index ^ flip
        base, after, first = column_place(info, slots, slot, width, columns)
        to_across = jnp.logical_xor(row < info[slot], even)
        to_base = lane >= first
        for comp in range(2):
            value = piece[comp].astype(f32)
            for sheet, kept in (
                (across_sum, jnp.where(to_across, value, 0.0)),
                (beside_sum, jnp.where(to_across, 0.0, value)),
            ):
                sheet[comp, :, pl.ds(base, width)] += jnp.where(to_base, kept, 0.0)
                sheet[comp, :, pl.ds(after, width)] += jnp.where(to_base, 0.0, kept)
    across_re[...] = across_sum[0].astype(bf16)
    across_im[...] = across_sum[1].astype(bf16)
    beside[...] = beside_sum[...].astype(bf16)


def place_center_kernel(slots, info, *refs):
    pieces, sheet = refs[:-1], refs[-1]
    depth_index = lax.axis_index("depth")
    columns = sheet.shape[-1]
    width = pieces[0].shape[-1]
    _, lane = iotas(pieces[0].shape[1], width)
    sheet[...] = jnp.zeros(sheet.shape, f32)
    for flip, piece in by_flip(pieces):
        base, after, first = column_place(info, slots, depth_index ^ flip, width, columns)
        to_base = lane >= first
        for comp in range(2):
            value = piece[comp].astype(f32)
            sheet[comp, :, pl.ds(base, width)] += jnp.where(to_base, value, 0.0)
            sheet[comp, :, pl.ds(after, width)] += jnp.where(to_base, 0.0, value)


def body(transmission, probe_wave, prop_phase, measured, scan_rows, scan_cols, live_counts):
    pixels = probe_wave.shape[-1]
    slots = measured.shape[0]
    rows = transmission.shape[2]
    columns = transmission.shape[3]
    count = lax.axis_size("depth")
    own = transmission[0]
    info, own = lax.optimization_barrier(
        (jnp.concatenate([scan_rows, scan_cols, live_counts]), own)
    )
    info = shifted(info, "scan", 1)
    strip = sds((rows, columns), bf16)
    whole, *strips = call(
        strip_kernel, [sds(own.shape, bf16), strip, strip], [own], [VMEM], name="strip"
    )
    info, whole, strips = lax.optimization_barrier((info, whole, strips))
    across = [swapped(piece, "scan", 1) for piece in strips]
    beside = swapped(whole, "scan", 0)

    part = sds((2, rows, pixels), bf16)
    centers = call(
        functools.partial(center_kernel, slots, pixels),
        [part] * count, [info, own], [SMEM, VMEM], name="cut_center",
    )

    def across_depth(pieces):
        return [pieces[0]] + [exchanged(piece, "depth", flip) for flip, piece in by_flip(pieces)[1:]]

    centers = list(centers)
    centers[-1], beside = lax.optimization_barrier((centers[-1], beside))
    centers = across_depth(centers)

    phase, centers[1] = lax.optimization_barrier((prop_phase, centers[1]))
    order = parity_order(pixels)
    square = sds((pixels, pixels), f32)
    prop_re, prop_im, amplitude = call(
        frequency_kernel,
        [square, square, sds((pixels, pixels), bf16)],
        [phase, jnp.asarray(order), jnp.asarray(order.T), measured],
        [VMEM] * 4, flops=24 * pixels**3, transcendentals=2 * pixels**2, name="frequency_order",
    )
    amplitude = shifted(amplitude, "scan", 1)

    stack = split_tables(pixels)
    made = call(
        functools.partial(table_kernel, slots),
        [sds((2, pixels, pixels), bf16)] + [sds((pixels, pixels), bf16)] * 8,
        [info, jnp.asarray(stack), jnp.asarray(stack.T), probe_wave],
        [SMEM, VMEM, VMEM, VMEM], flops=16 * pixels**3, name="tables",
    )
    centers, across, prop_re = lax.optimization_barrier((centers, across, prop_re))
    edges = call(
        functools.partial(edge_kernel, slots, pixels),
        [part] * count, [info, *across, beside], [SMEM] + [VMEM] * 3, name="cut_edges",
    )
    edges = across_depth(edges)

    args = [info, prop_re, prop_im, amplitude, *made, *centers, *edges]
    grads = call(
        functools.partial(wave_kernel, slots, count),
        [part] * (2 * count), args, [SMEM] + [VMEM] * (len(args) - 1),
        scratch=[
            pltpu.VMEM((count, 2, pixels, pixels), bf16),
            pltpu.VMEM((count + 1, 2, pixels, pixels), bf16),
            pltpu.VMEM((1, 2, pixels, pixels), bf16),
            pltpu.VMEM((count, 2, pixels, pixels), bf16),
        ],
        flops=(2 * count + 1) * 16 * pixels**3, name="waves",
    )
    out_centers, out_edges = grads[:count], grads[count:]
    out_edges = across_depth(out_edges)
    sheet_f32 = sds((2, rows, columns), f32)
    *to_across, to_beside = call(
        functools.partial(place_edges_kernel, slots),
        [strip, strip, whole], [info, *out_edges], [SMEM] + [VMEM] * count,
        scratch=[pltpu.VMEM(sheet_f32.shape, f32)] * 2, name="place_edges",
    )
    from_across = jnp.stack([swapped(piece, "scan", 1) for piece in to_across])
    from_beside = swapped(to_beside, "scan", 0)
    out_centers, from_beside = lax.optimization_barrier((out_centers, from_beside))
    out_centers = across_depth(out_centers)
    sheet = call(
        functools.partial(place_center_kernel, slots),
        sheet_f32, [info, *out_centers], [SMEM] + [VMEM] * count, name="place_center",
    )
    gradient = sheet + from_across.astype(f32) + from_beside.astype(f32)
    return gradient[None]


def solution(mesh):
    in_specs = (
        P("depth", None, "scan", None),
        P(),
        P(),
        P("scan", None, None),
        P("scan"),
        P("scan"),
        P("scan"),
    )
    out_specs = P("depth", None, "scan", None)
    return jax.shard_map(body, mesh=mesh, in_specs=in_specs, out_specs=out_specs, check_vma=False)
```

```python
import functools
import math

import jax
import jax.numpy as jnp
import ml_dtypes
import numpy as np
from jax import lax
from jax.experimental import pallas as pl
from jax.experimental.pallas import tpu as pltpu
from jax.sharding import PartitionSpec as P

epsilon = 1.0
bf16 = jnp.bfloat16
f32 = jnp.float32
VMEM = pl.BlockSpec(memory_space=pltpu.VMEM)
SMEM = pl.BlockSpec(memory_space=pltpu.SMEM)
LIMIT = 48 * 1024 * 1024
INFO_SIZE = 8192


def shifted(value, axis, steps):
    count = lax.axis_size(axis)
    pairs = [(source, (source + steps) % count) for source in range(count)]
    return lax.ppermute(value, axis, pairs)


def swapped(value, axis, first):
    count = lax.axis_size(axis)
    pairs = [
        (source, (source + (1 if source % 2 == first else -1)) % count) for source in range(count)
    ]
    return lax.ppermute(value, axis, pairs)


def exchanged(value, axis, flip):
    count = lax.axis_size(axis)
    return lax.ppermute(value, axis, [(source, source ^ flip) for source in range(count)])


def split_tables(pixels):
    indices = np.arange(pixels)
    angles = (indices[:, None] * indices[None, :] % pixels) * (2.0 * math.pi / pixels)
    norm_scale = 1.0 / math.sqrt(pixels)
    table_re = (np.cos(angles) * norm_scale).astype(np.float32).astype(ml_dtypes.bfloat16)
    table_im = (-np.sin(angles) * norm_scale).astype(np.float32).astype(ml_dtypes.bfloat16)
    return np.concatenate([table_re[0::2], table_im[0::2], table_re[1::2], table_im[1::2]], axis=0)


def parity_order(pixels):
    order = np.concatenate([np.arange(0, pixels, 2), np.arange(1, pixels, 2)])
    return (order[:, None] == np.arange(pixels)[None, :]).astype(np.float32)


def call(kernel, out_shape, args, specs, scratch=(), flops=0, transcendentals=0, name=None):
    outs = out_shape if isinstance(out_shape, (list, tuple)) else [out_shape]
    moved = sum(math.prod(a.shape) * a.dtype.itemsize for a in list(args) + list(outs))
    return pl.pallas_call(
        kernel,
        out_shape=out_shape,
        in_specs=specs,
        out_specs=jax.tree.map(lambda _: VMEM, out_shape),
        scratch_shapes=list(scratch),
        compiler_params=pltpu.CompilerParams(vmem_limit_bytes=LIMIT),
        cost_estimate=pl.CostEstimate(
            flops=flops, bytes_accessed=moved, transcendentals=transcendentals
        ),
        name=name,
    )(*args)


def sds(shape, dtype):
    return jax.ShapeDtypeStruct(shape, dtype)


def by_flip(pieces):
    return list(zip([0, *range(len(pieces) - 1, 0, -1)], pieces))


def column_place(info, slots, slot, width, columns):
    col = info[slots + slot]
    base = (col // width) * width
    after = jnp.minimum(base + width, columns - width)
    return pl.multiple_of(base, width), pl.multiple_of(after, width), col - base


def iotas(rows, cols):
    return (
        lax.broadcasted_iota(jnp.int32, (rows, cols), 0),
        lax.broadcasted_iota(jnp.int32, (rows, cols), 1),
    )


def strip_kernel(own, strip):
    strip[...] = own[...].astype(bf16)


def center_kernel(slots, width, info, own, *outs):
    depth_index = lax.axis_index("depth")
    columns = own.shape[-1]
    _, lane = iotas(own.shape[1], width)
    for flip, out in by_flip(outs):
        base, after, first = column_place(info, slots, depth_index ^ flip, width, columns)
        for comp in range(2):
            out[comp] = jnp.where(
                lane >= first, own[comp, :, pl.ds(base, width)], own[comp, :, pl.ds(after, width)]
            ).astype(bf16)


def edge_kernel(slots, width, info, across, beside, *outs):
    depth_index = lax.axis_index("depth")
    even = lax.rem(lax.axis_index("scan"), 2) == 0
    columns = across.shape[-1]
    row, lane = iotas(across.shape[1], width)
    for flip, out in by_flip(outs):
        slot = depth_index ^ flip
        base, after, first = column_place(info, slots, slot, width, columns)
        from_across = jnp.logical_xor(row < info[slot], even)

        def rows_at(comp, place):
            return jnp.where(
                from_across,
                across[comp, :, pl.ds(place, width)].astype(f32),
                beside[comp, :, pl.ds(place, width)].astype(f32),
            )

        for comp in range(2):
            out[comp] = jnp.where(
                lane >= first, rows_at(comp, base), rows_at(comp, after)
            ).astype(bf16)


def frequency_kernel(phase, order, order_t, measured, prop_re, prop_im, amplitude):
    def reorder(value):
        rows = jnp.dot(
            order[...], value, preferred_element_type=f32, precision=lax.Precision.HIGHEST
        )
        return jnp.dot(
            rows, order_t[...], preferred_element_type=f32, precision=lax.Precision.HIGHEST
        )

    turned = reorder(phase[...])
    prop_re[...] = jnp.cos(turned)
    prop_im[...] = jnp.sin(turned)
    amplitude[...] = reorder(measured[lax.axis_index("depth")]).astype(bf16)


def table_kernel(slots, info, stack, stack_t, probe, psi0, *tables):
    depth_index = lax.axis_index("depth")
    pixels = probe.shape[-1]
    half = pixels // 2
    row_shift = info[depth_index]
    col_shift = lax.rem(info[slots + depth_index], pixels)

    def shift_matrix(rows, cols, shift, transposed):
        row, lane = iotas(rows, cols)
        offset = (lane - row if transposed else row - lane) + shift
        return jnp.where((offset == 0) | (offset == pixels), 1.0, 0.0).astype(bf16)

    def pair(shift):
        cols = jnp.dot(
            stack[...], shift_matrix(pixels, half, shift, False), preferred_element_type=f32
        )
        rows = jnp.dot(
            shift_matrix(half, pixels, shift, True), stack_t[...], preferred_element_type=f32
        )
        forms, forms_t = [], []
        for parity in range(2):
            at = 2 * parity * half
            re, im = cols[at : at + half], cols[at + half : at + pixels]
            top = jnp.concatenate([re, -im], axis=1)
            bottom = jnp.concatenate([im, re], axis=1)
            forms.append(jnp.concatenate([top, bottom], axis=0).astype(bf16))
            re, im = rows[:, at : at + half], rows[:, at + half : at + pixels]
            top = jnp.concatenate([re, im], axis=1)
            bottom = jnp.concatenate([-im, re], axis=1)
            forms_t.append(jnp.concatenate([top, bottom], axis=0).astype(bf16))
        return forms, forms_t

    row_forms, row_forms_t = pair(row_shift)
    col_forms, col_forms_t = pair(col_shift)
    made = row_forms + col_forms_t + col_forms + row_forms_t
    for ref, value in zip(tables, made):
        ref[...] = value
    down = shift_matrix(pixels, pixels, row_shift, True)
    across = shift_matrix(pixels, pixels, col_shift, False)
    for comp in range(2):
        moved = jnp.dot(down, probe[comp].astype(bf16), preferred_element_type=f32).astype(bf16)
        psi0[comp] = jnp.dot(moved, across, preferred_element_type=f32).astype(bf16)


def wave_kernel(slots, depth_count, info, prop_re, prop_im, amplitude, psi0, *refs):
    tables = refs[:8]
    centers = refs[8 : 8 + depth_count]
    edges = refs[8 + depth_count : 8 + 2 * depth_count]
    out_centers = refs[8 + 2 * depth_count : 8 + 3 * depth_count]
    out_edges = refs[8 + 3 * depth_count : 8 + 4 * depth_count]
    patches, waves, adjoint, grads = refs[8 + 4 * depth_count :]
    depth_index = lax.axis_index("depth")
    pixels = psi0.shape[-1]
    half = pixels // 2
    live = depth_index < info[2 * slots]
    fwd_row_e, fwd_row_o, fwd_col_e, fwd_col_o, inv_col_e, inv_col_o, inv_row_e, inv_row_o = tables

    def dot(left, right):
        return jnp.dot(left, right, preferred_element_type=f32)

    def propagate(x_re, x_im, at_frequency):
        def rows_of(sign):
            mixed = [v[:half] + v[half:] if sign > 0 else v[:half] - v[half:] for v in (x_re, x_im)]
            return jnp.concatenate(mixed, axis=0).astype(bf16)

        u_even = dot(fwd_row_e[...], rows_of(1))
        u_odd = dot(fwd_row_o[...], rows_of(-1))

        def cols_of(sign):
            parts = []
            for u in (u_even, u_odd):
                mixed = u[:, :half] + u[:, half:] if sign > 0 else u[:, :half] - u[:, half:]
                parts.append(jnp.concatenate([mixed[:half], mixed[half:]], axis=1))
            return jnp.concatenate(parts, axis=0).astype(bf16)

        v_even = dot(cols_of(1), fwd_col_e[...])
        v_odd = dot(cols_of(-1), fwd_col_o[...])
        b_even = at_frequency(v_even[:, :half], v_even[:, half:], slice(0, half))
        b_odd = at_frequency(v_odd[:, :half], v_odd[:, half:], slice(half, pixels))
        w_even = dot(jnp.concatenate(b_even, axis=1).astype(bf16), inv_col_e[...])
        w_odd = dot(jnp.concatenate(b_odd, axis=1).astype(bf16), inv_col_o[...])
        w_low, w_high = w_even + w_odd, w_even - w_odd
        w_re = jnp.concatenate([w_low[:, :half], w_high[:, :half]], axis=1)
        w_im = jnp.concatenate([w_low[:, half:], w_high[:, half:]], axis=1)
        y_even = dot(
            inv_row_e[...], jnp.concatenate([w_re[:half], w_im[:half]], axis=0).astype(bf16)
        )
        y_odd = dot(
            inv_row_o[...], jnp.concatenate([w_re[half:], w_im[half:]], axis=0).astype(bf16)
        )
        low, high = y_even + y_odd, y_even - y_odd
        return (
            jnp.concatenate([low[:half], high[:half]], axis=0),
            jnp.concatenate([low[half:], high[half:]], axis=0),
        )

    def turn(re, im, cols):
        p_re, p_im = prop_re[:, cols], prop_im[:, cols]
        return [re * p_re - im * p_im, re * p_im + im * p_re]

    def turn_back(re, im, cols):
        p_re, p_im = prop_re[:, cols], prop_im[:, cols]
        return [re * p_re + im * p_im, im * p_re - re * p_im]

    def residual(re, im, cols):
        modulus = jnp.sqrt(re * re + im * im + epsilon)
        factor = 1.0 - amplitude[:, cols].astype(f32) / modulus
        return [factor * re, factor * im]

    def pair_of(ref, index):
        return ref[index, 0].astype(f32), ref[index, 1].astype(f32)

    @pl.when(live)
    def _():
        for (flip, center), edge in zip(by_flip(centers), edges):
            patches[depth_index ^ flip, :, half:] = center[...]
            patches[depth_index ^ flip, :, :half] = edge[...]
        waves[0] = psi0[...]

        def forward(k, carry):
            t_re, t_im = pair_of(patches, k)
            p_re, p_im = pair_of(waves, k)
            n_re, n_im = propagate(t_re * p_re - t_im * p_im, t_re * p_im + t_im * p_re, turn)
            waves[k + 1, 0] = n_re.astype(bf16)
            waves[k + 1, 1] = n_im.astype(bf16)
            return carry

        lax.fori_loop(0, depth_count, forward, 0)
        l_re, l_im = propagate(*pair_of(waves, depth_count), residual)
        adjoint[0, 0] = l_re.astype(bf16)
        adjoint[0, 1] = l_im.astype(bf16)

        def backward(step, carry):
            k = depth_count - 1 - step
            m_re, m_im = propagate(*pair_of(adjoint, 0), turn_back)
            t_re, t_im = pair_of(patches, k)
            p_re, p_im = pair_of(waves, k)
            grads[k ^ depth_index, 0] = (p_re * m_re + p_im * m_im).astype(bf16)
            grads[k ^ depth_index, 1] = (p_re * m_im - p_im * m_re).astype(bf16)
            adjoint[0, 0] = (t_re * m_re + t_im * m_im).astype(bf16)
            adjoint[0, 1] = (t_re * m_im - t_im * m_re).astype(bf16)
            return carry

        lax.fori_loop(0, depth_count, backward, 0)
        for (flip, center), edge in zip(by_flip(out_centers), out_edges):
            center[...] = grads[flip, :, half:]
            edge[...] = grads[flip, :, :half]

    @pl.when(jnp.logical_not(live))
    def _():
        for ref in out_centers + out_edges:
            ref[...] = jnp.zeros(ref.shape, ref.dtype)


def place_edges_kernel(slots, info, *refs):
    pieces, (across, beside) = refs[:-2], refs[-2:]
    depth_index = lax.axis_index("depth")
    even = lax.rem(lax.axis_index("scan"), 2) == 0
    rows, columns = across.shape[1:]
    width = pieces[0].shape[-1]
    row, lane = iotas(rows, width)
    masks = []
    for flip, _ in by_flip(pieces):
        slot = depth_index ^ flip
        base, after, first = column_place(info, slots, slot, width, columns)
        to_across = jnp.logical_xor(row < info[slot], even)
        masks.append((base, after, lane >= first, to_across))
    for start in range(0, columns, width):
        kept = [
            jnp.logical_or(
                jnp.logical_and(to_base, base == start),
                jnp.logical_and(jnp.logical_not(to_base), after == start),
            )
            for base, after, to_base, _ in masks
        ]
        for comp in range(2):
            across_sum = jnp.zeros((rows, width), f32)
            beside_sum = jnp.zeros((rows, width), f32)
            for piece, keep, (_, _, _, to_across) in zip(pieces, kept, masks):
                value = jnp.where(keep, piece[comp].astype(f32), 0.0)
                across_sum += jnp.where(to_across, value, 0.0)
                beside_sum += jnp.where(to_across, 0.0, value)
            across[comp, :, pl.ds(start, width)] = across_sum.astype(bf16)
            beside[comp, :, pl.ds(start, width)] = beside_sum.astype(bf16)


def place_center_kernel(slots, info, *refs):
    pieces, sheet = refs[:-1], refs[-1]
    depth_index = lax.axis_index("depth")
    columns = sheet.shape[-1]
    width = pieces[0].shape[-1]
    _, lane = iotas(pieces[0].shape[1], width)
    sheet[...] = jnp.zeros(sheet.shape, f32)
    for flip, piece in by_flip(pieces):
        base, after, first = column_place(info, slots, depth_index ^ flip, width, columns)
        to_base = lane >= first
        for comp in range(2):
            value = piece[comp].astype(f32)
            sheet[comp, :, pl.ds(base, width)] += jnp.where(to_base, value, 0.0)
            sheet[comp, :, pl.ds(after, width)] += jnp.where(to_base, 0.0, value)


def add_kernel(sheet, across, beside, out, total, sems):
    rows = sheet.shape[1] // 2
    copies = []
    for comp in range(2):
        for part in range(2):
            at = pl.ds(part * rows, rows)
            total[comp, at] = (
                sheet[comp, at] + across[comp, at].astype(f32) + beside[comp, at].astype(f32)
            )
            copies.append(
                pltpu.make_async_copy(
                    total.at[comp, at], out.at[comp, at], sems.at[2 * comp + part]
                )
            )
            copies[-1].start()
    for copy in copies:
        copy.wait()


def body(transmission, probe_wave, prop_phase, measured, scan_rows, scan_cols, live_counts):
    pixels = probe_wave.shape[-1]
    slots = measured.shape[0]
    rows = transmission.shape[2]
    columns = transmission.shape[3]
    count = lax.axis_size("depth")
    own = transmission[0]
    info, own = lax.optimization_barrier(
        (jnp.concatenate([scan_rows, scan_cols, live_counts]), own)
    )
    ints = info.shape[0]
    info = shifted(jnp.pad(info, (0, INFO_SIZE - ints)), "scan", 1)[:ints]
    strip = call(strip_kernel, sds(own.shape, bf16), [own], [VMEM], name="strip")
    across = swapped(strip, "scan", 1)
    beside = swapped(strip, "scan", 0)

    part = sds((2, rows, pixels), bf16)
    centers = call(
        functools.partial(center_kernel, slots, pixels),
        [part] * count, [info, own], [SMEM, VMEM], name="cut_center",
    )

    def across_depth(pieces):
        return [pieces[0]] + [exchanged(piece, "depth", flip) for flip, piece in by_flip(pieces)[1:]]

    centers = across_depth(centers)

    phase, centers[0] = lax.optimization_barrier((prop_phase, centers[0]))
    order = parity_order(pixels)
    square = sds((pixels, pixels), f32)
    prop_re, prop_im, amplitude = call(
        frequency_kernel,
        [square, square, sds((pixels, pixels), bf16)],
        [phase, jnp.asarray(order), jnp.asarray(order.T), measured],
        [VMEM] * 4, flops=2400 * pixels**3, transcendentals=2 * pixels**2, name="frequency_order",
    )
    amplitude = shifted(amplitude, "scan", 1)

    stack = split_tables(pixels)
    made = call(
        functools.partial(table_kernel, slots),
        [sds((2, pixels, pixels), bf16)] + [sds((pixels, pixels), bf16)] * 8,
        [info, jnp.asarray(stack), jnp.asarray(stack.T), probe_wave],
        [SMEM, VMEM, VMEM, VMEM], flops=16 * pixels**3, name="tables",
    )
    edges = call(
        functools.partial(edge_kernel, slots, pixels),
        [part] * count, [info, across, beside], [SMEM, VMEM, VMEM], name="cut_edges",
    )
    edges = across_depth(edges)

    args = [info, prop_re, prop_im, amplitude, *made, *centers, *edges]
    grads = call(
        functools.partial(wave_kernel, slots, count),
        [part] * (2 * count), args, [SMEM] + [VMEM] * (len(args) - 1),
        scratch=[
            pltpu.VMEM((count, 2, pixels, pixels), bf16),
            pltpu.VMEM((count + 1, 2, pixels, pixels), bf16),
            pltpu.VMEM((1, 2, pixels, pixels), bf16),
            pltpu.VMEM((count, 2, pixels, pixels), bf16),
        ],
        flops=(2 * count + 1) * 16 * pixels**3, name="waves",
    )
    out_centers, out_edges = grads[:count], grads[count:]
    out_edges = across_depth(out_edges)
    out_centers = across_depth(out_centers)
    sheet_bf16 = sds((2, rows, columns), bf16)
    sheet_f32 = sds((2, rows, columns), f32)
    to_across, to_beside = call(
        functools.partial(place_edges_kernel, slots),
        [sheet_bf16, sheet_bf16], [info, *out_edges], [SMEM] + [VMEM] * count,
        name="place_edges",
    )
    from_across = swapped(to_across, "scan", 1)
    from_beside = swapped(to_beside, "scan", 0)
    sheet = call(
        functools.partial(place_center_kernel, slots),
        sheet_f32, [info, *out_centers], [SMEM] + [VMEM] * count, name="place_center",
    )
    gradient = pl.pallas_call(
        add_kernel,
        out_shape=sheet_f32,
        in_specs=[VMEM] * 3,
        out_specs=pl.BlockSpec(memory_space=pl.ANY),
        scratch_shapes=[pltpu.VMEM(sheet_f32.shape, f32), pltpu.SemaphoreType.DMA((4,))],
        compiler_params=pltpu.CompilerParams(vmem_limit_bytes=LIMIT),
        name="add_edges",
    )(sheet, from_across, from_beside)
    return gradient[None]


def solution(mesh):
    in_specs = (
        P("depth", None, "scan", None),
        P(),
        P(),
        P("scan", None, None),
        P("scan"),
        P("scan"),
        P("scan"),
    )
    out_specs = P("depth", None, "scan", None)
    return jax.shard_map(body, mesh=mesh, in_specs=in_specs, out_specs=out_specs, check_vma=False)
```

```python
import functools
import math

import jax
import jax.numpy as jnp
import ml_dtypes
import numpy as np
from jax import lax
from jax.experimental import pallas as pl
from jax.experimental.pallas import tpu as pltpu
from jax.sharding import PartitionSpec as P

epsilon = 1.0
bf16 = jnp.bfloat16
f32 = jnp.float32
VMEM = pl.BlockSpec(memory_space=pltpu.VMEM)
SMEM = pl.BlockSpec(memory_space=pltpu.SMEM)
LIMIT = 48 * 1024 * 1024
INFO_SIZE = 8192


def shifted(value, axis, steps):
    count = lax.axis_size(axis)
    pairs = [(source, (source + steps) % count) for source in range(count)]
    return lax.ppermute(value, axis, pairs)


def swapped(value, axis, first):
    count = lax.axis_size(axis)
    pairs = [
        (source, (source + (1 if source % 2 == first else -1)) % count) for source in range(count)
    ]
    return lax.ppermute(value, axis, pairs)


def exchanged(value, axis, flip):
    count = lax.axis_size(axis)
    return lax.ppermute(value, axis, [(source, source ^ flip) for source in range(count)])


def split_tables(pixels):
    indices = np.arange(pixels)
    angles = (indices[:, None] * indices[None, :] % pixels) * (2.0 * math.pi / pixels)
    norm_scale = 1.0 / math.sqrt(pixels)
    table_re = (np.cos(angles) * norm_scale).astype(np.float32).astype(ml_dtypes.bfloat16)
    table_im = (-np.sin(angles) * norm_scale).astype(np.float32).astype(ml_dtypes.bfloat16)
    return np.concatenate([table_re[0::2], table_im[0::2], table_re[1::2], table_im[1::2]], axis=0)


def parity_order(pixels):
    order = np.concatenate([np.arange(0, pixels, 2), np.arange(1, pixels, 2)])
    return (order[:, None] == np.arange(pixels)[None, :]).astype(np.float32)


def call(kernel, out_shape, args, specs, scratch=(), flops=0, transcendentals=0, name=None):
    outs = out_shape if isinstance(out_shape, (list, tuple)) else [out_shape]
    moved = sum(math.prod(a.shape) * a.dtype.itemsize for a in list(args) + list(outs))
    return pl.pallas_call(
        kernel,
        out_shape=out_shape,
        in_specs=specs,
        out_specs=jax.tree.map(lambda _: VMEM, out_shape),
        scratch_shapes=list(scratch),
        compiler_params=pltpu.CompilerParams(vmem_limit_bytes=LIMIT),
        cost_estimate=pl.CostEstimate(
            flops=flops, bytes_accessed=moved, transcendentals=transcendentals
        ),
        name=name,
    )(*args)


def sds(shape, dtype):
    return jax.ShapeDtypeStruct(shape, dtype)


def by_flip(pieces):
    return list(zip([0, *range(len(pieces) - 1, 0, -1)], pieces))


def column_place(info, slots, slot, width, columns):
    col = info[slots + slot]
    base = (col // width) * width
    after = jnp.minimum(base + width, columns - width)
    return pl.multiple_of(base, width), pl.multiple_of(after, width), col - base


def iotas(rows, cols):
    return (
        lax.broadcasted_iota(jnp.int32, (rows, cols), 0),
        lax.broadcasted_iota(jnp.int32, (rows, cols), 1),
    )


def strip_kernel(own, strip, loaded, sems):
    parts = 4
    rows = own.shape[1] // parts
    copies = []
    for comp in range(2):
        for part in range(parts):
            at = pl.ds(part * rows, rows)
            copy = pltpu.make_async_copy(
                own.at[comp, at], loaded.at[comp, at], sems.at[comp * parts + part]
            )
            copy.start()
            copies.append((copy, comp, at))
    for copy, comp, at in copies:
        copy.wait()
        strip[comp, at] = loaded[comp, at].astype(bf16)


def center_kernel(slots, width, info, strip, *outs):
    depth_index = lax.axis_index("depth")
    columns = strip.shape[-1]
    _, lane = iotas(strip.shape[1], width)
    for flip, out in by_flip(outs):
        base, after, first = column_place(info, slots, depth_index ^ flip, width, columns)
        for comp in range(2):
            out[comp] = jnp.where(
                lane >= first,
                strip[comp, :, pl.ds(base, width)].astype(f32),
                strip[comp, :, pl.ds(after, width)].astype(f32),
            ).astype(bf16)


def edge_kernel(slots, width, info, across, beside, *outs):
    depth_index = lax.axis_index("depth")
    even = lax.rem(lax.axis_index("scan"), 2) == 0
    columns = across.shape[-1]
    row, lane = iotas(across.shape[1], width)
    for flip, out in by_flip(outs):
        slot = depth_index ^ flip
        base, after, first = column_place(info, slots, slot, width, columns)
        from_across = jnp.logical_xor(row < info[slot], even)

        def rows_at(comp, place):
            return jnp.where(
                from_across,
                across[comp, :, pl.ds(place, width)].astype(f32),
                beside[comp, :, pl.ds(place, width)].astype(f32),
            )

        for comp in range(2):
            out[comp] = jnp.where(
                lane >= first, rows_at(comp, base), rows_at(comp, after)
            ).astype(bf16)


def frequency_kernel(phase, order, order_t, measured, prop_re, prop_im, amplitude):
    def reorder(value):
        rows = jnp.dot(
            order[...], value, preferred_element_type=f32, precision=lax.Precision.HIGHEST
        )
        return jnp.dot(
            rows, order_t[...], preferred_element_type=f32, precision=lax.Precision.HIGHEST
        )

    turned = reorder(phase[...])
    prop_re[...] = jnp.cos(turned)
    prop_im[...] = jnp.sin(turned)
    amplitude[...] = reorder(measured[lax.axis_index("depth")]).astype(bf16)


def table_kernel(slots, info, stack, stack_t, probe, psi0, *tables):
    depth_index = lax.axis_index("depth")
    pixels = probe.shape[-1]
    half = pixels // 2
    row_shift = info[depth_index]
    col_shift = lax.rem(info[slots + depth_index], pixels)

    def shift_matrix(rows, cols, shift, transposed):
        row, lane = iotas(rows, cols)
        offset = (lane - row if transposed else row - lane) + shift
        return jnp.where((offset == 0) | (offset == pixels), 1.0, 0.0).astype(bf16)

    def pair(shift):
        cols = jnp.dot(
            stack[...], shift_matrix(pixels, half, shift, False), preferred_element_type=f32
        )
        rows = jnp.dot(
            shift_matrix(half, pixels, shift, True), stack_t[...], preferred_element_type=f32
        )
        forms, forms_t = [], []
        for parity in range(2):
            at = 2 * parity * half
            re, im = cols[at : at + half], cols[at + half : at + pixels]
            top = jnp.concatenate([re, -im], axis=1)
            bottom = jnp.concatenate([im, re], axis=1)
            forms.append(jnp.concatenate([top, bottom], axis=0).astype(bf16))
            re, im = rows[:, at : at + half], rows[:, at + half : at + pixels]
            top = jnp.concatenate([re, im], axis=1)
            bottom = jnp.concatenate([-im, re], axis=1)
            forms_t.append(jnp.concatenate([top, bottom], axis=0).astype(bf16))
        return forms, forms_t

    row_forms, row_forms_t = pair(row_shift)
    col_forms, col_forms_t = pair(col_shift)
    made = row_forms + col_forms_t + col_forms + row_forms_t
    for ref, value in zip(tables, made):
        ref[...] = value
    down = shift_matrix(pixels, pixels, row_shift, True)
    across = shift_matrix(pixels, pixels, col_shift, False)
    for comp in range(2):
        moved = jnp.dot(down, probe[comp].astype(bf16), preferred_element_type=f32).astype(bf16)
        psi0[comp] = jnp.dot(moved, across, preferred_element_type=f32).astype(bf16)


def wave_kernel(slots, depth_count, info, prop_re, prop_im, amplitude, psi0, *refs):
    tables = refs[:8]
    centers = refs[8 : 8 + depth_count]
    edges = refs[8 + depth_count : 8 + 2 * depth_count]
    out_centers = refs[8 + 2 * depth_count : 8 + 3 * depth_count]
    out_edges = refs[8 + 3 * depth_count : 8 + 4 * depth_count]
    patches, waves, adjoint, grads = refs[8 + 4 * depth_count :]
    depth_index = lax.axis_index("depth")
    pixels = psi0.shape[-1]
    half = pixels // 2
    live = depth_index < info[2 * slots]
    fwd_row_e, fwd_row_o, fwd_col_e, fwd_col_o, inv_col_e, inv_col_o, inv_row_e, inv_row_o = tables

    def dot(left, right):
        return jnp.dot(left, right, preferred_element_type=f32)

    def propagate(x_re, x_im, at_frequency):
        def rows_of(sign):
            mixed = [v[:half] + v[half:] if sign > 0 else v[:half] - v[half:] for v in (x_re, x_im)]
            return jnp.concatenate(mixed, axis=0).astype(bf16)

        u_even = dot(fwd_row_e[...], rows_of(1))
        u_odd = dot(fwd_row_o[...], rows_of(-1))

        def cols_of(sign):
            parts = []
            for u in (u_even, u_odd):
                mixed = u[:, :half] + u[:, half:] if sign > 0 else u[:, :half] - u[:, half:]
                parts.append(jnp.concatenate([mixed[:half], mixed[half:]], axis=1))
            return jnp.concatenate(parts, axis=0).astype(bf16)

        v_even = dot(cols_of(1), fwd_col_e[...])
        v_odd = dot(cols_of(-1), fwd_col_o[...])
        b_even = at_frequency(v_even[:, :half], v_even[:, half:], slice(0, half))
        b_odd = at_frequency(v_odd[:, :half], v_odd[:, half:], slice(half, pixels))
        w_even = dot(jnp.concatenate(b_even, axis=1).astype(bf16), inv_col_e[...])
        w_odd = dot(jnp.concatenate(b_odd, axis=1).astype(bf16), inv_col_o[...])
        w_low, w_high = w_even + w_odd, w_even - w_odd
        w_re = jnp.concatenate([w_low[:, :half], w_high[:, :half]], axis=1)
        w_im = jnp.concatenate([w_low[:, half:], w_high[:, half:]], axis=1)
        y_even = dot(
            inv_row_e[...], jnp.concatenate([w_re[:half], w_im[:half]], axis=0).astype(bf16)
        )
        y_odd = dot(
            inv_row_o[...], jnp.concatenate([w_re[half:], w_im[half:]], axis=0).astype(bf16)
        )
        low, high = y_even + y_odd, y_even - y_odd
        return (
            jnp.concatenate([low[:half], high[:half]], axis=0),
            jnp.concatenate([low[half:], high[half:]], axis=0),
        )

    def turn(re, im, cols):
        p_re, p_im = prop_re[:, cols], prop_im[:, cols]
        return [re * p_re - im * p_im, re * p_im + im * p_re]

    def turn_back(re, im, cols):
        p_re, p_im = prop_re[:, cols], prop_im[:, cols]
        return [re * p_re + im * p_im, im * p_re - re * p_im]

    def residual(re, im, cols):
        factor = 1.0 - amplitude[:, cols].astype(f32) * lax.rsqrt(re * re + im * im + epsilon)
        return [factor * re, factor * im]

    def pair_of(ref, index):
        return ref[index, 0].astype(f32), ref[index, 1].astype(f32)

    @pl.when(live)
    def _():
        for (flip, center), edge in zip(by_flip(centers), edges):
            patches[depth_index ^ flip, :, half:] = center[...]
            patches[depth_index ^ flip, :, :half] = edge[...]
        waves[0] = psi0[...]

        def forward(k, carry):
            t_re, t_im = pair_of(patches, k)
            p_re, p_im = pair_of(waves, k)
            n_re, n_im = propagate(t_re * p_re - t_im * p_im, t_re * p_im + t_im * p_re, turn)
            waves[k + 1, 0] = n_re.astype(bf16)
            waves[k + 1, 1] = n_im.astype(bf16)
            return carry

        lax.fori_loop(0, depth_count, forward, 0)
        l_re, l_im = propagate(*pair_of(waves, depth_count), residual)
        adjoint[0, 0] = l_re.astype(bf16)
        adjoint[0, 1] = l_im.astype(bf16)

        def backward(step, carry):
            k = depth_count - 1 - step
            m_re, m_im = propagate(*pair_of(adjoint, 0), turn_back)
            t_re, t_im = pair_of(patches, k)
            p_re, p_im = pair_of(waves, k)
            grads[k ^ depth_index, 0] = (p_re * m_re + p_im * m_im).astype(bf16)
            grads[k ^ depth_index, 1] = (p_re * m_im - p_im * m_re).astype(bf16)
            adjoint[0, 0] = (t_re * m_re + t_im * m_im).astype(bf16)
            adjoint[0, 1] = (t_re * m_im - t_im * m_re).astype(bf16)
            return carry

        lax.fori_loop(0, depth_count, backward, 0)
        for (flip, center), edge in zip(by_flip(out_centers), out_edges):
            center[...] = grads[flip, :, half:]
            edge[...] = grads[flip, :, :half]

    @pl.when(jnp.logical_not(live))
    def _():
        for ref in out_centers + out_edges:
            ref[...] = jnp.zeros(ref.shape, ref.dtype)


def place_edges_kernel(slots, info, *refs):
    pieces, (across, beside, across_sum, beside_sum) = refs[:-4], refs[-4:]
    depth_index = lax.axis_index("depth")
    even = lax.rem(lax.axis_index("scan"), 2) == 0
    columns = across.shape[-1]
    width = pieces[0].shape[-1]
    row, lane = iotas(pieces[0].shape[1], width)
    across_sum[...] = jnp.zeros(across_sum.shape, f32)
    beside_sum[...] = jnp.zeros(beside_sum.shape, f32)
    for flip, piece in by_flip(pieces):
        slot = depth_index ^ flip
        base, after, first = column_place(info, slots, slot, width, columns)
        to_across = jnp.logical_xor(row < info[slot], even)
        to_base = lane >= first
        for comp in range(2):
            value = piece[comp].astype(f32)
            for sheet, kept in (
                (across_sum, jnp.where(to_across, value, 0.0)),
                (beside_sum, jnp.where(to_across, 0.0, value)),
            ):
                sheet[comp, :, pl.ds(base, width)] += jnp.where(to_base, kept, 0.0)
                sheet[comp, :, pl.ds(after, width)] += jnp.where(to_base, 0.0, kept)
    across[...] = across_sum[...].astype(bf16)
    beside[...] = beside_sum[...].astype(bf16)


def place_center_kernel(slots, info, *refs):
    pieces, sheet = refs[:-1], refs[-1]
    depth_index = lax.axis_index("depth")
    columns = sheet.shape[-1]
    width = pieces[0].shape[-1]
    _, lane = iotas(pieces[0].shape[1], width)
    sheet[...] = jnp.zeros(sheet.shape, f32)
    for flip, piece in by_flip(pieces):
        base, after, first = column_place(info, slots, depth_index ^ flip, width, columns)
        to_base = lane >= first
        for comp in range(2):
            value = piece[comp].astype(f32)
            sheet[comp, :, pl.ds(base, width)] += jnp.where(to_base, value, 0.0)
            sheet[comp, :, pl.ds(after, width)] += jnp.where(to_base, 0.0, value)


def add_kernel(sheet, across, beside, out, total, sems):
    rows = sheet.shape[1] // 2
    copies = []
    for comp in range(2):
        for part in range(2):
            at = pl.ds(part * rows, rows)
            total[comp, at] = (
                sheet[comp, at] + across[comp, at].astype(f32) + beside[comp, at].astype(f32)
            )
            copies.append(
                pltpu.make_async_copy(
                    total.at[comp, at], out.at[comp, at], sems.at[2 * comp + part]
                )
            )
            copies[-1].start()
    for copy in copies:
        copy.wait()


def body(transmission, probe_wave, prop_phase, measured, scan_rows, scan_cols, live_counts):
    pixels = probe_wave.shape[-1]
    slots = measured.shape[0]
    rows = transmission.shape[2]
    columns = transmission.shape[3]
    count = lax.axis_size("depth")
    own = transmission[0]
    info = jnp.concatenate([scan_rows, scan_cols, live_counts])
    ints = info.shape[0]
    info = shifted(jnp.pad(info, (0, INFO_SIZE - ints)), "scan", 1)[:ints]
    strip = call(
        strip_kernel, sds(own.shape, bf16), [own], [pl.BlockSpec(memory_space=pltpu.HBM)],
        scratch=[pltpu.VMEM(own.shape, f32), pltpu.SemaphoreType.DMA((8,))], name="strip",
    )
    across = swapped(strip, "scan", 1)
    info, later_strip = lax.optimization_barrier((info, strip))
    beside = swapped(later_strip, "scan", 0)

    part = sds((2, rows, pixels), bf16)
    centers = call(
        functools.partial(center_kernel, slots, pixels),
        [part] * count, [info, strip], [SMEM, VMEM], name="cut_center",
    )

    def across_depth(pieces):
        return [pieces[0]] + [exchanged(piece, "depth", flip) for flip, piece in by_flip(pieces)[1:]]

    centers = across_depth(centers)

    phase, centers[0] = lax.optimization_barrier((prop_phase, centers[0]))
    order = parity_order(pixels)
    square = sds((pixels, pixels), f32)
    prop_re, prop_im, amplitude = call(
        frequency_kernel,
        [square, square, sds((pixels, pixels), bf16)],
        [phase, jnp.asarray(order), jnp.asarray(order.T), measured],
        [VMEM] * 4, flops=2400 * pixels**3, transcendentals=2 * pixels**2, name="frequency_order",
    )
    amplitude = shifted(amplitude, "scan", 1)

    stack = split_tables(pixels)
    made = call(
        functools.partial(table_kernel, slots),
        [sds((2, pixels, pixels), bf16)] + [sds((pixels, pixels), bf16)] * 8,
        [info, jnp.asarray(stack), jnp.asarray(stack.T), probe_wave],
        [SMEM, VMEM, VMEM, VMEM], flops=16 * pixels**3, name="tables",
    )
    edges = call(
        functools.partial(edge_kernel, slots, pixels),
        [part] * count, [info, across, beside], [SMEM, VMEM, VMEM], name="cut_edges",
    )
    edges = across_depth(edges)

    args = [info, prop_re, prop_im, amplitude, *made, *centers, *edges]
    grads = call(
        functools.partial(wave_kernel, slots, count),
        [part] * (2 * count), args, [SMEM] + [VMEM] * (len(args) - 1),
        scratch=[
            pltpu.VMEM((count, 2, pixels, pixels), bf16),
            pltpu.VMEM((count + 1, 2, pixels, pixels), bf16),
            pltpu.VMEM((1, 2, pixels, pixels), bf16),
            pltpu.VMEM((count, 2, pixels, pixels), bf16),
        ],
        flops=(2 * count + 1) * 16 * pixels**3, name="waves",
    )
    out_centers, out_edges = grads[:count], grads[count:]
    out_edges = across_depth(out_edges)
    out_centers = across_depth(out_centers)
    sheet_bf16 = sds((2, rows, columns), bf16)
    sheet_f32 = sds((2, rows, columns), f32)
    to_across, to_beside = call(
        functools.partial(place_edges_kernel, slots),
        [sheet_bf16, sheet_bf16], [info, *out_edges], [SMEM] + [VMEM] * count,
        scratch=[pltpu.VMEM(sheet_f32.shape, f32)] * 2, name="place_edges",
    )
    from_across = swapped(to_across, "scan", 1)
    from_beside = swapped(to_beside, "scan", 0)
    sheet = call(
        functools.partial(place_center_kernel, slots),
        sheet_f32, [info, *out_centers], [SMEM] + [VMEM] * count, name="place_center",
    )
    gradient = pl.pallas_call(
        add_kernel,
        out_shape=sheet_f32,
        in_specs=[VMEM] * 3,
        out_specs=pl.BlockSpec(memory_space=pl.ANY),
        scratch_shapes=[pltpu.VMEM(sheet_f32.shape, f32), pltpu.SemaphoreType.DMA((4,))],
        compiler_params=pltpu.CompilerParams(vmem_limit_bytes=LIMIT),
        name="add_edges",
    )(sheet, from_across, from_beside)
    return gradient[None]


def solution(mesh):
    in_specs = (
        P("depth", None, "scan", None),
        P(),
        P(),
        P("scan", None, None),
        P("scan"),
        P("scan"),
        P("scan"),
    )
    out_specs = P("depth", None, "scan", None)
    return jax.shard_map(body, mesh=mesh, in_specs=in_specs, out_specs=out_specs, check_vma=False)
```

```python
import functools
import math

import jax
import jax.numpy as jnp
import ml_dtypes
import numpy as np
from jax import lax
from jax.experimental import pallas as pl
from jax.experimental.pallas import tpu as pltpu
from jax.sharding import PartitionSpec as P

epsilon = 1.0
bf16 = jnp.bfloat16
f32 = jnp.float32
VMEM = pl.BlockSpec(memory_space=pltpu.VMEM)
SMEM = pl.BlockSpec(memory_space=pltpu.SMEM)
LIMIT = 48 * 1024 * 1024
INFO_SIZE = 8192


def shifted(value, axis, steps):
    count = lax.axis_size(axis)
    pairs = [(source, (source + steps) % count) for source in range(count)]
    return lax.ppermute(value, axis, pairs)


def swapped(value, axis, first):
    count = lax.axis_size(axis)
    pairs = [
        (source, (source + (1 if source % 2 == first else -1)) % count) for source in range(count)
    ]
    return lax.ppermute(value, axis, pairs)


def exchanged(value, axis, flip):
    count = lax.axis_size(axis)
    return lax.ppermute(value, axis, [(source, source ^ flip) for source in range(count)])


def split_tables(pixels):
    indices = np.arange(pixels)
    angles = (indices[:, None] * indices[None, :] % pixels) * (2.0 * math.pi / pixels)
    norm_scale = 1.0 / math.sqrt(pixels)
    table_re = (np.cos(angles) * norm_scale).astype(np.float32).astype(ml_dtypes.bfloat16)
    table_im = (-np.sin(angles) * norm_scale).astype(np.float32).astype(ml_dtypes.bfloat16)
    return np.concatenate([table_re[0::2], table_im[0::2], table_re[1::2], table_im[1::2]], axis=0)


def parity_order(pixels):
    order = np.concatenate([np.arange(0, pixels, 2), np.arange(1, pixels, 2)])
    return (order[:, None] == np.arange(pixels)[None, :]).astype(np.float32)


def call(kernel, out_shape, args, specs, scratch=(), flops=0, transcendentals=0, name=None):
    outs = out_shape if isinstance(out_shape, (list, tuple)) else [out_shape]
    moved = sum(math.prod(a.shape) * a.dtype.itemsize for a in list(args) + list(outs))
    return pl.pallas_call(
        kernel,
        out_shape=out_shape,
        in_specs=specs,
        out_specs=jax.tree.map(lambda _: VMEM, out_shape),
        scratch_shapes=list(scratch),
        compiler_params=pltpu.CompilerParams(vmem_limit_bytes=LIMIT),
        cost_estimate=pl.CostEstimate(
            flops=flops, bytes_accessed=moved, transcendentals=transcendentals
        ),
        name=name,
    )(*args)


def sds(shape, dtype):
    return jax.ShapeDtypeStruct(shape, dtype)


def by_flip(pieces):
    return list(zip([0, *range(len(pieces) - 1, 0, -1)], pieces))


def column_place(info, slots, slot, width, columns):
    col = info[slots + slot]
    base = (col // width) * width
    after = jnp.minimum(base + width, columns - width)
    return pl.multiple_of(base, width), pl.multiple_of(after, width), col - base


def iotas(rows, cols):
    return (
        lax.broadcasted_iota(jnp.int32, (rows, cols), 0),
        lax.broadcasted_iota(jnp.int32, (rows, cols), 1),
    )


def strip_kernel(own, strip):
    strip[...] = own[...].astype(bf16)


def center_kernel(slots, width, info, strip, *outs):
    depth_index = lax.axis_index("depth")
    columns = strip.shape[-1]
    _, lane = iotas(strip.shape[1], width)
    for flip, out in by_flip(outs):
        base, after, first = column_place(info, slots, depth_index ^ flip, width, columns)
        for comp in range(2):
            out[comp] = jnp.where(
                lane >= first,
                strip[comp, :, pl.ds(base, width)].astype(f32),
                strip[comp, :, pl.ds(after, width)].astype(f32),
            ).astype(bf16)


def edge_kernel(slots, width, info, across, beside, *outs):
    depth_index = lax.axis_index("depth")
    even = lax.rem(lax.axis_index("scan"), 2) == 0
    columns = across.shape[-1]
    row, lane = iotas(across.shape[1], width)
    for flip, out in by_flip(outs):
        slot = depth_index ^ flip
        base, after, first = column_place(info, slots, slot, width, columns)
        from_across = jnp.logical_xor(row < info[slot], even)

        def rows_at(comp, place):
            return jnp.where(
                from_across,
                across[comp, :, pl.ds(place, width)].astype(f32),
                beside[comp, :, pl.ds(place, width)].astype(f32),
            )

        for comp in range(2):
            out[comp] = jnp.where(
                lane >= first, rows_at(comp, base), rows_at(comp, after)
            ).astype(bf16)


def frequency_kernel(phase, order, order_t, measured, prop_re, prop_im, amplitude):
    def reorder(value):
        rows = jnp.dot(
            order[...], value, preferred_element_type=f32, precision=lax.Precision.HIGHEST
        )
        return jnp.dot(
            rows, order_t[...], preferred_element_type=f32, precision=lax.Precision.HIGHEST
        )

    turned = reorder(phase[...])
    prop_re[...] = jnp.cos(turned)
    prop_im[...] = jnp.sin(turned)
    amplitude[...] = reorder(measured[lax.axis_index("depth")]).astype(bf16)


def table_kernel(slots, info, stack, stack_t, probe, psi0, *tables):
    depth_index = lax.axis_index("depth")
    pixels = probe.shape[-1]
    half = pixels // 2
    row_shift = info[depth_index]
    col_shift = lax.rem(info[slots + depth_index], pixels)

    def shift_matrix(rows, cols, shift, transposed):
        row, lane = iotas(rows, cols)
        offset = (lane - row if transposed else row - lane) + shift
        return jnp.where((offset == 0) | (offset == pixels), 1.0, 0.0).astype(bf16)

    def pair(shift):
        cols = jnp.dot(
            stack[...], shift_matrix(pixels, half, shift, False), preferred_element_type=f32
        )
        rows = jnp.dot(
            shift_matrix(half, pixels, shift, True), stack_t[...], preferred_element_type=f32
        )
        forms, forms_t = [], []
        for parity in range(2):
            at = 2 * parity * half
            re, im = cols[at : at + half], cols[at + half : at + pixels]
            top = jnp.concatenate([re, -im], axis=1)
            bottom = jnp.concatenate([im, re], axis=1)
            forms.append(jnp.concatenate([top, bottom], axis=0).astype(bf16))
            re, im = rows[:, at : at + half], rows[:, at + half : at + pixels]
            top = jnp.concatenate([re, im], axis=1)
            bottom = jnp.concatenate([-im, re], axis=1)
            forms_t.append(jnp.concatenate([top, bottom], axis=0).astype(bf16))
        return forms, forms_t

    row_forms, row_forms_t = pair(row_shift)
    col_forms, col_forms_t = pair(col_shift)
    made = row_forms + col_forms_t + col_forms + row_forms_t
    for ref, value in zip(tables, made):
        ref[...] = value
    down = shift_matrix(pixels, pixels, row_shift, True)
    across = shift_matrix(pixels, pixels, col_shift, False)
    for comp in range(2):
        moved = jnp.dot(down, probe[comp].astype(bf16), preferred_element_type=f32).astype(bf16)
        psi0[comp] = jnp.dot(moved, across, preferred_element_type=f32).astype(bf16)


def wave_kernel(slots, depth_count, info, prop_re, prop_im, amplitude, psi0, *refs):
    tables = refs[:8]
    centers = refs[8 : 8 + depth_count]
    edges = refs[8 + depth_count : 8 + 2 * depth_count]
    out_centers = refs[8 + 2 * depth_count : 8 + 3 * depth_count]
    out_edges = refs[8 + 3 * depth_count : 8 + 4 * depth_count]
    patches, waves, adjoint, grads = refs[8 + 4 * depth_count :]
    depth_index = lax.axis_index("depth")
    pixels = psi0.shape[-1]
    half = pixels // 2
    live = depth_index < info[2 * slots]
    fwd_row_e, fwd_row_o, fwd_col_e, fwd_col_o, inv_col_e, inv_col_o, inv_row_e, inv_row_o = tables

    def dot(left, right):
        return jnp.dot(left, right, preferred_element_type=f32)

    def propagate(x_re, x_im, at_frequency):
        def rows_of(sign):
            mixed = [v[:half] + v[half:] if sign > 0 else v[:half] - v[half:] for v in (x_re, x_im)]
            return jnp.concatenate(mixed, axis=0).astype(bf16)

        u_even = dot(fwd_row_e[...], rows_of(1))
        u_odd = dot(fwd_row_o[...], rows_of(-1))

        def cols_of(sign):
            parts = []
            for u in (u_even, u_odd):
                mixed = u[:, :half] + u[:, half:] if sign > 0 else u[:, :half] - u[:, half:]
                parts.append(jnp.concatenate([mixed[:half], mixed[half:]], axis=1))
            return jnp.concatenate(parts, axis=0).astype(bf16)

        v_even = dot(cols_of(1), fwd_col_e[...])
        v_odd = dot(cols_of(-1), fwd_col_o[...])
        b_even = at_frequency(v_even[:, :half], v_even[:, half:], slice(0, half))
        b_odd = at_frequency(v_odd[:, :half], v_odd[:, half:], slice(half, pixels))
        w_even = dot(jnp.concatenate(b_even, axis=1).astype(bf16), inv_col_e[...])
        w_odd = dot(jnp.concatenate(b_odd, axis=1).astype(bf16), inv_col_o[...])
        w_low, w_high = w_even + w_odd, w_even - w_odd
        w_re = jnp.concatenate([w_low[:, :half], w_high[:, :half]], axis=1)
        w_im = jnp.concatenate([w_low[:, half:], w_high[:, half:]], axis=1)
        y_even = dot(
            inv_row_e[...], jnp.concatenate([w_re[:half], w_im[:half]], axis=0).astype(bf16)
        )
        y_odd = dot(
            inv_row_o[...], jnp.concatenate([w_re[half:], w_im[half:]], axis=0).astype(bf16)
        )
        low, high = y_even + y_odd, y_even - y_odd
        return (
            jnp.concatenate([low[:half], high[:half]], axis=0),
            jnp.concatenate([low[half:], high[half:]], axis=0),
        )

    def turn(re, im, cols):
        p_re, p_im = prop_re[:, cols], prop_im[:, cols]
        return [re * p_re - im * p_im, re * p_im + im * p_re]

    def turn_back(re, im, cols):
        p_re, p_im = prop_re[:, cols], prop_im[:, cols]
        return [re * p_re + im * p_im, im * p_re - re * p_im]

    def residual(re, im, cols):
        factor = 1.0 - amplitude[:, cols].astype(f32) * lax.rsqrt(re * re + im * im + epsilon)
        return [factor * re, factor * im]

    def pair_of(ref, index):
        return ref[index, 0].astype(f32), ref[index, 1].astype(f32)

    @pl.when(live)
    def _():
        for (flip, center), edge in zip(by_flip(centers), edges):
            patches[depth_index ^ flip, :, half:] = center[...]
            patches[depth_index ^ flip, :, :half] = edge[...]
        waves[0] = psi0[...]

        def forward(k, carry):
            t_re, t_im = pair_of(patches, k)
            p_re, p_im = pair_of(waves, k)
            n_re, n_im = propagate(t_re * p_re - t_im * p_im, t_re * p_im + t_im * p_re, turn)
            waves[k + 1, 0] = n_re.astype(bf16)
            waves[k + 1, 1] = n_im.astype(bf16)
            return carry

        lax.fori_loop(0, depth_count, forward, 0)
        l_re, l_im = propagate(*pair_of(waves, depth_count), residual)
        adjoint[0, 0] = l_re.astype(bf16)
        adjoint[0, 1] = l_im.astype(bf16)

        def backward(step, carry):
            k = depth_count - 1 - step
            m_re, m_im = propagate(*pair_of(adjoint, 0), turn_back)
            t_re, t_im = pair_of(patches, k)
            p_re, p_im = pair_of(waves, k)
            grads[k ^ depth_index, 0] = (p_re * m_re + p_im * m_im).astype(bf16)
            grads[k ^ depth_index, 1] = (p_re * m_im - p_im * m_re).astype(bf16)
            adjoint[0, 0] = (t_re * m_re + t_im * m_im).astype(bf16)
            adjoint[0, 1] = (t_re * m_im - t_im * m_re).astype(bf16)
            return carry

        lax.fori_loop(0, depth_count, backward, 0)
        for (flip, center), edge in zip(by_flip(out_centers), out_edges):
            center[...] = grads[flip, :, half:]
            edge[...] = grads[flip, :, :half]

    @pl.when(jnp.logical_not(live))
    def _():
        for ref in out_centers + out_edges:
            ref[...] = jnp.zeros(ref.shape, ref.dtype)


def place_edges_kernel(slots, info, *refs):
    pieces, (across, beside, across_sum, beside_sum) = refs[:-4], refs[-4:]
    depth_index = lax.axis_index("depth")
    even = lax.rem(lax.axis_index("scan"), 2) == 0
    columns = across.shape[-1]
    width = pieces[0].shape[-1]
    row, lane = iotas(pieces[0].shape[1], width)
    across_sum[...] = jnp.zeros(across_sum.shape, f32)
    beside_sum[...] = jnp.zeros(beside_sum.shape, f32)
    for flip, piece in by_flip(pieces):
        slot = depth_index ^ flip
        base, after, first = column_place(info, slots, slot, width, columns)
        to_across = jnp.logical_xor(row < info[slot], even)
        to_base = lane >= first
        for comp in range(2):
            value = piece[comp].astype(f32)
            for sheet, kept in (
                (across_sum, jnp.where(to_across, value, 0.0)),
                (beside_sum, jnp.where(to_across, 0.0, value)),
            ):
                sheet[comp, :, pl.ds(base, width)] += jnp.where(to_base, kept, 0.0)
                sheet[comp, :, pl.ds(after, width)] += jnp.where(to_base, 0.0, kept)
    across[...] = across_sum[...].astype(bf16)
    beside[...] = beside_sum[...].astype(bf16)


def place_center_kernel(slots, info, *refs):
    pieces, sheet = refs[:-1], refs[-1]
    depth_index = lax.axis_index("depth")
    columns = sheet.shape[-1]
    width = pieces[0].shape[-1]
    _, lane = iotas(pieces[0].shape[1], width)
    sheet[...] = jnp.zeros(sheet.shape, f32)
    for flip, piece in by_flip(pieces):
        base, after, first = column_place(info, slots, depth_index ^ flip, width, columns)
        to_base = lane >= first
        for comp in range(2):
            value = piece[comp].astype(f32)
            sheet[comp, :, pl.ds(base, width)] += jnp.where(to_base, value, 0.0)
            sheet[comp, :, pl.ds(after, width)] += jnp.where(to_base, 0.0, value)


def add_kernel(sheet, across, beside, out, total, sems):
    rows = sheet.shape[1] // 2
    copies = []
    for comp in range(2):
        for part in range(2):
            at = pl.ds(part * rows, rows)
            total[comp, at] = (
                sheet[comp, at] + across[comp, at].astype(f32) + beside[comp, at].astype(f32)
            )
            copies.append(
                pltpu.make_async_copy(
                    total.at[comp, at], out.at[comp, at], sems.at[2 * comp + part]
                )
            )
            copies[-1].start()
    for copy in copies:
        copy.wait()


def body(transmission, probe_wave, prop_phase, measured, scan_rows, scan_cols, live_counts):
    pixels = probe_wave.shape[-1]
    slots = measured.shape[0]
    rows = transmission.shape[2]
    columns = transmission.shape[3]
    count = lax.axis_size("depth")
    own = transmission[0]
    info = jnp.concatenate([scan_rows, scan_cols, live_counts])
    ints = info.shape[0]
    info = shifted(jnp.pad(info, (0, INFO_SIZE - ints)), "scan", 1)[:ints]
    strip = call(strip_kernel, sds(own.shape, bf16), [own], [VMEM], name="strip")
    across = swapped(strip, "scan", 1)
    info, later_strip = lax.optimization_barrier((info, strip))
    beside = swapped(later_strip, "scan", 0)

    part = sds((2, rows, pixels), bf16)
    centers = call(
        functools.partial(center_kernel, slots, pixels),
        [part] * count, [info, strip], [SMEM, VMEM], name="cut_center",
    )

    def across_depth(pieces):
        return [pieces[0]] + [exchanged(piece, "depth", flip) for flip, piece in by_flip(pieces)[1:]]

    centers = across_depth(centers)

    phase, centers[0] = lax.optimization_barrier((prop_phase, centers[0]))
    order = parity_order(pixels)
    square = sds((pixels, pixels), f32)
    prop_re, prop_im, amplitude = call(
        frequency_kernel,
        [square, square, sds((pixels, pixels), bf16)],
        [phase, jnp.asarray(order), jnp.asarray(order.T), measured],
        [VMEM] * 4, flops=2400 * pixels**3, transcendentals=2 * pixels**2, name="frequency_order",
    )
    amplitude, centers[1] = lax.optimization_barrier((amplitude, centers[1]))
    amplitude = shifted(amplitude, "scan", 1)

    stack = split_tables(pixels)
    made = call(
        functools.partial(table_kernel, slots),
        [sds((2, pixels, pixels), bf16)] + [sds((pixels, pixels), bf16)] * 8,
        [info, jnp.asarray(stack), jnp.asarray(stack.T), probe_wave],
        [SMEM, VMEM, VMEM, VMEM], flops=16 * pixels**3, name="tables",
    )
    edges = call(
        functools.partial(edge_kernel, slots, pixels),
        [part] * count, [info, across, beside], [SMEM, VMEM, VMEM], name="cut_edges",
    )
    edges = across_depth(edges)

    args = [info, prop_re, prop_im, amplitude, *made, *centers, *edges]
    grads = call(
        functools.partial(wave_kernel, slots, count),
        [part] * (2 * count), args, [SMEM] + [VMEM] * (len(args) - 1),
        scratch=[
            pltpu.VMEM((count, 2, pixels, pixels), bf16),
            pltpu.VMEM((count + 1, 2, pixels, pixels), bf16),
            pltpu.VMEM((1, 2, pixels, pixels), bf16),
            pltpu.VMEM((count, 2, pixels, pixels), bf16),
        ],
        flops=(2 * count + 1) * 16 * pixels**3, name="waves",
    )
    out_centers, out_edges = grads[:count], grads[count:]
    out_edges = across_depth(out_edges)
    sheet_bf16 = sds((2, rows, columns), bf16)
    sheet_f32 = sds((2, rows, columns), f32)
    to_across, to_beside = call(
        functools.partial(place_edges_kernel, slots),
        [sheet_bf16, sheet_bf16], [info, *out_edges], [SMEM] + [VMEM] * count,
        scratch=[pltpu.VMEM(sheet_f32.shape, f32)] * 2, name="place_edges",
    )
    from_across = swapped(to_across, "scan", 1)
    from_beside = swapped(to_beside, "scan", 0)
    out_centers = across_depth(out_centers)
    sheet = call(
        functools.partial(place_center_kernel, slots),
        sheet_f32, [info, *out_centers], [SMEM] + [VMEM] * count, name="place_center",
    )
    gradient = pl.pallas_call(
        add_kernel,
        out_shape=sheet_f32,
        in_specs=[VMEM] * 3,
        out_specs=pl.BlockSpec(memory_space=pl.ANY),
        scratch_shapes=[pltpu.VMEM(sheet_f32.shape, f32), pltpu.SemaphoreType.DMA((4,))],
        compiler_params=pltpu.CompilerParams(vmem_limit_bytes=LIMIT),
        name="add_edges",
    )(sheet, from_across, from_beside)
    return gradient[None]


def solution(mesh):
    in_specs = (
        P("depth", None, "scan", None),
        P(),
        P(),
        P("scan", None, None),
        P("scan"),
        P("scan"),
        P("scan"),
    )
    out_specs = P("depth", None, "scan", None)
    return jax.shard_map(body, mesh=mesh, in_specs=in_specs, out_specs=out_specs, check_vma=False)
```

```python
import functools
import math

import jax
import jax.numpy as jnp
import ml_dtypes
import numpy as np
from jax import lax
from jax.experimental import pallas as pl
from jax.experimental.pallas import tpu as pltpu
from jax.sharding import PartitionSpec as P

epsilon = 1.0
bf16 = jnp.bfloat16
f32 = jnp.float32
VMEM = pl.BlockSpec(memory_space=pltpu.VMEM)
SMEM = pl.BlockSpec(memory_space=pltpu.SMEM)
LIMIT = 48 * 1024 * 1024
INFO_SIZE = 8192


def shifted(value, axis, steps):
    count = lax.axis_size(axis)
    pairs = [(source, (source + steps) % count) for source in range(count)]
    return lax.ppermute(value, axis, pairs)


def swapped(value, axis, first):
    count = lax.axis_size(axis)
    pairs = [
        (source, (source + (1 if source % 2 == first else -1)) % count) for source in range(count)
    ]
    return lax.ppermute(value, axis, pairs)


def exchanged(value, axis, flip):
    count = lax.axis_size(axis)
    return lax.ppermute(value, axis, [(source, source ^ flip) for source in range(count)])


def split_tables(pixels):
    indices = np.arange(pixels)
    angles = (indices[:, None] * indices[None, :] % pixels) * (2.0 * math.pi / pixels)
    norm_scale = 1.0 / math.sqrt(pixels)
    table_re = (np.cos(angles) * norm_scale).astype(np.float32).astype(ml_dtypes.bfloat16)
    table_im = (-np.sin(angles) * norm_scale).astype(np.float32).astype(ml_dtypes.bfloat16)
    return np.concatenate([table_re[0::2], table_im[0::2], table_re[1::2], table_im[1::2]], axis=0)


def parity_order(pixels):
    order = np.concatenate([np.arange(0, pixels, 2), np.arange(1, pixels, 2)])
    return (order[:, None] == np.arange(pixels)[None, :]).astype(np.float32)


def call(kernel, out_shape, args, specs, scratch=(), flops=0, transcendentals=0, name=None):
    outs = out_shape if isinstance(out_shape, (list, tuple)) else [out_shape]
    moved = sum(math.prod(a.shape) * a.dtype.itemsize for a in list(args) + list(outs))
    return pl.pallas_call(
        kernel,
        out_shape=out_shape,
        in_specs=specs,
        out_specs=jax.tree.map(lambda _: VMEM, out_shape),
        scratch_shapes=list(scratch),
        compiler_params=pltpu.CompilerParams(vmem_limit_bytes=LIMIT),
        cost_estimate=pl.CostEstimate(
            flops=flops, bytes_accessed=moved, transcendentals=transcendentals
        ),
        name=name,
    )(*args)


def sds(shape, dtype):
    return jax.ShapeDtypeStruct(shape, dtype)


def by_flip(pieces):
    return list(zip([0, *range(len(pieces) - 1, 0, -1)], pieces))


def column_place(info, slots, slot, width, columns):
    col = info[slots + slot]
    base = (col // width) * width
    after = jnp.minimum(base + width, columns - width)
    return pl.multiple_of(base, width), pl.multiple_of(after, width), col - base


def iotas(rows, cols):
    return (
        lax.broadcasted_iota(jnp.int32, (rows, cols), 0),
        lax.broadcasted_iota(jnp.int32, (rows, cols), 1),
    )


def strip_kernel(own, strip):
    strip[...] = own[...].astype(bf16)


def center_kernel(slots, width, info, strip, *outs):
    depth_index = lax.axis_index("depth")
    columns = strip.shape[-1]
    _, lane = iotas(strip.shape[1], width)
    for flip, out in by_flip(outs):
        base, after, first = column_place(info, slots, depth_index ^ flip, width, columns)
        for comp in range(2):
            out[comp] = jnp.where(
                lane >= first,
                strip[comp, :, pl.ds(base, width)].astype(f32),
                strip[comp, :, pl.ds(after, width)].astype(f32),
            ).astype(bf16)


def edge_kernel(slots, width, info, across, beside, *outs):
    depth_index = lax.axis_index("depth")
    even = lax.rem(lax.axis_index("scan"), 2) == 0
    columns = across.shape[-1]
    row, lane = iotas(across.shape[1], width)
    for flip, out in by_flip(outs):
        slot = depth_index ^ flip
        base, after, first = column_place(info, slots, slot, width, columns)
        from_across = jnp.logical_xor(row < info[slot], even)

        def rows_at(comp, place):
            return jnp.where(
                from_across,
                across[comp, :, pl.ds(place, width)].astype(f32),
                beside[comp, :, pl.ds(place, width)].astype(f32),
            )

        for comp in range(2):
            out[comp] = jnp.where(
                lane >= first, rows_at(comp, base), rows_at(comp, after)
            ).astype(bf16)


def frequency_kernel(phase, order, order_t, measured, prop_re, prop_im, amplitude):
    def reorder(value):
        rows = jnp.dot(
            order[...], value, preferred_element_type=f32, precision=lax.Precision.HIGHEST
        )
        return jnp.dot(
            rows, order_t[...], preferred_element_type=f32, precision=lax.Precision.HIGHEST
        )

    turned = reorder(phase[...])
    prop_re[...] = jnp.cos(turned)
    prop_im[...] = jnp.sin(turned)
    amplitude[...] = reorder(measured[lax.axis_index("depth")]).astype(bf16)


def table_kernel(slots, info, stack, stack_t, probe, psi0, *tables):
    depth_index = lax.axis_index("depth")
    pixels = probe.shape[-1]
    half = pixels // 2
    row_shift = info[depth_index]
    col_shift = lax.rem(info[slots + depth_index], pixels)

    def shift_matrix(rows, cols, shift, transposed):
        row, lane = iotas(rows, cols)
        offset = (lane - row if transposed else row - lane) + shift
        return jnp.where((offset == 0) | (offset == pixels), 1.0, 0.0).astype(bf16)

    def pair(shift):
        cols = jnp.dot(
            stack[...], shift_matrix(pixels, half, shift, False), preferred_element_type=f32
        )
        rows = jnp.dot(
            shift_matrix(half, pixels, shift, True), stack_t[...], preferred_element_type=f32
        )
        forms, forms_t = [], []
        for parity in range(2):
            at = 2 * parity * half
            re, im = cols[at : at + half], cols[at + half : at + pixels]
            top = jnp.concatenate([re, -im], axis=1)
            bottom = jnp.concatenate([im, re], axis=1)
            forms.append(jnp.concatenate([top, bottom], axis=0).astype(bf16))
            re, im = rows[:, at : at + half], rows[:, at + half : at + pixels]
            top = jnp.concatenate([re, im], axis=1)
            bottom = jnp.concatenate([-im, re], axis=1)
            forms_t.append(jnp.concatenate([top, bottom], axis=0).astype(bf16))
        return forms, forms_t

    row_forms, row_forms_t = pair(row_shift)
    col_forms, col_forms_t = pair(col_shift)
    made = row_forms + col_forms_t + col_forms + row_forms_t
    for ref, value in zip(tables, made):
        ref[...] = value
    down = shift_matrix(pixels, pixels, row_shift, True)
    across = shift_matrix(pixels, pixels, col_shift, False)
    for comp in range(2):
        moved = jnp.dot(down, probe[comp].astype(bf16), preferred_element_type=f32).astype(bf16)
        psi0[comp] = jnp.dot(moved, across, preferred_element_type=f32).astype(bf16)


def wave_kernel(slots, depth_count, info, prop_re, prop_im, amplitude, psi0, *refs):
    tables = refs[:8]
    centers = refs[8 : 8 + depth_count]
    edges = refs[8 + depth_count : 8 + 2 * depth_count]
    out_centers = refs[8 + 2 * depth_count : 8 + 3 * depth_count]
    out_edges = refs[8 + 3 * depth_count : 8 + 4 * depth_count]
    patches, waves, adjoint, grads = refs[8 + 4 * depth_count :]
    depth_index = lax.axis_index("depth")
    pixels = psi0.shape[-1]
    half = pixels // 2
    live = depth_index < info[2 * slots]
    fwd_row_e, fwd_row_o, fwd_col_e, fwd_col_o, inv_col_e, inv_col_o, inv_row_e, inv_row_o = tables

    def dot(left, right):
        return jnp.dot(left, right, preferred_element_type=f32)

    def propagate(x_re, x_im, at_frequency):
        def rows_of(sign):
            mixed = [v[:half] + v[half:] if sign > 0 else v[:half] - v[half:] for v in (x_re, x_im)]
            return jnp.concatenate(mixed, axis=0).astype(bf16)

        u_even = dot(fwd_row_e[...], rows_of(1))
        u_odd = dot(fwd_row_o[...], rows_of(-1))

        def cols_of(sign):
            parts = []
            for u in (u_even, u_odd):
                mixed = u[:, :half] + u[:, half:] if sign > 0 else u[:, :half] - u[:, half:]
                parts.append(jnp.concatenate([mixed[:half], mixed[half:]], axis=1))
            return jnp.concatenate(parts, axis=0).astype(bf16)

        v_even = dot(cols_of(1), fwd_col_e[...])
        v_odd = dot(cols_of(-1), fwd_col_o[...])
        b_even = at_frequency(v_even[:, :half], v_even[:, half:], slice(0, half))
        b_odd = at_frequency(v_odd[:, :half], v_odd[:, half:], slice(half, pixels))
        w_even = dot(jnp.concatenate(b_even, axis=1).astype(bf16), inv_col_e[...])
        w_odd = dot(jnp.concatenate(b_odd, axis=1).astype(bf16), inv_col_o[...])
        w_low, w_high = w_even + w_odd, w_even - w_odd
        w_re = jnp.concatenate([w_low[:, :half], w_high[:, :half]], axis=1)
        w_im = jnp.concatenate([w_low[:, half:], w_high[:, half:]], axis=1)
        y_even = dot(
            inv_row_e[...], jnp.concatenate([w_re[:half], w_im[:half]], axis=0).astype(bf16)
        )
        y_odd = dot(
            inv_row_o[...], jnp.concatenate([w_re[half:], w_im[half:]], axis=0).astype(bf16)
        )
        low, high = y_even + y_odd, y_even - y_odd
        return (
            jnp.concatenate([low[:half], high[:half]], axis=0),
            jnp.concatenate([low[half:], high[half:]], axis=0),
        )

    def turn(re, im, cols):
        p_re, p_im = prop_re[:, cols], prop_im[:, cols]
        return [re * p_re - im * p_im, re * p_im + im * p_re]

    def turn_back(re, im, cols):
        p_re, p_im = prop_re[:, cols], prop_im[:, cols]
        return [re * p_re + im * p_im, im * p_re - re * p_im]

    def residual(re, im, cols):
        factor = 1.0 - amplitude[:, cols].astype(f32) * lax.rsqrt(re * re + im * im + epsilon)
        return [factor * re, factor * im]

    def pair_of(ref, index):
        return ref[index, 0].astype(f32), ref[index, 1].astype(f32)

    @pl.when(live)
    def _():
        for (flip, center), edge in zip(by_flip(centers), edges):
            patches[depth_index ^ flip, :, half:] = center[...]
            patches[depth_index ^ flip, :, :half] = edge[...]
        waves[0] = psi0[...]

        def forward(k, carry):
            t_re, t_im = pair_of(patches, k)
            p_re, p_im = pair_of(waves, k)
            n_re, n_im = propagate(t_re * p_re - t_im * p_im, t_re * p_im + t_im * p_re, turn)
            waves[k + 1, 0] = n_re.astype(bf16)
            waves[k + 1, 1] = n_im.astype(bf16)
            return carry

        lax.fori_loop(0, depth_count, forward, 0)
        l_re, l_im = propagate(*pair_of(waves, depth_count), residual)
        adjoint[0, 0] = l_re.astype(bf16)
        adjoint[0, 1] = l_im.astype(bf16)

        def backward(step, carry):
            k = depth_count - 1 - step
            m_re, m_im = propagate(*pair_of(adjoint, 0), turn_back)
            t_re, t_im = pair_of(patches, k)
            p_re, p_im = pair_of(waves, k)
            grads[k ^ depth_index, 0] = (p_re * m_re + p_im * m_im).astype(bf16)
            grads[k ^ depth_index, 1] = (p_re * m_im - p_im * m_re).astype(bf16)
            adjoint[0, 0] = (t_re * m_re + t_im * m_im).astype(bf16)
            adjoint[0, 1] = (t_re * m_im - t_im * m_re).astype(bf16)
            return carry

        lax.fori_loop(0, depth_count, backward, 0)
        for (flip, center), edge in zip(by_flip(out_centers), out_edges):
            center[...] = grads[flip, :, half:]
            edge[...] = grads[flip, :, :half]

    @pl.when(jnp.logical_not(live))
    def _():
        for ref in out_centers + out_edges:
            ref[...] = jnp.zeros(ref.shape, ref.dtype)


def stack_kernel(*refs):
    pieces, (others, stacked) = refs[:-2], refs[-2:]
    for at, piece in enumerate(pieces):
        stacked[at] = piece[...]
        if at:
            others[at - 1] = piece[...]


def place(sheet, comp, value, base, after, to_base):
    width = value.shape[-1]
    sheet[comp, :, pl.ds(base, width)] += jnp.where(to_base, value, 0.0)
    sheet[comp, :, pl.ds(after, width)] += jnp.where(to_base, 0.0, value)


def place_edge(sheet, comp, piece, info, slots, slot, upper):
    rows, width = piece.shape
    row, lane = iotas(rows, width)
    base, after, first = column_place(info, slots, slot, width, sheet.shape[-1])
    here = jnp.logical_xor(row < info[slot], upper)
    place(sheet, comp, jnp.where(here, piece.astype(f32), 0.0), base, after, lane >= first)


class Chosen:
    def __init__(self, first, info, others):
        self.first, self.info, self.others = first, info, others

    def __getitem__(self, at):
        return jnp.where(self.first, self.info[at], self.others[at])


def place_near_kernel(slots, own_info, info, second, beside, *refs):
    pieces, sheet = refs[:-1], refs[-1]
    depth_index = lax.axis_index("depth")
    even = lax.rem(lax.axis_index("scan"), 2) == 0
    near_info = Chosen(even, own_info, second)
    columns = sheet.shape[-1]
    width = pieces[0].shape[-1]
    _, lane = iotas(pieces[0].shape[1], width)
    sheet[...] = jnp.zeros(sheet.shape, f32)
    for at, (flip, piece) in enumerate(by_flip(pieces)):
        slot = depth_index ^ flip
        base, after, first = column_place(info, slots, slot, width, columns)
        for comp in range(2):
            place(sheet, comp, piece[comp].astype(f32), base, after, lane >= first)
            place_edge(sheet, comp, beside[at, comp], near_info, slots, slot, even)


def place_far_kernel(slots, own_info, second, sheet, own, others, out, total, sems):
    depth_index = lax.axis_index("depth")
    odd = lax.rem(lax.axis_index("scan"), 2) == 1
    far_info = Chosen(odd, own_info, second)
    copies = []
    for comp in range(2):
        total[comp] = sheet[comp]
        for at, (flip, _) in enumerate(by_flip(range(others.shape[0] + 1))):
            piece = others[at - 1, comp] if at else own[comp]
            place_edge(total, comp, piece, far_info, slots, depth_index ^ flip, odd)
        copies.append(pltpu.make_async_copy(total.at[comp], out.at[comp], sems.at[comp]))
        copies[-1].start()
    for copy in copies:
        copy.wait()


def body(transmission, probe_wave, prop_phase, measured, scan_rows, scan_cols, live_counts):
    pixels = probe_wave.shape[-1]
    slots = measured.shape[0]
    rows = transmission.shape[2]
    columns = transmission.shape[3]
    count = lax.axis_size("depth")
    own = transmission[0]
    own_info = jnp.concatenate([scan_rows, scan_cols, live_counts])
    ints = own_info.shape[0]
    info = shifted(jnp.pad(own_info, (0, INFO_SIZE - ints)), "scan", 1)[:ints]
    strip = call(strip_kernel, sds(own.shape, bf16), [own], [VMEM], name="strip")
    across = swapped(strip, "scan", 1)
    info, later_strip = lax.optimization_barrier((info, strip))
    beside = swapped(later_strip, "scan", 0)

    part = sds((2, rows, pixels), bf16)
    centers = call(
        functools.partial(center_kernel, slots, pixels),
        [part] * count, [info, strip], [SMEM, VMEM], name="cut_center",
    )

    def across_depth(pieces):
        return [pieces[0]] + [exchanged(piece, "depth", flip) for flip, piece in by_flip(pieces)[1:]]

    centers = across_depth(centers)

    phase, centers[0] = lax.optimization_barrier((prop_phase, centers[0]))
    order = parity_order(pixels)
    square = sds((pixels, pixels), f32)
    prop_re, prop_im, amplitude = call(
        frequency_kernel,
        [square, square, sds((pixels, pixels), bf16)],
        [phase, jnp.asarray(order), jnp.asarray(order.T), measured],
        [VMEM] * 4, flops=2400 * pixels**3, transcendentals=2 * pixels**2, name="frequency_order",
    )
    amplitude, centers[1] = lax.optimization_barrier((amplitude, centers[1]))
    amplitude = shifted(amplitude, "scan", 1)

    stack = split_tables(pixels)
    made = call(
        functools.partial(table_kernel, slots),
        [sds((2, pixels, pixels), bf16)] + [sds((pixels, pixels), bf16)] * 8,
        [info, jnp.asarray(stack), jnp.asarray(stack.T), probe_wave],
        [SMEM, VMEM, VMEM, VMEM], flops=16 * pixels**3, name="tables",
    )
    edges = call(
        functools.partial(edge_kernel, slots, pixels),
        [part] * count, [info, across, beside], [SMEM, VMEM, VMEM], name="cut_edges",
    )
    edges = across_depth(edges)

    args = [info, prop_re, prop_im, amplitude, *made, *centers, *edges]
    grads = call(
        functools.partial(wave_kernel, slots, count),
        [part] * (2 * count), args, [SMEM] + [VMEM] * (len(args) - 1),
        scratch=[
            pltpu.VMEM((count, 2, pixels, pixels), bf16),
            pltpu.VMEM((count + 1, 2, pixels, pixels), bf16),
            pltpu.VMEM((1, 2, pixels, pixels), bf16),
            pltpu.VMEM((count, 2, pixels, pixels), bf16),
        ],
        flops=(2 * count + 1) * 16 * pixels**3, name="waves",
    )
    out_centers, out_edges = grads[:count], grads[count:]
    far_own = swapped(out_edges[0], "scan", 1)
    second, out_edges = lax.optimization_barrier((own_info, out_edges))
    second = shifted(second, "scan", 2)
    out_edges = across_depth(out_edges)
    far_own, second, out_edges = lax.optimization_barrier((far_own, second, out_edges))
    others, stacked = call(
        stack_kernel, [sds((at, 2, rows, pixels), bf16) for at in (count - 1, count)],
        out_edges, [VMEM] * count, name="stack_edges",
    )
    far_others = swapped(others, "scan", 1)
    beside = swapped(stacked, "scan", 0)
    out_centers, stacked = lax.optimization_barrier((out_centers, stacked))
    out_centers = across_depth(out_centers)
    sheet_f32 = sds((2, rows, columns), f32)
    sheet = call(
        functools.partial(place_near_kernel, slots),
        sheet_f32, [own_info, info, second, beside, *out_centers],
        [SMEM] * 3 + [VMEM] * (count + 1), name="place_near",
    )
    gradient = pl.pallas_call(
        functools.partial(place_far_kernel, slots),
        out_shape=sheet_f32,
        in_specs=[SMEM] * 2 + [VMEM] * 3,
        out_specs=pl.BlockSpec(memory_space=pl.ANY),
        scratch_shapes=[pltpu.VMEM(sheet_f32.shape, f32), pltpu.SemaphoreType.DMA((2,))],
        compiler_params=pltpu.CompilerParams(vmem_limit_bytes=LIMIT),
        name="place_far",
    )(own_info, second, sheet, far_own, far_others)
    return gradient[None]


def solution(mesh):
    in_specs = (
        P("depth", None, "scan", None),
        P(),
        P(),
        P("scan", None, None),
        P("scan"),
        P("scan"),
        P("scan"),
    )
    out_specs = P("depth", None, "scan", None)
    return jax.shard_map(body, mesh=mesh, in_specs=in_specs, out_specs=out_specs, check_vma=False)
```

```python
import functools
import math

import jax
import jax.numpy as jnp
import ml_dtypes
import numpy as np
from jax import lax
from jax.experimental import pallas as pl
from jax.experimental.pallas import tpu as pltpu
from jax.sharding import PartitionSpec as P

epsilon = 1.0
bf16 = jnp.bfloat16
f32 = jnp.float32
VMEM = pl.BlockSpec(memory_space=pltpu.VMEM)
SMEM = pl.BlockSpec(memory_space=pltpu.SMEM)
LIMIT = 48 * 1024 * 1024


def shifted(value, axis, steps):
    count = lax.axis_size(axis)
    pairs = [(source, (source + steps) % count) for source in range(count)]
    return lax.ppermute(value, axis, pairs)


def swapped(value, axis, first):
    count = lax.axis_size(axis)
    pairs = [
        (source, (source + (1 if source % 2 == first else -1)) % count) for source in range(count)
    ]
    return lax.ppermute(value, axis, pairs)


def exchanged(value, axis, flip):
    count = lax.axis_size(axis)
    return lax.ppermute(value, axis, [(source, source ^ flip) for source in range(count)])


def split_tables(pixels):
    indices = np.arange(pixels)
    angles = (indices[:, None] * indices[None, :] % pixels) * (2.0 * math.pi / pixels)
    norm_scale = 1.0 / math.sqrt(pixels)
    table_re = (np.cos(angles) * norm_scale).astype(np.float32).astype(ml_dtypes.bfloat16)
    table_im = (-np.sin(angles) * norm_scale).astype(np.float32).astype(ml_dtypes.bfloat16)
    return np.concatenate([table_re[0::2], table_im[0::2], table_re[1::2], table_im[1::2]], axis=0)


def parity_order(pixels):
    order = np.concatenate([np.arange(0, pixels, 2), np.arange(1, pixels, 2)])
    return (order[:, None] == np.arange(pixels)[None, :]).astype(np.float32)


def call(kernel, out_shape, args, specs, scratch=(), flops=0, transcendentals=0, name=None):
    outs = out_shape if isinstance(out_shape, (list, tuple)) else [out_shape]
    moved = sum(math.prod(a.shape) * a.dtype.itemsize for a in list(args) + list(outs))
    return pl.pallas_call(
        kernel,
        out_shape=out_shape,
        in_specs=specs,
        out_specs=jax.tree.map(lambda _: VMEM, out_shape),
        scratch_shapes=list(scratch),
        compiler_params=pltpu.CompilerParams(vmem_limit_bytes=LIMIT),
        cost_estimate=pl.CostEstimate(
            flops=flops, bytes_accessed=moved, transcendentals=transcendentals
        ),
        name=name,
    )(*args)


def sds(shape, dtype):
    return jax.ShapeDtypeStruct(shape, dtype)


def by_flip(pieces):
    return list(zip([0, *range(len(pieces) - 1, 0, -1)], pieces))


def column_place(info, slots, slot, width, columns):
    col = info[slots + slot]
    base = (col // width) * width
    after = jnp.minimum(base + width, columns - width)
    return pl.multiple_of(base, width), pl.multiple_of(after, width), col - base


def iotas(rows, cols):
    return (
        lax.broadcasted_iota(jnp.int32, (rows, cols), 0),
        lax.broadcasted_iota(jnp.int32, (rows, cols), 1),
    )


class Chosen:
    def __init__(self, first, info, others):
        self.first, self.info, self.others = first, info, others

    def __getitem__(self, at):
        return jnp.where(self.first, self.info[at], self.others[at])


def cut(own, comp, info, slots, slot, width):
    rows, columns = own.shape[1:]
    _, lane = iotas(rows, width)
    base, after, first = column_place(info, slots, slot, width, columns)
    return jnp.where(
        lane >= first, own[comp, :, pl.ds(base, width)], own[comp, :, pl.ds(after, width)]
    ).astype(bf16)


def cut_far_kernel(slots, width, own_info, second, own, others):
    depth_index = lax.axis_index("depth")
    far_info = Chosen(lax.rem(lax.axis_index("scan"), 2) == 1, own_info, second)
    for at, (flip, _) in enumerate(by_flip(range(others.shape[0] + 1))[1:]):
        for comp in range(2):
            others[at, comp] = cut(own, comp, far_info, slots, depth_index ^ flip, width)


def cut_near_kernel(slots, width, own_info, second, info, own, far_own, beside, *centers):
    depth_index = lax.axis_index("depth")
    even = lax.rem(lax.axis_index("scan"), 2) == 0
    far_info = Chosen(jnp.logical_not(even), own_info, second)
    near_info = Chosen(even, own_info, second)
    for comp in range(2):
        far_own[comp] = cut(own, comp, far_info, slots, depth_index, width)
    for at, (flip, center) in enumerate(by_flip(centers)):
        for comp in range(2):
            center[comp] = cut(own, comp, info, slots, depth_index ^ flip, width)
            beside[at, comp] = cut(own, comp, near_info, slots, depth_index ^ flip, width)


def joined(far, near, first_row):
    even = lax.rem(lax.axis_index("scan"), 2) == 0
    row, _ = iotas(*far.shape)
    return jnp.where(
        jnp.logical_xor(row < first_row, even), far.astype(f32), near.astype(f32)
    ).astype(bf16)


def join_kernel(info, others, beside, *outs):
    depth_index = lax.axis_index("depth")
    for at, (flip, _) in enumerate(by_flip(range(len(outs) + 1))[1:]):
        for comp in range(2):
            outs[at][comp] = joined(
                others[at, comp], beside[at + 1, comp], info[depth_index ^ flip]
            )


def frequency_kernel(phase, order, order_t, measured, prop_re, prop_im, amplitude):
    def reorder(value):
        rows = jnp.dot(
            order[...], value, preferred_element_type=f32, precision=lax.Precision.HIGHEST
        )
        return jnp.dot(
            rows, order_t[...], preferred_element_type=f32, precision=lax.Precision.HIGHEST
        )

    turned = reorder(phase[...])
    prop_re[...] = jnp.cos(turned)
    prop_im[...] = jnp.sin(turned)
    amplitude[...] = reorder(measured[lax.axis_index("depth")]).astype(bf16)


def table_kernel(slots, info, stack, stack_t, probe, psi0, *tables):
    depth_index = lax.axis_index("depth")
    pixels = probe.shape[-1]
    half = pixels // 2
    row_shift = info[depth_index]
    col_shift = lax.rem(info[slots + depth_index], pixels)

    def shift_matrix(rows, cols, shift, transposed):
        row, lane = iotas(rows, cols)
        offset = (lane - row if transposed else row - lane) + shift
        return jnp.where((offset == 0) | (offset == pixels), 1.0, 0.0).astype(bf16)

    def pair(shift):
        cols = jnp.dot(
            stack[...], shift_matrix(pixels, half, shift, False), preferred_element_type=f32
        )
        rows = jnp.dot(
            shift_matrix(half, pixels, shift, True), stack_t[...], preferred_element_type=f32
        )
        forms, forms_t = [], []
        for parity in range(2):
            at = 2 * parity * half
            re, im = cols[at : at + half], cols[at + half : at + pixels]
            top = jnp.concatenate([re, -im], axis=1)
            bottom = jnp.concatenate([im, re], axis=1)
            forms.append(jnp.concatenate([top, bottom], axis=0).astype(bf16))
            re, im = rows[:, at : at + half], rows[:, at + half : at + pixels]
            top = jnp.concatenate([re, im], axis=1)
            bottom = jnp.concatenate([-im, re], axis=1)
            forms_t.append(jnp.concatenate([top, bottom], axis=0).astype(bf16))
        return forms, forms_t

    row_forms, row_forms_t = pair(row_shift)
    col_forms, col_forms_t = pair(col_shift)
    made = row_forms + col_forms_t + col_forms + row_forms_t
    for ref, value in zip(tables, made):
        ref[...] = value
    down = shift_matrix(pixels, pixels, row_shift, True)
    across = shift_matrix(pixels, pixels, col_shift, False)
    for comp in range(2):
        moved = jnp.dot(down, probe[comp].astype(bf16), preferred_element_type=f32).astype(bf16)
        psi0[comp] = jnp.dot(moved, across, preferred_element_type=f32).astype(bf16)


def wave_kernel(slots, depth_count, info, prop_re, prop_im, amplitude, psi0, *refs):
    tables = refs[:8]
    centers, edges = refs[8 : 8 + depth_count], refs[8 + depth_count : 7 + 2 * depth_count]
    beside, far_own = refs[7 + 2 * depth_count : 9 + 2 * depth_count]
    outs = refs[9 + 2 * depth_count : 9 + 4 * depth_count]
    out_centers, out_edges = outs[:depth_count], outs[depth_count:]
    patches, waves, adjoint, grads = refs[9 + 4 * depth_count :]
    depth_index = lax.axis_index("depth")
    pixels = psi0.shape[-1]
    half = pixels // 2
    live = depth_index < info[2 * slots]
    fwd_row_e, fwd_row_o, fwd_col_e, fwd_col_o, inv_col_e, inv_col_o, inv_row_e, inv_row_o = tables

    def dot(left, right):
        return jnp.dot(left, right, preferred_element_type=f32)

    def propagate(x_re, x_im, at_frequency):
        def rows_of(sign):
            mixed = [v[:half] + v[half:] if sign > 0 else v[:half] - v[half:] for v in (x_re, x_im)]
            return jnp.concatenate(mixed, axis=0).astype(bf16)

        u_even = dot(fwd_row_e[...], rows_of(1))
        u_odd = dot(fwd_row_o[...], rows_of(-1))

        def cols_of(sign):
            parts = []
            for u in (u_even, u_odd):
                mixed = u[:, :half] + u[:, half:] if sign > 0 else u[:, :half] - u[:, half:]
                parts.append(jnp.concatenate([mixed[:half], mixed[half:]], axis=1))
            return jnp.concatenate(parts, axis=0).astype(bf16)

        v_even = dot(cols_of(1), fwd_col_e[...])
        v_odd = dot(cols_of(-1), fwd_col_o[...])
        b_even = at_frequency(v_even[:, :half], v_even[:, half:], slice(0, half))
        b_odd = at_frequency(v_odd[:, :half], v_odd[:, half:], slice(half, pixels))
        w_even = dot(jnp.concatenate(b_even, axis=1).astype(bf16), inv_col_e[...])
        w_odd = dot(jnp.concatenate(b_odd, axis=1).astype(bf16), inv_col_o[...])
        w_low, w_high = w_even + w_odd, w_even - w_odd
        w_re = jnp.concatenate([w_low[:, :half], w_high[:, :half]], axis=1)
        w_im = jnp.concatenate([w_low[:, half:], w_high[:, half:]], axis=1)
        y_even = dot(
            inv_row_e[...], jnp.concatenate([w_re[:half], w_im[:half]], axis=0).astype(bf16)
        )
        y_odd = dot(
            inv_row_o[...], jnp.concatenate([w_re[half:], w_im[half:]], axis=0).astype(bf16)
        )
        low, high = y_even + y_odd, y_even - y_odd
        return (
            jnp.concatenate([low[:half], high[:half]], axis=0),
            jnp.concatenate([low[half:], high[half:]], axis=0),
        )

    def turn(re, im, cols):
        p_re, p_im = prop_re[:, cols], prop_im[:, cols]
        return [re * p_re - im * p_im, re * p_im + im * p_re]

    def turn_back(re, im, cols):
        p_re, p_im = prop_re[:, cols], prop_im[:, cols]
        return [re * p_re + im * p_im, im * p_re - re * p_im]

    def residual(re, im, cols):
        factor = 1.0 - amplitude[:, cols].astype(f32) * lax.rsqrt(re * re + im * im + epsilon)
        return [factor * re, factor * im]

    def pair_of(ref, index):
        return ref[index, 0].astype(f32), ref[index, 1].astype(f32)

    @pl.when(live)
    def _():
        for at, (flip, center) in enumerate(by_flip(centers)):
            patches[depth_index ^ flip, :, half:] = center[...]
            if at:
                patches[depth_index ^ flip, :, :half] = edges[at - 1][...]
        for comp in range(2):
            patches[depth_index, comp, :half] = joined(
                far_own[comp], beside[0, comp], info[depth_index]
            )
        waves[0] = psi0[...]

        def forward(k, carry):
            t_re, t_im = pair_of(patches, k)
            p_re, p_im = pair_of(waves, k)
            n_re, n_im = propagate(t_re * p_re - t_im * p_im, t_re * p_im + t_im * p_re, turn)
            waves[k + 1, 0] = n_re.astype(bf16)
            waves[k + 1, 1] = n_im.astype(bf16)
            return carry

        lax.fori_loop(0, depth_count, forward, 0)
        l_re, l_im = propagate(*pair_of(waves, depth_count), residual)
        adjoint[0, 0] = l_re.astype(bf16)
        adjoint[0, 1] = l_im.astype(bf16)

        def backward(step, carry):
            k = depth_count - 1 - step
            m_re, m_im = propagate(*pair_of(adjoint, 0), turn_back)
            t_re, t_im = pair_of(patches, k)
            p_re, p_im = pair_of(waves, k)
            grads[k ^ depth_index, 0] = (p_re * m_re + p_im * m_im).astype(bf16)
            grads[k ^ depth_index, 1] = (p_re * m_im - p_im * m_re).astype(bf16)
            adjoint[0, 0] = (t_re * m_re + t_im * m_im).astype(bf16)
            adjoint[0, 1] = (t_re * m_im - t_im * m_re).astype(bf16)
            return carry

        lax.fori_loop(0, depth_count, backward, 0)
        for (flip, center), edge in zip(by_flip(out_centers), out_edges):
            center[...] = grads[flip, :, half:]
            edge[...] = grads[flip, :, :half]

    @pl.when(jnp.logical_not(live))
    def _():
        for ref in out_centers + out_edges:
            ref[...] = jnp.zeros(ref.shape, ref.dtype)


def stack_kernel(*refs):
    pieces, (others, stacked) = refs[:-2], refs[-2:]
    for at, piece in enumerate(pieces):
        stacked[at] = piece[...]
        if at:
            others[at - 1] = piece[...]


def place(sheet, comp, at, value, base, after, to_base):
    width = value.shape[-1]
    sheet[comp, at, pl.ds(base, width)] += jnp.where(to_base, value, 0.0)
    sheet[comp, at, pl.ds(after, width)] += jnp.where(to_base, 0.0, value)


def place_edge(sheet, comp, at, piece, info, slots, slot, upper):
    value = piece[at].astype(f32)
    row, lane = iotas(*value.shape)
    base, after, first = column_place(info, slots, slot, value.shape[-1], sheet.shape[-1])
    here = jnp.logical_xor(row + at.start < info[slot], upper)
    place(sheet, comp, at, jnp.where(here, value, 0.0), base, after, lane >= first)


def place_beside_kernel(slots, own_info, second, far_own, beside, sheet):
    depth_index = lax.axis_index("depth")
    even = lax.rem(lax.axis_index("scan"), 2) == 0
    odd = jnp.logical_not(even)
    near_info = Chosen(even, own_info, second)
    far_info = Chosen(odd, own_info, second)
    whole = slice(0, sheet.shape[1])
    sheet[...] = jnp.zeros(sheet.shape, f32)
    for comp in range(2):
        place_edge(sheet, comp, whole, far_own.at[comp], far_info, slots, depth_index, odd)
        for at, (flip, _) in enumerate(by_flip(range(beside.shape[0]))):
            slot = depth_index ^ flip
            place_edge(sheet, comp, whole, beside.at[at, comp], near_info, slots, slot, even)


def place_center_kernel(slots, info, before, *refs):
    pieces, sheet = refs[:-1], refs[-1]
    depth_index = lax.axis_index("depth")
    columns = sheet.shape[-1]
    rows, width = pieces[0].shape[1:]
    _, lane = iotas(rows, width)
    sheet[...] = before[...]
    for flip, piece in by_flip(pieces):
        base, after, first = column_place(info, slots, depth_index ^ flip, width, columns)
        for comp in range(2):
            value = piece[comp].astype(f32)
            place(sheet, comp, slice(0, rows), value, base, after, lane >= first)


def place_far_kernel(slots, own_info, second, sheet, others, out, total, sems):
    depth_index = lax.axis_index("depth")
    odd = lax.rem(lax.axis_index("scan"), 2) == 1
    far_info = Chosen(odd, own_info, second)
    rows = sheet.shape[1] // 2
    copies = []
    for comp in range(2):
        for part in range(2):
            here = slice(part * rows, (part + 1) * rows)
            total[comp, here] = sheet[comp, here]
            for at, (flip, _) in enumerate(by_flip(range(others.shape[0] + 1))[1:]):
                slot = depth_index ^ flip
                place_edge(total, comp, here, others.at[at, comp], far_info, slots, slot, odd)
            copies.append(
                pltpu.make_async_copy(
                    total.at[comp, here], out.at[comp, here], sems.at[2 * comp + part]
                )
            )
            copies[-1].start()
    for copy in copies:
        copy.wait()


def body(transmission, probe_wave, prop_phase, measured, scan_rows, scan_cols, live_counts):
    pixels = probe_wave.shape[-1]
    slots = measured.shape[0]
    rows = transmission.shape[2]
    columns = transmission.shape[3]
    count = lax.axis_size("depth")
    own = transmission[0]
    own_info = jnp.concatenate([scan_rows, scan_cols, live_counts])
    second = shifted(own_info, "scan", 2)
    info = shifted(own_info, "scan", 1)
    info, second = lax.optimization_barrier((info, second))
    others_shape = sds((count - 1, 2, rows, pixels), bf16)
    stacked_shape = sds((count, 2, rows, pixels), bf16)
    part = sds((2, rows, pixels), bf16)
    others = call(
        functools.partial(cut_far_kernel, slots, pixels),
        others_shape, [own_info, second, own], [SMEM, SMEM, VMEM], name="cut_far",
    )
    others = swapped(others, "scan", 1)
    far_own, beside, *centers = call(
        functools.partial(cut_near_kernel, slots, pixels),
        [part, stacked_shape] + [part] * count, [own_info, second, info, own],
        [SMEM] * 3 + [VMEM], name="cut_near",
    )
    beside = swapped(beside, "scan", 0)

    def across_depth(pieces):
        return [exchanged(piece, "depth", flip) for flip, piece in by_flip([None, *pieces])[1:]]

    centers = [centers[0]] + across_depth(centers[1:])

    phase, centers[0] = lax.optimization_barrier((prop_phase, centers[0]))
    order = parity_order(pixels)
    square = sds((pixels, pixels), f32)
    prop_re, prop_im, amplitude = call(
        frequency_kernel,
        [square, square, sds((pixels, pixels), bf16)],
        [phase, jnp.asarray(order), jnp.asarray(order.T), measured],
        [VMEM] * 4, flops=2400 * pixels**3, transcendentals=2 * pixels**2, name="frequency_order",
    )
    amplitude, centers[1] = lax.optimization_barrier((amplitude, centers[1]))
    amplitude = shifted(amplitude, "scan", 1)

    stack = split_tables(pixels)
    made = call(
        functools.partial(table_kernel, slots),
        [sds((2, pixels, pixels), bf16)] + [sds((pixels, pixels), bf16)] * 8,
        [info, jnp.asarray(stack), jnp.asarray(stack.T), probe_wave],
        [SMEM, VMEM, VMEM, VMEM], flops=16 * pixels**3, name="tables",
    )
    others, far_own = lax.optimization_barrier((others, far_own))
    edges = call(
        join_kernel, [part] * (count - 1), [info, others, beside], [SMEM] + [VMEM] * 2,
        name="join_edges",
    )
    edges, far_own = lax.optimization_barrier((edges, far_own))
    edges = across_depth(edges)
    far_own = swapped(far_own, "scan", 1)

    args = [info, prop_re, prop_im, amplitude, *made, *centers, *edges, beside, far_own]
    grads = call(
        functools.partial(wave_kernel, slots, count),
        [part] * (2 * count), args, [SMEM] + [VMEM] * (len(args) - 1),
        scratch=[
            pltpu.VMEM((count, 2, pixels, pixels), bf16),
            pltpu.VMEM((count + 1, 2, pixels, pixels), bf16),
            pltpu.VMEM((1, 2, pixels, pixels), bf16),
            pltpu.VMEM((count, 2, pixels, pixels), bf16),
        ],
        flops=(2 * count + 1) * 16 * pixels**3, name="waves",
    )
    out_centers, out_edges = grads[:count], grads[count:]
    far_own = swapped(out_edges[0], "scan", 1)
    out_edges = [out_edges[0]] + across_depth(out_edges[1:])
    far_own, out_edges = lax.optimization_barrier((far_own, out_edges))
    others, stacked = call(
        stack_kernel, [others_shape, stacked_shape], out_edges, [VMEM] * count,
        name="stack_edges",
    )
    far_others = swapped(others, "scan", 1)
    beside = swapped(stacked, "scan", 0)
    out_centers, stacked = lax.optimization_barrier((out_centers, stacked))
    out_centers = [out_centers[0]] + across_depth(out_centers[1:])
    sheet_f32 = sds((2, rows, columns), f32)
    sheet = call(
        functools.partial(place_beside_kernel, slots),
        sheet_f32, [own_info, second, far_own, beside], [SMEM] * 2 + [VMEM] * 2,
        name="place_beside",
    )
    sheet = call(
        functools.partial(place_center_kernel, slots),
        sheet_f32, [info, sheet, *out_centers], [SMEM] + [VMEM] * (count + 1),
        name="place_center",
    )
    gradient = pl.pallas_call(
        functools.partial(place_far_kernel, slots),
        out_shape=sheet_f32,
        in_specs=[SMEM] * 2 + [VMEM] * 2,
        out_specs=pl.BlockSpec(memory_space=pl.ANY),
        scratch_shapes=[pltpu.VMEM(sheet_f32.shape, f32), pltpu.SemaphoreType.DMA((4,))],
        compiler_params=pltpu.CompilerParams(vmem_limit_bytes=LIMIT),
        name="place_far",
    )(own_info, second, sheet, far_others)
    return gradient[None]


def solution(mesh):
    in_specs = (
        P("depth", None, "scan", None),
        P(),
        P(),
        P("scan", None, None),
        P("scan"),
        P("scan"),
        P("scan"),
    )
    out_specs = P("depth", None, "scan", None)
    return jax.shard_map(body, mesh=mesh, in_specs=in_specs, out_specs=out_specs, check_vma=False)
```

```python
import functools
import math

import jax
import jax.numpy as jnp
import ml_dtypes
import numpy as np
from jax import lax
from jax.experimental import pallas as pl
from jax.experimental.pallas import tpu as pltpu
from jax.sharding import PartitionSpec as P

epsilon = 1.0
bf16 = jnp.bfloat16
f32 = jnp.float32
VMEM = pl.BlockSpec(memory_space=pltpu.VMEM)
SMEM = pl.BlockSpec(memory_space=pltpu.SMEM)
LIMIT = 48 * 1024 * 1024
INFO_SIZE = 8192


def shifted(value, axis, steps):
    count = lax.axis_size(axis)
    pairs = [(source, (source + steps) % count) for source in range(count)]
    return lax.ppermute(value, axis, pairs)


def swapped(value, axis, first):
    count = lax.axis_size(axis)
    pairs = [
        (source, (source + (1 if source % 2 == first else -1)) % count) for source in range(count)
    ]
    return lax.ppermute(value, axis, pairs)


def exchanged(value, axis, flip):
    count = lax.axis_size(axis)
    return lax.ppermute(value, axis, [(source, source ^ flip) for source in range(count)])


def split_tables(pixels):
    indices = np.arange(pixels)
    angles = (indices[:, None] * indices[None, :] % pixels) * (2.0 * math.pi / pixels)
    norm_scale = 1.0 / math.sqrt(pixels)
    table_re = (np.cos(angles) * norm_scale).astype(np.float32).astype(ml_dtypes.bfloat16)
    table_im = (-np.sin(angles) * norm_scale).astype(np.float32).astype(ml_dtypes.bfloat16)
    return np.concatenate([table_re[0::2], table_im[0::2], table_re[1::2], table_im[1::2]], axis=0)


def call(kernel, out_shape, args, specs, scratch=(), flops=0, transcendentals=0, name=None):
    outs = out_shape if isinstance(out_shape, (list, tuple)) else [out_shape]
    moved = sum(math.prod(a.shape) * a.dtype.itemsize for a in list(args) + list(outs))
    return pl.pallas_call(
        kernel,
        out_shape=out_shape,
        in_specs=specs,
        out_specs=jax.tree.map(lambda _: VMEM, out_shape),
        scratch_shapes=list(scratch),
        compiler_params=pltpu.CompilerParams(vmem_limit_bytes=LIMIT),
        cost_estimate=pl.CostEstimate(
            flops=flops, bytes_accessed=moved, transcendentals=transcendentals
        ),
        name=name,
    )(*args)


def sds(shape, dtype):
    return jax.ShapeDtypeStruct(shape, dtype)


def by_flip(pieces):
    return list(zip([0, *range(len(pieces) - 1, 0, -1)], pieces))


def column_place(info, slots, slot, width, columns):
    col = info[slots + slot]
    base = (col // width) * width
    after = jnp.minimum(base + width, columns - width)
    return pl.multiple_of(base, width), pl.multiple_of(after, width), col - base


def iotas(rows, cols):
    return (
        lax.broadcasted_iota(jnp.int32, (rows, cols), 0),
        lax.broadcasted_iota(jnp.int32, (rows, cols), 1),
    )


def strip_kernel(own, strip):
    strip[...] = own[...].astype(bf16)


class Chosen:
    def __init__(self, first, info, others):
        self.first, self.info, self.others = first, info, others

    def __getitem__(self, at):
        return jnp.where(self.first, self.info[at], self.others[at])


def cut(strip, comp, info, slots, slot, width):
    rows, columns = strip.shape[1:]
    _, lane = iotas(rows, width)
    base, after, first = column_place(info, slots, slot, width, columns)
    return jnp.where(
        lane >= first,
        strip[comp, :, pl.ds(base, width)].astype(f32),
        strip[comp, :, pl.ds(after, width)].astype(f32),
    ).astype(bf16)


def cut_far_kernel(slots, width, own_info, second, strip, others):
    depth_index = lax.axis_index("depth")
    far_info = Chosen(lax.rem(lax.axis_index("scan"), 2) == 1, own_info, second)
    for at, (flip, _) in enumerate(by_flip(range(others.shape[0] + 1))[1:]):
        for comp in range(2):
            others[at, comp] = cut(strip, comp, far_info, slots, depth_index ^ flip, width)


def cut_near_kernel(slots, width, own_info, second, info, strip, far_own, beside, *centers):
    depth_index = lax.axis_index("depth")
    even = lax.rem(lax.axis_index("scan"), 2) == 0
    far_info = Chosen(jnp.logical_not(even), own_info, second)
    near_info = Chosen(even, own_info, second)
    for comp in range(2):
        far_own[comp] = cut(strip, comp, far_info, slots, depth_index, width)
    for at, (flip, center) in enumerate(by_flip(centers)):
        for comp in range(2):
            center[comp] = cut(strip, comp, info, slots, depth_index ^ flip, width)
            beside[at, comp] = cut(strip, comp, near_info, slots, depth_index ^ flip, width)


def joined(far, near, first_row):
    even = lax.rem(lax.axis_index("scan"), 2) == 0
    row, _ = iotas(*far.shape)
    return jnp.where(
        jnp.logical_xor(row < first_row, even), far.astype(f32), near.astype(f32)
    ).astype(bf16)


def join_kernel(info, others, beside, *outs):
    depth_index = lax.axis_index("depth")
    for at, (flip, _) in enumerate(by_flip(range(len(outs) + 1))[1:]):
        for comp in range(2):
            outs[at][comp] = joined(
                others[at, comp], beside[at + 1, comp], info[depth_index ^ flip]
            )


def frequency_kernel(phase, measured, prop_re, prop_im, amplitude, own_measured, sem):
    load = pltpu.make_async_copy(measured.at[lax.axis_index("depth")], own_measured, sem)
    load.start()
    pixels = phase.shape[0]
    half = pixels // 2
    row, lane = iotas(pixels, pixels)

    def order(at, frequency):
        place = jnp.where(at < half, 2 * at, 2 * (at - half) + 1)
        return jnp.where(place == frequency, 1.0, 0.0).astype(f32)

    def reorder(value):
        high = lax.Precision.HIGHEST
        rows = jnp.dot(order(row, lane), value, preferred_element_type=f32, precision=high)
        return jnp.dot(rows, order(lane, row), preferred_element_type=f32, precision=high)

    turned = reorder(phase[...])
    prop_re[...] = jnp.cos(turned)
    prop_im[...] = jnp.sin(turned)
    load.wait()
    amplitude[...] = reorder(own_measured[...]).astype(bf16)


def table_kernel(slots, info, stack, stack_t, probe, psi0, *tables):
    depth_index = lax.axis_index("depth")
    pixels = probe.shape[-1]
    half = pixels // 2
    row_shift = info[depth_index]
    col_shift = lax.rem(info[slots + depth_index], pixels)

    def shift_matrix(rows, cols, shift, transposed):
        row, lane = iotas(rows, cols)
        offset = (lane - row if transposed else row - lane) + shift
        return jnp.where((offset == 0) | (offset == pixels), 1.0, 0.0).astype(bf16)

    def pair(shift):
        cols = jnp.dot(
            stack[...], shift_matrix(pixels, half, shift, False), preferred_element_type=f32
        )
        rows = jnp.dot(
            shift_matrix(half, pixels, shift, True), stack_t[...], preferred_element_type=f32
        )
        forms, forms_t = [], []
        for parity in range(2):
            at = 2 * parity * half
            re, im = cols[at : at + half], cols[at + half : at + pixels]
            top = jnp.concatenate([re, -im], axis=1)
            bottom = jnp.concatenate([im, re], axis=1)
            forms.append(jnp.concatenate([top, bottom], axis=0).astype(bf16))
            re, im = rows[:, at : at + half], rows[:, at + half : at + pixels]
            top = jnp.concatenate([re, im], axis=1)
            bottom = jnp.concatenate([-im, re], axis=1)
            forms_t.append(jnp.concatenate([top, bottom], axis=0).astype(bf16))
        return forms, forms_t

    row_forms, row_forms_t = pair(row_shift)
    col_forms, col_forms_t = pair(col_shift)
    made = row_forms + col_forms_t + col_forms + row_forms_t
    for ref, value in zip(tables, made):
        ref[...] = value
    down = shift_matrix(pixels, pixels, row_shift, True)
    across = shift_matrix(pixels, pixels, col_shift, False)
    for comp in range(2):
        moved = jnp.dot(down, probe[comp].astype(bf16), preferred_element_type=f32).astype(bf16)
        psi0[comp] = jnp.dot(moved, across, preferred_element_type=f32).astype(bf16)


def wave_kernel(slots, depth_count, info, prop_re, prop_im, amplitude, psi0, *refs):
    tables = refs[:8]
    centers, edges = refs[8 : 8 + depth_count], refs[8 + depth_count : 7 + 2 * depth_count]
    beside, far_own = refs[7 + 2 * depth_count : 9 + 2 * depth_count]
    outs = refs[9 + 2 * depth_count : 9 + 4 * depth_count]
    out_centers, out_edges = outs[:depth_count], outs[depth_count:]
    patches, waves, adjoint, grads = refs[9 + 4 * depth_count :]
    depth_index = lax.axis_index("depth")
    pixels = psi0.shape[-1]
    half = pixels // 2
    live = depth_index < info[2 * slots]
    fwd_row_e, fwd_row_o, fwd_col_e, fwd_col_o, inv_col_e, inv_col_o, inv_row_e, inv_row_o = tables

    def dot(left, right):
        return jnp.dot(left, right, preferred_element_type=f32)

    def propagate(x_re, x_im, at_frequency):
        def rows_of(sign):
            mixed = [v[:half] + v[half:] if sign > 0 else v[:half] - v[half:] for v in (x_re, x_im)]
            return jnp.concatenate(mixed, axis=0).astype(bf16)

        u_even = dot(fwd_row_e[...], rows_of(1))
        u_odd = dot(fwd_row_o[...], rows_of(-1))

        def cols_of(sign):
            parts = []
            for u in (u_even, u_odd):
                mixed = u[:, :half] + u[:, half:] if sign > 0 else u[:, :half] - u[:, half:]
                parts.append(jnp.concatenate([mixed[:half], mixed[half:]], axis=1))
            return jnp.concatenate(parts, axis=0).astype(bf16)

        v_even = dot(cols_of(1), fwd_col_e[...])
        v_odd = dot(cols_of(-1), fwd_col_o[...])
        b_even = at_frequency(v_even[:, :half], v_even[:, half:], slice(0, half))
        b_odd = at_frequency(v_odd[:, :half], v_odd[:, half:], slice(half, pixels))
        w_even = dot(jnp.concatenate(b_even, axis=1).astype(bf16), inv_col_e[...])
        w_odd = dot(jnp.concatenate(b_odd, axis=1).astype(bf16), inv_col_o[...])
        w_low, w_high = w_even + w_odd, w_even - w_odd
        w_re = jnp.concatenate([w_low[:, :half], w_high[:, :half]], axis=1)
        w_im = jnp.concatenate([w_low[:, half:], w_high[:, half:]], axis=1)
        y_even = dot(
            inv_row_e[...], jnp.concatenate([w_re[:half], w_im[:half]], axis=0).astype(bf16)
        )
        y_odd = dot(
            inv_row_o[...], jnp.concatenate([w_re[half:], w_im[half:]], axis=0).astype(bf16)
        )
        low, high = y_even + y_odd, y_even - y_odd
        return (
            jnp.concatenate([low[:half], high[:half]], axis=0),
            jnp.concatenate([low[half:], high[half:]], axis=0),
        )

    def turn(re, im, cols):
        p_re, p_im = prop_re[:, cols], prop_im[:, cols]
        return [re * p_re - im * p_im, re * p_im + im * p_re]

    def turn_back(re, im, cols):
        p_re, p_im = prop_re[:, cols], prop_im[:, cols]
        return [re * p_re + im * p_im, im * p_re - re * p_im]

    def residual(re, im, cols):
        factor = 1.0 - amplitude[:, cols].astype(f32) * lax.rsqrt(re * re + im * im + epsilon)
        return [factor * re, factor * im]

    def pair_of(ref, index):
        return ref[index, 0].astype(f32), ref[index, 1].astype(f32)

    @pl.when(live)
    def _():
        for at, (flip, center) in enumerate(by_flip(centers)):
            patches[depth_index ^ flip, :, half:] = center[...]
            if at:
                patches[depth_index ^ flip, :, :half] = edges[at - 1][...]
        for comp in range(2):
            patches[depth_index, comp, :half] = joined(
                far_own[comp], beside[0, comp], info[depth_index]
            )
        waves[0] = psi0[...]

        def forward(k, carry):
            t_re, t_im = pair_of(patches, k)
            p_re, p_im = pair_of(waves, k)
            n_re, n_im = propagate(t_re * p_re - t_im * p_im, t_re * p_im + t_im * p_re, turn)
            waves[k + 1, 0] = n_re.astype(bf16)
            waves[k + 1, 1] = n_im.astype(bf16)
            return carry

        lax.fori_loop(0, depth_count, forward, 0)
        l_re, l_im = propagate(*pair_of(waves, depth_count), residual)
        adjoint[0, 0] = l_re.astype(bf16)
        adjoint[0, 1] = l_im.astype(bf16)

        def backward(step, carry):
            k = depth_count - 1 - step
            m_re, m_im = propagate(*pair_of(adjoint, 0), turn_back)
            t_re, t_im = pair_of(patches, k)
            p_re, p_im = pair_of(waves, k)
            grads[k ^ depth_index, 0] = (p_re * m_re + p_im * m_im).astype(bf16)
            grads[k ^ depth_index, 1] = (p_re * m_im - p_im * m_re).astype(bf16)
            adjoint[0, 0] = (t_re * m_re + t_im * m_im).astype(bf16)
            adjoint[0, 1] = (t_re * m_im - t_im * m_re).astype(bf16)
            return carry

        lax.fori_loop(0, depth_count, backward, 0)
        for (flip, center), edge in zip(by_flip(out_centers), out_edges):
            center[...] = grads[flip, :, half:]
            edge[...] = grads[flip, :, :half]

    @pl.when(jnp.logical_not(live))
    def _():
        for ref in out_centers + out_edges:
            ref[...] = jnp.zeros(ref.shape, ref.dtype)


def stack_kernel(*refs):
    pieces, (others, stacked) = refs[:-2], refs[-2:]
    for at, piece in enumerate(pieces):
        stacked[at] = piece[...]
        if at:
            others[at - 1] = piece[...]


def place(sheet, comp, at, value, base, after, to_base):
    width = value.shape[-1]
    sheet[comp, at, pl.ds(base, width)] += jnp.where(to_base, value, 0.0)
    sheet[comp, at, pl.ds(after, width)] += jnp.where(to_base, 0.0, value)


def place_edge(sheet, comp, at, piece, info, slots, slot, upper):
    value = piece[at].astype(f32)
    row, lane = iotas(*value.shape)
    base, after, first = column_place(info, slots, slot, value.shape[-1], sheet.shape[-1])
    here = jnp.logical_xor(row + at.start < info[slot], upper)
    place(sheet, comp, at, jnp.where(here, value, 0.0), base, after, lane >= first)


def place_beside_kernel(slots, own_info, second, far_own, beside, sheet):
    depth_index = lax.axis_index("depth")
    even = lax.rem(lax.axis_index("scan"), 2) == 0
    odd = jnp.logical_not(even)
    near_info = Chosen(even, own_info, second)
    far_info = Chosen(odd, own_info, second)
    whole = slice(0, sheet.shape[1])
    sheet[...] = jnp.zeros(sheet.shape, f32)
    for comp in range(2):
        place_edge(sheet, comp, whole, far_own.at[comp], far_info, slots, depth_index, odd)
        for at, (flip, _) in enumerate(by_flip(range(beside.shape[0]))):
            slot = depth_index ^ flip
            place_edge(sheet, comp, whole, beside.at[at, comp], near_info, slots, slot, even)


def place_center_kernel(slots, info, before, *refs):
    pieces, sheet = refs[:-1], refs[-1]
    depth_index = lax.axis_index("depth")
    columns = sheet.shape[-1]
    rows, width = pieces[0].shape[1:]
    _, lane = iotas(rows, width)
    sheet[...] = before[...]
    for flip, piece in by_flip(pieces):
        base, after, first = column_place(info, slots, depth_index ^ flip, width, columns)
        for comp in range(2):
            value = piece[comp].astype(f32)
            place(sheet, comp, slice(0, rows), value, base, after, lane >= first)


def place_far_kernel(slots, own_info, second, sheet, others, out, total, sems):
    depth_index = lax.axis_index("depth")
    odd = lax.rem(lax.axis_index("scan"), 2) == 1
    far_info = Chosen(odd, own_info, second)
    rows = sheet.shape[1] // 2
    copies = []
    for comp in range(2):
        for part in range(2):
            here = slice(part * rows, (part + 1) * rows)
            total[comp, here] = sheet[comp, here]
            for at, (flip, _) in enumerate(by_flip(range(others.shape[0] + 1))[1:]):
                slot = depth_index ^ flip
                place_edge(total, comp, here, others.at[at, comp], far_info, slots, slot, odd)
            copies.append(
                pltpu.make_async_copy(
                    total.at[comp, here], out.at[comp, here], sems.at[2 * comp + part]
                )
            )
            copies[-1].start()
    for copy in copies:
        copy.wait()


def body(transmission, probe_wave, prop_phase, measured, scan_rows, scan_cols, live_counts):
    pixels = probe_wave.shape[-1]
    slots = measured.shape[0]
    rows = transmission.shape[2]
    columns = transmission.shape[3]
    count = lax.axis_size("depth")
    own = transmission[0]
    own_info = jnp.concatenate([scan_rows, scan_cols, live_counts])
    second = shifted(own_info, "scan", 2)
    ints = own_info.shape[0]
    info = shifted(jnp.pad(own_info, (0, INFO_SIZE - ints)), "scan", 1)[:ints]
    strip = call(strip_kernel, sds(own.shape, bf16), [own], [VMEM], name="strip")
    second, strip = lax.optimization_barrier((second, strip))
    others_shape = sds((count - 1, 2, rows, pixels), bf16)
    stacked_shape = sds((count, 2, rows, pixels), bf16)
    part = sds((2, rows, pixels), bf16)
    others = call(
        functools.partial(cut_far_kernel, slots, pixels),
        others_shape, [own_info, second, strip], [SMEM, SMEM, VMEM], name="cut_far",
    )
    others = swapped(others, "scan", 1)
    far_own, beside, *centers = call(
        functools.partial(cut_near_kernel, slots, pixels),
        [part, stacked_shape] + [part] * count, [own_info, second, info, strip],
        [SMEM] * 3 + [VMEM], name="cut_near",
    )
    beside = swapped(beside, "scan", 0)

    def across_depth(pieces):
        return [exchanged(piece, "depth", flip) for flip, piece in by_flip([None, *pieces])[1:]]

    centers = [centers[0]] + across_depth(centers[1:])

    phase, centers[0] = lax.optimization_barrier((prop_phase, centers[0]))
    square = sds((pixels, pixels), f32)
    prop_re, prop_im, amplitude = call(
        frequency_kernel,
        [square, square, sds((pixels, pixels), bf16)],
        [phase, measured], [VMEM, pl.BlockSpec(memory_space=pltpu.HBM)],
        scratch=[pltpu.VMEM(square.shape, f32), pltpu.SemaphoreType.DMA],
        flops=2400 * pixels**3, transcendentals=2 * pixels**2, name="frequency_order",
    )
    amplitude, centers[1] = lax.optimization_barrier((amplitude, centers[1]))
    amplitude = shifted(amplitude, "scan", 1)

    stack = split_tables(pixels)
    made = call(
        functools.partial(table_kernel, slots),
        [sds((2, pixels, pixels), bf16)] + [sds((pixels, pixels), bf16)] * 8,
        [info, jnp.asarray(stack), jnp.asarray(stack.T), probe_wave],
        [SMEM, VMEM, VMEM, VMEM], flops=16 * pixels**3, name="tables",
    )
    others, far_own = lax.optimization_barrier((others, far_own))
    edges = call(
        join_kernel, [part] * (count - 1), [info, others, beside], [SMEM] + [VMEM] * 2,
        name="join_edges",
    )
    edges, far_own = lax.optimization_barrier((edges, far_own))
    edges = across_depth(edges)
    far_own = swapped(far_own, "scan", 1)

    args = [info, prop_re, prop_im, amplitude, *made, *centers, *edges, beside, far_own]
    grads = call(
        functools.partial(wave_kernel, slots, count),
        [part] * (2 * count), args, [SMEM] + [VMEM] * (len(args) - 1),
        scratch=[
            pltpu.VMEM((count, 2, pixels, pixels), bf16),
            pltpu.VMEM((count + 1, 2, pixels, pixels), bf16),
            pltpu.VMEM((1, 2, pixels, pixels), bf16),
            pltpu.VMEM((count, 2, pixels, pixels), bf16),
        ],
        flops=(2 * count + 1) * 16 * pixels**3, name="waves",
    )
    out_centers, out_edges = grads[:count], grads[count:]
    far_own = swapped(out_edges[0], "scan", 1)
    out_edges = [out_edges[0]] + across_depth(out_edges[1:])
    far_own, out_edges = lax.optimization_barrier((far_own, out_edges))
    others, stacked = call(
        stack_kernel, [others_shape, stacked_shape], out_edges, [VMEM] * count,
        name="stack_edges",
    )
    far_others = swapped(others, "scan", 1)
    beside = swapped(stacked, "scan", 0)
    out_centers, stacked = lax.optimization_barrier((out_centers, stacked))
    out_centers = [out_centers[0]] + across_depth(out_centers[1:])
    sheet_f32 = sds((2, rows, columns), f32)
    sheet = call(
        functools.partial(place_beside_kernel, slots),
        sheet_f32, [own_info, second, far_own, beside], [SMEM] * 2 + [VMEM] * 2,
        name="place_beside",
    )
    sheet = call(
        functools.partial(place_center_kernel, slots),
        sheet_f32, [info, sheet, *out_centers], [SMEM] + [VMEM] * (count + 1),
        name="place_center",
    )
    gradient = pl.pallas_call(
        functools.partial(place_far_kernel, slots),
        out_shape=sheet_f32,
        in_specs=[SMEM] * 2 + [VMEM] * 2,
        out_specs=pl.BlockSpec(memory_space=pl.ANY),
        scratch_shapes=[pltpu.VMEM(sheet_f32.shape, f32), pltpu.SemaphoreType.DMA((4,))],
        compiler_params=pltpu.CompilerParams(vmem_limit_bytes=LIMIT),
        name="place_far",
    )(own_info, second, sheet, far_others)
    return gradient[None]


def solution(mesh):
    in_specs = (
        P("depth", None, "scan", None),
        P(),
        P(),
        P("scan", None, None),
        P("scan"),
        P("scan"),
        P("scan"),
    )
    out_specs = P("depth", None, "scan", None)
    return jax.shard_map(body, mesh=mesh, in_specs=in_specs, out_specs=out_specs, check_vma=False)
```

```python
import functools
import math

import jax
import jax.numpy as jnp
import ml_dtypes
import numpy as np
from jax import lax
from jax.experimental import pallas as pl
from jax.experimental.pallas import tpu as pltpu
from jax.sharding import PartitionSpec as P

epsilon = 1.0
bf16 = jnp.bfloat16
f32 = jnp.float32
VMEM = pl.BlockSpec(memory_space=pltpu.VMEM)
SMEM = pl.BlockSpec(memory_space=pltpu.SMEM)
LIMIT = 48 * 1024 * 1024
INFO_SIZE = 8192


def shifted(value, axis, steps):
    count = lax.axis_size(axis)
    pairs = [(source, (source + steps) % count) for source in range(count)]
    return lax.ppermute(value, axis, pairs)


def swapped(value, axis, first):
    count = lax.axis_size(axis)
    pairs = [
        (source, (source + (1 if source % 2 == first else -1)) % count) for source in range(count)
    ]
    return lax.ppermute(value, axis, pairs)


def exchanged(value, axis, flip):
    count = lax.axis_size(axis)
    return lax.ppermute(value, axis, [(source, source ^ flip) for source in range(count)])


def split_tables(pixels):
    indices = np.arange(pixels)
    angles = (indices[:, None] * indices[None, :] % pixels) * (2.0 * math.pi / pixels)
    norm_scale = 1.0 / math.sqrt(pixels)
    table_re = (np.cos(angles) * norm_scale).astype(np.float32).astype(ml_dtypes.bfloat16)
    table_im = (-np.sin(angles) * norm_scale).astype(np.float32).astype(ml_dtypes.bfloat16)
    return np.concatenate([table_re[0::2], table_im[0::2], table_re[1::2], table_im[1::2]], axis=0)


def parity_order(pixels):
    order = np.concatenate([np.arange(0, pixels, 2), np.arange(1, pixels, 2)])
    return (order[:, None] == np.arange(pixels)[None, :]).astype(np.float32)


def call(kernel, out_shape, args, specs, scratch=(), flops=0, transcendentals=0, name=None):
    outs = out_shape if isinstance(out_shape, (list, tuple)) else [out_shape]
    moved = sum(math.prod(a.shape) * a.dtype.itemsize for a in list(args) + list(outs))
    return pl.pallas_call(
        kernel,
        out_shape=out_shape,
        in_specs=specs,
        out_specs=jax.tree.map(lambda _: VMEM, out_shape),
        scratch_shapes=list(scratch),
        compiler_params=pltpu.CompilerParams(vmem_limit_bytes=LIMIT),
        cost_estimate=pl.CostEstimate(
            flops=flops, bytes_accessed=moved, transcendentals=transcendentals
        ),
        name=name,
    )(*args)


def sds(shape, dtype):
    return jax.ShapeDtypeStruct(shape, dtype)


def by_flip(pieces):
    return list(zip([0, *range(len(pieces) - 1, 0, -1)], pieces))


def column_place(info, slots, slot, width, columns):
    col = info[slots + slot]
    base = (col // width) * width
    after = jnp.minimum(base + width, columns - width)
    return pl.multiple_of(base, width), pl.multiple_of(after, width), col - base


def iotas(rows, cols):
    return (
        lax.broadcasted_iota(jnp.int32, (rows, cols), 0),
        lax.broadcasted_iota(jnp.int32, (rows, cols), 1),
    )


def strip_kernel(own, strip):
    strip[...] = own[...].astype(bf16)


def center_kernel(slots, width, info, strip, *outs):
    depth_index = lax.axis_index("depth")
    columns = strip.shape[-1]
    _, lane = iotas(strip.shape[1], width)
    for flip, out in by_flip(outs):
        base, after, first = column_place(info, slots, depth_index ^ flip, width, columns)
        for comp in range(2):
            out[comp] = jnp.where(
                lane >= first,
                strip[comp, :, pl.ds(base, width)].astype(f32),
                strip[comp, :, pl.ds(after, width)].astype(f32),
            ).astype(bf16)


def edge_kernel(slots, width, info, across, beside, *outs):
    depth_index = lax.axis_index("depth")
    even = lax.rem(lax.axis_index("scan"), 2) == 0
    columns = across.shape[-1]
    row, lane = iotas(across.shape[1], width)
    for flip, out in by_flip(outs):
        slot = depth_index ^ flip
        base, after, first = column_place(info, slots, slot, width, columns)
        from_across = jnp.logical_xor(row < info[slot], even)

        def rows_at(comp, place):
            return jnp.where(
                from_across,
                across[comp, :, pl.ds(place, width)].astype(f32),
                beside[comp, :, pl.ds(place, width)].astype(f32),
            )

        for comp in range(2):
            out[comp] = jnp.where(
                lane >= first, rows_at(comp, base), rows_at(comp, after)
            ).astype(bf16)


def frequency_kernel(phase, order, order_t, measured, prop_re, prop_im, amplitude):
    def reorder(value):
        rows = jnp.dot(
            order[...], value, preferred_element_type=f32, precision=lax.Precision.HIGHEST
        )
        return jnp.dot(
            rows, order_t[...], preferred_element_type=f32, precision=lax.Precision.HIGHEST
        )

    turned = reorder(phase[...])
    prop_re[...] = jnp.cos(turned)
    prop_im[...] = jnp.sin(turned)
    amplitude[...] = reorder(measured[lax.axis_index("depth")]).astype(bf16)


def table_kernel(slots, info, stack, stack_t, probe, psi0, *tables):
    depth_index = lax.axis_index("depth")
    pixels = probe.shape[-1]
    half = pixels // 2
    row_shift = info[depth_index]
    col_shift = lax.rem(info[slots + depth_index], pixels)

    def shift_matrix(rows, cols, shift, transposed):
        row, lane = iotas(rows, cols)
        offset = (lane - row if transposed else row - lane) + shift
        return jnp.where((offset == 0) | (offset == pixels), 1.0, 0.0).astype(bf16)

    def pair(shift):
        cols = jnp.dot(
            stack[...], shift_matrix(pixels, half, shift, False), preferred_element_type=f32
        )
        rows = jnp.dot(
            shift_matrix(half, pixels, shift, True), stack_t[...], preferred_element_type=f32
        )
        forms, forms_t = [], []
        for parity in range(2):
            at = 2 * parity * half
            re, im = cols[at : at + half], cols[at + half : at + pixels]
            top = jnp.concatenate([re, -im], axis=1)
            bottom = jnp.concatenate([im, re], axis=1)
            forms.append(jnp.concatenate([top, bottom], axis=0).astype(bf16))
            re, im = rows[:, at : at + half], rows[:, at + half : at + pixels]
            top = jnp.concatenate([re, im], axis=1)
            bottom = jnp.concatenate([-im, re], axis=1)
            forms_t.append(jnp.concatenate([top, bottom], axis=0).astype(bf16))
        return forms, forms_t

    row_forms, row_forms_t = pair(row_shift)
    col_forms, col_forms_t = pair(col_shift)
    made = row_forms + col_forms_t + col_forms + row_forms_t
    for ref, value in zip(tables, made):
        ref[...] = value
    down = shift_matrix(pixels, pixels, row_shift, True)
    across = shift_matrix(pixels, pixels, col_shift, False)
    for comp in range(2):
        moved = jnp.dot(down, probe[comp].astype(bf16), preferred_element_type=f32).astype(bf16)
        psi0[comp] = jnp.dot(moved, across, preferred_element_type=f32).astype(bf16)


def wave_kernel(slots, depth_count, info, prop_re, prop_im, amplitude, psi0, *refs):
    tables = refs[:8]
    centers = refs[8 : 8 + depth_count]
    edges = refs[8 + depth_count : 8 + 2 * depth_count]
    out_centers = refs[8 + 2 * depth_count : 8 + 3 * depth_count]
    out_edges = refs[8 + 3 * depth_count : 8 + 4 * depth_count]
    patches, waves, adjoint, grads = refs[8 + 4 * depth_count :]
    depth_index = lax.axis_index("depth")
    pixels = psi0.shape[-1]
    half = pixels // 2
    live = depth_index < info[2 * slots]
    fwd_row_e, fwd_row_o, fwd_col_e, fwd_col_o, inv_col_e, inv_col_o, inv_row_e, inv_row_o = tables

    def dot(left, right):
        return jnp.dot(left, right, preferred_element_type=f32)

    def propagate(x_re, x_im, at_frequency):
        def rows_of(sign):
            mixed = [v[:half] + v[half:] if sign > 0 else v[:half] - v[half:] for v in (x_re, x_im)]
            return jnp.concatenate(mixed, axis=0).astype(bf16)

        u_even = dot(fwd_row_e[...], rows_of(1))
        u_odd = dot(fwd_row_o[...], rows_of(-1))

        def cols_of(sign):
            parts = []
            for u in (u_even, u_odd):
                mixed = u[:, :half] + u[:, half:] if sign > 0 else u[:, :half] - u[:, half:]
                parts.append(jnp.concatenate([mixed[:half], mixed[half:]], axis=1))
            return jnp.concatenate(parts, axis=0).astype(bf16)

        v_even = dot(cols_of(1), fwd_col_e[...])
        v_odd = dot(cols_of(-1), fwd_col_o[...])
        b_even = at_frequency(v_even[:, :half], v_even[:, half:], slice(0, half))
        b_odd = at_frequency(v_odd[:, :half], v_odd[:, half:], slice(half, pixels))
        w_even = dot(jnp.concatenate(b_even, axis=1).astype(bf16), inv_col_e[...])
        w_odd = dot(jnp.concatenate(b_odd, axis=1).astype(bf16), inv_col_o[...])
        w_low, w_high = w_even + w_odd, w_even - w_odd
        w_re = jnp.concatenate([w_low[:, :half], w_high[:, :half]], axis=1)
        w_im = jnp.concatenate([w_low[:, half:], w_high[:, half:]], axis=1)
        y_even = dot(
            inv_row_e[...], jnp.concatenate([w_re[:half], w_im[:half]], axis=0).astype(bf16)
        )
        y_odd = dot(
            inv_row_o[...], jnp.concatenate([w_re[half:], w_im[half:]], axis=0).astype(bf16)
        )
        low, high = y_even + y_odd, y_even - y_odd
        return (
            jnp.concatenate([low[:half], high[:half]], axis=0),
            jnp.concatenate([low[half:], high[half:]], axis=0),
        )

    def turn(re, im, cols):
        p_re, p_im = prop_re[:, cols], prop_im[:, cols]
        return [re * p_re - im * p_im, re * p_im + im * p_re]

    def turn_back(re, im, cols):
        p_re, p_im = prop_re[:, cols], prop_im[:, cols]
        return [re * p_re + im * p_im, im * p_re - re * p_im]

    def residual(re, im, cols):
        factor = 1.0 - amplitude[:, cols].astype(f32) * lax.rsqrt(re * re + im * im + epsilon)
        return [factor * re, factor * im]

    def pair_of(ref, index):
        return ref[index, 0].astype(f32), ref[index, 1].astype(f32)

    @pl.when(live)
    def _():
        for (flip, center), edge in zip(by_flip(centers), edges):
            patches[depth_index ^ flip, :, half:] = center[...]
            patches[depth_index ^ flip, :, :half] = edge[...]
        waves[0] = psi0[...]

        def forward(k, carry):
            t_re, t_im = pair_of(patches, k)
            p_re, p_im = pair_of(waves, k)
            n_re, n_im = propagate(t_re * p_re - t_im * p_im, t_re * p_im + t_im * p_re, turn)
            waves[k + 1, 0] = n_re.astype(bf16)
            waves[k + 1, 1] = n_im.astype(bf16)
            return carry

        lax.fori_loop(0, depth_count, forward, 0)
        l_re, l_im = propagate(*pair_of(waves, depth_count), residual)
        adjoint[0, 0] = l_re.astype(bf16)
        adjoint[0, 1] = l_im.astype(bf16)

        def backward(step, carry):
            k = depth_count - 1 - step
            m_re, m_im = propagate(*pair_of(adjoint, 0), turn_back)
            t_re, t_im = pair_of(patches, k)
            p_re, p_im = pair_of(waves, k)
            grads[k ^ depth_index, 0] = (p_re * m_re + p_im * m_im).astype(bf16)
            grads[k ^ depth_index, 1] = (p_re * m_im - p_im * m_re).astype(bf16)
            adjoint[0, 0] = (t_re * m_re + t_im * m_im).astype(bf16)
            adjoint[0, 1] = (t_re * m_im - t_im * m_re).astype(bf16)
            return carry

        lax.fori_loop(0, depth_count, backward, 0)
        for (flip, center), edge in zip(by_flip(out_centers), out_edges):
            center[...] = grads[flip, :, half:]
            edge[...] = grads[flip, :, :half]

    @pl.when(jnp.logical_not(live))
    def _():
        for ref in out_centers + out_edges:
            ref[...] = jnp.zeros(ref.shape, ref.dtype)


class Chosen:
    def __init__(self, first, info, others):
        self.first, self.info, self.others = first, info, others

    def __getitem__(self, at):
        return jnp.where(self.first, self.info[at], self.others[at])


def stack_kernel(*refs):
    pieces, (others, stacked) = refs[:-2], refs[-2:]
    for at, piece in enumerate(pieces):
        stacked[at] = piece[...]
        if at:
            others[at - 1] = piece[...]


def place(sheet, comp, at, value, base, after, to_base):
    width = value.shape[-1]
    sheet[comp, at, pl.ds(base, width)] += jnp.where(to_base, value, 0.0)
    sheet[comp, at, pl.ds(after, width)] += jnp.where(to_base, 0.0, value)


def place_edge(sheet, comp, at, piece, info, slots, slot, upper):
    value = piece[at].astype(f32)
    row, lane = iotas(*value.shape)
    base, after, first = column_place(info, slots, slot, value.shape[-1], sheet.shape[-1])
    here = jnp.logical_xor(row + at.start < info[slot], upper)
    place(sheet, comp, at, jnp.where(here, value, 0.0), base, after, lane >= first)


def place_beside_kernel(slots, own_info, second, far_own, beside, sheet):
    depth_index = lax.axis_index("depth")
    even = lax.rem(lax.axis_index("scan"), 2) == 0
    odd = jnp.logical_not(even)
    near_info = Chosen(even, own_info, second)
    far_info = Chosen(odd, own_info, second)
    whole = slice(0, sheet.shape[1])
    sheet[...] = jnp.zeros(sheet.shape, f32)
    for comp in range(2):
        place_edge(sheet, comp, whole, far_own.at[comp], far_info, slots, depth_index, odd)
        for at, (flip, _) in enumerate(by_flip(range(beside.shape[0]))):
            slot = depth_index ^ flip
            place_edge(sheet, comp, whole, beside.at[at, comp], near_info, slots, slot, even)


def place_center_kernel(slots, info, before, *refs):
    pieces, sheet = refs[:-1], refs[-1]
    depth_index = lax.axis_index("depth")
    columns = sheet.shape[-1]
    rows, width = pieces[0].shape[1:]
    _, lane = iotas(rows, width)
    sheet[...] = before[...]
    for flip, piece in by_flip(pieces):
        base, after, first = column_place(info, slots, depth_index ^ flip, width, columns)
        for comp in range(2):
            value = piece[comp].astype(f32)
            place(sheet, comp, slice(0, rows), value, base, after, lane >= first)


def place_far_kernel(slots, own_info, second, sheet, others, out, total, sems):
    depth_index = lax.axis_index("depth")
    odd = lax.rem(lax.axis_index("scan"), 2) == 1
    far_info = Chosen(odd, own_info, second)
    rows = sheet.shape[1] // 2
    copies = []
    for comp in range(2):
        for part in range(2):
            here = slice(part * rows, (part + 1) * rows)
            total[comp, here] = sheet[comp, here]
            for at, (flip, _) in enumerate(by_flip(range(others.shape[0] + 1))[1:]):
                slot = depth_index ^ flip
                place_edge(total, comp, here, others.at[at, comp], far_info, slots, slot, odd)
            copies.append(
                pltpu.make_async_copy(
                    total.at[comp, here], out.at[comp, here], sems.at[2 * comp + part]
                )
            )
            copies[-1].start()
    for copy in copies:
        copy.wait()


def body(transmission, probe_wave, prop_phase, measured, scan_rows, scan_cols, live_counts):
    pixels = probe_wave.shape[-1]
    slots = measured.shape[0]
    rows = transmission.shape[2]
    columns = transmission.shape[3]
    count = lax.axis_size("depth")
    own = transmission[0]
    own_info = jnp.concatenate([scan_rows, scan_cols, live_counts])
    ints = own_info.shape[0]
    info = shifted(jnp.pad(own_info, (0, INFO_SIZE - ints)), "scan", 1)[:ints]
    strip = call(strip_kernel, sds(own.shape, bf16), [own], [VMEM], name="strip")
    across = swapped(strip, "scan", 1)
    info, later_strip = lax.optimization_barrier((info, strip))
    beside = swapped(later_strip, "scan", 0)

    part = sds((2, rows, pixels), bf16)
    centers = call(
        functools.partial(center_kernel, slots, pixels),
        [part] * count, [info, strip], [SMEM, VMEM], name="cut_center",
    )

    def across_depth(pieces):
        return [pieces[0]] + [exchanged(piece, "depth", flip) for flip, piece in by_flip(pieces)[1:]]

    centers = across_depth(centers)

    phase, centers[0] = lax.optimization_barrier((prop_phase, centers[0]))
    order = parity_order(pixels)
    square = sds((pixels, pixels), f32)
    prop_re, prop_im, amplitude = call(
        frequency_kernel,
        [square, square, sds((pixels, pixels), bf16)],
        [phase, jnp.asarray(order), jnp.asarray(order.T), measured],
        [VMEM] * 4, flops=2400 * pixels**3, transcendentals=2 * pixels**2, name="frequency_order",
    )
    amplitude, centers[1] = lax.optimization_barrier((amplitude, centers[1]))
    amplitude = shifted(amplitude, "scan", 1)

    stack = split_tables(pixels)
    made = call(
        functools.partial(table_kernel, slots),
        [sds((2, pixels, pixels), bf16)] + [sds((pixels, pixels), bf16)] * 8,
        [info, jnp.asarray(stack), jnp.asarray(stack.T), probe_wave],
        [SMEM, VMEM, VMEM, VMEM], flops=16 * pixels**3, name="tables",
    )
    edges = call(
        functools.partial(edge_kernel, slots, pixels),
        [part] * count, [info, across, beside], [SMEM, VMEM, VMEM], name="cut_edges",
    )
    edges = across_depth(edges)

    args = [info, prop_re, prop_im, amplitude, *made, *centers, *edges]
    grads = call(
        functools.partial(wave_kernel, slots, count),
        [part] * (2 * count), args, [SMEM] + [VMEM] * (len(args) - 1),
        scratch=[
            pltpu.VMEM((count, 2, pixels, pixels), bf16),
            pltpu.VMEM((count + 1, 2, pixels, pixels), bf16),
            pltpu.VMEM((1, 2, pixels, pixels), bf16),
            pltpu.VMEM((count, 2, pixels, pixels), bf16),
        ],
        flops=(2 * count + 1) * 16 * pixels**3, name="waves",
    )
    out_centers, out_edges = grads[:count], grads[count:]
    far_own = swapped(out_edges[0], "scan", 1)
    second, far_own = lax.optimization_barrier((own_info, far_own))
    second = shifted(second, "scan", 2)
    out_edges = across_depth(out_edges)
    second, out_edges = lax.optimization_barrier((second, out_edges))
    others, stacked = call(
        stack_kernel, [sds((at, 2, rows, pixels), bf16) for at in (count - 1, count)],
        out_edges, [VMEM] * count, name="stack_edges",
    )
    far_others = swapped(others, "scan", 1)
    beside = swapped(stacked, "scan", 0)
    out_centers, stacked = lax.optimization_barrier((out_centers, stacked))
    out_centers = across_depth(out_centers)
    sheet_f32 = sds((2, rows, columns), f32)
    sheet = call(
        functools.partial(place_beside_kernel, slots),
        sheet_f32, [own_info, second, far_own, beside], [SMEM] * 2 + [VMEM] * 2,
        name="place_beside",
    )
    sheet = call(
        functools.partial(place_center_kernel, slots),
        sheet_f32, [info, sheet, *out_centers], [SMEM] + [VMEM] * (count + 1),
        name="place_center",
    )
    gradient = pl.pallas_call(
        functools.partial(place_far_kernel, slots),
        out_shape=sheet_f32,
        in_specs=[SMEM] * 2 + [VMEM] * 2,
        out_specs=pl.BlockSpec(memory_space=pl.ANY),
        scratch_shapes=[pltpu.VMEM(sheet_f32.shape, f32), pltpu.SemaphoreType.DMA((4,))],
        compiler_params=pltpu.CompilerParams(vmem_limit_bytes=LIMIT),
        name="place_far",
    )(own_info, second, sheet, far_others)
    return gradient[None]


def solution(mesh):
    in_specs = (
        P("depth", None, "scan", None),
        P(),
        P(),
        P("scan", None, None),
        P("scan"),
        P("scan"),
        P("scan"),
    )
    out_specs = P("depth", None, "scan", None)
    return jax.shard_map(body, mesh=mesh, in_specs=in_specs, out_specs=out_specs, check_vma=False)
```

```python
import functools
import math

import jax
import jax.numpy as jnp
import ml_dtypes
import numpy as np
from jax import lax
from jax.experimental import pallas as pl
from jax.experimental.pallas import tpu as pltpu
from jax.sharding import PartitionSpec as P

epsilon = 1.0
bf16 = jnp.bfloat16
f32 = jnp.float32
VMEM = pl.BlockSpec(memory_space=pltpu.VMEM)
SMEM = pl.BlockSpec(memory_space=pltpu.SMEM)
LIMIT = 48 * 1024 * 1024
INFO_SIZE = 8192


def shifted(value, axis, steps):
    count = lax.axis_size(axis)
    pairs = [(source, (source + steps) % count) for source in range(count)]
    return lax.ppermute(value, axis, pairs)


def swapped(value, axis, first):
    count = lax.axis_size(axis)
    pairs = [
        (source, (source + (1 if source % 2 == first else -1)) % count) for source in range(count)
    ]
    return lax.ppermute(value, axis, pairs)


def exchanged(value, axis, flip):
    count = lax.axis_size(axis)
    return lax.ppermute(value, axis, [(source, source ^ flip) for source in range(count)])


def split_tables(pixels):
    indices = np.arange(pixels)
    angles = (indices[:, None] * indices[None, :] % pixels) * (2.0 * math.pi / pixels)
    norm_scale = 1.0 / math.sqrt(pixels)
    table_re = (np.cos(angles) * norm_scale).astype(np.float32).astype(ml_dtypes.bfloat16)
    table_im = (-np.sin(angles) * norm_scale).astype(np.float32).astype(ml_dtypes.bfloat16)
    return np.concatenate([table_re[0::2], table_im[0::2], table_re[1::2], table_im[1::2]], axis=0)


def parity_order(pixels):
    order = np.concatenate([np.arange(0, pixels, 2), np.arange(1, pixels, 2)])
    return (order[:, None] == np.arange(pixels)[None, :]).astype(np.float32)


def call(kernel, out_shape, args, specs, scratch=(), flops=0, transcendentals=0, name=None):
    outs = out_shape if isinstance(out_shape, (list, tuple)) else [out_shape]
    moved = sum(math.prod(a.shape) * a.dtype.itemsize for a in list(args) + list(outs))
    return pl.pallas_call(
        kernel,
        out_shape=out_shape,
        in_specs=specs,
        out_specs=jax.tree.map(lambda _: VMEM, out_shape),
        scratch_shapes=list(scratch),
        compiler_params=pltpu.CompilerParams(vmem_limit_bytes=LIMIT),
        cost_estimate=pl.CostEstimate(
            flops=flops, bytes_accessed=moved, transcendentals=transcendentals
        ),
        name=name,
    )(*args)


def sds(shape, dtype):
    return jax.ShapeDtypeStruct(shape, dtype)


def by_flip(pieces):
    return list(zip([0, *range(len(pieces) - 1, 0, -1)], pieces))


def column_place(info, slots, slot, width, columns):
    col = info[slots + slot]
    base = (col // width) * width
    after = jnp.minimum(base + width, columns - width)
    return pl.multiple_of(base, width), pl.multiple_of(after, width), col - base


def iotas(rows, cols):
    return (
        lax.broadcasted_iota(jnp.int32, (rows, cols), 0),
        lax.broadcasted_iota(jnp.int32, (rows, cols), 1),
    )


def strip_kernel(own, strip):
    strip[...] = own[...].astype(bf16)


def center_kernel(slots, width, info, strip, *outs):
    depth_index = lax.axis_index("depth")
    columns = strip.shape[-1]
    _, lane = iotas(strip.shape[1], width)
    for flip, out in by_flip(outs):
        base, after, first = column_place(info, slots, depth_index ^ flip, width, columns)
        for comp in range(2):
            out[comp] = jnp.where(
                lane >= first,
                strip[comp, :, pl.ds(base, width)].astype(f32),
                strip[comp, :, pl.ds(after, width)].astype(f32),
            ).astype(bf16)


def edge_kernel(slots, width, info, across, beside, *outs):
    depth_index = lax.axis_index("depth")
    even = lax.rem(lax.axis_index("scan"), 2) == 0
    columns = across.shape[-1]
    row, lane = iotas(across.shape[1], width)
    for flip, out in by_flip(outs):
        slot = depth_index ^ flip
        base, after, first = column_place(info, slots, slot, width, columns)
        from_across = jnp.logical_xor(row < info[slot], even)

        def rows_at(comp, place):
            return jnp.where(
                from_across,
                across[comp, :, pl.ds(place, width)].astype(f32),
                beside[comp, :, pl.ds(place, width)].astype(f32),
            )

        for comp in range(2):
            out[comp] = jnp.where(
                lane >= first, rows_at(comp, base), rows_at(comp, after)
            ).astype(bf16)


def frequency_kernel(phase, order, order_t, measured, prop_re, prop_im, amplitude):
    def reorder(value):
        rows = jnp.dot(
            order[...], value, preferred_element_type=f32, precision=lax.Precision.HIGHEST
        )
        return jnp.dot(
            rows, order_t[...], preferred_element_type=f32, precision=lax.Precision.HIGHEST
        )

    turned = reorder(phase[...])
    prop_re[...] = jnp.cos(turned)
    prop_im[...] = jnp.sin(turned)
    amplitude[...] = reorder(measured[lax.axis_index("depth")]).astype(bf16)


def table_kernel(slots, info, stack, stack_t, probe, psi0, *tables):
    depth_index = lax.axis_index("depth")
    pixels = probe.shape[-1]
    half = pixels // 2
    row_shift = info[depth_index]
    col_shift = lax.rem(info[slots + depth_index], pixels)

    def shift_matrix(rows, cols, shift, transposed):
        row, lane = iotas(rows, cols)
        offset = (lane - row if transposed else row - lane) + shift
        return jnp.where((offset == 0) | (offset == pixels), 1.0, 0.0).astype(bf16)

    def pair(shift):
        cols = jnp.dot(
            stack[...], shift_matrix(pixels, half, shift, False), preferred_element_type=f32
        )
        rows = jnp.dot(
            shift_matrix(half, pixels, shift, True), stack_t[...], preferred_element_type=f32
        )
        forms, forms_t = [], []
        for parity in range(2):
            at = 2 * parity * half
            re, im = cols[at : at + half], cols[at + half : at + pixels]
            top = jnp.concatenate([re, -im], axis=1)
            bottom = jnp.concatenate([im, re], axis=1)
            forms.append(jnp.concatenate([top, bottom], axis=0).astype(bf16))
            re, im = rows[:, at : at + half], rows[:, at + half : at + pixels]
            top = jnp.concatenate([re, im], axis=1)
            bottom = jnp.concatenate([-im, re], axis=1)
            forms_t.append(jnp.concatenate([top, bottom], axis=0).astype(bf16))
        return forms, forms_t

    row_forms, row_forms_t = pair(row_shift)
    col_forms, col_forms_t = pair(col_shift)
    made = row_forms + col_forms_t + col_forms + row_forms_t
    for ref, value in zip(tables, made):
        ref[...] = value
    down = shift_matrix(pixels, pixels, row_shift, True)
    across = shift_matrix(pixels, pixels, col_shift, False)
    for comp in range(2):
        moved = jnp.dot(down, probe[comp].astype(bf16), preferred_element_type=f32).astype(bf16)
        psi0[comp] = jnp.dot(moved, across, preferred_element_type=f32).astype(bf16)


def wave_kernel(slots, depth_count, info, prop_re, prop_im, amplitude, psi0, *refs):
    tables = refs[:8]
    centers = refs[8 : 8 + depth_count]
    edges = refs[8 + depth_count : 8 + 2 * depth_count]
    out_centers = refs[8 + 2 * depth_count : 8 + 3 * depth_count]
    out_edges = refs[8 + 3 * depth_count : 8 + 4 * depth_count]
    patches, waves, adjoint, grads = refs[8 + 4 * depth_count :]
    depth_index = lax.axis_index("depth")
    pixels = psi0.shape[-1]
    half = pixels // 2
    live = depth_index < info[2 * slots]
    fwd_row_e, fwd_row_o, fwd_col_e, fwd_col_o, inv_col_e, inv_col_o, inv_row_e, inv_row_o = tables

    def dot(left, right):
        return jnp.dot(left, right, preferred_element_type=f32)

    def propagate(x_re, x_im, at_frequency):
        def rows_of(sign):
            mixed = [v[:half] + v[half:] if sign > 0 else v[:half] - v[half:] for v in (x_re, x_im)]
            return jnp.concatenate(mixed, axis=0).astype(bf16)

        u_even = dot(fwd_row_e[...], rows_of(1))
        u_odd = dot(fwd_row_o[...], rows_of(-1))

        def cols_of(sign):
            parts = []
            for u in (u_even, u_odd):
                mixed = u[:, :half] + u[:, half:] if sign > 0 else u[:, :half] - u[:, half:]
                parts.append(jnp.concatenate([mixed[:half], mixed[half:]], axis=1))
            return jnp.concatenate(parts, axis=0).astype(bf16)

        v_even = dot(cols_of(1), fwd_col_e[...])
        v_odd = dot(cols_of(-1), fwd_col_o[...])
        b_even = at_frequency(v_even[:, :half], v_even[:, half:], slice(0, half))
        b_odd = at_frequency(v_odd[:, :half], v_odd[:, half:], slice(half, pixels))
        w_even = dot(jnp.concatenate(b_even, axis=1).astype(bf16), inv_col_e[...])
        w_odd = dot(jnp.concatenate(b_odd, axis=1).astype(bf16), inv_col_o[...])
        w_low, w_high = w_even + w_odd, w_even - w_odd
        w_re = jnp.concatenate([w_low[:, :half], w_high[:, :half]], axis=1)
        w_im = jnp.concatenate([w_low[:, half:], w_high[:, half:]], axis=1)
        y_even = dot(
            inv_row_e[...], jnp.concatenate([w_re[:half], w_im[:half]], axis=0).astype(bf16)
        )
        y_odd = dot(
            inv_row_o[...], jnp.concatenate([w_re[half:], w_im[half:]], axis=0).astype(bf16)
        )
        low, high = y_even + y_odd, y_even - y_odd
        return (
            jnp.concatenate([low[:half], high[:half]], axis=0),
            jnp.concatenate([low[half:], high[half:]], axis=0),
        )

    def turn(re, im, cols):
        p_re, p_im = prop_re[:, cols], prop_im[:, cols]
        return [re * p_re - im * p_im, re * p_im + im * p_re]

    def turn_back(re, im, cols):
        p_re, p_im = prop_re[:, cols], prop_im[:, cols]
        return [re * p_re + im * p_im, im * p_re - re * p_im]

    def residual(re, im, cols):
        factor = 1.0 - amplitude[:, cols].astype(f32) * lax.rsqrt(re * re + im * im + epsilon)
        return [factor * re, factor * im]

    def pair_of(ref, index):
        return ref[index, 0].astype(f32), ref[index, 1].astype(f32)

    @pl.when(live)
    def _():
        for (flip, center), edge in zip(by_flip(centers), edges):
            patches[depth_index ^ flip, :, half:] = center[...]
            patches[depth_index ^ flip, :, :half] = edge[...]
        waves[0] = psi0[...]

        def forward(k, carry):
            t_re, t_im = pair_of(patches, k)
            p_re, p_im = pair_of(waves, k)
            n_re, n_im = propagate(t_re * p_re - t_im * p_im, t_re * p_im + t_im * p_re, turn)
            waves[k + 1, 0] = n_re.astype(bf16)
            waves[k + 1, 1] = n_im.astype(bf16)
            return carry

        lax.fori_loop(0, depth_count, forward, 0)
        l_re, l_im = propagate(*pair_of(waves, depth_count), residual)
        adjoint[0, 0] = l_re.astype(bf16)
        adjoint[0, 1] = l_im.astype(bf16)

        def backward(step, carry):
            k = depth_count - 1 - step
            m_re, m_im = propagate(*pair_of(adjoint, 0), turn_back)
            t_re, t_im = pair_of(patches, k)
            p_re, p_im = pair_of(waves, k)
            grads[k ^ depth_index, 0] = (p_re * m_re + p_im * m_im).astype(bf16)
            grads[k ^ depth_index, 1] = (p_re * m_im - p_im * m_re).astype(bf16)
            adjoint[0, 0] = (t_re * m_re + t_im * m_im).astype(bf16)
            adjoint[0, 1] = (t_re * m_im - t_im * m_re).astype(bf16)
            return carry

        lax.fori_loop(0, depth_count, backward, 0)
        for (flip, center), edge in zip(by_flip(out_centers), out_edges):
            center[...] = grads[flip, :, half:]
            edge[...] = grads[flip, :, :half]

    @pl.when(jnp.logical_not(live))
    def _():
        for ref in out_centers + out_edges:
            ref[...] = jnp.zeros(ref.shape, ref.dtype)


class Chosen:
    def __init__(self, first, info, others):
        self.first, self.info, self.others = first, info, others

    def __getitem__(self, at):
        return jnp.where(self.first, self.info[at], self.others[at])


def stack_kernel(*refs):
    pieces, (others, stacked) = refs[:-2], refs[-2:]
    for at, piece in enumerate(pieces):
        stacked[at] = piece[...]
        if at:
            others[at - 1] = piece[...]


def place(sheet, comp, at, value, base, after, to_base):
    width = value.shape[-1]
    sheet[comp, at, pl.ds(base, width)] += jnp.where(to_base, value, 0.0)
    sheet[comp, at, pl.ds(after, width)] += jnp.where(to_base, 0.0, value)


def place_edge(sheet, comp, at, piece, info, slots, slot, upper):
    value = piece[at].astype(f32)
    row, lane = iotas(*value.shape)
    base, after, first = column_place(info, slots, slot, value.shape[-1], sheet.shape[-1])
    here = jnp.logical_xor(row + at.start < info[slot], upper)
    place(sheet, comp, at, jnp.where(here, value, 0.0), base, after, lane >= first)


def place_beside_kernel(slots, own_info, second, far_own, beside, sheet):
    depth_index = lax.axis_index("depth")
    even = lax.rem(lax.axis_index("scan"), 2) == 0
    odd = jnp.logical_not(even)
    near_info = Chosen(even, own_info, second)
    far_info = Chosen(odd, own_info, second)
    whole = slice(0, sheet.shape[1])
    sheet[...] = jnp.zeros(sheet.shape, f32)
    for comp in range(2):
        place_edge(sheet, comp, whole, far_own.at[comp], far_info, slots, depth_index, odd)
        for at, (flip, _) in enumerate(by_flip(range(beside.shape[0]))):
            slot = depth_index ^ flip
            place_edge(sheet, comp, whole, beside.at[at, comp], near_info, slots, slot, even)


def place_center_kernel(slots, info, before, *refs):
    pieces, sheet = refs[:-1], refs[-1]
    depth_index = lax.axis_index("depth")
    columns = sheet.shape[-1]
    rows, width = pieces[0].shape[1:]
    _, lane = iotas(rows, width)
    sheet[...] = before[...]
    for flip, piece in by_flip(pieces):
        base, after, first = column_place(info, slots, depth_index ^ flip, width, columns)
        for comp in range(2):
            value = piece[comp].astype(f32)
            place(sheet, comp, slice(0, rows), value, base, after, lane >= first)


def place_far_kernel(slots, own_info, second, sheet, others, out, total, sems):
    depth_index = lax.axis_index("depth")
    odd = lax.rem(lax.axis_index("scan"), 2) == 1
    far_info = Chosen(odd, own_info, second)
    rows = sheet.shape[1] // 2
    copies = []
    for comp in range(2):
        for part in range(2):
            here = slice(part * rows, (part + 1) * rows)
            total[comp, here] = sheet[comp, here]
            for at, (flip, _) in enumerate(by_flip(range(others.shape[0] + 1))[1:]):
                slot = depth_index ^ flip
                place_edge(total, comp, here, others.at[at, comp], far_info, slots, slot, odd)
            copies.append(
                pltpu.make_async_copy(
                    total.at[comp, here], out.at[comp, here], sems.at[2 * comp + part]
                )
            )
            copies[-1].start()
    for copy in copies:
        copy.wait()


def body(transmission, probe_wave, prop_phase, measured, scan_rows, scan_cols, live_counts):
    pixels = probe_wave.shape[-1]
    slots = measured.shape[0]
    rows = transmission.shape[2]
    columns = transmission.shape[3]
    count = lax.axis_size("depth")
    own = transmission[0]
    own_info = jnp.concatenate([scan_rows, scan_cols, live_counts])
    ints = own_info.shape[0]
    info = shifted(jnp.pad(own_info, (0, INFO_SIZE - ints)), "scan", 1)[:ints]
    strip = call(strip_kernel, sds(own.shape, bf16), [own], [VMEM], name="strip")
    across = swapped(strip, "scan", 1)
    info, later_strip = lax.optimization_barrier((info, strip))
    beside = swapped(later_strip, "scan", 0)

    part = sds((2, rows, pixels), bf16)
    centers = call(
        functools.partial(center_kernel, slots, pixels),
        [part] * count, [info, strip], [SMEM, VMEM], name="cut_center",
    )

    def across_depth(pieces):
        return [pieces[0]] + [exchanged(piece, "depth", flip) for flip, piece in by_flip(pieces)[1:]]

    centers = across_depth(centers)

    phase, centers[0] = lax.optimization_barrier((prop_phase, centers[0]))
    order = parity_order(pixels)
    square = sds((pixels, pixels), f32)
    prop_re, prop_im, amplitude = call(
        frequency_kernel,
        [square, square, sds((pixels, pixels), bf16)],
        [phase, jnp.asarray(order), jnp.asarray(order.T), measured],
        [VMEM] * 4, flops=2400 * pixels**3, transcendentals=2 * pixels**2, name="frequency_order",
    )
    amplitude, centers[1] = lax.optimization_barrier((amplitude, centers[1]))
    amplitude = shifted(amplitude, "scan", 1)

    stack = split_tables(pixels)
    made = call(
        functools.partial(table_kernel, slots),
        [sds((2, pixels, pixels), bf16)] + [sds((pixels, pixels), bf16)] * 8,
        [info, jnp.asarray(stack), jnp.asarray(stack.T), probe_wave],
        [SMEM, VMEM, VMEM, VMEM], flops=16 * pixels**3, name="tables",
    )
    edges = call(
        functools.partial(edge_kernel, slots, pixels),
        [part] * count, [info, across, beside], [SMEM, VMEM, VMEM], name="cut_edges",
    )
    edges = across_depth(edges)

    args = [info, prop_re, prop_im, amplitude, *made, *centers, *edges]
    grads = call(
        functools.partial(wave_kernel, slots, count),
        [part] * (2 * count), args, [SMEM] + [VMEM] * (len(args) - 1),
        scratch=[
            pltpu.VMEM((count, 2, pixels, pixels), bf16),
            pltpu.VMEM((count + 1, 2, pixels, pixels), bf16),
            pltpu.VMEM((1, 2, pixels, pixels), bf16),
            pltpu.VMEM((count, 2, pixels, pixels), bf16),
        ],
        flops=(2 * count + 1) * 16 * pixels**3, name="waves",
    )
    out_centers, out_edges = grads[:count], grads[count:]
    far_own = swapped(out_edges[0], "scan", 1)
    second, out_edges = lax.optimization_barrier((own_info, out_edges))
    second = shifted(second, "scan", 2)
    out_edges = across_depth(out_edges)
    far_own, second, out_edges = lax.optimization_barrier((far_own, second, out_edges))
    others, stacked = call(
        stack_kernel, [sds((at, 2, rows, pixels), bf16) for at in (count - 1, count)],
        out_edges, [VMEM] * count, name="stack_edges",
    )
    far_others = swapped(others, "scan", 1)
    beside = swapped(stacked, "scan", 0)
    out_centers, stacked = lax.optimization_barrier((out_centers, stacked))
    out_centers = across_depth(out_centers)
    sheet_f32 = sds((2, rows, columns), f32)
    sheet = call(
        functools.partial(place_beside_kernel, slots),
        sheet_f32, [own_info, second, far_own, beside], [SMEM] * 2 + [VMEM] * 2,
        name="place_beside",
    )
    sheet = call(
        functools.partial(place_center_kernel, slots),
        sheet_f32, [info, sheet, *out_centers], [SMEM] + [VMEM] * (count + 1),
        name="place_center",
    )
    gradient = pl.pallas_call(
        functools.partial(place_far_kernel, slots),
        out_shape=sheet_f32,
        in_specs=[SMEM] * 2 + [VMEM] * 2,
        out_specs=pl.BlockSpec(memory_space=pl.ANY),
        scratch_shapes=[pltpu.VMEM(sheet_f32.shape, f32), pltpu.SemaphoreType.DMA((4,))],
        compiler_params=pltpu.CompilerParams(vmem_limit_bytes=LIMIT),
        name="place_far",
    )(own_info, second, sheet, far_others)
    return gradient[None]


def solution(mesh):
    in_specs = (
        P("depth", None, "scan", None),
        P(),
        P(),
        P("scan", None, None),
        P("scan"),
        P("scan"),
        P("scan"),
    )
    out_specs = P("depth", None, "scan", None)
    return jax.shard_map(body, mesh=mesh, in_specs=in_specs, out_specs=out_specs, check_vma=False)
```

```python
import functools
import math

import jax
import jax.numpy as jnp
import ml_dtypes
import numpy as np
from jax import lax
from jax.experimental import pallas as pl
from jax.experimental.pallas import tpu as pltpu
from jax.sharding import PartitionSpec as P

epsilon = 1.0
bf16 = jnp.bfloat16
f32 = jnp.float32
VMEM = pl.BlockSpec(memory_space=pltpu.VMEM)
SMEM = pl.BlockSpec(memory_space=pltpu.SMEM)
LIMIT = 48 * 1024 * 1024
INFO_SIZE = 8192


def shifted(value, axis, steps):
    count = lax.axis_size(axis)
    pairs = [(source, (source + steps) % count) for source in range(count)]
    return lax.ppermute(value, axis, pairs)


def swapped(value, axis, first):
    count = lax.axis_size(axis)
    pairs = [
        (source, (source + (1 if source % 2 == first else -1)) % count) for source in range(count)
    ]
    return lax.ppermute(value, axis, pairs)


def exchanged(value, axis, flip):
    count = lax.axis_size(axis)
    return lax.ppermute(value, axis, [(source, source ^ flip) for source in range(count)])


def split_tables(pixels):
    indices = np.arange(pixels)
    angles = (indices[:, None] * indices[None, :] % pixels) * (2.0 * math.pi / pixels)
    norm_scale = 1.0 / math.sqrt(pixels)
    table_re = (np.cos(angles) * norm_scale).astype(np.float32).astype(ml_dtypes.bfloat16)
    table_im = (-np.sin(angles) * norm_scale).astype(np.float32).astype(ml_dtypes.bfloat16)
    return np.concatenate([table_re[0::2], table_im[0::2], table_re[1::2], table_im[1::2]], axis=0)


def parity_order(pixels):
    order = np.concatenate([np.arange(0, pixels, 2), np.arange(1, pixels, 2)])
    return (order[:, None] == np.arange(pixels)[None, :]).astype(np.float32)


def call(kernel, out_shape, args, specs, scratch=(), flops=0, transcendentals=0, name=None):
    outs = out_shape if isinstance(out_shape, (list, tuple)) else [out_shape]
    moved = sum(math.prod(a.shape) * a.dtype.itemsize for a in list(args) + list(outs))
    return pl.pallas_call(
        kernel,
        out_shape=out_shape,
        in_specs=specs,
        out_specs=jax.tree.map(lambda _: VMEM, out_shape),
        scratch_shapes=list(scratch),
        compiler_params=pltpu.CompilerParams(vmem_limit_bytes=LIMIT),
        cost_estimate=pl.CostEstimate(
            flops=flops, bytes_accessed=moved, transcendentals=transcendentals
        ),
        name=name,
    )(*args)


def sds(shape, dtype):
    return jax.ShapeDtypeStruct(shape, dtype)


def by_flip(pieces):
    return list(zip([0, *range(len(pieces) - 1, 0, -1)], pieces))


def column_place(info, slots, slot, width, columns):
    col = info[slots + slot]
    base = (col // width) * width
    after = jnp.minimum(base + width, columns - width)
    return pl.multiple_of(base, width), pl.multiple_of(after, width), col - base


def iotas(rows, cols):
    return (
        lax.broadcasted_iota(jnp.int32, (rows, cols), 0),
        lax.broadcasted_iota(jnp.int32, (rows, cols), 1),
    )


def strip_kernel(own, strip):
    strip[...] = own[...].astype(bf16)


def center_kernel(slots, width, info, strip, *outs):
    depth_index = lax.axis_index("depth")
    columns = strip.shape[-1]
    _, lane = iotas(strip.shape[1], width)
    for flip, out in by_flip(outs):
        base, after, first = column_place(info, slots, depth_index ^ flip, width, columns)
        for comp in range(2):
            out[comp] = jnp.where(
                lane >= first,
                strip[comp, :, pl.ds(base, width)].astype(f32),
                strip[comp, :, pl.ds(after, width)].astype(f32),
            ).astype(bf16)


def edge_kernel(slots, width, info, across, beside, *outs):
    depth_index = lax.axis_index("depth")
    even = lax.rem(lax.axis_index("scan"), 2) == 0
    columns = across.shape[-1]
    row, lane = iotas(across.shape[1], width)
    for flip, out in by_flip(outs):
        slot = depth_index ^ flip
        base, after, first = column_place(info, slots, slot, width, columns)
        from_across = jnp.logical_xor(row < info[slot], even)

        def rows_at(comp, place):
            return jnp.where(
                from_across,
                across[comp, :, pl.ds(place, width)].astype(f32),
                beside[comp, :, pl.ds(place, width)].astype(f32),
            )

        for comp in range(2):
            out[comp] = jnp.where(
                lane >= first, rows_at(comp, base), rows_at(comp, after)
            ).astype(bf16)


def frequency_kernel(phase, order, order_t, measured, prop_re, prop_im, amplitude):
    def reorder(value):
        rows = jnp.dot(
            order[...], value, preferred_element_type=f32, precision=lax.Precision.HIGHEST
        )
        return jnp.dot(
            rows, order_t[...], preferred_element_type=f32, precision=lax.Precision.HIGHEST
        )

    turned = reorder(phase[...])
    prop_re[...] = jnp.cos(turned)
    prop_im[...] = jnp.sin(turned)
    amplitude[...] = reorder(measured[lax.axis_index("depth")]).astype(bf16)


def table_kernel(slots, info, stack, stack_t, probe, psi0, *tables):
    depth_index = lax.axis_index("depth")
    pixels = probe.shape[-1]
    half = pixels // 2
    row_shift = info[depth_index]
    col_shift = lax.rem(info[slots + depth_index], pixels)

    def shift_matrix(rows, cols, shift, transposed):
        row, lane = iotas(rows, cols)
        offset = (lane - row if transposed else row - lane) + shift
        return jnp.where((offset == 0) | (offset == pixels), 1.0, 0.0).astype(bf16)

    def pair(shift):
        cols = jnp.dot(
            stack[...], shift_matrix(pixels, half, shift, False), preferred_element_type=f32
        )
        rows = jnp.dot(
            shift_matrix(half, pixels, shift, True), stack_t[...], preferred_element_type=f32
        )
        forms, forms_t = [], []
        for parity in range(2):
            at = 2 * parity * half
            re, im = cols[at : at + half], cols[at + half : at + pixels]
            top = jnp.concatenate([re, -im], axis=1)
            bottom = jnp.concatenate([im, re], axis=1)
            forms.append(jnp.concatenate([top, bottom], axis=0).astype(bf16))
            re, im = rows[:, at : at + half], rows[:, at + half : at + pixels]
            top = jnp.concatenate([re, im], axis=1)
            bottom = jnp.concatenate([-im, re], axis=1)
            forms_t.append(jnp.concatenate([top, bottom], axis=0).astype(bf16))
        return forms, forms_t

    row_forms, row_forms_t = pair(row_shift)
    col_forms, col_forms_t = pair(col_shift)
    made = row_forms + col_forms_t + col_forms + row_forms_t
    for ref, value in zip(tables, made):
        ref[...] = value
    down = shift_matrix(pixels, pixels, row_shift, True)
    across = shift_matrix(pixels, pixels, col_shift, False)
    for comp in range(2):
        moved = jnp.dot(down, probe[comp].astype(bf16), preferred_element_type=f32).astype(bf16)
        psi0[comp] = jnp.dot(moved, across, preferred_element_type=f32).astype(bf16)


def wave_kernel(slots, depth_count, info, prop_re, prop_im, amplitude, psi0, *refs):
    tables = refs[:8]
    centers = refs[8 : 8 + depth_count]
    edges = refs[8 + depth_count : 8 + 2 * depth_count]
    out_centers = refs[8 + 2 * depth_count : 8 + 3 * depth_count]
    out_edges = refs[8 + 3 * depth_count : 8 + 4 * depth_count]
    patches, waves, adjoint, grads = refs[8 + 4 * depth_count :]
    depth_index = lax.axis_index("depth")
    pixels = psi0.shape[-1]
    half = pixels // 2
    live = depth_index < info[2 * slots]
    fwd_row_e, fwd_row_o, fwd_col_e, fwd_col_o, inv_col_e, inv_col_o, inv_row_e, inv_row_o = tables

    def dot(left, right):
        return jnp.dot(left, right, preferred_element_type=f32)

    def propagate(x_re, x_im, at_frequency):
        def rows_of(sign):
            mixed = [v[:half] + v[half:] if sign > 0 else v[:half] - v[half:] for v in (x_re, x_im)]
            return jnp.concatenate(mixed, axis=0).astype(bf16)

        u_even = dot(fwd_row_e[...], rows_of(1))
        u_odd = dot(fwd_row_o[...], rows_of(-1))

        def cols_of(sign):
            parts = []
            for u in (u_even, u_odd):
                mixed = u[:, :half] + u[:, half:] if sign > 0 else u[:, :half] - u[:, half:]
                parts.append(jnp.concatenate([mixed[:half], mixed[half:]], axis=1))
            return jnp.concatenate(parts, axis=0).astype(bf16)

        v_even = dot(cols_of(1), fwd_col_e[...])
        v_odd = dot(cols_of(-1), fwd_col_o[...])
        b_even = at_frequency(v_even[:, :half], v_even[:, half:], slice(0, half))
        b_odd = at_frequency(v_odd[:, :half], v_odd[:, half:], slice(half, pixels))
        w_even = dot(jnp.concatenate(b_even, axis=1).astype(bf16), inv_col_e[...])
        w_odd = dot(jnp.concatenate(b_odd, axis=1).astype(bf16), inv_col_o[...])
        w_low, w_high = w_even + w_odd, w_even - w_odd
        w_re = jnp.concatenate([w_low[:, :half], w_high[:, :half]], axis=1)
        w_im = jnp.concatenate([w_low[:, half:], w_high[:, half:]], axis=1)
        y_even = dot(
            inv_row_e[...], jnp.concatenate([w_re[:half], w_im[:half]], axis=0).astype(bf16)
        )
        y_odd = dot(
            inv_row_o[...], jnp.concatenate([w_re[half:], w_im[half:]], axis=0).astype(bf16)
        )
        low, high = y_even + y_odd, y_even - y_odd
        return (
            jnp.concatenate([low[:half], high[:half]], axis=0),
            jnp.concatenate([low[half:], high[half:]], axis=0),
        )

    def turn(re, im, cols):
        p_re, p_im = prop_re[:, cols], prop_im[:, cols]
        return [re * p_re - im * p_im, re * p_im + im * p_re]

    def turn_back(re, im, cols):
        p_re, p_im = prop_re[:, cols], prop_im[:, cols]
        return [re * p_re + im * p_im, im * p_re - re * p_im]

    def residual(re, im, cols):
        factor = 1.0 - amplitude[:, cols].astype(f32) * lax.rsqrt(re * re + im * im + epsilon)
        return [factor * re, factor * im]

    def pair_of(ref, index):
        return ref[index, 0].astype(f32), ref[index, 1].astype(f32)

    @pl.when(live)
    def _():
        for (flip, center), edge in zip(by_flip(centers), edges):
            patches[depth_index ^ flip, :, half:] = center[...]
            patches[depth_index ^ flip, :, :half] = edge[...]
        waves[0] = psi0[...]

        def forward(k, carry):
            t_re, t_im = pair_of(patches, k)
            p_re, p_im = pair_of(waves, k)
            n_re, n_im = propagate(t_re * p_re - t_im * p_im, t_re * p_im + t_im * p_re, turn)
            waves[k + 1, 0] = n_re.astype(bf16)
            waves[k + 1, 1] = n_im.astype(bf16)
            return carry

        lax.fori_loop(0, depth_count, forward, 0, unroll=True)
        l_re, l_im = propagate(*pair_of(waves, depth_count), residual)
        adjoint[0, 0] = l_re.astype(bf16)
        adjoint[0, 1] = l_im.astype(bf16)

        def backward(step, carry):
            k = depth_count - 1 - step
            m_re, m_im = propagate(*pair_of(adjoint, 0), turn_back)
            t_re, t_im = pair_of(patches, k)
            p_re, p_im = pair_of(waves, k)
            grads[k ^ depth_index, 0] = (p_re * m_re + p_im * m_im).astype(bf16)
            grads[k ^ depth_index, 1] = (p_re * m_im - p_im * m_re).astype(bf16)
            adjoint[0, 0] = (t_re * m_re + t_im * m_im).astype(bf16)
            adjoint[0, 1] = (t_re * m_im - t_im * m_re).astype(bf16)
            return carry

        lax.fori_loop(0, depth_count, backward, 0, unroll=True)
        for (flip, center), edge in zip(by_flip(out_centers), out_edges):
            center[...] = grads[flip, :, half:]
            edge[...] = grads[flip, :, :half]

    @pl.when(jnp.logical_not(live))
    def _():
        for ref in out_centers + out_edges:
            ref[...] = jnp.zeros(ref.shape, ref.dtype)


class Chosen:
    def __init__(self, first, info, others):
        self.first, self.info, self.others = first, info, others

    def __getitem__(self, at):
        return jnp.where(self.first, self.info[at], self.others[at])


def stack_kernel(*refs):
    pieces, (others, stacked) = refs[:-2], refs[-2:]
    for at, piece in enumerate(pieces):
        stacked[at] = piece[...]
        if at:
            others[at - 1] = piece[...]


def place(sheet, comp, at, value, base, after, to_base):
    width = value.shape[-1]
    sheet[comp, at, pl.ds(base, width)] += jnp.where(to_base, value, 0.0)
    sheet[comp, at, pl.ds(after, width)] += jnp.where(to_base, 0.0, value)


def place_edge(sheet, comp, at, piece, info, slots, slot, upper):
    value = piece[at].astype(f32)
    row, lane = iotas(*value.shape)
    base, after, first = column_place(info, slots, slot, value.shape[-1], sheet.shape[-1])
    here = jnp.logical_xor(row + at.start < info[slot], upper)
    place(sheet, comp, at, jnp.where(here, value, 0.0), base, after, lane >= first)


def place_beside_kernel(slots, own_info, second, far_own, beside, sheet):
    depth_index = lax.axis_index("depth")
    even = lax.rem(lax.axis_index("scan"), 2) == 0
    odd = jnp.logical_not(even)
    near_info = Chosen(even, own_info, second)
    far_info = Chosen(odd, own_info, second)
    whole = slice(0, sheet.shape[1])
    sheet[...] = jnp.zeros(sheet.shape, f32)
    for comp in range(2):
        place_edge(sheet, comp, whole, far_own.at[comp], far_info, slots, depth_index, odd)
        for at, (flip, _) in enumerate(by_flip(range(beside.shape[0]))):
            slot = depth_index ^ flip
            place_edge(sheet, comp, whole, beside.at[at, comp], near_info, slots, slot, even)


def place_center_kernel(slots, info, before, *refs):
    pieces, sheet = refs[:-1], refs[-1]
    depth_index = lax.axis_index("depth")
    columns = sheet.shape[-1]
    rows, width = pieces[0].shape[1:]
    _, lane = iotas(rows, width)
    sheet[...] = before[...]
    for flip, piece in by_flip(pieces):
        base, after, first = column_place(info, slots, depth_index ^ flip, width, columns)
        for comp in range(2):
            value = piece[comp].astype(f32)
            place(sheet, comp, slice(0, rows), value, base, after, lane >= first)


def place_far_kernel(slots, own_info, second, sheet, others, out, total, sems):
    depth_index = lax.axis_index("depth")
    odd = lax.rem(lax.axis_index("scan"), 2) == 1
    far_info = Chosen(odd, own_info, second)
    rows = sheet.shape[1] // 2
    copies = []
    for comp in range(2):
        for part in range(2):
            here = slice(part * rows, (part + 1) * rows)
            total[comp, here] = sheet[comp, here]
            for at, (flip, _) in enumerate(by_flip(range(others.shape[0] + 1))[1:]):
                slot = depth_index ^ flip
                place_edge(total, comp, here, others.at[at, comp], far_info, slots, slot, odd)
            copies.append(
                pltpu.make_async_copy(
                    total.at[comp, here], out.at[comp, here], sems.at[2 * comp + part]
                )
            )
            copies[-1].start()
    for copy in copies:
        copy.wait()


def body(transmission, probe_wave, prop_phase, measured, scan_rows, scan_cols, live_counts):
    pixels = probe_wave.shape[-1]
    slots = measured.shape[0]
    rows = transmission.shape[2]
    columns = transmission.shape[3]
    count = lax.axis_size("depth")
    own = transmission[0]
    own_info = jnp.concatenate([scan_rows, scan_cols, live_counts])
    ints = own_info.shape[0]
    info = shifted(jnp.pad(own_info, (0, INFO_SIZE - ints)), "scan", 1)[:ints]
    strip = call(strip_kernel, sds(own.shape, bf16), [own], [VMEM], name="strip")
    across = swapped(strip, "scan", 1)
    info, later_strip = lax.optimization_barrier((info, strip))
    beside = swapped(later_strip, "scan", 0)

    part = sds((2, rows, pixels), bf16)
    centers = call(
        functools.partial(center_kernel, slots, pixels),
        [part] * count, [info, strip], [SMEM, VMEM], name="cut_center",
    )

    def across_depth(pieces):
        return [pieces[0]] + [exchanged(piece, "depth", flip) for flip, piece in by_flip(pieces)[1:]]

    centers = across_depth(centers)

    phase, centers[0] = lax.optimization_barrier((prop_phase, centers[0]))
    order = parity_order(pixels)
    square = sds((pixels, pixels), f32)
    prop_re, prop_im, amplitude = call(
        frequency_kernel,
        [square, square, sds((pixels, pixels), bf16)],
        [phase, jnp.asarray(order), jnp.asarray(order.T), measured],
        [VMEM] * 4, flops=2400 * pixels**3, transcendentals=2 * pixels**2, name="frequency_order",
    )
    amplitude, centers[1] = lax.optimization_barrier((amplitude, centers[1]))
    amplitude = shifted(amplitude, "scan", 1)

    stack = split_tables(pixels)
    made = call(
        functools.partial(table_kernel, slots),
        [sds((2, pixels, pixels), bf16)] + [sds((pixels, pixels), bf16)] * 8,
        [info, jnp.asarray(stack), jnp.asarray(stack.T), probe_wave],
        [SMEM, VMEM, VMEM, VMEM], flops=16 * pixels**3, name="tables",
    )
    edges = call(
        functools.partial(edge_kernel, slots, pixels),
        [part] * count, [info, across, beside], [SMEM, VMEM, VMEM], name="cut_edges",
    )
    edges = across_depth(edges)

    args = [info, prop_re, prop_im, amplitude, *made, *centers, *edges]
    grads = call(
        functools.partial(wave_kernel, slots, count),
        [part] * (2 * count), args, [SMEM] + [VMEM] * (len(args) - 1),
        scratch=[
            pltpu.VMEM((count, 2, pixels, pixels), bf16),
            pltpu.VMEM((count + 1, 2, pixels, pixels), bf16),
            pltpu.VMEM((1, 2, pixels, pixels), bf16),
            pltpu.VMEM((count, 2, pixels, pixels), bf16),
        ],
        flops=(2 * count + 1) * 16 * pixels**3, name="waves",
    )
    out_centers, out_edges = grads[:count], grads[count:]
    far_own = swapped(out_edges[0], "scan", 1)
    second, out_edges = lax.optimization_barrier((own_info, out_edges))
    second = shifted(second, "scan", 2)
    out_edges = across_depth(out_edges)
    far_own, second, out_edges = lax.optimization_barrier((far_own, second, out_edges))
    others, stacked = call(
        stack_kernel, [sds((at, 2, rows, pixels), bf16) for at in (count - 1, count)],
        out_edges, [VMEM] * count, name="stack_edges",
    )
    far_others = swapped(others, "scan", 1)
    beside = swapped(stacked, "scan", 0)
    out_centers, stacked = lax.optimization_barrier((out_centers, stacked))
    out_centers = across_depth(out_centers)
    sheet_f32 = sds((2, rows, columns), f32)
    sheet = call(
        functools.partial(place_beside_kernel, slots),
        sheet_f32, [own_info, second, far_own, beside], [SMEM] * 2 + [VMEM] * 2,
        name="place_beside",
    )
    sheet = call(
        functools.partial(place_center_kernel, slots),
        sheet_f32, [info, sheet, *out_centers], [SMEM] + [VMEM] * (count + 1),
        name="place_center",
    )
    gradient = pl.pallas_call(
        functools.partial(place_far_kernel, slots),
        out_shape=sheet_f32,
        in_specs=[SMEM] * 2 + [VMEM] * 2,
        out_specs=pl.BlockSpec(memory_space=pl.ANY),
        scratch_shapes=[pltpu.VMEM(sheet_f32.shape, f32), pltpu.SemaphoreType.DMA((4,))],
        compiler_params=pltpu.CompilerParams(vmem_limit_bytes=LIMIT),
        name="place_far",
    )(own_info, second, sheet, far_others)
    return gradient[None]


def solution(mesh):
    in_specs = (
        P("depth", None, "scan", None),
        P(),
        P(),
        P("scan", None, None),
        P("scan"),
        P("scan"),
        P("scan"),
    )
    out_specs = P("depth", None, "scan", None)
    return jax.shard_map(body, mesh=mesh, in_specs=in_specs, out_specs=out_specs, check_vma=False)
```

```python
import functools
import math

import jax
import jax.numpy as jnp
import ml_dtypes
import numpy as np
from jax import lax
from jax.experimental import pallas as pl
from jax.experimental.pallas import tpu as pltpu
from jax.sharding import PartitionSpec as P

epsilon = 1.0
bf16 = jnp.bfloat16
f32 = jnp.float32
VMEM = pl.BlockSpec(memory_space=pltpu.VMEM)
SMEM = pl.BlockSpec(memory_space=pltpu.SMEM)
LIMIT = 48 * 1024 * 1024
INFO_SIZE = 8192


def shifted(value, axis, steps):
    count = lax.axis_size(axis)
    pairs = [(source, (source + steps) % count) for source in range(count)]
    return lax.ppermute(value, axis, pairs)


def swapped(value, axis, first):
    count = lax.axis_size(axis)
    pairs = [
        (source, (source + (1 if source % 2 == first else -1)) % count) for source in range(count)
    ]
    return lax.ppermute(value, axis, pairs)


def exchanged(value, axis, flip):
    count = lax.axis_size(axis)
    return lax.ppermute(value, axis, [(source, source ^ flip) for source in range(count)])


def split_tables(pixels):
    indices = np.arange(pixels)
    angles = (indices[:, None] * indices[None, :] % pixels) * (2.0 * math.pi / pixels)
    norm_scale = 1.0 / math.sqrt(pixels)
    table_re = (np.cos(angles) * norm_scale).astype(np.float32).astype(ml_dtypes.bfloat16)
    table_im = (-np.sin(angles) * norm_scale).astype(np.float32).astype(ml_dtypes.bfloat16)
    return np.concatenate([table_re[0::2], table_im[0::2], table_re[1::2], table_im[1::2]], axis=0)


def parity_order(pixels):
    order = np.concatenate([np.arange(0, pixels, 2), np.arange(1, pixels, 2)])
    return (order[:, None] == np.arange(pixels)[None, :]).astype(np.float32)


def call(kernel, out_shape, args, specs, scratch=(), flops=0, transcendentals=0, name=None):
    outs = out_shape if isinstance(out_shape, (list, tuple)) else [out_shape]
    moved = sum(math.prod(a.shape) * a.dtype.itemsize for a in list(args) + list(outs))
    return pl.pallas_call(
        kernel,
        out_shape=out_shape,
        in_specs=specs,
        out_specs=jax.tree.map(lambda _: VMEM, out_shape),
        scratch_shapes=list(scratch),
        compiler_params=pltpu.CompilerParams(vmem_limit_bytes=LIMIT),
        cost_estimate=pl.CostEstimate(
            flops=flops, bytes_accessed=moved, transcendentals=transcendentals
        ),
        name=name,
    )(*args)


def sds(shape, dtype):
    return jax.ShapeDtypeStruct(shape, dtype)


def by_flip(pieces):
    return list(zip([0, *range(len(pieces) - 1, 0, -1)], pieces))


def column_place(info, slots, slot, width, columns):
    col = info[slots + slot]
    base = (col // width) * width
    after = jnp.minimum(base + width, columns - width)
    return pl.multiple_of(base, width), pl.multiple_of(after, width), col - base


def iotas(rows, cols):
    return (
        lax.broadcasted_iota(jnp.int32, (rows, cols), 0),
        lax.broadcasted_iota(jnp.int32, (rows, cols), 1),
    )


def strip_kernel(own, strip):
    strip[...] = own[...].astype(bf16)


def center_kernel(slots, width, info, strip, *outs):
    depth_index = lax.axis_index("depth")
    columns = strip.shape[-1]
    _, lane = iotas(strip.shape[1], width)
    for flip, out in by_flip(outs):
        base, after, first = column_place(info, slots, depth_index ^ flip, width, columns)
        for comp in range(2):
            out[comp] = jnp.where(
                lane >= first,
                strip[comp, :, pl.ds(base, width)].astype(f32),
                strip[comp, :, pl.ds(after, width)].astype(f32),
            ).astype(bf16)


def edge_kernel(slots, width, info, across, beside, *outs):
    depth_index = lax.axis_index("depth")
    even = lax.rem(lax.axis_index("scan"), 2) == 0
    columns = across.shape[-1]
    row, lane = iotas(across.shape[1], width)
    for flip, out in by_flip(outs):
        slot = depth_index ^ flip
        base, after, first = column_place(info, slots, slot, width, columns)
        from_across = jnp.logical_xor(row < info[slot], even)

        def rows_at(comp, place):
            return jnp.where(
                from_across,
                across[comp, :, pl.ds(place, width)].astype(f32),
                beside[comp, :, pl.ds(place, width)].astype(f32),
            )

        for comp in range(2):
            out[comp] = jnp.where(
                lane >= first, rows_at(comp, base), rows_at(comp, after)
            ).astype(bf16)


def frequency_kernel(phase, order, order_t, measured, prop_re, prop_im, amplitude):
    def reorder(value):
        rows = jnp.dot(
            order[...], value, preferred_element_type=f32, precision=lax.Precision.HIGHEST
        )
        return jnp.dot(
            rows, order_t[...], preferred_element_type=f32, precision=lax.Precision.HIGHEST
        )

    turned = reorder(phase[...])
    prop_re[...] = jnp.cos(turned)
    prop_im[...] = jnp.sin(turned)
    amplitude[...] = reorder(measured[lax.axis_index("depth")]).astype(bf16)


def table_kernel(slots, info, stack, stack_t, probe, psi0, *tables):
    depth_index = lax.axis_index("depth")
    pixels = probe.shape[-1]
    half = pixels // 2
    row_shift = info[depth_index]
    col_shift = lax.rem(info[slots + depth_index], pixels)

    def shift_matrix(rows, cols, shift, transposed):
        row, lane = iotas(rows, cols)
        offset = (lane - row if transposed else row - lane) + shift
        return jnp.where((offset == 0) | (offset == pixels), 1.0, 0.0).astype(bf16)

    def pair(shift):
        cols = jnp.dot(
            stack[...], shift_matrix(pixels, half, shift, False), preferred_element_type=f32
        )
        rows = jnp.dot(
            shift_matrix(half, pixels, shift, True), stack_t[...], preferred_element_type=f32
        )
        forms, forms_t = [], []
        for parity in range(2):
            at = 2 * parity * half
            re, im = cols[at : at + half], cols[at + half : at + pixels]
            top = jnp.concatenate([re, -im], axis=1)
            bottom = jnp.concatenate([im, re], axis=1)
            forms.append(jnp.concatenate([top, bottom], axis=0).astype(bf16))
            re, im = rows[:, at : at + half], rows[:, at + half : at + pixels]
            top = jnp.concatenate([re, im], axis=1)
            bottom = jnp.concatenate([-im, re], axis=1)
            forms_t.append(jnp.concatenate([top, bottom], axis=0).astype(bf16))
        return forms, forms_t

    row_forms, row_forms_t = pair(row_shift)
    col_forms, col_forms_t = pair(col_shift)
    made = row_forms + col_forms_t + col_forms + row_forms_t
    for ref, value in zip(tables, made):
        ref[...] = value
    down = shift_matrix(pixels, pixels, row_shift, True)
    across = shift_matrix(pixels, pixels, col_shift, False)
    for comp in range(2):
        moved = jnp.dot(down, probe[comp].astype(bf16), preferred_element_type=f32).astype(bf16)
        psi0[comp] = jnp.dot(moved, across, preferred_element_type=f32).astype(bf16)


def wave_kernel(slots, depth_count, info, prop_re, prop_im, amplitude, psi0, *refs):
    tables = refs[:8]
    centers = refs[8 : 8 + depth_count]
    edges = refs[8 + depth_count : 8 + 2 * depth_count]
    out_centers = refs[8 + 2 * depth_count : 8 + 3 * depth_count]
    out_edges = refs[8 + 3 * depth_count : 8 + 4 * depth_count]
    patches, waves, grads = refs[8 + 4 * depth_count :]
    depth_index = lax.axis_index("depth")
    pixels = psi0.shape[-1]
    half = pixels // 2
    live = depth_index < info[2 * slots]
    fwd_row_e, fwd_row_o, fwd_col_e, fwd_col_o, inv_col_e, inv_col_o, inv_row_e, inv_row_o = tables

    def dot(left, right):
        return jnp.dot(left, right, preferred_element_type=f32)

    def propagate(x_re, x_im, at_frequency):
        def rows_of(sign):
            mixed = [v[:half] + v[half:] if sign > 0 else v[:half] - v[half:] for v in (x_re, x_im)]
            return jnp.concatenate(mixed, axis=0).astype(bf16)

        u_even = dot(fwd_row_e[...], rows_of(1))
        u_odd = dot(fwd_row_o[...], rows_of(-1))

        def cols_of(sign):
            parts = []
            for u in (u_even, u_odd):
                mixed = u[:, :half] + u[:, half:] if sign > 0 else u[:, :half] - u[:, half:]
                parts.append(jnp.concatenate([mixed[:half], mixed[half:]], axis=1))
            return jnp.concatenate(parts, axis=0).astype(bf16)

        v_even = dot(cols_of(1), fwd_col_e[...])
        v_odd = dot(cols_of(-1), fwd_col_o[...])
        b_even = at_frequency(v_even[:, :half], v_even[:, half:], slice(0, half))
        b_odd = at_frequency(v_odd[:, :half], v_odd[:, half:], slice(half, pixels))
        w_even = dot(jnp.concatenate(b_even, axis=1).astype(bf16), inv_col_e[...])
        w_odd = dot(jnp.concatenate(b_odd, axis=1).astype(bf16), inv_col_o[...])
        w_low, w_high = w_even + w_odd, w_even - w_odd
        w_re = jnp.concatenate([w_low[:, :half], w_high[:, :half]], axis=1)
        w_im = jnp.concatenate([w_low[:, half:], w_high[:, half:]], axis=1)
        y_even = dot(
            inv_row_e[...], jnp.concatenate([w_re[:half], w_im[:half]], axis=0).astype(bf16)
        )
        y_odd = dot(
            inv_row_o[...], jnp.concatenate([w_re[half:], w_im[half:]], axis=0).astype(bf16)
        )
        low, high = y_even + y_odd, y_even - y_odd
        return (
            jnp.concatenate([low[:half], high[:half]], axis=0),
            jnp.concatenate([low[half:], high[half:]], axis=0),
        )

    def turn(re, im, cols):
        p_re, p_im = prop_re[:, cols], prop_im[:, cols]
        return [re * p_re - im * p_im, re * p_im + im * p_re]

    def turn_back(re, im, cols):
        p_re, p_im = prop_re[:, cols], prop_im[:, cols]
        return [re * p_re + im * p_im, im * p_re - re * p_im]

    def residual(re, im, cols):
        factor = 1.0 - amplitude[:, cols].astype(f32) * lax.rsqrt(re * re + im * im + epsilon)
        return [factor * re, factor * im]

    def pair_of(ref, index):
        return ref[index, 0].astype(f32), ref[index, 1].astype(f32)

    @pl.when(live)
    def _():
        for (flip, center), edge in zip(by_flip(centers), edges):
            patches[depth_index ^ flip, :, half:] = center[...]
            patches[depth_index ^ flip, :, :half] = edge[...]
        waves[0] = psi0[...]
        wave = pair_of(waves, 0)
        for k in range(depth_count):
            t_re, t_im = pair_of(patches, k)
            p_re, p_im = wave
            moved = propagate(t_re * p_re - t_im * p_im, t_re * p_im + t_im * p_re, turn)
            n_re, n_im = [v.astype(bf16) for v in moved]
            if k + 1 < depth_count:
                waves[k + 1, 0], waves[k + 1, 1] = n_re, n_im
            wave = n_re.astype(f32), n_im.astype(f32)
        adjoint = propagate(*wave, residual)
        for k in range(depth_count - 1, -1, -1):
            l_re, l_im = [v.astype(bf16).astype(f32) for v in adjoint]
            m_re, m_im = propagate(l_re, l_im, turn_back)
            t_re, t_im = pair_of(patches, k)
            p_re, p_im = pair_of(waves, k)
            grads[k ^ depth_index, 0] = (p_re * m_re + p_im * m_im).astype(bf16)
            grads[k ^ depth_index, 1] = (p_re * m_im - p_im * m_re).astype(bf16)
            adjoint = t_re * m_re + t_im * m_im, t_re * m_im - t_im * m_re
        for (flip, center), edge in zip(by_flip(out_centers), out_edges):
            center[...] = grads[flip, :, half:]
            edge[...] = grads[flip, :, :half]

    @pl.when(jnp.logical_not(live))
    def _():
        for ref in out_centers + out_edges:
            ref[...] = jnp.zeros(ref.shape, ref.dtype)


class Chosen:
    def __init__(self, first, info, others):
        self.first, self.info, self.others = first, info, others

    def __getitem__(self, at):
        return jnp.where(self.first, self.info[at], self.others[at])


def stack_kernel(*refs):
    pieces, (others, stacked) = refs[:-2], refs[-2:]
    for at, piece in enumerate(pieces):
        stacked[at] = piece[...]
        if at:
            others[at - 1] = piece[...]


def place(sheet, comp, at, value, base, after, to_base):
    width = value.shape[-1]
    sheet[comp, at, pl.ds(base, width)] += jnp.where(to_base, value, 0.0)
    sheet[comp, at, pl.ds(after, width)] += jnp.where(to_base, 0.0, value)


def place_edge(sheet, comp, at, piece, info, slots, slot, upper):
    value = piece[at].astype(f32)
    row, lane = iotas(*value.shape)
    base, after, first = column_place(info, slots, slot, value.shape[-1], sheet.shape[-1])
    here = jnp.logical_xor(row + at.start < info[slot], upper)
    place(sheet, comp, at, jnp.where(here, value, 0.0), base, after, lane >= first)


def place_beside_kernel(slots, own_info, second, far_own, beside, sheet):
    depth_index = lax.axis_index("depth")
    even = lax.rem(lax.axis_index("scan"), 2) == 0
    odd = jnp.logical_not(even)
    near_info = Chosen(even, own_info, second)
    far_info = Chosen(odd, own_info, second)
    whole = slice(0, sheet.shape[1])
    sheet[...] = jnp.zeros(sheet.shape, f32)
    for comp in range(2):
        place_edge(sheet, comp, whole, far_own.at[comp], far_info, slots, depth_index, odd)
        for at, (flip, _) in enumerate(by_flip(range(beside.shape[0]))):
            slot = depth_index ^ flip
            place_edge(sheet, comp, whole, beside.at[at, comp], near_info, slots, slot, even)


def place_center_kernel(slots, info, before, *refs):
    pieces, sheet = refs[:-1], refs[-1]
    depth_index = lax.axis_index("depth")
    columns = sheet.shape[-1]
    rows, width = pieces[0].shape[1:]
    _, lane = iotas(rows, width)
    sheet[...] = before[...]
    for flip, piece in by_flip(pieces):
        base, after, first = column_place(info, slots, depth_index ^ flip, width, columns)
        for comp in range(2):
            value = piece[comp].astype(f32)
            place(sheet, comp, slice(0, rows), value, base, after, lane >= first)


def place_far_kernel(slots, own_info, second, sheet, others, out, total, sems):
    depth_index = lax.axis_index("depth")
    odd = lax.rem(lax.axis_index("scan"), 2) == 1
    far_info = Chosen(odd, own_info, second)
    rows = sheet.shape[1] // 2
    copies = []
    for comp in range(2):
        for part in range(2):
            here = slice(part * rows, (part + 1) * rows)
            total[comp, here] = sheet[comp, here]
            for at, (flip, _) in enumerate(by_flip(range(others.shape[0] + 1))[1:]):
                slot = depth_index ^ flip
                place_edge(total, comp, here, others.at[at, comp], far_info, slots, slot, odd)
            copies.append(
                pltpu.make_async_copy(
                    total.at[comp, here], out.at[comp, here], sems.at[2 * comp + part]
                )
            )
            copies[-1].start()
    for copy in copies:
        copy.wait()


def body(transmission, probe_wave, prop_phase, measured, scan_rows, scan_cols, live_counts):
    pixels = probe_wave.shape[-1]
    slots = measured.shape[0]
    rows = transmission.shape[2]
    columns = transmission.shape[3]
    count = lax.axis_size("depth")
    own = transmission[0]
    own_info = jnp.concatenate([scan_rows, scan_cols, live_counts])
    ints = own_info.shape[0]
    info = shifted(jnp.pad(own_info, (0, INFO_SIZE - ints)), "scan", 1)[:ints]
    strip = call(strip_kernel, sds(own.shape, bf16), [own], [VMEM], name="strip")
    across = swapped(strip, "scan", 1)
    info, later_strip = lax.optimization_barrier((info, strip))
    beside = swapped(later_strip, "scan", 0)

    part = sds((2, rows, pixels), bf16)
    centers = call(
        functools.partial(center_kernel, slots, pixels),
        [part] * count, [info, strip], [SMEM, VMEM], name="cut_center",
    )

    def across_depth(pieces):
        return [pieces[0]] + [exchanged(piece, "depth", flip) for flip, piece in by_flip(pieces)[1:]]

    centers = across_depth(centers)

    phase, centers[0] = lax.optimization_barrier((prop_phase, centers[0]))
    order = parity_order(pixels)
    square = sds((pixels, pixels), f32)
    prop_re, prop_im, amplitude = call(
        frequency_kernel,
        [square, square, sds((pixels, pixels), bf16)],
        [phase, jnp.asarray(order), jnp.asarray(order.T), measured],
        [VMEM] * 4, flops=2400 * pixels**3, transcendentals=2 * pixels**2, name="frequency_order",
    )
    amplitude, centers[1] = lax.optimization_barrier((amplitude, centers[1]))
    amplitude = shifted(amplitude, "scan", 1)

    stack = split_tables(pixels)
    made = call(
        functools.partial(table_kernel, slots),
        [sds((2, pixels, pixels), bf16)] + [sds((pixels, pixels), bf16)] * 8,
        [info, jnp.asarray(stack), jnp.asarray(stack.T), probe_wave],
        [SMEM, VMEM, VMEM, VMEM], flops=16 * pixels**3, name="tables",
    )
    edges = call(
        functools.partial(edge_kernel, slots, pixels),
        [part] * count, [info, across, beside], [SMEM, VMEM, VMEM], name="cut_edges",
    )
    edges = across_depth(edges)

    args = [info, prop_re, prop_im, amplitude, *made, *centers, *edges]
    grads = call(
        functools.partial(wave_kernel, slots, count),
        [part] * (2 * count), args, [SMEM] + [VMEM] * (len(args) - 1),
        scratch=[
            pltpu.VMEM((count, 2, pixels, pixels), bf16),
            pltpu.VMEM((count, 2, pixels, pixels), bf16),
            pltpu.VMEM((count, 2, pixels, pixels), bf16),
        ],
        flops=(2 * count + 1) * 16 * pixels**3, name="waves",
    )
    out_centers, out_edges = grads[:count], grads[count:]
    far_own = swapped(out_edges[0], "scan", 1)
    second, out_edges = lax.optimization_barrier((own_info, out_edges))
    second = shifted(second, "scan", 2)
    out_edges = across_depth(out_edges)
    far_own, second, out_edges = lax.optimization_barrier((far_own, second, out_edges))
    others, stacked = call(
        stack_kernel, [sds((at, 2, rows, pixels), bf16) for at in (count - 1, count)],
        out_edges, [VMEM] * count, name="stack_edges",
    )
    far_others = swapped(others, "scan", 1)
    beside = swapped(stacked, "scan", 0)
    out_centers, stacked = lax.optimization_barrier((out_centers, stacked))
    out_centers = across_depth(out_centers)
    sheet_f32 = sds((2, rows, columns), f32)
    sheet = call(
        functools.partial(place_beside_kernel, slots),
        sheet_f32, [own_info, second, far_own, beside], [SMEM] * 2 + [VMEM] * 2,
        name="place_beside",
    )
    sheet = call(
        functools.partial(place_center_kernel, slots),
        sheet_f32, [info, sheet, *out_centers], [SMEM] + [VMEM] * (count + 1),
        name="place_center",
    )
    gradient = pl.pallas_call(
        functools.partial(place_far_kernel, slots),
        out_shape=sheet_f32,
        in_specs=[SMEM] * 2 + [VMEM] * 2,
        out_specs=pl.BlockSpec(memory_space=pl.ANY),
        scratch_shapes=[pltpu.VMEM(sheet_f32.shape, f32), pltpu.SemaphoreType.DMA((4,))],
        compiler_params=pltpu.CompilerParams(vmem_limit_bytes=LIMIT),
        name="place_far",
    )(own_info, second, sheet, far_others)
    return gradient[None]


def solution(mesh):
    in_specs = (
        P("depth", None, "scan", None),
        P(),
        P(),
        P("scan", None, None),
        P("scan"),
        P("scan"),
        P("scan"),
    )
    out_specs = P("depth", None, "scan", None)
    return jax.shard_map(body, mesh=mesh, in_specs=in_specs, out_specs=out_specs, check_vma=False)
```
